32 devices in a mesh: prompt: 4 (over y, x), resp: 8 (over z, core).
Axes of the slice: x: 2, y: 2, z: 4, core: 2. Of those that a mesh axis runs over, the one named last changes fastest.
Arguments:
- question_key_matrix: bfloat16 [8, 1024, 256], P('resp', 'prompt'), may hold values from -0.31835938 to 0.31835938
- prompt_values: bfloat16 [8, 1024, 256], P('resp', 'prompt'), may hold values from -6 to 6
- prompt_gates: float32 [8, 2, 1024], P('resp', None, 'prompt'), may hold values from -2.3 to 0, as said below
- resp_queries: bfloat16 [128, 512, 256], P(('prompt', 'resp')), may hold values from -0.31835938 to 0.31835938
- resp_keys: bfloat16 [128, 512, 256], P(('prompt', 'resp')), may hold values from -0.31835938 to 0.31835938
- response_value_rows: bfloat16 [128, 512, 256], P(('prompt', 'resp')), may hold values from -6 to 6
- resp_gates: float32 [128, 2, 512], P(('prompt', 'resp')), may hold values from -2.3 to 0, as said below
- resp_cotangent: bfloat16 [128, 512, 256], P(('prompt', 'resp')), may hold values from -0.59765625 to 0.59765625
- group_ids: int32 [128], P(('prompt', 'resp')), may hold values from 0 to 7, as said below
- resp_lengths: int32 [32, 4], P(('prompt', 'resp')), may hold values from 1 to 512, 1536 in all within a row
- loss_mask: int32 [128, 512], P(('prompt', 'resp')), may hold values 0 or 1
- advantages: int32 [128], P(('prompt', 'resp')), may hold values from -2048 to 2048
Outputs:
- resp_out: bfloat16 [128, 512, 256], P(('prompt', 'resp'))
- resp_dq: bfloat16 [128, 512, 256], P(('prompt', 'resp'))
- answer_key_derivative: bfloat16 [128, 512, 256], P(('prompt', 'resp'))
- resp_dv: bfloat16 [128, 512, 256], P(('prompt', 'resp'))
- prompt_dk: bfloat16 [8, 1024, 256], P('resp', 'prompt')
- prompt_dv: bfloat16 [8, 1024, 256], P('resp', 'prompt')
The draws below stay inside these ranges and needn't reach their ends.
Inputs may be any that keep to these rules, and one draw needn't show every extreme that they name: `group_ids`: never falling along the responses; every prompt has at least one response. `resp_lengths`: the lengths of one device's 4 responses sum to 1536. `prompt_gates`: negative log decays. `resp_gates`: negative log decays.
All inputs are finite; a program needn't handle non-finite values. No bound on the sum of `loss_mask` on one device may be relied on, other than what follows from the above.
Results may differ from the reference program's by a relative error of at most 0.012.
Values may be sent and summed in bfloat16 or wider, within the bound.
No kernel may reach another device: no remote copies, remote signals or barrier semaphores. Data moves between devices by JAX's collectives and lax.ppermute only.
A program may use at most 64 MiB of HBM per device.

```python
import math
import jax
import jax.numpy as jnp
import numpy as np
from jax import lax

H = 2
DH = 128
RMAX = 512
RESP_DEV = 4
NPR = 8
PLEN = 1024
NRESP = 128
LIVE_DEV = 1536
N_PROMPT = 4
N_RESP = 8


def gate_law(key, rows, token_count):
    keys_all = jax.random.split(key, 4)
    slow_head = jax.random.randint(keys_all[0], (rows, 1), 0, H)
    slow = jnp.arange(H)[None, :] == slow_head
    factor = jnp.exp(jax.random.uniform(keys_all[1], (rows, H, token_count), jnp.float32, -0.7, 0.7))
    slow_rate = math.log(10.0) / (4.0 * token_count)
    fading_multiplier = jnp.where(slow[:, :, None], slow_rate, 1.0 / 40.0) * factor
    place_indices = jax.random.randint(keys_all[2], (rows, H, 3), 0, token_count)
    discarded_places = jnp.log(jax.random.uniform(keys_all[3], (rows, H, 3), jnp.float32, 0.5, 0.8))
    cohort_batch = jnp.sum(jnp.where(place_indices[..., None] == jnp.arange(token_count), discarded_places[..., None], 0.0), axis=2)
    return (cohort_batch - fading_multiplier).astype(jnp.float32)


def draw_prompt_gates(key, part):
    return gate_law(key, NPR, PLEN)


def draw_resp_gates(key, part):
    return gate_law(key, NRESP, RMAX)


def draw_group_ids(key, part):
    base = jnp.arange(NPR, dtype=jnp.int32)
    extra = jax.random.randint(key, (NRESP - NPR,), 0, NPR, dtype=jnp.int32)
    return jnp.sort(jnp.concatenate([base, extra]))


def plant(array, rng, least, largest):
    longest = array.shape.index(max(array.shape))
    spots = []
    for shift in (0, 1):
        where = [jax.random.randint(jax.random.fold_in(rng, axis), (), 0, length) for axis, length in enumerate(array.shape)]
        where[longest] = (where[longest] + shift) % array.shape[longest]
        spots.append(tuple(where))
    return array.at[spots[0]].set(least).at[spots[1]].set(largest)


def shard_levels(rng, extent, cuts, low, largest):
    gain = 1.0
    for axis_at, parts in cuts:
        draws = jax.random.uniform(jax.random.fold_in(jax.random.fold_in(rng, 6), axis_at), (parts,), jnp.float32, low / len(cuts), largest / len(cuts))
        gain = gain * jnp.repeat(jnp.exp(draws), extent[axis_at] // parts).reshape((-1,) + (1,) * (len(extent) - 1 - axis_at))
    return gain


def profile(amount, total, limit, lean):
    weights = [(1 << 20) // math.isqrt(grade ** lean) + 1 for grade in range(2, amount + 1)]
    spare, counts = total - limit - (amount - 1), [1] * (amount - 1)
    while spare > 0:
        candidates = [i for i in range(amount - 1) if counts[i] < limit]
        whole, budget = sum([weights[i] for i in candidates]), spare
        for i in candidates:
            addition = min(limit - counts[i], max(1, budget * weights[i] // whole), spare)
            counts[i] = counts[i] + addition
            spare = spare - addition
    return np.array([limit] + counts)


def ragged_sizes(key, amount, total, limit, skew):
    if amount == 2:
        one = jax.random.randint(key, (), max(1, total - limit), min(limit, total - 1) + 1)
        return jnp.stack([one, total - one])
    tallies = jnp.asarray(profile(amount, total, limit, skew), jnp.int32)
    couples = (amount - 1) // 2
    source_of, taker = tallies[1:1 + 2 * couples:2], tallies[2:2 + 2 * couples:2]
    room = jnp.minimum(source_of - 1, limit - taker)
    moved = jax.random.randint(jax.random.fold_in(key, 1), (couples,), 0, 1 << 20) % (room + 1)
    tallies = tallies.at[1:1 + 2 * couples:2].set(source_of - moved).at[2:2 + 2 * couples:2].set(taker + moved)
    return tallies[jax.random.permutation(jax.random.fold_in(key, 2), amount)]


def noise(key, extent, scale, limit, cuts=(), kind=jnp.bfloat16):
    values = jax.random.normal(key, extent, jnp.float32) * scale
    if len(cuts) > 0:
        values = shard_levels(key, extent, cuts, -0.22, 0.18) * values
    return jnp.clip(values, min=-limit, max=limit).astype(kind)


def setup_inputs(seed: int = 0) -> dict:
    key_list = jax.random.split(jax.random.key(seed), 13)
    question_key_matrix = noise(key_list[0], (NPR, PLEN, H * DH), 0.053, 0.31835938, ((0, 8), (1, 4)))
    prompt_values = noise(key_list[1], (NPR, PLEN, H * DH), 1.0, 6.0, ((0, 8), (1, 4)))
    prompt_gates = draw_prompt_gates(jax.random.fold_in(key_list[12], 71), 0)
    resp_queries = noise(key_list[3], (NRESP, RMAX, H * DH), 0.053, 0.31835938, ((0, 32),))
    resp_keys = noise(key_list[4], (NRESP, RMAX, H * DH), 0.053, 0.31835938, ((0, 32),))
    response_value_rows = noise(key_list[5], (NRESP, RMAX, H * DH), 1.0, 6.0, ((0, 32),))
    resp_gates = draw_resp_gates(jax.random.fold_in(key_list[12], 71), 0)
    resp_cotangent = noise(key_list[7], (NRESP, RMAX, H * DH), 0.1, 0.59765625, ((0, 32),))
    group_ids = draw_group_ids(jax.random.fold_in(key_list[12], 71), 0)
    resp_lengths = jax.vmap(lambda own: ragged_sizes(own, RESP_DEV, LIVE_DEV, RMAX, 2))(jax.random.split(key_list[9], (N_PROMPT * N_RESP))).reshape((N_PROMPT * N_RESP, RESP_DEV)).astype(jnp.int32)
    loss_mask = plant((jax.random.randint(key_list[10], (NRESP, RMAX), 0, 4) < 3).astype(jnp.int32), jax.random.fold_in(key_list[10], 1), 0, 1)
    advantages = plant(jax.random.randint(key_list[11], (NRESP,), -2048, 2049), jax.random.fold_in(key_list[11], 1), -2048, 2048).astype(jnp.int32)
    return dict(question_key_matrix=question_key_matrix, prompt_values=prompt_values, prompt_gates=prompt_gates, resp_queries=resp_queries, resp_keys=resp_keys, response_value_rows=response_value_rows, resp_gates=resp_gates, resp_cotangent=resp_cotangent, group_ids=group_ids, resp_lengths=resp_lengths, loss_mask=loss_mask, advantages=advantages)


def head_pass(query_h, key_h, value_h, gate_h, start_h, cot_h, weight, live_rows, open_rows):
    cum_gate = jnp.cumsum(gate_h)
    places = jnp.arange(gate_h.shape[0])
    causal = places[:, None] >= places[None, :]
    decay = jnp.where(causal, jnp.exp(jnp.where(causal, cum_gate[:, None] - cum_gate[None, :], 0.0)), 0.0)
    carried = jnp.exp(cum_gate)[:, None]
    start_b = start_h.astype(jnp.bfloat16)
    scores = jnp.dot(query_h, key_h.T, preferred_element_type=jnp.float32)
    mixing = (scores * decay).astype(jnp.bfloat16)
    output = carried * jnp.dot(query_h, start_b, preferred_element_type=jnp.float32)
    output = (output + jnp.dot(mixing, value_h, preferred_element_type=jnp.float32)) * open_rows[:, None]
    grad_out = (cot_h.astype(jnp.float32) * (live_rows * weight)[:, None]).astype(jnp.bfloat16)
    grad_mix = jnp.dot(grad_out, value_h.T, preferred_element_type=jnp.float32)
    grad_scores = (grad_mix * decay).astype(jnp.bfloat16)
    grad_query = jnp.dot(grad_scores, key_h, preferred_element_type=jnp.float32)
    grad_query = grad_query + carried * jnp.dot(grad_out, start_b.T, preferred_element_type=jnp.float32)
    grad_key = jnp.dot(grad_scores.T, query_h, preferred_element_type=jnp.float32)
    grad_value = jnp.dot(mixing.T, grad_out, preferred_element_type=jnp.float32)
    scaled_out = (carried * grad_out.astype(jnp.float32)).astype(jnp.bfloat16)
    opening_memory_derivative = jnp.dot(query_h.T, scaled_out, preferred_element_type=jnp.float32)
    return output, grad_query, grad_key, grad_value, opening_memory_derivative


def response_sweep(queries, keys_in, values, gates, start, cotangent, weight, live_rows, open_rows):
    width = start.shape[1]
    pieces = []
    for head_index in range(start.shape[0]):
        lower = head_index * width
        upper = lower + width
        pieces.append(head_pass(queries[:, lower:upper], keys_in[:, lower:upper], values[:, lower:upper],
                                gates[head_index], start[head_index], cotangent[:, lower:upper],
                                weight, live_rows, open_rows))
    joined = [jnp.concatenate([entry[slot] for entry in pieces], axis=1).astype(jnp.bfloat16) for slot in range(4)]
    opening_memory_derivative = jnp.stack([entry[4] for entry in pieces])
    return joined[0], joined[1], joined[2], joined[3], opening_memory_derivative


def prompt_state(keys_in, values, gates):
    width = keys_in.shape[1] // gates.shape[0]
    states = []
    for head_index in range(gates.shape[0]):
        lower = head_index * width
        suffix = jnp.cumsum(gates[head_index][::-1])[::-1] - gates[head_index]
        key_f = keys_in[:, lower:lower + width].astype(jnp.float32)
        value_f = values[:, lower:lower + width].astype(jnp.float32)
        states.append(jnp.dot(key_f.T, jnp.exp(suffix)[:, None] * value_f, precision=lax.Precision.HIGHEST))
    return jnp.stack(states)


def prompt_grads(keys_in, values, gates, grad_state):
    width = keys_in.shape[1] // gates.shape[0]
    grad_keys = []
    grad_values = []
    for head_index in range(gates.shape[0]):
        lower = head_index * width
        suffix = jnp.cumsum(gates[head_index][::-1])[::-1] - gates[head_index]
        factor = jnp.exp(suffix)[:, None]
        key_f = keys_in[:, lower:lower + width].astype(jnp.float32)
        value_f = values[:, lower:lower + width].astype(jnp.float32)
        grad_keys.append(factor * jnp.dot(value_f, grad_state[head_index].T, precision=lax.Precision.HIGHEST))
        grad_values.append(factor * jnp.dot(key_f, grad_state[head_index], precision=lax.Precision.HIGHEST))
    return (jnp.concatenate(grad_keys, axis=1).astype(jnp.bfloat16),
            jnp.concatenate(grad_values, axis=1).astype(jnp.bfloat16))


def reference(question_key_matrix, prompt_values, prompt_gates, resp_queries, resp_keys, response_value_rows, resp_gates,
              resp_cotangent, group_ids, resp_lengths, loss_mask, advantages):
    def state_item(item):
        return prompt_state(item[0], item[1], item[2])

    states = lax.map(state_item, (question_key_matrix, prompt_values, prompt_gates))
    lengths = resp_lengths.reshape(-1)
    places = jnp.arange(RMAX)
    open_rows = (places[None, :] < lengths[:, None]).astype(jnp.float32)
    live_rows = loss_mask.astype(jnp.float32) * open_rows
    weights = advantages.astype(jnp.float32) / 1024.0

    def resp_item(item):
        start = lax.dynamic_index_in_dim(states, item[5].astype(jnp.int32), 0, keepdims=False)
        return response_sweep(item[0], item[1], item[2], item[3], start, item[4], item[6], item[7], item[8])

    outs = lax.map(resp_item, (resp_queries, resp_keys, response_value_rows, resp_gates, resp_cotangent,
                               group_ids, weights, live_rows, open_rows))
    grad_final = jax.ops.segment_sum(outs[4], group_ids, num_segments=NPR)

    def grad_item(item):
        return prompt_grads(item[0], item[1], item[2], item[3])

    prompt_dk, prompt_dv = lax.map(grad_item, (question_key_matrix, prompt_values, prompt_gates, grad_final))
    return (outs[0], outs[1], outs[2], outs[3], prompt_dk, prompt_dv)
```

```python
import jax
import jax.numpy as jnp
from jax import lax
from jax.experimental import pallas as pl
from jax.experimental.pallas import tpu as pltpu
from jax.sharding import PartitionSpec as P

H = 2
DH = 128
HALF = 256
F32 = jnp.float32
BF16 = jnp.bfloat16
NEVER = -1e30
VMEM = pl.BlockSpec(memory_space=pltpu.VMEM)
SMEM = pl.BlockSpec(memory_space=pltpu.SMEM)


def params():
    return pltpu.CompilerParams(vmem_limit_bytes=40 * 1024 * 1024)


def mm(a, b):
    return lax.dot_general(a, b, (((1,), (0,)), ((), ())), preferred_element_type=F32)


def mm_nt(a, b):
    return lax.dot_general(a, b, (((1,), (1,)), ((), ())), preferred_element_type=F32)


def mm_tn(a, b):
    return lax.dot_general(a, b, (((0,), (0,)), ((), ())), preferred_element_type=F32)


def lane_cumsum(x):
    width = x.shape[1]
    lane = lax.broadcasted_iota(jnp.int32, x.shape, 1)
    step = 1
    while step < width:
        x = x + jnp.where(lane >= step, pltpu.roll(x, step, 1), 0.0)
        step *= 2
    return x


def to_columns(rows):
    padded = jnp.concatenate([rows, jnp.zeros((128 - rows.shape[0], rows.shape[1]), F32)], axis=0)
    return padded.T


def piece_kernel(n, me_ref, keys_ref, values_ref, gates_ref, *refs):
    outs, suffix_ref, state = refs[:n], refs[n], refs[n + 1]
    gates = gates_ref[0]
    cum = lane_cumsum(jnp.concatenate([gates, jnp.zeros((8 - H, gates.shape[1]), F32)], axis=0))
    total = cum[:, -1:]
    cols = to_columns(total - cum)
    suffix_ref[...] = cols
    for h in range(H):
        lanes = slice(h * DH, (h + 1) * DH)
        scaled = jnp.exp(cols[:, h : h + 1]) * values_ref[0, :, lanes].astype(F32)
        high = scaled.astype(BF16)
        low = (scaled - high.astype(F32)).astype(BF16)
        both = mm_tn(keys_ref[0, :, lanes], jnp.concatenate([high, low], axis=1))
        state[h] = both[:, :DH] + both[:, DH:]
    part = DH // n
    logs = jnp.broadcast_to(total, (8, DH))
    for k in range(n):
        q = lax.rem(me_ref[0] + k, n)
        for h in range(H):
            outs[k][h * part : (h + 1) * part, :] = state[h, pl.ds(q * part, part), :]
        outs[k][H * part :, :] = logs


def join_kernel(n, me_ref, *refs):
    parts, final_ref, later_ref = refs[:n], refs[n], refs[n + 1]
    part = DH // n
    me = me_ref[0]
    place = [lax.rem(me + n - k, n) for k in range(n)]
    logs = [parts[k][H * part :, :] for k in range(n)]
    totals = [None] * H
    for k in range(n):
        later = jnp.zeros_like(logs[0])
        for other in range(n):
            if other != k:
                later = later + jnp.where(place[other] > place[k], 1.0, 0.0) * logs[other]
        if k == 0:
            later_ref[...] = later
        decay = jnp.exp(later)
        for h in range(H):
            term = decay[h : h + 1, :] * parts[k][h * part : (h + 1) * part, :]
            totals[h] = term if k == 0 else totals[h] + term
    for h in range(H):
        final_ref[h] = totals[h].astype(BF16)


def opening_kernel(n, steps, me_ref, ids_ref, lens_ref, adv_ref, gates_ref, mask_ref, q_ref, c_ref, *refs):
    outs, cols_ref, rows_ref, acc, cols = refs[:n], refs[n], refs[n + 1], refs[n + 2], refs[n + 3]
    r = pl.program_id(0)
    count = gates_ref.shape[0]
    slots = gates_ref.shape[2]

    @pl.when(r == 0)
    def _():
        acc[...] = jnp.zeros_like(acc)
        cum = lane_cumsum(jnp.concatenate([gates_ref[i] for i in range(count)], axis=0))
        carried = jnp.exp(cum)
        place = lax.broadcasted_iota(jnp.int32, (1, slots), 1)
        rows = []
        for i in range(count):
            weight = adv_ref[i].astype(F32) / 1024.0
            opened = jnp.where(place < lens_ref[0, i], 1.0, 0.0)
            live = mask_ref[i : i + 1, :].astype(F32) * opened * weight
            rows += [cum[H * i : H * i + H], carried[H * i : H * i + H], live, opened]
            rows.append(jnp.zeros((2, slots), F32))
        rows = jnp.concatenate(rows, axis=0)
        rows_ref[...] = rows.reshape(count, 8, slots)
        cols[...] = to_columns(rows)
        cols_ref[...] = cols[...]

    mine = pltpu.roll(cols[...], lax.rem(128 - 8 * r, 128), 1)
    live = mine[:, 4:5]
    p = ids_ref[r]
    for h in range(H):
        lanes = slice(h * DH, (h + 1) * DH)
        grad_out = (c_ref[0, :, lanes].astype(F32) * live).astype(BF16)
        scaled = (mine[:, 2 + h : 3 + h] * grad_out.astype(F32)).astype(BF16)
        acc[p, h] += mm_tn(q_ref[0, :, lanes], scaled)

    @pl.when(r == steps - 1)
    def _():
        part = DH // n
        for k in range(n):
            q = lax.rem(me_ref[0] + k, n)
            outs[k][...] = acc[:, :, pl.ds(q * part, part), :].astype(BF16)


def sweep_kernel(cols_ref, rows_ref, q_ref, k_ref, v_ref, c_ref, out_ref, dq_ref, dk_ref, dv_ref):
    r = pl.program_id(0)
    mine = pltpu.roll(cols_ref[...], lax.rem(128 - 8 * r, 128), 1)
    rows = rows_ref[0]
    live = mine[:, 4:5]
    causal = lax.broadcasted_iota(jnp.int32, (HALF, HALF), 0) >= lax.broadcasted_iota(
        jnp.int32, (HALF, HALF), 1
    )
    blocks = q_ref.shape[1] // HALF
    for h in range(H):
        lanes = slice(h * DH, (h + 1) * DH)
        cum = mine[:, h : h + 1]
        dk = [None] * blocks
        dv = [None] * blocks
        for t in range(blocks):
            at = slice(t * HALF, (t + 1) * HALF)
            query = q_ref[0, at, lanes]
            grad_out = (c_ref[0, at, lanes].astype(F32) * live[at]).astype(BF16)
            out = None
            dq = None
            for s in range(t + 1):
                of = slice(s * HALF, (s + 1) * HALF)
                key = k_ref[0, of, lanes]
                value = v_ref[0, of, lanes]
                diff = cum[at] - rows[h : h + 1, of]
                if s == t:
                    diff = jnp.where(causal, diff, NEVER)
                decay = jnp.exp(diff)
                mixing = (mm_nt(query, key) * decay).astype(BF16)
                scores = (mm_nt(grad_out, value) * decay).astype(BF16)
                o_new = mm(mixing, value)
                q_new = mm(scores, key)
                k_new = mm_tn(scores, query)
                v_new = mm_tn(mixing, grad_out)
                out = o_new if out is None else out + o_new
                dq = q_new if dq is None else dq + q_new
                dk[s] = k_new if dk[s] is None else dk[s] + k_new
                dv[s] = v_new if dv[s] is None else dv[s] + v_new
            out_ref[0, at, lanes] = out
            dq_ref[0, at, lanes] = dq
        for s in range(blocks):
            of = slice(s * HALF, (s + 1) * HALF)
            dk_ref[0, of, lanes] = dk[s].astype(BF16)
            dv_ref[0, of, lanes] = dv[s].astype(BF16)


def close_kernel(n, place_ref, ids_ref, cols_ref, q_ref, c_ref, po_ref, pdq_ref, *refs):
    states, out_ref, dq_ref, start = refs[:n], refs[n], refs[n + 1], refs[n + 2]
    r = pl.program_id(0)
    prompts = states[0].shape[0]
    part = DH // n
    slot = lax.rem(place_ref[1] + prompts - ids_ref[r], prompts)
    for m in range(n):
        q = lax.rem(place_ref[0] + n - m, n)
        for h in range(H):
            start[h, pl.ds(q * part, part), :] = states[m][slot, h]
    mine = pltpu.roll(cols_ref[...], lax.rem(128 - 8 * r, 128), 1)
    live = mine[:, 4:5]
    opened = mine[:, 5:6]
    for h in range(H):
        lanes = slice(h * DH, (h + 1) * DH)
        carried = mine[:, 2 + h : 3 + h]
        grad_out = (c_ref[0, :, lanes].astype(F32) * live).astype(BF16)
        out = po_ref[0, :, lanes] + carried * mm(q_ref[0, :, lanes], start[h])
        out_ref[0, :, lanes] = (opened * out).astype(BF16)
        dq = pdq_ref[0, :, lanes] + carried * mm_nt(grad_out, start[h])
        dq_ref[0, :, lanes] = dq.astype(BF16)


def share_kernel(n, count, me_ref, *refs):
    parts, outs = refs[:n], refs[n : n + count]
    for k in range(count):
        p = lax.rem(me_ref[0] + k, count)
        total = parts[0][p].astype(F32)
        for part in parts[1:]:
            total = total + part[p].astype(F32)
        outs[k][...] = total.astype(BF16)


def prompt_kernel(n, me_ref, keys_ref, values_ref, suffix_ref, later_ref, *refs):
    parts, dk_ref, dv_ref, grad = refs[:n], refs[n], refs[n + 1], refs[n + 2]
    part = DH // n
    for m in range(n):
        q = lax.rem(me_ref[0] + n - m, n)
        for h in range(H):
            grad[h, pl.ds(q * part, part), :] = parts[m][h]
    for h in range(H):
        lanes = slice(h * DH, (h + 1) * DH)
        factor = jnp.exp(suffix_ref[:, h : h + 1] + later_ref[h : h + 1, 0:1])
        dk_ref[0, :, lanes] = (factor * mm_nt(values_ref[0, :, lanes], grad[h])).astype(BF16)
        dv_ref[0, :, lanes] = (factor * mm(keys_ref[0, :, lanes], grad[h])).astype(BF16)


def shift(x, axis, k):
    n = lax.axis_size(axis)
    return lax.ppermute(x, axis, [(s, (s + k) % n) for s in range(n)])


def shards(
    keys,
    values,
    prompt_gates,
    queries,
    resp_keys,
    resp_values,
    resp_gates,
    cotangent,
    group_ids,
    resp_lengths,
    loss_mask,
    advantages,
):
    n = lax.axis_size("prompt")
    count = lax.axis_size("resp")
    row = lax.axis_index("prompt").astype(jnp.int32)[None]
    col = lax.axis_index("resp").astype(jnp.int32)[None]
    responses, slots, width = queries.shape
    part = DH // n
    tokens = keys.shape[1]
    shape = jax.ShapeDtypeStruct

    pieces = pl.pallas_call(
        lambda *refs: piece_kernel(n, *refs),
        out_shape=[shape((H * part + 8, DH), F32)] * n + [shape((tokens, 128), F32)],
        in_specs=[SMEM, VMEM, VMEM, VMEM],
        out_specs=[VMEM] * (n + 1),
        scratch_shapes=[pltpu.VMEM((H, DH, DH), F32)],
        compiler_params=params(),
        name="piece_state",
    )(row, keys, values, prompt_gates)
    suffix = pieces[n]
    arrived = [pieces[0]] + [shift(pieces[k], "prompt", k) for k in range(1, n)]

    block = pl.BlockSpec((1, slots, width), lambda r: (r, 0, 0))
    opening = pl.pallas_call(
        lambda *refs: opening_kernel(n, responses, *refs),
        grid=(responses,),
        out_shape=[shape((count, H, part, DH), BF16)] * n
        + [shape((slots, 128), F32), shape((responses, 8, slots), F32)],
        in_specs=[SMEM, SMEM, SMEM, SMEM, VMEM, VMEM, block, block],
        out_specs=[VMEM] * (n + 2),
        scratch_shapes=[pltpu.VMEM((count, H, DH, DH), F32), pltpu.VMEM((slots, 128), F32)],
        compiler_params=params(),
        name="state_gradient",
    )(row, group_ids, resp_lengths, advantages, resp_gates, loss_mask, queries, cotangent)
    cols, rows = opening[n], opening[n + 1]
    sums = [opening[0]] + [shift(opening[k], "prompt", k) for k in range(1, n)]

    final, later = pl.pallas_call(
        lambda *refs: join_kernel(n, *refs),
        out_shape=[shape((H, part, DH), BF16), shape((8, DH), F32)],
        in_specs=[SMEM] + [VMEM] * n,
        out_specs=[VMEM, VMEM],
        compiler_params=params(),
        name="join_pieces",
    )(row, *arrived)
    column = jnp.stack([final] + [shift(final, "resp", k) for k in range(1, count)])

    shared = pl.pallas_call(
        lambda *refs: share_kernel(n, count, *refs),
        out_shape=[shape((H, part, DH), BF16)] * count,
        in_specs=[SMEM] + [VMEM] * n,
        out_specs=[VMEM] * count,
        compiler_params=params(),
        name="share_sums",
    )(col, *sums)
    states = [column] + [shift(column, "prompt", k) for k in range(1, n)]
    total = shared[0].astype(F32)
    for k in range(1, count):
        total = total + shift(shared[k], "resp", k).astype(F32)
    total = total.astype(BF16)

    lane_block = pl.BlockSpec((slots, 128), lambda r: (0, 0))
    row_block = pl.BlockSpec((1, 8, slots), lambda r: (r, 0, 0))
    like = shape(queries.shape, F32)
    like_out = shape(queries.shape, BF16)
    partial_out, partial_dq, resp_dk, resp_dv = pl.pallas_call(
        sweep_kernel,
        grid=(responses,),
        out_shape=[like, like, like_out, like_out],
        in_specs=[lane_block, row_block, block, block, block, block],
        out_specs=[block] * 4,
        compiler_params=params(),
        name="sweep",
    )(cols, rows, queries, resp_keys, resp_values, cotangent)

    grads = [total] + [shift(total, "prompt", k) for k in range(1, n)]

    resp_out, resp_dq = pl.pallas_call(
        lambda *refs: close_kernel(n, *refs),
        grid=(responses,),
        out_shape=[like_out, like_out],
        in_specs=[SMEM, SMEM, lane_block, block, block, block, block] + [VMEM] * n,
        out_specs=[block, block],
        scratch_shapes=[pltpu.VMEM((H, DH, DH), BF16)],
        compiler_params=params(),
        name="close",
    )(jnp.concatenate([row, col]), group_ids, cols, queries, cotangent, partial_out, partial_dq, *states)

    prompt_dk, prompt_dv = pl.pallas_call(
        lambda *refs: prompt_kernel(n, *refs),
        out_shape=[shape(keys.shape, BF16), shape(keys.shape, BF16)],
        in_specs=[SMEM] + [VMEM] * (4 + n),
        out_specs=[VMEM, VMEM],
        scratch_shapes=[pltpu.VMEM((H, DH, DH), BF16)],
        compiler_params=params(),
        name="prompt_gradient",
    )(row, keys, values, suffix, later, *grads)
    return (resp_out, resp_dq, resp_dk, resp_dv, prompt_dk, prompt_dv)


def solution(mesh):
    spread = P(("prompt", "resp"))
    three = P(("prompt", "resp"), None, None)
    two = P(("prompt", "resp"), None)
    prompt = P("resp", "prompt", None)
    return jax.shard_map(
        shards,
        mesh=mesh,
        in_specs=(
            prompt,
            prompt,
            P("resp", None, "prompt"),
            three,
            three,
            three,
            three,
            three,
            spread,
            two,
            two,
            spread,
        ),
        out_specs=(three, three, three, three, prompt, prompt),
        check_vma=False,
    )
```

```python
import jax
import jax.numpy as jnp
from jax import lax
from jax.experimental import pallas as pl
from jax.experimental.pallas import tpu as pltpu
from jax.sharding import PartitionSpec as P

H = 2
DH = 128
HALF = 256
F32 = jnp.float32
BF16 = jnp.bfloat16
NEVER = -1e30
VMEM = pl.BlockSpec(memory_space=pltpu.VMEM)
SMEM = pl.BlockSpec(memory_space=pltpu.SMEM)


def params(mebibytes=62):
    return pltpu.CompilerParams(vmem_limit_bytes=mebibytes * 1024 * 1024)


def mm(a, b):
    return lax.dot_general(a, b, (((1,), (0,)), ((), ())), preferred_element_type=F32)


def mm_nt(a, b):
    return lax.dot_general(a, b, (((1,), (1,)), ((), ())), preferred_element_type=F32)


def mm_tn(a, b):
    return lax.dot_general(a, b, (((0,), (0,)), ((), ())), preferred_element_type=F32)


def lane_cumsum(x):
    width = x.shape[1]
    lane = lax.broadcasted_iota(jnp.int32, x.shape, 1)
    step = 1
    while step < width:
        x = x + jnp.where(lane >= step, pltpu.roll(x, step, 1), 0.0)
        step *= 2
    return x


def to_columns(rows):
    padded = jnp.concatenate([rows, jnp.zeros((128 - rows.shape[0], rows.shape[1]), F32)], axis=0)
    return padded.T


def first_kernel(
    n, ids_ref, lens_ref, adv_ref, keys_hbm, values_hbm, pgates_hbm, gates_hbm, mask_hbm, q_hbm, c_hbm,
    msg_ref, suffix_ref, cols_ref, rows_ref,
    keys, values, pgates, gates, mask, q, c, sems,
):
    pairs = [(pgates_hbm, pgates), (keys_hbm, keys), (values_hbm, values), (gates_hbm, gates), (mask_hbm, mask)]
    count = gates.shape[0]
    slots = gates.shape[2]
    for i in range(count):
        pairs += [(q_hbm.at[i], q.at[i]), (c_hbm.at[i], c.at[i])]
    copies = [pltpu.make_async_copy(a, b, sems.at[i]) for i, (a, b) in enumerate(pairs)]
    for copy in copies:
        copy.start()
    for copy in copies[:3]:
        copy.wait()
    part = DH // n
    piece = pgates[0]
    cum = lane_cumsum(jnp.concatenate([piece, jnp.zeros((8 - H, piece.shape[1]), F32)], axis=0))
    total = cum[:, -1:]
    suffix = to_columns(total - cum)
    suffix_ref[...] = suffix
    for h in range(H):
        lanes = slice(h * DH, (h + 1) * DH)
        scaled = jnp.exp(suffix[:, h : h + 1]) * values[0, :, lanes].astype(F32)
        high = scaled.astype(BF16)
        low = (scaled - high.astype(F32)).astype(BF16)
        both = mm_tn(keys[0, :, lanes], jnp.concatenate([high, low], axis=1))
        state = (both[:, :DH] + both[:, DH:]).astype(BF16)
        for k in range(n):
            msg_ref[k, h * part : (h + 1) * part, :] = state[k * part : (k + 1) * part]
    high = total.astype(BF16).astype(F32)
    middle = (total - high).astype(BF16).astype(F32)
    low = total - high - middle
    notes = [jnp.broadcast_to(x[h : h + 1], (1, DH)) for x in (high, middle, low) for h in range(H)]
    notes += [jnp.full((1, DH), ids_ref[i].astype(F32)) for i in range(count)]
    notes.append(jnp.zeros((16 - len(notes), DH), F32))
    notes = jnp.concatenate(notes, axis=0).astype(BF16)
    for k in range(n):
        msg_ref[k, H * part : H * part + 16, :] = notes

    for copy in copies[3:5]:
        copy.wait()
    cum = lane_cumsum(jnp.concatenate([gates[i] for i in range(count)], axis=0))
    carried = jnp.exp(cum)
    place = lax.broadcasted_iota(jnp.int32, (1, slots), 1)
    rows = []
    for i in range(count):
        weight = adv_ref[i].astype(F32) / 1024.0
        opened = jnp.where(place < lens_ref[0, i], 1.0, 0.0)
        live = mask[i : i + 1, :].astype(F32) * opened * weight
        rows += [cum[H * i : H * i + H], carried[H * i : H * i + H], live, opened, jnp.zeros((2, slots), F32)]
    rows = jnp.concatenate(rows, axis=0)
    rows_ref[...] = rows.reshape(count, 8, slots)
    cols = to_columns(rows)
    cols_ref[...] = cols
    for i in range(count):
        copies[5 + 2 * i].wait()
        copies[6 + 2 * i].wait()
        for h in range(H):
            lanes = slice(h * DH, (h + 1) * DH)
            grad_out = (c[i, :, lanes].astype(F32) * cols[:, 8 * i + 4 : 8 * i + 5]).astype(BF16)
            scaled = (cols[:, 8 * i + 2 + h : 8 * i + 3 + h] * grad_out.astype(F32)).astype(BF16)
            grad = mm_tn(q[i, :, lanes], scaled).astype(BF16)
            for k in range(n):
                at = H * part + 16 + (i * H + h) * part
                msg_ref[k, at : at + part, :] = grad[k * part : (k + 1) * part]


def pick(ids, p):
    return jnp.where(ids == p, 1.0, 0.0)


def second_kernel(n, count, me_ref, got_ref, msg_ref, later_ref, sums):
    part = DH // n
    block = H * part
    notes = [got_ref[k, block : block + 16, :].astype(F32) for k in range(n)]
    logs = [x[0:H] + x[H : 2 * H] + x[2 * H : 3 * H] for x in notes]
    final = [None] * H
    later = jnp.zeros_like(logs[0])
    mine = jnp.zeros_like(logs[0])
    for k in range(n - 1, -1, -1):
        mine = jnp.where(me_ref[0] == k, later, mine)
        decay = jnp.exp(later)
        for h in range(H):
            term = decay[h : h + 1] * got_ref[k, h * part : (h + 1) * part, :].astype(F32)
            final[h] = term if final[h] is None else final[h] + term
        later = later + logs[k]
    later_ref[...] = jnp.concatenate([mine, jnp.zeros((8 - H, DH), F32)], axis=0)
    final = jnp.concatenate(final, axis=0).astype(BF16)
    sums[...] = jnp.zeros_like(sums)
    responses = (got_ref.shape[1] - block - 16) // block
    for k in range(n):
        for i in range(responses):
            at = block + 16 + i * block
            p = jnp.max(notes[k][3 * H + i : 3 * H + i + 1]).astype(jnp.int32)
            sums[p] += got_ref[k, at : at + block, :].astype(F32)
    for p in range(count):
        msg_ref[p, 0:block, :] = final
        msg_ref[p, block : 2 * block, :] = sums[p].astype(BF16)


def third_kernel(n, count, first_ref, got_ref, msg_ref):
    part = DH // n
    block = H * part
    responses = (first_ref.shape[1] - block - 16) // block
    total = got_ref[0, block:, :].astype(F32)
    for p in range(1, count):
        total = total + got_ref[p, block:, :].astype(F32)
    total = total.astype(BF16)
    for k in range(n):
        notes = first_ref[k, block : block + 16, :].astype(F32)
        for i in range(responses):
            p = jnp.max(notes[3 * H + i : 3 * H + i + 1]).astype(jnp.int32)
            msg_ref[k, i * block : (i + 1) * block, :] = got_ref[p, 0:block, :]
        msg_ref[k, responses * block :, :] = total


def sweep_kernel(cols_ref, rows_ref, q_ref, k_ref, v_ref, c_ref, out_ref, dq_ref, dk_ref, dv_ref):
    r = pl.program_id(0)
    mine = pltpu.roll(cols_ref[...], lax.rem(128 - 8 * r, 128), 1)
    rows = rows_ref[0]
    live = mine[:, 4:5]
    causal = lax.broadcasted_iota(jnp.int32, (HALF, HALF), 0) >= lax.broadcasted_iota(
        jnp.int32, (HALF, HALF), 1
    )
    blocks = q_ref.shape[1] // HALF
    for h in range(H):
        lanes = slice(h * DH, (h + 1) * DH)
        cum = mine[:, h : h + 1]
        dk = [None] * blocks
        dv = [None] * blocks
        for t in range(blocks):
            at = slice(t * HALF, (t + 1) * HALF)
            query = q_ref[0, at, lanes]
            grad_out = (c_ref[0, at, lanes].astype(F32) * live[at]).astype(BF16)
            out = None
            dq = None
            for s in range(t + 1):
                of = slice(s * HALF, (s + 1) * HALF)
                key = k_ref[0, of, lanes]
                value = v_ref[0, of, lanes]
                diff = cum[at] - rows[h : h + 1, of]
                if s == t:
                    diff = jnp.where(causal, diff, NEVER)
                decay = jnp.exp(diff)
                mixing = (mm_nt(query, key) * decay).astype(BF16)
                scores = (mm_nt(grad_out, value) * decay).astype(BF16)
                o_new = mm(mixing, value)
                q_new = mm(scores, key)
                k_new = mm_tn(scores, query)
                v_new = mm_tn(mixing, grad_out)
                out = o_new if out is None else out + o_new
                dq = q_new if dq is None else dq + q_new
                dk[s] = k_new if dk[s] is None else dk[s] + k_new
                dv[s] = v_new if dv[s] is None else dv[s] + v_new
            out_ref[0, at, lanes] = out
            dq_ref[0, at, lanes] = dq
        for s in range(blocks):
            of = slice(s * HALF, (s + 1) * HALF)
            dk_ref[0, of, lanes] = dk[s].astype(BF16)
            dv_ref[0, of, lanes] = dv[s].astype(BF16)


def last_kernel(
    n, steps, cols_ref, q_ref, c_ref, po_ref, pdq_ref, got_ref, keys_ref, values_ref, suffix_ref, later_ref,
    out_ref, dq_ref, dk_ref, dv_ref, start,
):
    r = pl.program_id(0)
    part = DH // n
    for k in range(n):
        for h in range(H):
            at = pl.multiple_of((r * H + h) * part, part)
            start[h, k * part : (k + 1) * part, :] = got_ref[k, pl.ds(at, part), :]
    mine = pltpu.roll(cols_ref[...], lax.rem(128 - 8 * r, 128), 1)
    live = mine[:, 4:5]
    opened = mine[:, 5:6]
    for h in range(H):
        lanes = slice(h * DH, (h + 1) * DH)
        carried = mine[:, 2 + h : 3 + h]
        grad_out = (c_ref[0, :, lanes].astype(F32) * live).astype(BF16)
        out = po_ref[0, :, lanes] + carried * mm(q_ref[0, :, lanes], start[h])
        out_ref[0, :, lanes] = (opened * out).astype(BF16)
        dq = pdq_ref[0, :, lanes] + carried * mm_nt(grad_out, start[h])
        dq_ref[0, :, lanes] = dq.astype(BF16)

    @pl.when(r == 0)
    def _():
        for h in range(H):
            lanes = slice(h * DH, (h + 1) * DH)
            at = (steps * H + h) * part
            grad = jnp.concatenate([got_ref[k, at : at + part, :] for k in range(n)], axis=0)
            factor = jnp.exp(suffix_ref[:, h : h + 1] + later_ref[h : h + 1, 0:1])
            dk_ref[0, :, lanes] = (factor * mm_nt(values_ref[0, :, lanes], grad)).astype(BF16)
            dv_ref[0, :, lanes] = (factor * mm(keys_ref[0, :, lanes], grad)).astype(BF16)


def exchange(x, axis):
    return lax.all_to_all(x, axis, 0, 0, tiled=True)


def shards(
    keys,
    values,
    prompt_gates,
    queries,
    resp_keys,
    resp_values,
    resp_gates,
    cotangent,
    group_ids,
    resp_lengths,
    loss_mask,
    advantages,
):
    n = lax.axis_size("prompt")
    count = lax.axis_size("resp")
    row = lax.axis_index("prompt").astype(jnp.int32)[None]
    responses, slots, width = queries.shape
    block_rows = H * DH // n
    tokens = keys.shape[1]
    shape = jax.ShapeDtypeStruct
    HBM = pl.BlockSpec(memory_space=pltpu.HBM)

    msg, suffix, cols, rows = pl.pallas_call(
        lambda *refs: first_kernel(n, *refs),
        out_shape=[
            shape((n, block_rows * (1 + responses) + 16, DH), BF16),
            shape((tokens, 128), F32),
            shape((slots, 128), F32),
            shape((responses, 8, slots), F32),
        ],
        in_specs=[SMEM] * 3 + [HBM] * 7,
        out_specs=[VMEM] * 4,
        scratch_shapes=[
            pltpu.VMEM(keys.shape, BF16),
            pltpu.VMEM(values.shape, BF16),
            pltpu.VMEM(prompt_gates.shape, F32),
            pltpu.VMEM(resp_gates.shape, F32),
            pltpu.VMEM(loss_mask.shape, jnp.int32),
            pltpu.VMEM(queries.shape, BF16),
            pltpu.VMEM(queries.shape, BF16),
            pltpu.SemaphoreType.DMA((5 + 2 * responses,)),
        ],
        compiler_params=params(),
        name="first",
    )(
        group_ids, resp_lengths, advantages, keys, values, prompt_gates, resp_gates, loss_mask, queries, cotangent
    )
    got1 = exchange(msg, "prompt")
    msg, later = pl.pallas_call(
        lambda *refs: second_kernel(n, count, *refs),
        out_shape=[shape((count, 2 * block_rows, DH), BF16), shape((8, DH), F32)],
        in_specs=[SMEM, VMEM],
        out_specs=[VMEM, VMEM],
        scratch_shapes=[pltpu.VMEM((count, block_rows, DH), F32)],
        compiler_params=params(16),
        name="second",
    )(row, got1)
    got2 = exchange(msg, "resp")
    msg = pl.pallas_call(
        lambda *refs: third_kernel(n, count, *refs),
        out_shape=shape((n, (responses + 1) * block_rows, DH), BF16),
        in_specs=[VMEM, VMEM],
        out_specs=VMEM,
        compiler_params=params(16),
        name="third",
    )(got1, got2)
    got3 = exchange(msg, "prompt")

    block = pl.BlockSpec((1, slots, width), lambda r: (r, 0, 0))
    lane_block = pl.BlockSpec((slots, 128), lambda r: (0, 0))
    row_block = pl.BlockSpec((1, 8, slots), lambda r: (r, 0, 0))
    like = shape(queries.shape, F32)
    like_out = shape(queries.shape, BF16)
    partial_out, partial_dq, resp_dk, resp_dv = pl.pallas_call(
        sweep_kernel,
        grid=(responses,),
        out_shape=[like, like, like_out, like_out],
        in_specs=[lane_block, row_block, block, block, block, block],
        out_specs=[block] * 4,
        compiler_params=params(),
        name="sweep",
    )(cols, rows, queries, resp_keys, resp_values, cotangent)

    resp_out, resp_dq, prompt_dk, prompt_dv = pl.pallas_call(
        lambda *refs: last_kernel(n, responses, *refs),
        grid=(responses,),
        out_shape=[like_out, like_out, shape(keys.shape, BF16), shape(keys.shape, BF16)],
        in_specs=[lane_block, block, block, block, block] + [VMEM] * 5,
        out_specs=[block, block, VMEM, VMEM],
        scratch_shapes=[pltpu.VMEM((H, DH, DH), BF16)],
        compiler_params=params(),
        name="last",
    )(cols, queries, cotangent, partial_out, partial_dq, got3, keys, values, suffix, later)
    return (resp_out, resp_dq, resp_dk, resp_dv, prompt_dk, prompt_dv)


def solution(mesh):
    spread = P(("prompt", "resp"))
    three = P(("prompt", "resp"), None, None)
    two = P(("prompt", "resp"), None)
    prompt = P("resp", "prompt", None)
    return jax.shard_map(
        shards,
        mesh=mesh,
        in_specs=(
            prompt,
            prompt,
            P("resp", None, "prompt"),
            three,
            three,
            three,
            three,
            three,
            spread,
            two,
            two,
            spread,
        ),
        out_specs=(three, three, three, three, prompt, prompt),
        check_vma=False,
    )
```

```python
import jax
import jax.numpy as jnp
from jax import lax
from jax.experimental import pallas as pl
from jax.experimental.pallas import tpu as pltpu
from jax.sharding import PartitionSpec as P

H = 2
DH = 128
HALF = 256
F32 = jnp.float32
BF16 = jnp.bfloat16
NEVER = -1e30
VMEM = pl.BlockSpec(memory_space=pltpu.VMEM)
SMEM = pl.BlockSpec(memory_space=pltpu.SMEM)


def params(mebibytes=62):
    return pltpu.CompilerParams(vmem_limit_bytes=mebibytes * 1024 * 1024)


def mm(a, b):
    return lax.dot_general(a, b, (((1,), (0,)), ((), ())), preferred_element_type=F32)


def mm_nt(a, b):
    return lax.dot_general(a, b, (((1,), (1,)), ((), ())), preferred_element_type=F32)


def mm_tn(a, b):
    return lax.dot_general(a, b, (((0,), (0,)), ((), ())), preferred_element_type=F32)


def lane_cumsum(x):
    width = x.shape[1]
    lane = lax.broadcasted_iota(jnp.int32, x.shape, 1)
    step = 1
    while step < width:
        x = x + jnp.where(lane >= step, pltpu.roll(x, step, 1), 0.0)
        step *= 2
    return x


def to_columns(rows):
    padded = jnp.concatenate([rows, jnp.zeros((128 - rows.shape[0], rows.shape[1]), F32)], axis=0)
    return padded.T


def row_block(matrices, k, m):
    part = DH // m
    return jnp.concatenate([x[k * part : (k + 1) * part] for x in matrices], axis=0).astype(BF16)


def from_blocks(blocks, h):
    part = blocks[0].shape[0] // H
    rows = [x.astype(F32)[h * part : (h + 1) * part] for x in blocks]
    return jnp.concatenate(rows, axis=0).astype(BF16)


def first_kernel(
    m, ids_ref, lens_ref, adv_ref, keys_hbm, values_hbm, pgates_hbm, gates_hbm, mask_hbm, q_hbm, c_hbm,
    msg_ref, suffix_ref, cols_ref, rows_ref,
    keys, values, pgates, gates, mask, q, c, sems,
):
    pairs = [(pgates_hbm, pgates), (keys_hbm, keys), (values_hbm, values), (gates_hbm, gates), (mask_hbm, mask)]
    count = gates.shape[0]
    slots = gates.shape[2]
    for i in range(count):
        pairs += [(q_hbm.at[i], q.at[i]), (c_hbm.at[i], c.at[i])]
    copies = [pltpu.make_async_copy(a, b, sems.at[i]) for i, (a, b) in enumerate(pairs)]
    for copy in copies:
        copy.start()
    for copy in copies[:3]:
        copy.wait()
    block = H * DH // m
    piece = pgates[0]
    cum = lane_cumsum(jnp.concatenate([piece, jnp.zeros((8 - H, piece.shape[1]), F32)], axis=0))
    total = cum[:, -1:]
    suffix = to_columns(total - cum)
    suffix_ref[...] = suffix
    states = []
    for h in range(H):
        lanes = slice(h * DH, (h + 1) * DH)
        scaled = jnp.exp(suffix[:, h : h + 1]) * values[0, :, lanes].astype(F32)
        high = scaled.astype(BF16)
        low = (scaled - high.astype(F32)).astype(BF16)
        both = mm_tn(keys[0, :, lanes], jnp.concatenate([high, low], axis=1))
        states.append(both[:, :DH] + both[:, DH:])
    for k in range(m):
        msg_ref[k, 0:block, :] = row_block(states, k, m)
    high = total.astype(BF16).astype(F32)
    middle = (total - high).astype(BF16).astype(F32)
    low = total - high - middle
    notes = [jnp.broadcast_to(x[h : h + 1], (1, DH)) for x in (high, middle, low) for h in range(H)]
    notes += [jnp.full((1, DH), ids_ref[i].astype(F32)) for i in range(count)]
    notes.append(jnp.zeros((16 - len(notes), DH), F32))
    notes = jnp.concatenate(notes, axis=0).astype(BF16)
    for k in range(m):
        msg_ref[k, block : block + 16, :] = notes

    for copy in copies[3:5]:
        copy.wait()
    cum = lane_cumsum(jnp.concatenate([gates[i] for i in range(count)], axis=0))
    carried = jnp.exp(cum)
    place = lax.broadcasted_iota(jnp.int32, (1, slots), 1)
    rows = []
    for i in range(count):
        weight = adv_ref[i].astype(F32) / 1024.0
        opened = jnp.where(place < lens_ref[0, i], 1.0, 0.0)
        live = mask[i : i + 1, :].astype(F32) * opened * weight
        rows += [cum[H * i : H * i + H], carried[H * i : H * i + H], live, opened, jnp.zeros((2, slots), F32)]
    rows = jnp.concatenate(rows, axis=0)
    rows_ref[...] = rows.reshape(count, 8, slots)
    cols = to_columns(rows)
    cols_ref[...] = cols
    for i in range(count):
        copies[5 + 2 * i].wait()
        copies[6 + 2 * i].wait()
        grads = []
        for h in range(H):
            lanes = slice(h * DH, (h + 1) * DH)
            grad_out = (c[i, :, lanes].astype(F32) * cols[:, 8 * i + 4 : 8 * i + 5]).astype(BF16)
            scaled = (cols[:, 8 * i + 2 + h : 8 * i + 3 + h] * grad_out.astype(F32)).astype(BF16)
            grads.append(mm_tn(q[i, :, lanes], scaled))
        at = block * (1 + i) + 16
        for k in range(m):
            msg_ref[k, at : at + block, :] = row_block(grads, k, m)


def noted_prompt(notes, i):
    return jnp.max(notes[3 * H + i : 3 * H + i + 1]).astype(jnp.int32)


def second_kernel(m, chips, me_ref, got_ref, msg_ref, later_ref, sums):
    cores = msg_ref.shape[1] * m // (2 * H * DH)
    block = H * DH // m
    responses = (got_ref.shape[1] - block - 16) // block
    notes = [got_ref[k, block : block + 16, :].astype(F32) for k in range(m)]
    logs = [x[0:H] + x[H : 2 * H] + x[2 * H : 3 * H] for x in notes]
    mine = jnp.zeros_like(logs[0])
    for c in range(cores):
        final = jnp.zeros((block, DH), F32)
        later = jnp.zeros_like(logs[0])
        for k in range(m - cores + c, -1, -cores):
            mine = jnp.where(me_ref[0] == k, later, mine)
            decay = jnp.exp(later)
            decay = [jnp.broadcast_to(decay[h : h + 1], (block // H, DH)) for h in range(H)]
            final = final + jnp.concatenate(decay, axis=0) * got_ref[k, 0:block, :].astype(F32)
            later = later + logs[k]
        for z in range(chips):
            msg_ref[z, c * block : (c + 1) * block, :] = final.astype(BF16)
    later_ref[...] = jnp.concatenate([mine, jnp.zeros((8 - H, DH), F32)], axis=0)
    sums[...] = jnp.zeros_like(sums)
    for k in range(m):
        for i in range(responses):
            at = block * (1 + i) + 16
            sums[noted_prompt(notes[k], i)] += got_ref[k, at : at + block, :].astype(F32)
    for z in range(chips):
        for c in range(cores):
            at = (cores + c) * block
            msg_ref[z, at : at + block, :] = sums[z * cores + c].astype(BF16)


def third_kernel(m, chips, first_ref, got_ref, msg_ref):
    block = H * DH // m
    cores = got_ref.shape[1] // (2 * block)
    responses = (first_ref.shape[1] - block - 16) // block
    totals = []
    for c in range(cores):
        at = (cores + c) * block
        total = got_ref[0, at : at + block, :].astype(F32)
        for z in range(1, chips):
            total = total + got_ref[z, at : at + block, :].astype(F32)
        totals.append(total.astype(BF16))
    for k in range(m):
        notes = first_ref[k, block : block + 16, :].astype(F32)
        for i in range(responses):
            p = noted_prompt(notes, i)
            at = pl.multiple_of(lax.rem(p, cores) * block, block)
            msg_ref[k, i * block : (i + 1) * block, :] = got_ref[lax.div(p, cores), pl.ds(at, block), :]
        msg_ref[k, responses * block :, :] = totals[k % cores]


def sweep_kernel(cols_ref, rows_ref, q_ref, k_ref, v_ref, c_ref, out_ref, dq_ref, dk_ref, dv_ref):
    r = pl.program_id(0)
    mine = pltpu.roll(cols_ref[...], lax.rem(128 - 8 * r, 128), 1)
    rows = rows_ref[0]
    live = mine[:, 4:5]
    causal = lax.broadcasted_iota(jnp.int32, (HALF, HALF), 0) >= lax.broadcasted_iota(
        jnp.int32, (HALF, HALF), 1
    )
    blocks = q_ref.shape[1] // HALF
    for h in range(H):
        lanes = slice(h * DH, (h + 1) * DH)
        cum = mine[:, h : h + 1]
        dk = [None] * blocks
        dv = [None] * blocks
        for t in range(blocks):
            at = slice(t * HALF, (t + 1) * HALF)
            query = q_ref[0, at, lanes]
            grad_out = (c_ref[0, at, lanes].astype(F32) * live[at]).astype(BF16)
            out = None
            dq = None
            for s in range(t + 1):
                of = slice(s * HALF, (s + 1) * HALF)
                key = k_ref[0, of, lanes]
                value = v_ref[0, of, lanes]
                diff = cum[at] - rows[h : h + 1, of]
                if s == t:
                    diff = jnp.where(causal, diff, NEVER)
                decay = jnp.exp(diff)
                mixing = (mm_nt(query, key) * decay).astype(BF16)
                scores = (mm_nt(grad_out, value) * decay).astype(BF16)
                o_new = mm(mixing, value)
                q_new = mm(scores, key)
                k_new = mm_tn(scores, query)
                v_new = mm_tn(mixing, grad_out)
                out = o_new if out is None else out + o_new
                dq = q_new if dq is None else dq + q_new
                dk[s] = k_new if dk[s] is None else dk[s] + k_new
                dv[s] = v_new if dv[s] is None else dv[s] + v_new
            out_ref[0, at, lanes] = out
            dq_ref[0, at, lanes] = dq
        for s in range(blocks):
            of = slice(s * HALF, (s + 1) * HALF)
            dk_ref[0, of, lanes] = dk[s].astype(BF16)
            dv_ref[0, of, lanes] = dv[s].astype(BF16)


def last_kernel(
    m, steps, cols_ref, q_ref, c_ref, po_ref, pdq_ref, got_ref, keys_ref, values_ref, suffix_ref, later_ref,
    out_ref, dq_ref, dk_ref, dv_ref,
):
    r = pl.program_id(0)
    block = H * DH // m
    blocks = [got_ref[k, pl.ds(pl.multiple_of(r * block, block), block), :] for k in range(m)]
    start = [from_blocks(blocks, h) for h in range(H)]
    mine = pltpu.roll(cols_ref[...], lax.rem(128 - 8 * r, 128), 1)
    live = mine[:, 4:5]
    opened = mine[:, 5:6]
    for h in range(H):
        lanes = slice(h * DH, (h + 1) * DH)
        carried = mine[:, 2 + h : 3 + h]
        grad_out = (c_ref[0, :, lanes].astype(F32) * live).astype(BF16)
        out = po_ref[0, :, lanes] + carried * mm(q_ref[0, :, lanes], start[h])
        out_ref[0, :, lanes] = (opened * out).astype(BF16)
        dq = pdq_ref[0, :, lanes] + carried * mm_nt(grad_out, start[h])
        dq_ref[0, :, lanes] = dq.astype(BF16)

    @pl.when(r == 0)
    def _():
        blocks = [got_ref[k, steps * block : (steps + 1) * block, :] for k in range(m)]
        for h in range(H):
            lanes = slice(h * DH, (h + 1) * DH)
            grad = from_blocks(blocks, h)
            factor = jnp.exp(suffix_ref[:, h : h + 1] + later_ref[h : h + 1, 0:1])
            dk_ref[0, :, lanes] = (factor * mm_nt(values_ref[0, :, lanes], grad)).astype(BF16)
            dv_ref[0, :, lanes] = (factor * mm(keys_ref[0, :, lanes], grad)).astype(BF16)


def exchange(x, axis):
    return lax.all_to_all(x, axis, 0, 0, tiled=True)


def shards(
    keys,
    values,
    prompt_gates,
    queries,
    resp_keys,
    resp_values,
    resp_gates,
    cotangent,
    group_ids,
    resp_lengths,
    loss_mask,
    advantages,
):
    plane = ("prompt", "core")
    cores = lax.axis_size("core")
    chips = lax.axis_size("z")
    m = lax.axis_size("prompt") * cores
    place = lax.axis_index(plane).astype(jnp.int32)[None]
    responses, slots, width = queries.shape
    block_rows = H * DH // m
    tokens = keys.shape[1]
    shape = jax.ShapeDtypeStruct
    HBM = pl.BlockSpec(memory_space=pltpu.HBM)

    msg, suffix, cols, rows = pl.pallas_call(
        lambda *refs: first_kernel(m, *refs),
        out_shape=[
            shape((m, block_rows * (1 + responses) + 16, DH), BF16),
            shape((tokens, 128), F32),
            shape((slots, 128), F32),
            shape((responses, 8, slots), F32),
        ],
        in_specs=[SMEM] * 3 + [HBM] * 7,
        out_specs=[VMEM] * 4,
        scratch_shapes=[
            pltpu.VMEM(keys.shape, BF16),
            pltpu.VMEM(values.shape, BF16),
            pltpu.VMEM(prompt_gates.shape, F32),
            pltpu.VMEM(resp_gates.shape, F32),
            pltpu.VMEM(loss_mask.shape, jnp.int32),
            pltpu.VMEM(queries.shape, BF16),
            pltpu.VMEM(queries.shape, BF16),
            pltpu.SemaphoreType.DMA((5 + 2 * responses,)),
        ],
        compiler_params=params(),
        name="first",
    )(
        group_ids, resp_lengths, advantages, keys, values, prompt_gates, resp_gates, loss_mask, queries, cotangent
    )
    got1 = exchange(msg, plane)
    msg, later = pl.pallas_call(
        lambda *refs: second_kernel(m, chips, *refs),
        out_shape=[shape((chips, 2 * cores * block_rows, DH), BF16), shape((8, DH), F32)],
        in_specs=[SMEM, VMEM],
        out_specs=[VMEM, VMEM],
        scratch_shapes=[pltpu.VMEM((chips * cores, block_rows, DH), F32)],
        compiler_params=params(16),
        name="second",
    )(place, got1)
    got2 = exchange(msg, "z")
    msg = pl.pallas_call(
        lambda *refs: third_kernel(m, chips, *refs),
        out_shape=shape((m, (responses + 1) * block_rows, DH), BF16),
        in_specs=[VMEM, VMEM],
        out_specs=VMEM,
        compiler_params=params(16),
        name="third",
    )(got1, got2)
    got3 = exchange(msg, plane)

    block = pl.BlockSpec((1, slots, width), lambda r: (r, 0, 0))
    lane_block = pl.BlockSpec((slots, 128), lambda r: (0, 0))
    row_block = pl.BlockSpec((1, 8, slots), lambda r: (r, 0, 0))
    like = shape(queries.shape, F32)
    like_out = shape(queries.shape, BF16)
    partial_out, partial_dq, resp_dk, resp_dv = pl.pallas_call(
        sweep_kernel,
        grid=(responses,),
        out_shape=[like, like, like_out, like_out],
        in_specs=[lane_block, row_block, block, block, block, block],
        out_specs=[block] * 4,
        compiler_params=params(),
        name="sweep",
    )(cols, rows, queries, resp_keys, resp_values, cotangent)

    resp_out, resp_dq, prompt_dk, prompt_dv = pl.pallas_call(
        lambda *refs: last_kernel(m, responses, *refs),
        grid=(responses,),
        out_shape=[like_out, like_out, shape(keys.shape, BF16), shape(keys.shape, BF16)],
        in_specs=[lane_block, block, block, block, block] + [VMEM] * 5,
        out_specs=[block, block, VMEM, VMEM],
        compiler_params=params(),
        name="last",
    )(cols, queries, cotangent, partial_out, partial_dq, got3, keys, values, suffix, later)
    return (resp_out, resp_dq, resp_dk, resp_dv, prompt_dk, prompt_dv)


def solution(mesh):
    n, count = mesh.shape["prompt"], mesh.shape["resp"]
    cores = 2 if count % 2 == 0 else 1
    mesh = jax.sharding.Mesh(mesh.devices.reshape(n, count // cores, cores), ("prompt", "z", "core"))
    spread = P(("prompt", "z", "core"))
    three = P(("prompt", "z", "core"), None, None)
    two = P(("prompt", "z", "core"), None)
    prompt = P(("z", "core"), "prompt", None)
    return jax.shard_map(
        shards,
        mesh=mesh,
        in_specs=(
            prompt,
            prompt,
            P(("z", "core"), None, "prompt"),
            three,
            three,
            three,
            three,
            three,
            spread,
            two,
            two,
            spread,
        ),
        out_specs=(three, three, three, three, prompt, prompt),
        check_vma=False,
    )
```

```python
import jax
import jax.numpy as jnp
from jax import lax
from jax.experimental import pallas as pl
from jax.experimental.pallas import tpu as pltpu
from jax.sharding import PartitionSpec as P

H = 2
DH = 128
HALF = 256
F32 = jnp.float32
BF16 = jnp.bfloat16
NEVER = -1e30
VMEM = pl.BlockSpec(memory_space=pltpu.VMEM)
ANY = pl.BlockSpec(memory_space=pl.ANY)
SMEM = pl.BlockSpec(memory_space=pltpu.SMEM)


def params(mebibytes=16):
    return pltpu.CompilerParams(vmem_limit_bytes=mebibytes * 1024 * 1024)


def mm(a, b):
    return lax.dot_general(a, b, (((1,), (0,)), ((), ())), preferred_element_type=F32)


def mm_nt(a, b):
    return lax.dot_general(a, b, (((1,), (1,)), ((), ())), preferred_element_type=F32)


def mm_tn(a, b):
    return lax.dot_general(a, b, (((0,), (0,)), ((), ())), preferred_element_type=F32)


def lane_cumsum(x):
    width = x.shape[1]
    lane = lax.broadcasted_iota(jnp.int32, x.shape, 1)
    step = 1
    while step < width:
        x = x + jnp.where(lane >= step, pltpu.roll(x, step, 1), 0.0)
        step *= 2
    return x


def to_columns(rows):
    padded = jnp.concatenate([rows, jnp.zeros((128 - rows.shape[0], rows.shape[1]), F32)], axis=0)
    return padded.T


def first_kernel(
    n, me_ref, ids_ref, lens_ref, adv_ref, keys_hbm, values_hbm, pgates_hbm, gates_hbm, mask_hbm, q_hbm, c_hbm,
    *refs,
):
    msgs, (suffix_ref, cols_ref, rows_ref) = refs[:n], refs[n : n + 3]
    keys, values, pgates, gates, mask, q, c, matrices, sems = refs[n + 3 :]
    pairs = [(pgates_hbm, pgates), (keys_hbm, keys), (values_hbm, values), (gates_hbm, gates), (mask_hbm, mask)]
    count = gates.shape[0]
    slots = gates.shape[2]
    for i in range(count):
        pairs += [(q_hbm.at[i], q.at[i]), (c_hbm.at[i], c.at[i])]
    copies = [pltpu.make_async_copy(a, b, sems.at[i]) for i, (a, b) in enumerate(pairs)]
    for copy in copies:
        copy.start()
    for copy in copies[:3]:
        copy.wait()
    part = DH // n
    block = H * part
    targets = [lax.rem(me_ref[0] + k, n) for k in range(n)]
    piece = pgates[0]
    cum = lane_cumsum(jnp.concatenate([piece, jnp.zeros((8 - H, piece.shape[1]), F32)], axis=0))
    total = cum[:, -1:]
    suffix = to_columns(total - cum)
    suffix_ref[...] = suffix
    for h in range(H):
        lanes = slice(h * DH, (h + 1) * DH)
        scaled = jnp.exp(suffix[:, h : h + 1]) * values[0, :, lanes].astype(F32)
        high = scaled.astype(BF16)
        low = (scaled - high.astype(F32)).astype(BF16)
        both = mm_tn(keys[0, :, lanes], jnp.concatenate([high, low], axis=1))
        matrices[h] = both[:, :DH] + both[:, DH:]
        for k in range(n):
            rows = matrices[h, pl.ds(targets[k] * part, part), :]
            msgs[k][h * part : (h + 1) * part, :] = rows.astype(BF16)
    high = total.astype(BF16).astype(F32)
    middle = (total - high).astype(BF16).astype(F32)
    low = total - high - middle
    notes = [jnp.broadcast_to(x[h : h + 1], (1, DH)) for x in (high, middle, low) for h in range(H)]
    notes += [jnp.full((1, DH), ids_ref[i].astype(F32)) for i in range(count)]
    notes.append(jnp.zeros((16 - len(notes), DH), F32))
    notes = jnp.concatenate(notes, axis=0).astype(BF16)
    for k in range(n):
        msgs[k][block : block + 16, :] = notes

    for copy in copies[3:5]:
        copy.wait()
    cum = lane_cumsum(jnp.concatenate([gates[i] for i in range(count)], axis=0))
    carried = jnp.exp(cum)
    place = lax.broadcasted_iota(jnp.int32, (1, slots), 1)
    rows = []
    for i in range(count):
        weight = adv_ref[i].astype(F32) / 1024.0
        opened = jnp.where(place < lens_ref[0, i], 1.0, 0.0)
        live = mask[i : i + 1, :].astype(F32) * opened * weight
        rows += [cum[H * i : H * i + H], carried[H * i : H * i + H], live, opened, jnp.zeros((2, slots), F32)]
    rows = jnp.concatenate(rows, axis=0)
    rows_ref[...] = rows.reshape(count, 8, slots)
    cols = to_columns(rows)
    cols_ref[...] = cols
    for i in range(count):
        copies[5 + 2 * i].wait()
        copies[6 + 2 * i].wait()
        for h in range(H):
            lanes = slice(h * DH, (h + 1) * DH)
            grad_out = (c[i, :, lanes].astype(F32) * cols[:, 8 * i + 4 : 8 * i + 5]).astype(BF16)
            scaled = (cols[:, 8 * i + 2 + h : 8 * i + 3 + h] * grad_out.astype(F32)).astype(BF16)
            at = H * (1 + i) + h
            matrices[at] = mm_tn(q[i, :, lanes], scaled)
            for k in range(n):
                rows = matrices[at, pl.ds(targets[k] * part, part), :]
                msgs[k][at * part + 16 : (at + 1) * part + 16, :] = rows.astype(BF16)


def noted_prompt(notes, i):
    return jnp.max(notes[3 * H + i : 3 * H + i + 1]).astype(jnp.int32)


def second_kernel(n, chips, cores, place_ref, *refs):
    got, msgs, later_ref, sums = refs[:n], refs[n + 1 : n + 1 + chips], refs[-2], refs[-1]
    part = DH // n
    block = H * part
    responses = (got[0].shape[0] - block - 16) // block
    place = [lax.rem(place_ref[0] + n - k, n) for k in range(n)]
    notes = [got[k][block : block + 16, :].astype(F32) for k in range(n)]
    logs = [x[0:H] + x[H : 2 * H] + x[2 * H : 3 * H] for x in notes]
    final = jnp.zeros((block, DH), F32)
    for k in range(n):
        later = jnp.zeros_like(logs[0])
        for other in range(n):
            if other != k:
                later = later + jnp.where(place[other] > place[k], logs[other], 0.0)
        if k == 0:
            later_ref[...] = jnp.concatenate([later, jnp.zeros((8 - H, DH), F32)], axis=0)
        decay = jnp.exp(later)
        decay = [jnp.broadcast_to(decay[h : h + 1], (part, DH)) for h in range(H)]
        final = final + jnp.concatenate(decay, axis=0) * got[k][0:block, :].astype(F32)
    sums[...] = jnp.zeros_like(sums)
    for k in range(n):
        for i in range(responses):
            at = block * (1 + i) + 16
            sums[noted_prompt(notes[k], i)] += got[k][at : at + block, :].astype(F32)
    final = final.astype(BF16)
    for k in range(chips):
        z = lax.rem(place_ref[1] + k, chips)
        msgs[k][0:block, :] = final
        for c in range(cores):
            msgs[k][(1 + c) * block : (2 + c) * block, :] = sums[z * cores + c].astype(BF16)


def swap_kernel(chips, place_ref, *refs):
    got, sent_ref, kept_ref = refs[:chips], refs[chips + 1], refs[chips + 2]
    block = got[0].shape[0] // 3
    totals = []
    for c in range(2):
        total = got[0][(1 + c) * block : (2 + c) * block, :].astype(F32)
        for k in range(1, chips):
            total = total + got[k][(1 + c) * block : (2 + c) * block, :].astype(F32)
        totals.append(total)
    for k in range(chips):
        final = got[k][0:block, :]
        sent_ref[k * block : (k + 1) * block, :] = final
        kept_ref[k * block : (k + 1) * block, :] = final
    low = place_ref[2] == 0
    sent_ref[chips * block :, :] = jnp.where(low, totals[1], totals[0]).astype(BF16)
    kept_ref[chips * block :, :] = jnp.where(low, totals[0], totals[1]).astype(BF16)


def third_kernel(n, chips, place_ref, *refs):
    noted, kept_ref, got_ref, msgs = refs[:n], refs[n], refs[n + 1], refs[n + 3 :]
    block = H * DH // n
    responses = (noted[0].shape[0] - block - 16) // block
    total = kept_ref[chips * block :, :].astype(F32) + got_ref[chips * block :, :].astype(F32)
    total = total.astype(BF16)
    for k in range(n):
        notes = noted[(n - k) % n][block : block + 16, :].astype(F32)
        for i in range(responses):
            p = noted_prompt(notes, i)
            slot = lax.rem(place_ref[1] + chips - lax.div(p, 2), chips)
            at = pl.ds(pl.multiple_of(slot * block, block), block)
            same = lax.rem(p, 2) == place_ref[2]
            state = jnp.where(same, kept_ref[at, :].astype(F32), got_ref[at, :].astype(F32))
            msgs[k][i * block : (i + 1) * block, :] = state.astype(BF16)
        msgs[k][responses * block :, :] = total


def sweep_kernel(r, cols_ref, rows_ref, q_ref, k_ref, v_ref, c_ref, *refs):
    out_ref, dq_ref, dk_hbm, dv_hbm, token_ref, dk_buf, dv_buf, sems = refs[-8:]
    token_ref[...] = jnp.zeros_like(token_ref)
    live = cols_ref[:, 8 * r + 4 : 8 * r + 5]
    causal = lax.broadcasted_iota(jnp.int32, (HALF, HALF), 0) >= lax.broadcasted_iota(
        jnp.int32, (HALF, HALF), 1
    )
    blocks = q_ref.shape[1] // HALF
    copies = []
    for h in range(H):
        lanes = slice(h * DH, (h + 1) * DH)
        cum = cols_ref[:, 8 * r + h : 8 * r + h + 1]
        dk = [None] * blocks
        dv = [None] * blocks
        for t in range(blocks):
            at = slice(t * HALF, (t + 1) * HALF)
            query = q_ref[r, at, lanes]
            grad_out = (c_ref[r, at, lanes].astype(F32) * live[at]).astype(BF16)
            out = None
            dq = None
            for s in range(t + 1):
                of = slice(s * HALF, (s + 1) * HALF)
                key = k_ref[r, of, lanes]
                value = v_ref[r, of, lanes]
                diff = cum[at] - rows_ref[r, h : h + 1, of]
                if s == t:
                    diff = jnp.where(causal, diff, NEVER)
                decay = jnp.exp(diff)
                mixing = (mm_nt(query, key) * decay).astype(BF16)
                scores = (mm_nt(grad_out, value) * decay).astype(BF16)
                o_new = mm(mixing, value)
                q_new = mm(scores, key)
                k_new = mm_tn(scores, query)
                v_new = mm_tn(mixing, grad_out)
                out = o_new if out is None else out + o_new
                dq = q_new if dq is None else dq + q_new
                dk[s] = k_new if dk[s] is None else dk[s] + k_new
                dv[s] = v_new if dv[s] is None else dv[s] + v_new
            out_ref[r, at, lanes] = out
            dq_ref[r, at, lanes] = dq
        for s in range(blocks):
            of = slice(s * HALF, (s + 1) * HALF)
            dk_buf[of, lanes] = dk[s].astype(BF16)
            dv_buf[of, lanes] = dv[s].astype(BF16)
        copies += [
            pltpu.make_async_copy(dk_buf.at[:, lanes], dk_hbm.at[r, :, lanes], sems.at[2 * h]),
            pltpu.make_async_copy(dv_buf.at[:, lanes], dv_hbm.at[r, :, lanes], sems.at[2 * h + 1]),
        ]
        copies[-2].start()
        copies[-1].start()
    for copy in copies:
        copy.wait()


def last_kernel(n, steps, place_ref, cols_ref, q_ref, c_ref, po_ref, pdq_ref, keys_ref, values_ref, suffix_ref, later_ref, *refs):
    got, (out_ref, dq_ref, dk_ref, dv_ref, start) = refs[:n], refs[n + 1 :]
    r = pl.program_id(0)
    part = DH // n
    block = H * part
    place = [lax.rem(place_ref[0] + n - k, n) * part for k in range(n)]

    def assemble(at):
        for k in range(n):
            for h in range(H):
                of = pl.multiple_of(at + h * part, part)
                start[h, pl.ds(pl.multiple_of(place[k], part), part), :] = got[k][pl.ds(of, part), :]

    @pl.when(r == 0)
    def _():
        assemble(steps * block)
        for h in range(H):
            lanes = slice(h * DH, (h + 1) * DH)
            factor = jnp.exp(suffix_ref[:, h : h + 1] + later_ref[h : h + 1, 0:1])
            dk_ref[0, :, lanes] = (factor * mm_nt(values_ref[0, :, lanes], start[h])).astype(BF16)
            dv_ref[0, :, lanes] = (factor * mm(keys_ref[0, :, lanes], start[h])).astype(BF16)

    assemble(r * block)
    mine = pltpu.roll(cols_ref[...], lax.rem(128 - 8 * r, 128), 1)
    live = mine[:, 4:5]
    opened = mine[:, 5:6]
    for h in range(H):
        lanes = slice(h * DH, (h + 1) * DH)
        carried = mine[:, 2 + h : 3 + h]
        grad_out = (c_ref[r, :, lanes].astype(F32) * live).astype(BF16)
        out = po_ref[r, :, lanes] + carried * mm(q_ref[r, :, lanes], start[h])
        out_ref[0, :, lanes] = (opened * out).astype(BF16)
        dq = pdq_ref[r, :, lanes] + carried * mm_nt(grad_out, start[h])
        dq_ref[0, :, lanes] = dq.astype(BF16)


def exchange(xs, axis):
    n = lax.axis_size(axis)
    moved = [lax.ppermute(xs[k], axis, [(s, (s + k) % n) for s in range(n)]) for k in range(1, n)]
    return [xs[0]] + moved


def shards(
    keys,
    values,
    prompt_gates,
    queries,
    resp_keys,
    resp_values,
    resp_gates,
    cotangent,
    group_ids,
    resp_lengths,
    loss_mask,
    advantages,
):
    n = lax.axis_size("prompt")
    chips = lax.axis_size("z")
    cores = lax.axis_size("core")
    place = jnp.stack([lax.axis_index(axis).astype(jnp.int32) for axis in ("prompt", "z", "core")])
    responses, slots, width = queries.shape
    block = H * DH // n
    tokens = keys.shape[1]
    shape = jax.ShapeDtypeStruct

    outs = pl.pallas_call(
        lambda *refs: first_kernel(n, *refs),
        out_shape=[shape((block * (1 + responses) + 16, DH), BF16)] * n
        + [shape((tokens, 128), F32), shape((slots, 128), F32), shape((responses, 8, slots), F32)],
        in_specs=[SMEM] * 4 + [ANY] * 7,
        out_specs=[VMEM] * (n + 3),
        scratch_shapes=[
            pltpu.VMEM(keys.shape, BF16),
            pltpu.VMEM(values.shape, BF16),
            pltpu.VMEM(prompt_gates.shape, F32),
            pltpu.VMEM(resp_gates.shape, F32),
            pltpu.VMEM(loss_mask.shape, jnp.int32),
            pltpu.VMEM(queries.shape, BF16),
            pltpu.VMEM(queries.shape, BF16),
            pltpu.VMEM((H * (1 + responses), DH, DH), F32),
            pltpu.SemaphoreType.DMA((5 + 2 * responses,)),
        ],
        compiler_params=params(62),
        name="first",
    )(
        place, group_ids, resp_lengths, advantages,
        keys, values, prompt_gates, resp_gates, loss_mask, queries, cotangent,
    )
    msgs, (suffix, cols, rows) = outs[:n], outs[n:]

    like = shape(queries.shape, F32)
    like_out = shape(queries.shape, BF16)

    def sweep(r, before, token):
        outs = pl.pallas_call(
            lambda *refs: sweep_kernel(r, *refs),
            out_shape=[like, like, like_out, like_out, shape((8, 128), F32)],
            in_specs=[VMEM] * 6 + [ANY] * (1 + len(before)),
            out_specs=[VMEM, VMEM, ANY, ANY, VMEM],
            scratch_shapes=[
                pltpu.VMEM((slots, width), BF16),
                pltpu.VMEM((slots, width), BF16),
                pltpu.SemaphoreType.DMA((2 * H,)),
            ],
            input_output_aliases={7 + k: k for k in range(len(before))},
            compiler_params=params(),
            name="sweep",
        )(cols, rows, queries, resp_keys, resp_values, cotangent, token, *before)
        return outs[:4], outs[4]

    got1 = exchange(msgs, "prompt")
    held, token = sweep(0, [], cols)
    outs = pl.pallas_call(
        lambda *refs: second_kernel(n, chips, cores, *refs),
        out_shape=[shape(((1 + cores) * block, DH), BF16)] * chips + [shape((8, DH), F32)],
        in_specs=[SMEM] + [VMEM] * n + [ANY],
        out_specs=[VMEM] * (chips + 1),
        scratch_shapes=[pltpu.VMEM((chips * cores, block, DH), F32)],
        compiler_params=params(),
        name="second",
    )(place, *got1, token)
    msgs, later = outs[:chips], outs[chips]
    got2 = exchange(msgs, "z")
    held, token = sweep(1, held, later)
    sent, kept = pl.pallas_call(
        lambda *refs: swap_kernel(chips, *refs),
        out_shape=[shape(((chips + 1) * block, DH), BF16)] * 2,
        in_specs=[SMEM] + [VMEM] * chips + [ANY],
        out_specs=[VMEM, VMEM],
        compiler_params=params(),
        name="swap",
    )(place, *got2, token)
    swapped = exchange([kept, sent], "core")[1]
    held, token = sweep(2, held, kept)
    msgs = pl.pallas_call(
        lambda *refs: third_kernel(n, chips, *refs),
        out_shape=[shape(((responses + 1) * block, DH), BF16)] * n,
        in_specs=[SMEM] + [VMEM] * (n + 2) + [ANY],
        out_specs=[VMEM] * n,
        compiler_params=params(),
        name="third",
    )(place, *got1, kept, swapped, token)
    got3 = exchange(msgs, "prompt")
    held, token = sweep(3, held, msgs[0])
    partial_out, partial_dq, resp_dk, resp_dv = held

    step = pl.BlockSpec((1, slots, width), lambda r: (r, 0, 0))
    resp_out, resp_dq, prompt_dk, prompt_dv = pl.pallas_call(
        lambda *refs: last_kernel(n, responses, *refs),
        grid=(responses,),
        out_shape=[like_out, like_out, shape(keys.shape, BF16), shape(keys.shape, BF16)],
        in_specs=[SMEM] + [VMEM] * (9 + n) + [ANY],
        out_specs=[step, step, VMEM, VMEM],
        scratch_shapes=[pltpu.VMEM((H, DH, DH), BF16)],
        compiler_params=params(),
        name="last",
    )(
        place, cols, queries, cotangent, partial_out, partial_dq, keys, values, suffix, later, *got3, token
    )
    return (resp_out, resp_dq, resp_dk, resp_dv, prompt_dk, prompt_dv)


def solution(mesh):
    n, count = mesh.shape["prompt"], mesh.shape["resp"]
    mesh = jax.sharding.Mesh(mesh.devices.reshape(n, count // 2, 2), ("prompt", "z", "core"))
    spread = P(("prompt", "z", "core"))
    three = P(("prompt", "z", "core"), None, None)
    two = P(("prompt", "z", "core"), None)
    prompt = P(("z", "core"), "prompt", None)
    return jax.shard_map(
        shards,
        mesh=mesh,
        in_specs=(
            prompt,
            prompt,
            P(("z", "core"), None, "prompt"),
            three,
            three,
            three,
            three,
            three,
            spread,
            two,
            two,
            spread,
        ),
        out_specs=(three, three, three, three, prompt, prompt),
        check_vma=False,
    )
```

```python
import jax
import jax.numpy as jnp
from jax import lax
from jax.experimental import pallas as pl
from jax.experimental.pallas import tpu as pltpu
from jax.sharding import PartitionSpec as P

H = 2
DH = 128
HALF = 256
F32 = jnp.float32
BF16 = jnp.bfloat16
NEVER = -1e30
VMEM = pl.BlockSpec(memory_space=pltpu.VMEM)
ANY = pl.BlockSpec(memory_space=pl.ANY)
SMEM = pl.BlockSpec(memory_space=pltpu.SMEM)


def params(mebibytes=16):
    return pltpu.CompilerParams(vmem_limit_bytes=mebibytes * 1024 * 1024)


def mm(a, b):
    return lax.dot_general(a, b, (((1,), (0,)), ((), ())), preferred_element_type=F32)


def mm_nt(a, b):
    return lax.dot_general(a, b, (((1,), (1,)), ((), ())), preferred_element_type=F32)


def mm_tn(a, b):
    return lax.dot_general(a, b, (((0,), (0,)), ((), ())), preferred_element_type=F32)


def in_hbm(x):
    return pltpu.with_memory_space_constraint(x, pltpu.HBM)


def three_terms(x):
    high = x.astype(BF16)
    rest = x - high.astype(F32)
    middle = rest.astype(BF16)
    return high, middle, (rest - middle.astype(F32)).astype(BF16)


def lane_cumsum(x):
    rows, width = x.shape
    ones = lax.broadcasted_iota(jnp.int32, (128, 128), 0) <= lax.broadcasted_iota(jnp.int32, (128, 128), 1)
    terms = jnp.concatenate(three_terms(x), axis=0)
    starts = range(0, width, 128)
    sums = mm(jnp.concatenate([terms[:, b : b + 128] for b in starts], axis=0), ones.astype(F32).astype(BF16))
    parts = []
    before = jnp.zeros((rows, 1), F32)
    for b in range(len(starts)):
        at = 3 * rows * b
        part = sums[at : at + rows] + sums[at + rows : at + 2 * rows] + sums[at + 2 * rows : at + 3 * rows]
        part = part + before
        before = part[:, 127:128]
        parts.append(part)
    return jnp.concatenate(parts, axis=1)


def first_kernel(
    n, ids_ref, lens_ref, adv_ref, keys_hbm, values_hbm, pgates_hbm, gates_hbm, mask_hbm, q_hbm, c_hbm, k_hbm, v_hbm,
    *refs,
):
    msgs, (cols_ref, rows_ref, q, c, k_out, v_out) = refs[:n], refs[n : n + 6]
    keys, values, pgates, gates, mask, matrices, sems = refs[n + 6 :]
    pairs = [(pgates_hbm, pgates), (gates_hbm, gates), (mask_hbm, mask), (keys_hbm, keys), (values_hbm, values)]
    count = gates.shape[0]
    slots = gates.shape[2]
    tokens = keys.shape[1]
    for i in range(count):
        pairs += [(q_hbm.at[i], q.at[i]), (c_hbm.at[i], c.at[i])]
    pairs += [(k_hbm, k_out), (v_hbm, v_out)]
    copies = [pltpu.make_async_copy(a, b, sems.at[i]) for i, (a, b) in enumerate(pairs)]
    for copy in copies:
        copy.start()
    part = DH // n
    block = H * part
    me = lax.axis_index("prompt")
    targets = [lax.rem(me + k, n) for k in range(n)]

    def spread(at):
        for k in range(n):
            of = pl.ds(pl.multiple_of(targets[k] * part, part), part)
            msgs[k][at * part + (16 if at >= H else 0) : (at + 1) * part + (16 if at >= H else 0), :] = matrices[
                at, of, :
            ].astype(BF16)

    for copy in copies[:3]:
        copy.wait()
    piece = jnp.concatenate([pgates[0], jnp.zeros((H, slots - tokens), F32)], axis=1)
    gate_rows = [gates[i] for i in range(count)] + [piece, jnp.zeros((16 - H * (count + 1), slots), F32)]
    cum = lane_cumsum(jnp.concatenate(gate_rows, axis=0))
    carried = jnp.exp(cum)
    place = lax.broadcasted_iota(jnp.int32, (1, slots), 1)
    rows = []
    factors = []
    for i in range(count):
        weight = adv_ref[i].astype(F32) / 1024.0
        opened = jnp.where(place < lens_ref[0, i], 1.0, 0.0)
        live = mask[i : i + 1, :].astype(F32) * opened * weight
        rows += [cum[H * i : H * i + H], carried[H * i : H * i + H], live, opened, jnp.zeros((2, slots), F32)]
        factors.append(carried[H * i : H * i + H] * live)
    rows_ref[...] = jnp.concatenate(rows, axis=0).reshape(count, 8, slots)
    piece = cum[H * count : H * count + H]
    total = piece[:, -1:]
    suffix = total - piece
    rows += [suffix, jnp.zeros((128 - 8 * count - H, slots), F32)]
    cols_ref[...] = jnp.concatenate(rows, axis=0).T

    for copy in copies[3:5]:
        copy.wait()
    turned = keys[0].T
    later = jnp.exp(suffix[:, :tokens])
    for h in range(H):
        lanes = slice(h * DH, (h + 1) * DH)
        scaled = turned[lanes].astype(F32) * later[h : h + 1]
        high = scaled.astype(BF16)
        low = (scaled - high.astype(F32)).astype(BF16)
        both = mm(jnp.concatenate([high, low], axis=0), values[0, :, lanes])
        matrices[h] = both[:DH] + both[DH:]
        spread(h)
    notes = [jnp.broadcast_to(x[h : h + 1].astype(F32), (1, DH)) for x in three_terms(total) for h in range(H)]
    notes += [jnp.full((1, DH), ids_ref[i].astype(F32)) for i in range(count)]
    notes.append(jnp.zeros((16 - len(notes), DH), F32))
    notes = jnp.concatenate(notes, axis=0).astype(BF16)
    for k in range(n):
        msgs[k][block : block + 16, :] = notes

    for i in range(count):
        copies[5 + 2 * i].wait()
        turned = q[i].T
        copies[6 + 2 * i].wait()
        for h in range(H):
            lanes = slice(h * DH, (h + 1) * DH)
            scaled = (turned[lanes].astype(F32) * factors[i][h : h + 1]).astype(BF16)
            matrices[H * (1 + i) + h] = mm(scaled, c[i, :, lanes])
            spread(H * (1 + i) + h)
    for copy in copies[5 + 2 * count :]:
        copy.wait()


def noted_prompt(notes, i):
    return jnp.max(notes[3 * H + i : 3 * H + i + 1]).astype(jnp.int32)


def second_kernel(n, chips, cores, *refs):
    row, z_at = lax.axis_index("prompt"), lax.axis_index("z")
    got, msgs, later_ref, sums = refs[:n], refs[n + 1 : n + 1 + chips], refs[-2], refs[-1]
    part = DH // n
    block = H * part
    responses = (got[0].shape[0] - block - 16) // block
    place = [lax.rem(row + n - k, n) for k in range(n)]
    notes = [got[k][block : block + 16, :].astype(F32) for k in range(n)]
    logs = [x[0:H] + x[H : 2 * H] + x[2 * H : 3 * H] for x in notes]
    final = jnp.zeros((block, DH), F32)
    for k in range(n):
        later = jnp.zeros_like(logs[0])
        for other in range(n):
            if other != k:
                later = later + jnp.where(place[other] > place[k], logs[other], 0.0)
        if k == 0:
            later_ref[...] = jnp.concatenate([later, jnp.zeros((8 - H, DH), F32)], axis=0)
        decay = jnp.exp(later)
        decay = [jnp.broadcast_to(decay[h : h + 1], (part, DH)) for h in range(H)]
        final = final + jnp.concatenate(decay, axis=0) * got[k][0:block, :].astype(F32)
    sums[...] = jnp.zeros_like(sums)
    for k in range(n):
        for i in range(responses):
            at = block * (1 + i) + 16
            sums[noted_prompt(notes[k], i)] += got[k][at : at + block, :].astype(F32)
    final = final.astype(BF16)
    for k in range(chips):
        z = lax.rem(z_at + k, chips)
        msgs[k][0:block, :] = final
        for c in range(cores):
            msgs[k][(1 + c) * block : (2 + c) * block, :] = sums[z * cores + c].astype(BF16)


def swap_kernel(chips, *refs):
    got, sent_ref, kept_ref = refs[:chips], refs[chips + 1], refs[chips + 2]
    block = got[0].shape[0] // 3
    totals = []
    for c in range(2):
        total = got[0][(1 + c) * block : (2 + c) * block, :].astype(F32)
        for k in range(1, chips):
            total = total + got[k][(1 + c) * block : (2 + c) * block, :].astype(F32)
        totals.append(total)
    for k in range(chips):
        final = got[k][0:block, :]
        sent_ref[k * block : (k + 1) * block, :] = final
        kept_ref[k * block : (k + 1) * block, :] = final
    low = lax.axis_index("core") == 0
    sent_ref[chips * block :, :] = jnp.where(low, totals[1], totals[0]).astype(BF16)
    kept_ref[chips * block :, :] = jnp.where(low, totals[0], totals[1]).astype(BF16)


def third_kernel(n, chips, *refs):
    z_at, core = lax.axis_index("z"), lax.axis_index("core")
    noted, kept_ref, got_ref, msgs = refs[:n], refs[n], refs[n + 1], refs[n + 3 :]
    block = H * DH // n
    responses = (noted[0].shape[0] - block - 16) // block
    total = kept_ref[chips * block :, :].astype(F32) + got_ref[chips * block :, :].astype(F32)
    total = total.astype(BF16)
    for k in range(n):
        notes = noted[(n - k) % n][block : block + 16, :].astype(F32)
        for i in range(responses):
            p = noted_prompt(notes, i)
            slot = lax.rem(z_at + chips - lax.div(p, 2), chips)
            at = pl.ds(pl.multiple_of(slot * block, block), block)
            same = lax.rem(p, 2) == core
            state = jnp.where(same, kept_ref[at, :].astype(F32), got_ref[at, :].astype(F32))
            msgs[k][i * block : (i + 1) * block, :] = state.astype(BF16)
        msgs[k][responses * block :, :] = total


def sweep_kernel(r, cols_ref, rows_ref, q_ref, k_ref, v_ref, c_ref, *refs):
    out_ref, dq_ref, dk_hbm, dv_hbm, token_ref, dk_buf, dv_buf, sems = refs[-8:]
    token_ref[...] = jnp.zeros_like(token_ref)
    live = cols_ref[:, 8 * r + 4 : 8 * r + 5]
    causal = lax.broadcasted_iota(jnp.int32, (HALF, HALF), 0) >= lax.broadcasted_iota(
        jnp.int32, (HALF, HALF), 1
    )
    blocks = q_ref.shape[1] // HALF
    copies = []
    for h in range(H):
        lanes = slice(h * DH, (h + 1) * DH)
        cum = cols_ref[:, 8 * r + h : 8 * r + h + 1]
        dk = [None] * blocks
        dv = [None] * blocks
        for t in range(blocks):
            at = slice(t * HALF, (t + 1) * HALF)
            query = q_ref[r, at, lanes]
            grad_out = (c_ref[r, at, lanes].astype(F32) * live[at]).astype(BF16)
            out = None
            dq = None
            for s in range(t + 1):
                of = slice(s * HALF, (s + 1) * HALF)
                key = k_ref[r, of, lanes]
                value = v_ref[r, of, lanes]
                diff = cum[at] - rows_ref[r, h : h + 1, of]
                if s == t:
                    diff = jnp.where(causal, diff, NEVER)
                decay = jnp.exp(diff)
                mixing = (mm_nt(query, key) * decay).astype(BF16)
                scores = (mm_nt(grad_out, value) * decay).astype(BF16)
                o_new = mm(mixing, value)
                q_new = mm(scores, key)
                k_new = mm_tn(scores, query)
                v_new = mm_tn(mixing, grad_out)
                out = o_new if out is None else out + o_new
                dq = q_new if dq is None else dq + q_new
                dk[s] = k_new if dk[s] is None else dk[s] + k_new
                dv[s] = v_new if dv[s] is None else dv[s] + v_new
            out_ref[r, at, lanes] = out
            dq_ref[r, at, lanes] = dq
        for s in range(blocks):
            of = slice(s * HALF, (s + 1) * HALF)
            dk_buf[of, lanes] = dk[s].astype(BF16)
            dv_buf[of, lanes] = dv[s].astype(BF16)
        copies += [
            pltpu.make_async_copy(dk_buf.at[:, lanes], dk_hbm.at[r, :, lanes], sems.at[2 * h]),
            pltpu.make_async_copy(dv_buf.at[:, lanes], dv_hbm.at[r, :, lanes], sems.at[2 * h + 1]),
        ]
        copies[-2].start()
        copies[-1].start()
    for copy in copies:
        copy.wait()


def last_kernel(n, count, cols_ref, q_ref, c_ref, po_ref, pdq_ref, keys_ref, values_ref, later_ref, *refs):
    got, (out_hbm, dq_hbm, dk_ref, dv_ref, start, out_buf, dq_buf, sems) = refs[:n], refs[n + 1 :]
    part = DH // n
    block = H * part
    row = lax.axis_index("prompt")
    for r in range(count + 1):
        for k in range(n):
            of = pl.ds(pl.multiple_of(lax.rem(row + n - k, n) * part, part), part)
            for h in range(H):
                start[r, h, of, :] = got[k][r * block + h * part : r * block + (h + 1) * part, :]
    copies = []
    for r in range(count):
        live = cols_ref[:, 8 * r + 4 : 8 * r + 5]
        opened = cols_ref[:, 8 * r + 5 : 8 * r + 6]
        for h in range(H):
            lanes = slice(h * DH, (h + 1) * DH)
            carried = cols_ref[:, 8 * r + 2 + h : 8 * r + 3 + h]
            grad_out = (c_ref[r, :, lanes].astype(F32) * live).astype(BF16)
            out = po_ref[r, :, lanes] + carried * mm(q_ref[r, :, lanes], start[r, h])
            out_buf[r, :, lanes] = (opened * out).astype(BF16)
            dq = pdq_ref[r, :, lanes] + carried * mm_nt(grad_out, start[r, h])
            dq_buf[r, :, lanes] = dq.astype(BF16)
        copies += [
            pltpu.make_async_copy(out_buf.at[r], out_hbm.at[r], sems.at[2 * r]),
            pltpu.make_async_copy(dq_buf.at[r], dq_hbm.at[r], sems.at[2 * r + 1]),
        ]
        copies[-2].start()
        copies[-1].start()
    tokens = keys_ref.shape[1]
    for h in range(H):
        lanes = slice(h * DH, (h + 1) * DH)
        suffix = cols_ref[:tokens, 8 * count + h : 8 * count + h + 1]
        factor = jnp.exp(suffix + later_ref[h : h + 1, 0:1])
        dk_ref[0, :, lanes] = (factor * mm_nt(values_ref[0, :, lanes], start[count, h])).astype(BF16)
        dv_ref[0, :, lanes] = (factor * mm(keys_ref[0, :, lanes], start[count, h])).astype(BF16)
    for copy in copies:
        copy.wait()


def exchange(xs, axis):
    n = lax.axis_size(axis)
    moved = [lax.ppermute(xs[k], axis, [(s, (s + k) % n) for s in range(n)]) for k in range(1, n)]
    return [xs[0]] + moved


def shards(
    keys,
    values,
    prompt_gates,
    queries,
    resp_keys,
    resp_values,
    resp_gates,
    cotangent,
    group_ids,
    resp_lengths,
    loss_mask,
    advantages,
):
    n = lax.axis_size("prompt")
    chips = lax.axis_size("z")
    cores = lax.axis_size("core")
    responses, slots, width = queries.shape
    block = H * DH // n
    shape = jax.ShapeDtypeStruct

    outs = pl.pallas_call(
        lambda *refs: first_kernel(n, *refs),
        out_shape=[shape((block * (1 + responses) + 16, DH), BF16)] * n
        + [shape((slots, 128), F32), shape((responses, 8, slots), F32)]
        + [shape(queries.shape, BF16)] * 4,
        in_specs=[SMEM] * 3 + [ANY] * 9,
        out_specs=[VMEM] * (n + 6),
        scratch_shapes=[
            pltpu.VMEM(keys.shape, BF16),
            pltpu.VMEM(values.shape, BF16),
            pltpu.VMEM(prompt_gates.shape, F32),
            pltpu.VMEM(resp_gates.shape, F32),
            pltpu.VMEM(loss_mask.shape, jnp.int32),
            pltpu.VMEM((H * (1 + responses), DH, DH), F32),
            pltpu.SemaphoreType.DMA((7 + 2 * responses,)),
        ],
        compiler_params=params(32),
        name="first",
    )(
        *[in_hbm(x) for x in (group_ids, resp_lengths, advantages, keys, values, prompt_gates, resp_gates)],
        *[in_hbm(x) for x in (loss_mask, queries, cotangent, resp_keys, resp_values)],
    )
    msgs, (cols, rows, queries, cotangent, resp_keys, resp_values) = outs[:n], outs[n:]

    like = shape(queries.shape, F32)
    like_out = shape(queries.shape, BF16)

    def sweep(r, before, token):
        outs = pl.pallas_call(
            lambda *refs: sweep_kernel(r, *refs),
            out_shape=[like, like, like_out, like_out, shape((8, 128), F32)],
            in_specs=[VMEM] * 6 + [ANY] * (1 + len(before)),
            out_specs=[VMEM, VMEM, ANY, ANY, VMEM],
            scratch_shapes=[
                pltpu.VMEM((slots, width), BF16),
                pltpu.VMEM((slots, width), BF16),
                pltpu.SemaphoreType.DMA((2 * H,)),
            ],
            input_output_aliases={7 + k: k for k in range(len(before))},
            compiler_params=params(),
            name="sweep",
        )(cols, rows, queries, resp_keys, resp_values, cotangent, token, *before)
        return outs[:4], outs[4]

    got1 = exchange(msgs, "prompt")
    held, token = sweep(0, [], cols)
    outs = pl.pallas_call(
        lambda *refs: second_kernel(n, chips, cores, *refs),
        out_shape=[shape(((1 + cores) * block, DH), BF16)] * chips + [shape((8, DH), F32)],
        in_specs=[VMEM] * n + [ANY],
        out_specs=[VMEM] * (chips + 1),
        scratch_shapes=[pltpu.VMEM((chips * cores, block, DH), F32)],
        compiler_params=params(),
        name="second",
    )(*got1, token)
    msgs, later = outs[:chips], outs[chips]
    got2 = exchange(msgs, "z")
    held, token = sweep(1, held, later)
    sent, kept = pl.pallas_call(
        lambda *refs: swap_kernel(chips, *refs),
        out_shape=[shape(((chips + 1) * block, DH), BF16)] * 2,
        in_specs=[VMEM] * chips + [ANY],
        out_specs=[VMEM, VMEM],
        compiler_params=params(),
        name="swap",
    )(*got2, token)
    swapped = exchange([kept, sent], "core")[1]
    held, token = sweep(2, held, kept)
    msgs = pl.pallas_call(
        lambda *refs: third_kernel(n, chips, *refs),
        out_shape=[shape(((responses + 1) * block, DH), BF16)] * n,
        in_specs=[VMEM] * (n + 2) + [ANY],
        out_specs=[VMEM] * n,
        compiler_params=params(),
        name="third",
    )(*got1, kept, swapped, token)
    got3 = exchange(msgs, "prompt")
    held, token = sweep(3, held, msgs[0])
    partial_out, partial_dq, resp_dk, resp_dv = held

    resp_out, resp_dq, prompt_dk, prompt_dv = pl.pallas_call(
        lambda *refs: last_kernel(n, responses, *refs),
        out_shape=[like_out, like_out, shape(keys.shape, BF16), shape(keys.shape, BF16)],
        in_specs=[VMEM] * (8 + n) + [ANY],
        out_specs=[ANY, ANY, VMEM, VMEM],
        scratch_shapes=[
            pltpu.VMEM((responses + 1, H, DH, DH), BF16),
            pltpu.VMEM(queries.shape, BF16),
            pltpu.VMEM(queries.shape, BF16),
            pltpu.SemaphoreType.DMA((2 * responses,)),
        ],
        compiler_params=params(),
        name="last",
    )(cols, queries, cotangent, partial_out, partial_dq, keys, values, later, *got3, token)
    return (resp_out, resp_dq, resp_dk, resp_dv, prompt_dk, prompt_dv)


def solution(mesh):
    n, count = mesh.shape["prompt"], mesh.shape["resp"]
    mesh = jax.sharding.Mesh(mesh.devices.reshape(n, count // 2, 2), ("prompt", "z", "core"))
    spread = P(("prompt", "z", "core"))
    three = P(("prompt", "z", "core"), None, None)
    two = P(("prompt", "z", "core"), None)
    prompt = P(("z", "core"), "prompt", None)
    return jax.shard_map(
        shards,
        mesh=mesh,
        in_specs=(
            prompt,
            prompt,
            P(("z", "core"), None, "prompt"),
            three,
            three,
            three,
            three,
            three,
            spread,
            two,
            two,
            spread,
        ),
        out_specs=(three, three, three, three, prompt, prompt),
        check_vma=False,
    )
```

```python
import jax
import jax.numpy as jnp
from jax import lax
from jax.experimental import pallas as pl
from jax.experimental.pallas import tpu as pltpu
from jax.sharding import PartitionSpec as P

H = 2
DH = 128
HALF = 256
LOG2E = 1.4426950408889634
F32 = jnp.float32
BF16 = jnp.bfloat16
NEVER = -1e30
VMEM = pl.BlockSpec(memory_space=pltpu.VMEM)
ANY = pl.BlockSpec(memory_space=pl.ANY)
SMEM = pl.BlockSpec(memory_space=pltpu.SMEM)


def params(mebibytes=16):
    return pltpu.CompilerParams(vmem_limit_bytes=mebibytes * 1024 * 1024)


def mm(a, b):
    return lax.dot_general(a, b, (((1,), (0,)), ((), ())), preferred_element_type=F32)


def mm_nt(a, b):
    return lax.dot_general(a, b, (((1,), (1,)), ((), ())), preferred_element_type=F32)


def mm_tn(a, b):
    return lax.dot_general(a, b, (((0,), (0,)), ((), ())), preferred_element_type=F32)


def in_hbm(x):
    return pltpu.with_memory_space_constraint(x, pltpu.HBM)


def three_terms(x):
    high = x.astype(BF16)
    rest = x - high.astype(F32)
    middle = rest.astype(BF16)
    return high, middle, (rest - middle.astype(F32)).astype(BF16)


def lane_cumsum(x):
    rows, width = x.shape
    ones = lax.broadcasted_iota(jnp.int32, (128, 128), 0) <= lax.broadcasted_iota(jnp.int32, (128, 128), 1)
    terms = jnp.concatenate(three_terms(x), axis=0)
    starts = range(0, width, 128)
    sums = mm(jnp.concatenate([terms[:, b : b + 128] for b in starts], axis=0), ones.astype(F32).astype(BF16))
    parts = []
    before = jnp.zeros((rows, 1), F32)
    for b in range(len(starts)):
        at = 3 * rows * b
        part = sums[at : at + rows] + sums[at + rows : at + 2 * rows] + sums[at + 2 * rows : at + 3 * rows]
        part = part + before
        before = part[:, 127:128]
        parts.append(part)
    return jnp.concatenate(parts, axis=1)


def first_kernel(
    n, ids_ref, lens_ref, adv_ref, keys_hbm, values_hbm, pgates_hbm, gates_hbm, mask_hbm, q_hbm, c_hbm, k_hbm, v_hbm,
    *refs,
):
    msgs, (cols_ref, rows_ref, q, c, k_out, v_out) = refs[:n], refs[n : n + 6]
    keys, values, pgates, gates, mask, matrices, sems = refs[n + 6 :]
    pairs = [(pgates_hbm, pgates), (gates_hbm, gates), (mask_hbm, mask), (keys_hbm, keys), (values_hbm, values)]
    count = gates.shape[0]
    slots = gates.shape[2]
    tokens = keys.shape[1]
    for i in range(count):
        pairs += [(q_hbm.at[i], q.at[i]), (c_hbm.at[i], c.at[i])]
    pairs += [(k_hbm, k_out), (v_hbm, v_out)]
    copies = [pltpu.make_async_copy(a, b, sems.at[i]) for i, (a, b) in enumerate(pairs)]
    for copy in copies:
        copy.start()
    part = DH // n
    block = H * part
    me = lax.axis_index("prompt")
    targets = [lax.bitwise_xor(me, k) for k in range(n)]

    def spread(at):
        for k in range(n):
            of = pl.ds(pl.multiple_of(targets[k] * part, part), part)
            msgs[k][at * part + (16 if at >= H else 0) : (at + 1) * part + (16 if at >= H else 0), :] = matrices[
                at, of, :
            ].astype(BF16)

    for copy in copies[:3]:
        copy.wait()
    piece = jnp.concatenate([pgates[0], jnp.zeros((H, slots - tokens), F32)], axis=1)
    gate_rows = [gates[i] for i in range(count)] + [piece, jnp.zeros((16 - H * (count + 1), slots), F32)]
    cum = lane_cumsum(jnp.concatenate(gate_rows, axis=0))
    carried = jnp.exp(cum)
    place = lax.broadcasted_iota(jnp.int32, (1, slots), 1)
    rows = []
    factors = []
    for i in range(count):
        weight = adv_ref[i].astype(F32) / 1024.0
        opened = jnp.where(place < lens_ref[0, i], 1.0, 0.0)
        live = mask[i : i + 1, :].astype(F32) * opened * weight
        rows += [cum[H * i : H * i + H], carried[H * i : H * i + H], live, opened, jnp.zeros((2, slots), F32)]
        factors.append(carried[H * i : H * i + H] * live)
    rows_ref[...] = jnp.concatenate(rows, axis=0).reshape(count, 8, slots)
    piece = cum[H * count : H * count + H]
    total = piece[:, -1:]
    suffix = total - piece
    rows += [suffix, jnp.zeros((128 - 8 * count - H, slots), F32)]
    cols_ref[...] = jnp.concatenate(rows, axis=0).T

    for copy in copies[3:5]:
        copy.wait()
    turned = keys[0].T
    later = jnp.exp(suffix[:, :tokens])
    for h in range(H):
        lanes = slice(h * DH, (h + 1) * DH)
        scaled = turned[lanes].astype(F32) * later[h : h + 1]
        high = scaled.astype(BF16)
        low = (scaled - high.astype(F32)).astype(BF16)
        both = mm(jnp.concatenate([high, low], axis=0), values[0, :, lanes])
        matrices[h] = both[:DH] + both[DH:]
        spread(h)
    notes = [jnp.broadcast_to(x[h : h + 1].astype(F32), (1, DH)) for x in three_terms(total) for h in range(H)]
    notes += [jnp.full((1, DH), ids_ref[i].astype(F32)) for i in range(count)]
    notes.append(jnp.zeros((16 - len(notes), DH), F32))
    notes = jnp.concatenate(notes, axis=0).astype(BF16)
    for k in range(n):
        msgs[k][block : block + 16, :] = notes

    for i in range(count):
        copies[5 + 2 * i].wait()
        turned = q[i].T
        copies[6 + 2 * i].wait()
        for h in range(H):
            lanes = slice(h * DH, (h + 1) * DH)
            scaled = (turned[lanes].astype(F32) * factors[i][h : h + 1]).astype(BF16)
            matrices[H * (1 + i) + h] = mm(scaled, c[i, :, lanes])
            spread(H * (1 + i) + h)
    for copy in copies[5 + 2 * count :]:
        copy.wait()


def noted_prompt(notes, i):
    return jnp.max(notes[3 * H + i : 3 * H + i + 1]).astype(jnp.int32)


def second_kernel(n, chips, cores, *refs):
    row, z_at = lax.axis_index("prompt"), lax.axis_index("z")
    got, msgs, later_ref, sums = refs[:n], refs[n + 1 : n + 1 + chips], refs[-2], refs[-1]
    part = DH // n
    block = H * part
    responses = (got[0].shape[0] - block - 16) // block
    place = [lax.bitwise_xor(row, k) for k in range(n)]
    notes = [got[k][block : block + 16, :].astype(F32) for k in range(n)]
    logs = [x[0:H] + x[H : 2 * H] + x[2 * H : 3 * H] for x in notes]
    final = jnp.zeros((block, DH), F32)
    for k in range(n):
        later = jnp.zeros_like(logs[0])
        for other in range(n):
            if other != k:
                later = later + jnp.where(place[other] > place[k], logs[other], 0.0)
        if k == 0:
            later_ref[...] = jnp.concatenate([later, jnp.zeros((8 - H, DH), F32)], axis=0)
        decay = jnp.exp(later)
        decay = [jnp.broadcast_to(decay[h : h + 1], (part, DH)) for h in range(H)]
        final = final + jnp.concatenate(decay, axis=0) * got[k][0:block, :].astype(F32)
    sums[...] = jnp.zeros_like(sums)
    for k in range(n):
        for i in range(responses):
            at = block * (1 + i) + 16
            sums[noted_prompt(notes[k], i)] += got[k][at : at + block, :].astype(F32)
    final = final.astype(BF16)
    for k in range(chips):
        z = lax.bitwise_xor(z_at, k)
        msgs[k][0:block, :] = final
        for c in range(cores):
            msgs[k][(1 + c) * block : (2 + c) * block, :] = sums[z * cores + c].astype(BF16)


def swap_kernel(chips, *refs):
    got, sent_ref, kept_ref = refs[:chips], refs[chips + 1], refs[chips + 2]
    block = got[0].shape[0] // 3
    totals = []
    for c in range(2):
        total = got[0][(1 + c) * block : (2 + c) * block, :].astype(F32)
        for k in range(1, chips):
            total = total + got[k][(1 + c) * block : (2 + c) * block, :].astype(F32)
        totals.append(total)
    for k in range(chips):
        final = got[k][0:block, :]
        sent_ref[k * block : (k + 1) * block, :] = final
        kept_ref[k * block : (k + 1) * block, :] = final
    low = lax.axis_index("core") == 0
    sent_ref[chips * block :, :] = jnp.where(low, totals[1], totals[0]).astype(BF16)
    kept_ref[chips * block :, :] = jnp.where(low, totals[0], totals[1]).astype(BF16)


def third_kernel(n, chips, *refs):
    z_at, core = lax.axis_index("z"), lax.axis_index("core")
    noted, kept_ref, got_ref, msgs = refs[:n], refs[n], refs[n + 1], refs[n + 3 :]
    block = H * DH // n
    responses = (noted[0].shape[0] - block - 16) // block
    total = kept_ref[chips * block :, :].astype(F32) + got_ref[chips * block :, :].astype(F32)
    total = total.astype(BF16)
    for k in range(n):
        notes = noted[k][block : block + 16, :].astype(F32)
        for i in range(responses):
            p = noted_prompt(notes, i)
            slot = lax.bitwise_xor(z_at, lax.div(p, 2))
            at = pl.ds(pl.multiple_of(slot * block, block), block)
            same = lax.rem(p, 2) == core
            state = jnp.where(same, kept_ref[at, :].astype(F32), got_ref[at, :].astype(F32))
            msgs[k][i * block : (i + 1) * block, :] = state.astype(BF16)
        msgs[k][responses * block :, :] = total


def sweep_kernel(r, cols_ref, rows_ref, q_ref, k_ref, v_ref, c_ref, *refs):
    out_ref, dq_ref, dk_hbm, dv_hbm, token_ref, dk_buf, dv_buf, sems = refs[-8:]
    token_ref[...] = jnp.zeros_like(token_ref)
    slots = q_ref.shape[1]
    live = cols_ref[:, 8 * r + 4 : 8 * r + 5]
    quarter = HALF // 2
    causal = lax.broadcasted_iota(jnp.int32, (quarter, quarter), 0) >= lax.broadcasted_iota(
        jnp.int32, (quarter, quarter), 1
    )
    blank = jnp.zeros((quarter, quarter), BF16)
    grad_all = (c_ref[r].astype(F32) * live).astype(BF16)
    query_turned = q_ref[r].T
    grad_turned = grad_all.T
    blocks = slots // HALF
    copies = []

    def decayed(products, cum, row, diagonal):
        if not diagonal:
            decay = jnp.exp2(cum - row)
            return [(x * decay).astype(BF16) for x in products]
        first = jnp.exp2(jnp.where(causal, cum[:quarter] - row[:, :quarter], NEVER))
        left = jnp.exp2(cum[quarter:] - row[:, :quarter])
        right = jnp.exp2(jnp.where(causal, cum[quarter:] - row[:, quarter:], NEVER))
        results = []
        for x in products:
            upper = jnp.concatenate([(x[:quarter, :quarter] * first).astype(BF16), blank], axis=1)
            lower = [(x[quarter:, :quarter] * left).astype(BF16), (x[quarter:, quarter:] * right).astype(BF16)]
            results.append(jnp.concatenate([upper, jnp.concatenate(lower, axis=1)], axis=0))
        return results

    for h in range(H):
        lanes = slice(h * DH, (h + 1) * DH)
        cum = cols_ref[:, 8 * r + h : 8 * r + h + 1] * LOG2E
        row = rows_ref[r, h : h + 1, :] * LOG2E
        dk = [None] * blocks
        dv = [None] * blocks
        for t in range(blocks):
            at = slice(t * HALF, (t + 1) * HALF)
            query = q_ref[r, at, lanes]
            grad_out = grad_all[at, lanes]
            out = None
            dq = None
            for s in range(t + 1):
                of = slice(s * HALF, (s + 1) * HALF)
                key = k_ref[r, of, lanes]
                value = v_ref[r, of, lanes]
                mixing, scores = decayed(
                    [mm_nt(query, key), mm_nt(grad_out, value)], cum[at], row[:, of], s == t
                )
                o_new = mm(mixing, value)
                q_new = mm(scores, key)
                k_new = mm(query_turned[lanes, at], scores)
                v_new = mm(grad_turned[lanes, at], mixing)
                out = o_new if out is None else out + o_new
                dq = q_new if dq is None else dq + q_new
                dk[s] = k_new if dk[s] is None else dk[s] + k_new
                dv[s] = v_new if dv[s] is None else dv[s] + v_new
            out_ref[r, at, lanes] = out
            dq_ref[r, at, lanes] = dq
        for s in range(blocks):
            of = slice(s * HALF, (s + 1) * HALF)
            dk_buf[of, lanes] = dk[s].astype(BF16).T
            dv_buf[of, lanes] = dv[s].astype(BF16).T
        copies += [
            pltpu.make_async_copy(dk_buf.at[:, lanes], dk_hbm.at[r, :, lanes], sems.at[2 * h]),
            pltpu.make_async_copy(dv_buf.at[:, lanes], dv_hbm.at[r, :, lanes], sems.at[2 * h + 1]),
        ]
        copies[-2].start()
        copies[-1].start()
    for copy in copies:
        copy.wait()


def last_kernel(n, count, cols_ref, q_ref, c_ref, po_ref, pdq_ref, keys_ref, values_ref, later_ref, *refs):
    got, refs = refs[:n], refs[n + 1 :]
    out_hbm, dq_hbm, dk_hbm, dv_hbm, start, out_buf, dq_buf, dk_buf, dv_buf, sems = refs
    part = DH // n
    block = H * part
    row = lax.axis_index("prompt")
    slots = q_ref.shape[1]
    tokens = keys_ref.shape[1]
    copies = []

    def send(a, b):
        copies.append(pltpu.make_async_copy(a, b, sems.at[len(copies)]))
        copies[-1].start()

    start[...] = jnp.zeros_like(start)
    for r in range(count + 1):
        for k in range(n):
            for h in range(H):
                of = pl.ds(pl.multiple_of(h * DH + lax.bitwise_xor(row, k) * part, part), part)
                rows = got[k][r * block + h * part : r * block + (h + 1) * part, :]
                start[r, of, h * DH : (h + 1) * DH] = rows
    factor = [
        jnp.exp(cols_ref[:tokens, 8 * count + h : 8 * count + h + 1] + later_ref[h : h + 1, 0:1]) for h in range(H)
    ]
    for buf, x in ((dk_buf, mm_nt(values_ref[0], start[count])), (dv_buf, mm(keys_ref[0], start[count]))):
        for h in range(H):
            lanes = slice(h * DH, (h + 1) * DH)
            buf[:, lanes] = (factor[h] * x[:, lanes]).astype(BF16)
    send(dk_buf, dk_hbm.at[0])
    send(dv_buf, dv_hbm.at[0])
    for r in range(count):
        for t in range(0, slots, HALF):
            at = slice(t, t + HALF)
            live = cols_ref[at, 8 * r + 4 : 8 * r + 5]
            opened = cols_ref[at, 8 * r + 5 : 8 * r + 6]
            grad_out = (c_ref[r, at, :].astype(F32) * live).astype(BF16)
            x = mm(q_ref[r, at, :], start[r])
            y = mm_nt(grad_out, start[r])
            for h in range(H):
                lanes = slice(h * DH, (h + 1) * DH)
                carried = cols_ref[at, 8 * r + 2 + h : 8 * r + 3 + h]
                out_buf[r, at, lanes] = (opened * (po_ref[r, at, lanes] + carried * x[:, lanes])).astype(BF16)
                dq_buf[r, at, lanes] = (pdq_ref[r, at, lanes] + carried * y[:, lanes]).astype(BF16)
            send(out_buf.at[r, at], out_hbm.at[r, at])
            send(dq_buf.at[r, at], dq_hbm.at[r, at])
    for copy in copies:
        copy.wait()


def exchange(xs, axis):
    n = lax.axis_size(axis)
    moved = [lax.ppermute(xs[k], axis, [(s, s ^ k) for s in range(n)]) for k in range(1, n)]
    return [xs[0]] + moved


def shards(
    keys,
    values,
    prompt_gates,
    queries,
    resp_keys,
    resp_values,
    resp_gates,
    cotangent,
    group_ids,
    resp_lengths,
    loss_mask,
    advantages,
):
    n = lax.axis_size("prompt")
    chips = lax.axis_size("z")
    cores = lax.axis_size("core")
    responses, slots, width = queries.shape
    block = H * DH // n
    shape = jax.ShapeDtypeStruct

    outs = pl.pallas_call(
        lambda *refs: first_kernel(n, *refs),
        out_shape=[shape((block * (1 + responses) + 16, DH), BF16)] * n
        + [shape((slots, 128), F32), shape((responses, 8, slots), F32)]
        + [shape(queries.shape, BF16)] * 4,
        in_specs=[SMEM] * 3 + [ANY] * 9,
        out_specs=[VMEM] * (n + 6),
        scratch_shapes=[
            pltpu.VMEM(keys.shape, BF16),
            pltpu.VMEM(values.shape, BF16),
            pltpu.VMEM(prompt_gates.shape, F32),
            pltpu.VMEM(resp_gates.shape, F32),
            pltpu.VMEM(loss_mask.shape, jnp.int32),
            pltpu.VMEM((H * (1 + responses), DH, DH), F32),
            pltpu.SemaphoreType.DMA((7 + 2 * responses,)),
        ],
        compiler_params=params(32),
        name="first",
    )(
        *[in_hbm(x) for x in (group_ids, resp_lengths, advantages, keys, values, prompt_gates, resp_gates)],
        *[in_hbm(x) for x in (loss_mask, queries, cotangent, resp_keys, resp_values)],
    )
    msgs, (cols, rows, queries, cotangent, resp_keys, resp_values) = outs[:n], outs[n:]

    like = shape(queries.shape, F32)
    like_out = shape(queries.shape, BF16)

    def sweep(r, before, token):
        outs = pl.pallas_call(
            lambda *refs: sweep_kernel(r, *refs),
            out_shape=[like, like, like_out, like_out, shape((8, 128), F32)],
            in_specs=[VMEM] * 6 + [ANY] * (1 + len(before)),
            out_specs=[VMEM, VMEM, ANY, ANY, VMEM],
            scratch_shapes=[
                pltpu.VMEM((slots, width), BF16),
                pltpu.VMEM((slots, width), BF16),
                pltpu.SemaphoreType.DMA((2 * H,)),
            ],
            input_output_aliases={7 + k: k for k in range(len(before))},
            compiler_params=params(),
            name="sweep",
        )(cols, rows, queries, resp_keys, resp_values, cotangent, token, *before)
        return outs[:4], outs[4]

    got1 = exchange(msgs, "prompt")
    held, token = sweep(0, [], cols)
    outs = pl.pallas_call(
        lambda *refs: second_kernel(n, chips, cores, *refs),
        out_shape=[shape(((1 + cores) * block, DH), BF16)] * chips + [shape((8, DH), F32)],
        in_specs=[VMEM] * n + [ANY],
        out_specs=[VMEM] * (chips + 1),
        scratch_shapes=[pltpu.VMEM((chips * cores, block, DH), F32)],
        compiler_params=params(),
        name="second",
    )(*got1, token)
    msgs, later = outs[:chips], outs[chips]
    got2 = exchange(msgs, "z")
    held, token = sweep(1, held, later)
    sent, kept = pl.pallas_call(
        lambda *refs: swap_kernel(chips, *refs),
        out_shape=[shape(((chips + 1) * block, DH), BF16)] * 2,
        in_specs=[VMEM] * chips + [ANY],
        out_specs=[VMEM, VMEM],
        compiler_params=params(),
        name="swap",
    )(*got2, token)
    swapped = exchange([kept, sent], "core")[1]
    held, token = sweep(2, held, kept)
    msgs = pl.pallas_call(
        lambda *refs: third_kernel(n, chips, *refs),
        out_shape=[shape(((responses + 1) * block, DH), BF16)] * n,
        in_specs=[VMEM] * (n + 2) + [ANY],
        out_specs=[VMEM] * n,
        compiler_params=params(),
        name="third",
    )(*got1, kept, swapped, token)
    got3 = exchange(msgs, "prompt")
    held, token = sweep(3, held, msgs[0])
    partial_out, partial_dq, resp_dk, resp_dv = held

    resp_out, resp_dq, prompt_dk, prompt_dv = pl.pallas_call(
        lambda *refs: last_kernel(n, responses, *refs),
        out_shape=[like_out, like_out, shape(keys.shape, BF16), shape(keys.shape, BF16)],
        in_specs=[VMEM] * (8 + n) + [ANY],
        out_specs=[ANY] * 4,
        scratch_shapes=[
            pltpu.VMEM((responses + 1, width, width), BF16),
            pltpu.VMEM(queries.shape, BF16),
            pltpu.VMEM(queries.shape, BF16),
            pltpu.VMEM(keys.shape[1:], BF16),
            pltpu.VMEM(keys.shape[1:], BF16),
            pltpu.SemaphoreType.DMA((2 + 2 * responses * (slots // HALF),)),
        ],
        compiler_params=params(),
        name="last",
    )(cols, queries, cotangent, partial_out, partial_dq, keys, values, later, *got3, token)
    return (resp_out, resp_dq, resp_dk, resp_dv, prompt_dk, prompt_dv)


def solution(mesh):
    n, count = mesh.shape["prompt"], mesh.shape["resp"]
    mesh = jax.sharding.Mesh(mesh.devices.reshape(n, count // 2, 2), ("prompt", "z", "core"))
    spread = P(("prompt", "z", "core"))
    three = P(("prompt", "z", "core"), None, None)
    two = P(("prompt", "z", "core"), None)
    prompt = P(("z", "core"), "prompt", None)
    return jax.shard_map(
        shards,
        mesh=mesh,
        in_specs=(
            prompt,
            prompt,
            P(("z", "core"), None, "prompt"),
            three,
            three,
            three,
            three,
            three,
            spread,
            two,
            two,
            spread,
        ),
        out_specs=(three, three, three, three, prompt, prompt),
        check_vma=False,
    )
```

```python
import jax
import jax.numpy as jnp
from jax import lax
from jax.experimental import pallas as pl
from jax.experimental.pallas import tpu as pltpu
from jax.sharding import PartitionSpec as P

H = 2
DH = 128
HALF = 256
LOG2E = 1.4426950408889634
F32 = jnp.float32
BF16 = jnp.bfloat16
NEVER = -1e30
VMEM = pl.BlockSpec(memory_space=pltpu.VMEM)
ANY = pl.BlockSpec(memory_space=pl.ANY)
SMEM = pl.BlockSpec(memory_space=pltpu.SMEM)


def params(mebibytes=16):
    return pltpu.CompilerParams(vmem_limit_bytes=mebibytes * 1024 * 1024)


def mm(a, b):
    return lax.dot_general(a, b, (((1,), (0,)), ((), ())), preferred_element_type=F32)


def mm_nt(a, b):
    return lax.dot_general(a, b, (((1,), (1,)), ((), ())), preferred_element_type=F32)


def mm_tn(a, b):
    return lax.dot_general(a, b, (((0,), (0,)), ((), ())), preferred_element_type=F32)


def in_hbm(x):
    return pltpu.with_memory_space_constraint(x, pltpu.HBM)


def three_terms(x):
    high = x.astype(BF16)
    rest = x - high.astype(F32)
    middle = rest.astype(BF16)
    return high, middle, (rest - middle.astype(F32)).astype(BF16)


def lane_cumsum(x):
    rows, width = x.shape
    ones = lax.broadcasted_iota(jnp.int32, (128, 128), 0) <= lax.broadcasted_iota(jnp.int32, (128, 128), 1)
    terms = jnp.concatenate(three_terms(x), axis=0)
    starts = range(0, width, 128)
    sums = mm(jnp.concatenate([terms[:, b : b + 128] for b in starts], axis=0), ones.astype(F32).astype(BF16))
    parts = []
    before = jnp.zeros((rows, 1), F32)
    for b in range(len(starts)):
        at = 3 * rows * b
        part = sums[at : at + rows] + sums[at + rows : at + 2 * rows] + sums[at + 2 * rows : at + 3 * rows]
        part = part + before
        before = part[:, 127:128]
        parts.append(part)
    return jnp.concatenate(parts, axis=1)


def first_kernel(
    n, ids_hbm, lens_hbm, adv_hbm, keys_hbm, values_hbm, pgates_hbm, gates_hbm, mask_hbm, q_hbm, c_hbm, k_hbm, v_hbm,
    *refs,
):
    msgs, (cols_ref, rows_ref, q, c, k_out, v_out) = refs[:n], refs[n : n + 6]
    keys, values, pgates, gates, mask, ids_ref, lens_ref, adv_ref, matrices, sems = refs[n + 6 :]
    pairs = [(pgates_hbm, pgates), (gates_hbm, gates), (mask_hbm, mask)]
    pairs += [(ids_hbm, ids_ref), (lens_hbm, lens_ref), (adv_hbm, adv_ref), (keys_hbm, keys), (values_hbm, values)]
    count = gates.shape[0]
    slots = gates.shape[2]
    tokens = keys.shape[1]
    for i in range(count):
        pairs += [(q_hbm.at[i], q.at[i]), (c_hbm.at[i], c.at[i])]
    pairs += [(k_hbm, k_out), (v_hbm, v_out)]
    copies = [pltpu.make_async_copy(a, b, sems.at[i]) for i, (a, b) in enumerate(pairs)]
    for copy in copies:
        copy.start()
    part = DH // n
    block = H * part
    me = lax.axis_index("prompt")
    targets = [lax.bitwise_xor(me, k) for k in range(n)]

    def spread(at):
        for k in range(n):
            of = pl.ds(pl.multiple_of(targets[k] * part, part), part)
            msgs[k][at * part + (16 if at >= H else 0) : (at + 1) * part + (16 if at >= H else 0), :] = matrices[
                at, of, :
            ].astype(BF16)

    for copy in copies[:6]:
        copy.wait()
    piece = jnp.concatenate([pgates[0], jnp.zeros((H, slots - tokens), F32)], axis=1)
    gate_rows = [gates[i] for i in range(count)] + [piece, jnp.zeros((16 - H * (count + 1), slots), F32)]
    cum = lane_cumsum(jnp.concatenate(gate_rows, axis=0))
    carried = jnp.exp(cum)
    place = lax.broadcasted_iota(jnp.int32, (1, slots), 1)
    rows = []
    factors = []
    for i in range(count):
        weight = adv_ref[i].astype(F32) / 1024.0
        opened = jnp.where(place < lens_ref[0, i], 1.0, 0.0)
        live = mask[i : i + 1, :].astype(F32) * opened * weight
        rows += [cum[H * i : H * i + H], carried[H * i : H * i + H] * opened, live, opened, jnp.zeros((2, slots), F32)]
        factors.append(carried[H * i : H * i + H] * live)
    rows_ref[...] = jnp.concatenate(rows, axis=0).reshape(count, 8, slots)
    piece = cum[H * count : H * count + H]
    total = piece[:, -1:]
    suffix = total - piece
    rows += [suffix, jnp.zeros((128 - 8 * count - H, slots), F32)]
    cols_ref[...] = jnp.concatenate(rows, axis=0).T

    for copy in copies[6:8]:
        copy.wait()
    turned = keys[0].T
    later = jnp.exp(suffix[:, :tokens])
    for h in range(H):
        lanes = slice(h * DH, (h + 1) * DH)
        scaled = turned[lanes].astype(F32) * later[h : h + 1]
        high = scaled.astype(BF16)
        low = (scaled - high.astype(F32)).astype(BF16)
        both = mm(jnp.concatenate([high, low], axis=0), values[0, :, lanes])
        matrices[h] = both[:DH] + both[DH:]
        spread(h)
    notes = [jnp.broadcast_to(x[h : h + 1].astype(F32), (1, DH)) for x in three_terms(total) for h in range(H)]
    notes += [jnp.full((1, DH), ids_ref[i].astype(F32)) for i in range(count)]
    notes.append(jnp.zeros((16 - len(notes), DH), F32))
    notes = jnp.concatenate(notes, axis=0).astype(BF16)
    for k in range(n):
        msgs[k][block : block + 16, :] = notes

    for i in range(count):
        copies[8 + 2 * i].wait()
        turned = q[i].T
        copies[9 + 2 * i].wait()
        for h in range(H):
            lanes = slice(h * DH, (h + 1) * DH)
            scaled = (turned[lanes].astype(F32) * factors[i][h : h + 1]).astype(BF16)
            matrices[H * (1 + i) + h] = mm(scaled, c[i, :, lanes])
            spread(H * (1 + i) + h)
    for copy in copies[8 + 2 * count :]:
        copy.wait()


def noted_prompt(notes, i):
    return jnp.max(notes[3 * H + i : 3 * H + i + 1]).astype(jnp.int32)


def second_kernel(n, chips, cores, *refs):
    row, z_at = lax.axis_index("prompt"), lax.axis_index("z")
    got, msgs, later_ref, sums = refs[:n], refs[n + 1 : n + 1 + chips], refs[-2], refs[-1]
    part = DH // n
    block = H * part
    responses = (got[0].shape[0] - block - 16) // block
    place = [lax.bitwise_xor(row, k) for k in range(n)]
    notes = [got[k][block : block + 16, :].astype(F32) for k in range(n)]
    logs = [x[0:H] + x[H : 2 * H] + x[2 * H : 3 * H] for x in notes]
    final = jnp.zeros((block, DH), F32)
    for k in range(n):
        later = jnp.zeros_like(logs[0])
        for other in range(n):
            if other != k:
                later = later + jnp.where(place[other] > place[k], logs[other], 0.0)
        if k == 0:
            later_ref[...] = jnp.concatenate([later, jnp.zeros((8 - H, DH), F32)], axis=0)
        decay = jnp.exp(later)
        decay = [jnp.broadcast_to(decay[h : h + 1], (part, DH)) for h in range(H)]
        final = final + jnp.concatenate(decay, axis=0) * got[k][0:block, :].astype(F32)
    sums[...] = jnp.zeros_like(sums)
    for k in range(n):
        for i in range(responses):
            at = block * (1 + i) + 16
            sums[noted_prompt(notes[k], i)] += got[k][at : at + block, :].astype(F32)
    final = final.astype(BF16)
    for k in range(chips):
        z = lax.bitwise_xor(z_at, k)
        msgs[k][0:block, :] = final
        for c in range(cores):
            msgs[k][(1 + c) * block : (2 + c) * block, :] = sums[z * cores + c].astype(BF16)


def swap_kernel(chips, *refs):
    got, sent_ref, kept_ref = refs[:chips], refs[chips + 1], refs[chips + 2]
    block = got[0].shape[0] // 3
    totals = []
    for c in range(2):
        total = got[0][(1 + c) * block : (2 + c) * block, :].astype(F32)
        for k in range(1, chips):
            total = total + got[k][(1 + c) * block : (2 + c) * block, :].astype(F32)
        totals.append(total)
    for k in range(chips):
        final = got[k][0:block, :]
        sent_ref[k * block : (k + 1) * block, :] = final
        kept_ref[k * block : (k + 1) * block, :] = final
    low = lax.axis_index("core") == 0
    sent_ref[chips * block :, :] = jnp.where(low, totals[1], totals[0]).astype(BF16)
    kept_ref[chips * block :, :] = jnp.where(low, totals[0], totals[1]).astype(BF16)


def third_kernel(n, chips, *refs):
    z_at, core = lax.axis_index("z"), lax.axis_index("core")
    noted, kept_ref, got_ref, msgs = refs[:n], refs[n], refs[n + 1], refs[n + 2 :]
    block = H * DH // n
    responses = (noted[0].shape[0] - block - 16) // block
    total = kept_ref[chips * block :, :].astype(F32) + got_ref[chips * block :, :].astype(F32)
    total = total.astype(BF16)
    for k in range(n):
        notes = noted[k][block : block + 16, :].astype(F32)
        for i in range(responses):
            p = noted_prompt(notes, i)
            slot = lax.bitwise_xor(z_at, lax.div(p, 2))
            at = pl.ds(pl.multiple_of(slot * block, block), block)
            same = lax.rem(p, 2) == core
            state = jnp.where(same, kept_ref[at, :].astype(F32), got_ref[at, :].astype(F32))
            msgs[k][i * block : (i + 1) * block, :] = state.astype(BF16)
        msgs[k][responses * block :, :] = total


def sweep_kernel(units, cols_ref, rows_ref, q_ref, k_ref, v_ref, c_ref, *refs):
    out_ref, dq_ref, grad_ref, dk_hbm, dv_hbm, token_ref, dk_buf, dv_buf, sems = refs[-9:]
    token_ref[...] = jnp.zeros_like(token_ref)
    quarter = HALF // 2
    causal = lax.broadcasted_iota(jnp.int32, (quarter, quarter), 0) >= lax.broadcasted_iota(
        jnp.int32, (quarter, quarter), 1
    )
    blank = jnp.zeros((quarter, quarter), BF16)
    blocks = q_ref.shape[1] // HALF
    copies = []

    def decayed(products, cum, row, diagonal):
        if not diagonal:
            decay = jnp.exp2(cum - row)
            return [(x * decay).astype(BF16) for x in products]
        first = jnp.exp2(jnp.where(causal, cum[:quarter] - row[:, :quarter], NEVER))
        left = jnp.exp2(cum[quarter:] - row[:, :quarter])
        right = jnp.exp2(jnp.where(causal, cum[quarter:] - row[:, quarter:], NEVER))
        results = []
        for x in products:
            upper = jnp.concatenate([(x[:quarter, :quarter] * first).astype(BF16), blank], axis=1)
            lower = [(x[quarter:, :quarter] * left).astype(BF16), (x[quarter:, quarter:] * right).astype(BF16)]
            results.append(jnp.concatenate([upper, jnp.concatenate(lower, axis=1)], axis=0))
        return results

    for u, (r, h) in enumerate(units):
        lanes = slice(h * DH, (h + 1) * DH)
        cum = cols_ref[:, 8 * r + h : 8 * r + h + 1] * LOG2E
        row = rows_ref[r, h : h + 1, :] * LOG2E
        live = cols_ref[:, 8 * r + 4 : 8 * r + 5]
        opened = cols_ref[:, 8 * r + 5 : 8 * r + 6]
        grad_all = (c_ref[r, :, lanes].astype(F32) * live).astype(BF16)
        grad_ref[r, :, lanes] = grad_all
        query_turned = q_ref[r, :, lanes].T
        grad_turned = grad_all.T
        dk = [None] * blocks
        dv = [None] * blocks
        for t in range(blocks):
            at = slice(t * HALF, (t + 1) * HALF)
            query = q_ref[r, at, lanes]
            grad_out = grad_all[at]
            out = None
            dq = None
            for s in range(t + 1):
                of = slice(s * HALF, (s + 1) * HALF)
                key = k_ref[r, of, lanes]
                value = v_ref[r, of, lanes]
                mixing, scores = decayed(
                    [mm_nt(query, key), mm_nt(grad_out, value)], cum[at], row[:, of], s == t
                )
                o_new = mm(mixing, value)
                q_new = mm(scores, key)
                k_new = mm(query_turned[:, at], scores)
                v_new = mm(grad_turned[:, at], mixing)
                out = o_new if out is None else out + o_new
                dq = q_new if dq is None else dq + q_new
                dk[s] = k_new if dk[s] is None else dk[s] + k_new
                dv[s] = v_new if dv[s] is None else dv[s] + v_new
            out_ref[r, at, lanes] = out * opened[at]
            dq_ref[r, at, lanes] = dq
        for s in range(blocks):
            of = slice(s * HALF, (s + 1) * HALF)
            dk_buf[u, of, :] = dk[s].astype(BF16).T
            dv_buf[u, of, :] = dv[s].astype(BF16).T
        copies += [
            pltpu.make_async_copy(dk_buf.at[u], dk_hbm.at[r, :, lanes], sems.at[2 * u]),
            pltpu.make_async_copy(dv_buf.at[u], dv_hbm.at[r, :, lanes], sems.at[2 * u + 1]),
        ]
        copies[-2].start()
        copies[-1].start()
    for copy in copies:
        copy.wait()


def last_kernel(n, count, cols_ref, q_ref, grad_ref, po_ref, pdq_ref, keys_ref, values_ref, later_ref, *refs):
    got, refs = refs[:n], refs[n + 1 :]
    out_hbm, dq_hbm, dk_hbm, dv_hbm, start, out_buf, dq_buf, dk_buf, dv_buf, sems = refs
    part = DH // n
    block = H * part
    row = lax.axis_index("prompt")
    slots = q_ref.shape[1]
    tokens = keys_ref.shape[1]
    copies = []

    def send(a, b):
        copies.append(pltpu.make_async_copy(a, b, sems.at[len(copies)]))
        copies[-1].start()

    start[...] = jnp.zeros_like(start)
    for r in range(count + 1):
        for k in range(n):
            for h in range(H):
                of = pl.ds(pl.multiple_of(h * DH + lax.bitwise_xor(row, k) * part, part), part)
                rows = got[k][r * block + h * part : r * block + (h + 1) * part, :]
                start[r, of, h * DH : (h + 1) * DH] = rows
    factor = [
        jnp.exp(cols_ref[:tokens, 8 * count + h : 8 * count + h + 1] + later_ref[h : h + 1, 0:1]) for h in range(H)
    ]
    for buf, x in ((dk_buf, mm_nt(values_ref[0], start[count])), (dv_buf, mm(keys_ref[0], start[count]))):
        for h in range(H):
            lanes = slice(h * DH, (h + 1) * DH)
            buf[:, lanes] = (factor[h] * x[:, lanes]).astype(BF16)
    send(dk_buf, dk_hbm.at[0])
    send(dv_buf, dv_hbm.at[0])
    for r in range(count):
        for t in range(0, slots, HALF):
            at = slice(t, t + HALF)
            x = mm(q_ref[r, at, :], start[r])
            y = mm_nt(grad_ref[r, at, :], start[r])
            for h in range(H):
                lanes = slice(h * DH, (h + 1) * DH)
                carried = cols_ref[at, 8 * r + 2 + h : 8 * r + 3 + h]
                out_buf[r, at, lanes] = (po_ref[r, at, lanes] + carried * x[:, lanes]).astype(BF16)
                dq_buf[r, at, lanes] = (pdq_ref[r, at, lanes] + carried * y[:, lanes]).astype(BF16)
            send(out_buf.at[r, at], out_hbm.at[r, at])
            send(dq_buf.at[r, at], dq_hbm.at[r, at])
    for copy in copies:
        copy.wait()


def exchange(xs, axis):
    n = lax.axis_size(axis)
    got = [xs[0]] + [None] * (n - 1)
    for k in sorted(range(1, n), key=lambda k: -k.bit_count()):
        got[k] = lax.ppermute(xs[k], axis, [(s, s ^ k) for s in range(n)])
    return got


def shards(
    keys,
    values,
    prompt_gates,
    queries,
    resp_keys,
    resp_values,
    resp_gates,
    cotangent,
    group_ids,
    resp_lengths,
    loss_mask,
    advantages,
):
    n = lax.axis_size("prompt")
    chips = lax.axis_size("z")
    cores = lax.axis_size("core")
    responses, slots, width = queries.shape
    block = H * DH // n
    shape = jax.ShapeDtypeStruct

    outs = pl.pallas_call(
        lambda *refs: first_kernel(n, *refs),
        out_shape=[shape((block * (1 + responses) + 16, DH), BF16)] * n
        + [shape((slots, 128), F32), shape((responses, 8, slots), F32)]
        + [shape(queries.shape, BF16)] * 4,
        in_specs=[ANY] * 12,
        out_specs=[VMEM] * (n + 6),
        scratch_shapes=[
            pltpu.VMEM(keys.shape, BF16),
            pltpu.VMEM(values.shape, BF16),
            pltpu.VMEM(prompt_gates.shape, F32),
            pltpu.VMEM(resp_gates.shape, F32),
            pltpu.VMEM(loss_mask.shape, jnp.int32),
            pltpu.SMEM(group_ids.shape, jnp.int32),
            pltpu.SMEM(resp_lengths.shape, jnp.int32),
            pltpu.SMEM(advantages.shape, jnp.int32),
            pltpu.VMEM((H * (1 + responses), DH, DH), F32),
            pltpu.SemaphoreType.DMA((10 + 2 * responses,)),
        ],
        compiler_params=params(32),
        name="first",
    )(
        *[in_hbm(x) for x in (group_ids, resp_lengths, advantages, keys, values, prompt_gates, resp_gates)],
        *[in_hbm(x) for x in (loss_mask, queries, cotangent, resp_keys, resp_values)],
    )
    msgs, (cols, rows, queries, cotangent, resp_keys, resp_values) = outs[:n], outs[n:]

    like = shape(queries.shape, F32)
    like_out = shape(queries.shape, BF16)

    def sweep(units, before, token):
        outs = pl.pallas_call(
            lambda *refs: sweep_kernel(units, *refs),
            out_shape=[like, like, like_out, like_out, like_out, shape((8, 128), F32)],
            in_specs=[VMEM] * 6 + [ANY] * (1 + len(before)),
            out_specs=[VMEM, VMEM, VMEM, ANY, ANY, VMEM],
            scratch_shapes=[
                pltpu.VMEM((len(units), slots, DH), BF16),
                pltpu.VMEM((len(units), slots, DH), BF16),
                pltpu.SemaphoreType.DMA((2 * len(units),)),
            ],
            input_output_aliases={7 + k: k for k in range(len(before))},
            compiler_params=params(),
            name="sweep",
        )(cols, rows, queries, resp_keys, resp_values, cotangent, token, *before)
        return outs[:5], outs[5]

    units = [(r, h) for r in range(responses) for h in range(H)]
    got1 = exchange(msgs, "prompt")
    held, token = sweep(units[:3], [], cols)
    outs = pl.pallas_call(
        lambda *refs: second_kernel(n, chips, cores, *refs),
        out_shape=[shape(((1 + cores) * block, DH), BF16)] * chips + [shape((8, DH), F32)],
        in_specs=[VMEM] * n + [ANY],
        out_specs=[VMEM] * (chips + 1),
        scratch_shapes=[pltpu.VMEM((chips * cores, block, DH), F32)],
        compiler_params=params(),
        name="second",
    )(*got1, token)
    msgs, later = outs[:chips], outs[chips]
    got2 = exchange(msgs, "z")
    held, token = sweep(units[3:6], held, later)
    sent, kept = pl.pallas_call(
        lambda *refs: swap_kernel(chips, *refs),
        out_shape=[shape(((chips + 1) * block, DH), BF16)] * 2,
        in_specs=[VMEM] * chips + [ANY],
        out_specs=[VMEM, VMEM],
        compiler_params=params(),
        name="swap",
    )(*got2, token)
    swapped = exchange([kept, sent], "core")[1]
    msgs = pl.pallas_call(
        lambda *refs: third_kernel(n, chips, *refs),
        out_shape=[shape(((responses + 1) * block, DH), BF16)] * n,
        in_specs=[VMEM] * (n + 2),
        out_specs=[VMEM] * n,
        compiler_params=params(),
        name="third",
    )(*got1, kept, swapped)
    got3 = exchange(msgs, "prompt")
    held, token = sweep(units[6:], held, msgs[0])
    partial_out, partial_dq, grad_out, resp_dk, resp_dv = held

    resp_out, resp_dq, prompt_dk, prompt_dv = pl.pallas_call(
        lambda *refs: last_kernel(n, responses, *refs),
        out_shape=[like_out, like_out, shape(keys.shape, BF16), shape(keys.shape, BF16)],
        in_specs=[VMEM] * (8 + n) + [ANY],
        out_specs=[ANY] * 4,
        scratch_shapes=[
            pltpu.VMEM((responses + 1, width, width), BF16),
            pltpu.VMEM(queries.shape, BF16),
            pltpu.VMEM(queries.shape, BF16),
            pltpu.VMEM(keys.shape[1:], BF16),
            pltpu.VMEM(keys.shape[1:], BF16),
            pltpu.SemaphoreType.DMA((2 + 2 * responses * (slots // HALF),)),
        ],
        compiler_params=params(),
        name="last",
    )(cols, queries, grad_out, partial_out, partial_dq, keys, values, later, *got3, token)
    return (resp_out, resp_dq, resp_dk, resp_dv, prompt_dk, prompt_dv)


def solution(mesh):
    n, count = mesh.shape["prompt"], mesh.shape["resp"]
    mesh = jax.sharding.Mesh(mesh.devices.reshape(n, count // 2, 2), ("prompt", "z", "core"))
    spread = P(("prompt", "z", "core"))
    three = P(("prompt", "z", "core"), None, None)
    two = P(("prompt", "z", "core"), None)
    prompt = P(("z", "core"), "prompt", None)
    return jax.shard_map(
        shards,
        mesh=mesh,
        in_specs=(
            prompt,
            prompt,
            P(("z", "core"), None, "prompt"),
            three,
            three,
            three,
            three,
            three,
            spread,
            two,
            two,
            spread,
        ),
        out_specs=(three, three, three, three, prompt, prompt),
        check_vma=False,
    )
```

```python
import jax
import jax.numpy as jnp
from jax import lax
from jax.experimental import pallas as pl
from jax.experimental.pallas import tpu as pltpu
from jax.sharding import PartitionSpec as P

H = 2
DH = 128
HALF = 256
LOG2E = 1.4426950408889634
F32 = jnp.float32
BF16 = jnp.bfloat16
NEVER = -1e30
VMEM = pl.BlockSpec(memory_space=pltpu.VMEM)
ANY = pl.BlockSpec(memory_space=pl.ANY)
SMEM = pl.BlockSpec(memory_space=pltpu.SMEM)


def params(mebibytes=16):
    return pltpu.CompilerParams(vmem_limit_bytes=mebibytes * 1024 * 1024)


def mm(a, b):
    return lax.dot_general(a, b, (((1,), (0,)), ((), ())), preferred_element_type=F32)


def mm_nt(a, b):
    return lax.dot_general(a, b, (((1,), (1,)), ((), ())), preferred_element_type=F32)


def mm_tn(a, b):
    return lax.dot_general(a, b, (((0,), (0,)), ((), ())), preferred_element_type=F32)


def in_hbm(x):
    return pltpu.with_memory_space_constraint(x, pltpu.HBM)


def three_terms(x):
    high = x.astype(BF16)
    rest = x - high.astype(F32)
    middle = rest.astype(BF16)
    return high, middle, (rest - middle.astype(F32)).astype(BF16)


def lane_cumsum(x):
    rows, width = x.shape
    ones = lax.broadcasted_iota(jnp.int32, (128, 128), 0) <= lax.broadcasted_iota(jnp.int32, (128, 128), 1)
    terms = jnp.concatenate(three_terms(x), axis=0)
    starts = range(0, width, 128)
    sums = mm(jnp.concatenate([terms[:, b : b + 128] for b in starts], axis=0), ones.astype(F32).astype(BF16))
    parts = []
    before = jnp.zeros((rows, 1), F32)
    for b in range(len(starts)):
        at = 3 * rows * b
        part = sums[at : at + rows] + sums[at + rows : at + 2 * rows] + sums[at + 2 * rows : at + 3 * rows]
        part = part + before
        before = part[:, 127:128]
        parts.append(part)
    return jnp.concatenate(parts, axis=1)


def first_kernel(
    n, ids_hbm, lens_hbm, adv_hbm, keys_hbm, values_hbm, pgates_hbm, gates_hbm, mask_hbm, q_hbm, c_hbm, k_hbm, v_hbm,
    *refs,
):
    msgs, (cols_ref, rows_ref, q, c, k_out, v_out) = refs[:n], refs[n : n + 6]
    keys, values, pgates, gates, mask, ids_ref, lens_ref, adv_ref, matrices, sems = refs[n + 6 :]
    pairs = [(pgates_hbm, pgates), (gates_hbm, gates), (mask_hbm, mask)]
    pairs += [(ids_hbm, ids_ref), (lens_hbm, lens_ref), (adv_hbm, adv_ref), (keys_hbm, keys), (values_hbm, values)]
    count = gates.shape[0]
    slots = gates.shape[2]
    tokens = keys.shape[1]
    for i in range(count):
        pairs += [(q_hbm.at[i], q.at[i]), (c_hbm.at[i], c.at[i])]
    pairs += [(k_hbm, k_out), (v_hbm, v_out)]
    copies = [pltpu.make_async_copy(a, b, sems.at[i]) for i, (a, b) in enumerate(pairs)]
    for copy in copies:
        copy.start()
    part = DH // n
    block = H * part
    me = lax.axis_index("prompt")
    targets = [lax.bitwise_xor(me, k) for k in range(n)]

    def spread(at):
        for k in range(n):
            of = pl.ds(pl.multiple_of(targets[k] * part, part), part)
            msgs[k][at * part + (16 if at >= H else 0) : (at + 1) * part + (16 if at >= H else 0), :] = matrices[
                at, of, :
            ].astype(BF16)

    for copy in copies[:6]:
        copy.wait()
    piece = jnp.concatenate([pgates[0], jnp.zeros((H, slots - tokens), F32)], axis=1)
    gate_rows = [gates[i] for i in range(count)] + [piece, jnp.zeros((16 - H * (count + 1), slots), F32)]
    cum = lane_cumsum(jnp.concatenate(gate_rows, axis=0))
    carried = jnp.exp(cum)
    place = lax.broadcasted_iota(jnp.int32, (1, slots), 1)
    rows = []
    factors = []
    for i in range(count):
        weight = adv_ref[i].astype(F32) / 1024.0
        opened = jnp.where(place < lens_ref[0, i], 1.0, 0.0)
        live = mask[i : i + 1, :].astype(F32) * opened * weight
        rows += [cum[H * i : H * i + H], carried[H * i : H * i + H] * opened, live, opened, jnp.zeros((2, slots), F32)]
        factors.append(carried[H * i : H * i + H] * live)
    rows_ref[...] = jnp.concatenate(rows, axis=0).reshape(count, 8, slots)
    piece = cum[H * count : H * count + H]
    total = piece[:, -1:]
    suffix = total - piece
    rows += [suffix, jnp.zeros((128 - 8 * count - H, slots), F32)]
    cols_ref[...] = jnp.concatenate(rows, axis=0).T

    for copy in copies[6:8]:
        copy.wait()
    turned = keys[0].T
    later = jnp.exp(suffix[:, :tokens])
    for h in range(H):
        lanes = slice(h * DH, (h + 1) * DH)
        scaled = turned[lanes].astype(F32) * later[h : h + 1]
        high = scaled.astype(BF16)
        low = (scaled - high.astype(F32)).astype(BF16)
        both = mm(jnp.concatenate([high, low], axis=0), values[0, :, lanes])
        matrices[h] = both[:DH] + both[DH:]
        spread(h)
    notes = [jnp.broadcast_to(x[h : h + 1].astype(F32), (1, DH)) for x in three_terms(total) for h in range(H)]
    notes += [jnp.full((1, DH), ids_ref[i].astype(F32)) for i in range(count)]
    notes.append(jnp.zeros((16 - len(notes), DH), F32))
    notes = jnp.concatenate(notes, axis=0).astype(BF16)
    for k in range(n):
        msgs[k][block : block + 16, :] = notes

    for i in range(count):
        copies[8 + 2 * i].wait()
        turned = q[i].T
        copies[9 + 2 * i].wait()
        for h in range(H):
            lanes = slice(h * DH, (h + 1) * DH)
            scaled = (turned[lanes].astype(F32) * factors[i][h : h + 1]).astype(BF16)
            matrices[H * (1 + i) + h] = mm(scaled, c[i, :, lanes])
            spread(H * (1 + i) + h)
    for copy in copies[8 + 2 * count :]:
        copy.wait()


def noted_prompt(notes, i):
    return jnp.max(notes[3 * H + i : 3 * H + i + 1]).astype(jnp.int32)


def second_kernel(n, chips, cores, *refs):
    row, z_at = lax.axis_index("prompt"), lax.axis_index("z")
    got, msgs, later_ref, sums = by_partner(refs[:n]), refs[n + 1 : n + 1 + chips], refs[-2], refs[-1]
    part = DH // n
    block = H * part
    responses = (got[0].shape[0] - block - 16) // block
    place = [lax.bitwise_xor(row, k) for k in range(n)]
    notes = [got[k][block : block + 16, :].astype(F32) for k in range(n)]
    logs = [x[0:H] + x[H : 2 * H] + x[2 * H : 3 * H] for x in notes]
    final = jnp.zeros((block, DH), F32)
    for k in range(n):
        later = jnp.zeros_like(logs[0])
        for other in range(n):
            if other != k:
                later = later + jnp.where(place[other] > place[k], logs[other], 0.0)
        if k == 0:
            later_ref[...] = jnp.concatenate([later, jnp.zeros((8 - H, DH), F32)], axis=0)
        decay = jnp.exp(later)
        decay = [jnp.broadcast_to(decay[h : h + 1], (part, DH)) for h in range(H)]
        final = final + jnp.concatenate(decay, axis=0) * got[k][0:block, :].astype(F32)
    sums[...] = jnp.zeros_like(sums)
    for k in range(n):
        for i in range(responses):
            at = block * (1 + i) + 16
            sums[noted_prompt(notes[k], i)] += got[k][at : at + block, :].astype(F32)
    final = final.astype(BF16)
    for k in range(chips):
        z = lax.bitwise_xor(z_at, k)
        msgs[k][0:block, :] = final
        for c in range(cores):
            msgs[k][(1 + c) * block : (2 + c) * block, :] = sums[z * cores + c].astype(BF16)


def swap_kernel(chips, *refs):
    got, sent_ref, kept_ref = by_partner(refs[:chips]), refs[chips + 1], refs[chips + 2]
    block = got[0].shape[0] // 3
    totals = []
    for c in range(2):
        total = got[0][(1 + c) * block : (2 + c) * block, :].astype(F32)
        for k in range(1, chips):
            total = total + got[k][(1 + c) * block : (2 + c) * block, :].astype(F32)
        totals.append(total)
    for k in range(chips):
        final = got[k][0:block, :]
        sent_ref[k * block : (k + 1) * block, :] = final
        kept_ref[k * block : (k + 1) * block, :] = final
    low = lax.axis_index("core") == 0
    sent_ref[chips * block :, :] = jnp.where(low, totals[1], totals[0]).astype(BF16)
    kept_ref[chips * block :, :] = jnp.where(low, totals[0], totals[1]).astype(BF16)


def third_kernel(n, chips, *refs):
    z_at, core = lax.axis_index("z"), lax.axis_index("core")
    noted, kept_ref, got_ref, msgs = by_partner(refs[:n]), refs[n], refs[n + 1], refs[n + 3 :]
    block = H * DH // n
    responses = (noted[0].shape[0] - block - 16) // block
    total = kept_ref[chips * block :, :].astype(F32) + got_ref[chips * block :, :].astype(F32)
    total = total.astype(BF16)
    for k in range(n):
        notes = noted[k][block : block + 16, :].astype(F32)
        for i in range(responses):
            p = noted_prompt(notes, i)
            slot = lax.bitwise_xor(z_at, lax.div(p, 2))
            at = pl.ds(pl.multiple_of(slot * block, block), block)
            same = lax.rem(p, 2) == core
            state = jnp.where(same, kept_ref[at, :].astype(F32), got_ref[at, :].astype(F32))
            msgs[k][i * block : (i + 1) * block, :] = state.astype(BF16)
        msgs[k][responses * block :, :] = total


def sweep_kernel(units, cols_ref, rows_ref, q_ref, k_ref, v_ref, c_ref, *refs):
    out_ref, dq_ref, grad_ref, dk_hbm, dv_hbm, token_ref, dk_buf, dv_buf, sems = refs[-9:]
    token_ref[...] = jnp.zeros_like(token_ref)
    quarter = HALF // 2
    causal = lax.broadcasted_iota(jnp.int32, (quarter, quarter), 0) >= lax.broadcasted_iota(
        jnp.int32, (quarter, quarter), 1
    )
    blank = jnp.zeros((quarter, quarter), BF16)
    blocks = q_ref.shape[1] // HALF
    copies = []

    def decayed(products, cum, row, diagonal):
        if not diagonal:
            decay = jnp.exp2(cum - row)
            return [(x * decay).astype(BF16) for x in products]
        first = jnp.exp2(jnp.where(causal, cum[:quarter] - row[:, :quarter], NEVER))
        left = jnp.exp2(cum[quarter:] - row[:, :quarter])
        right = jnp.exp2(jnp.where(causal, cum[quarter:] - row[:, quarter:], NEVER))
        results = []
        for x in products:
            upper = jnp.concatenate([(x[:quarter, :quarter] * first).astype(BF16), blank], axis=1)
            lower = [(x[quarter:, :quarter] * left).astype(BF16), (x[quarter:, quarter:] * right).astype(BF16)]
            results.append(jnp.concatenate([upper, jnp.concatenate(lower, axis=1)], axis=0))
        return results

    for u, (r, h) in enumerate(units):
        lanes = slice(h * DH, (h + 1) * DH)
        cum = cols_ref[:, 8 * r + h : 8 * r + h + 1] * LOG2E
        row = rows_ref[r, h : h + 1, :] * LOG2E
        live = cols_ref[:, 8 * r + 4 : 8 * r + 5]
        opened = cols_ref[:, 8 * r + 5 : 8 * r + 6]
        grad_all = (c_ref[r, :, lanes].astype(F32) * live).astype(BF16)
        grad_ref[r, :, lanes] = grad_all
        query_turned = q_ref[r, :, lanes].T
        grad_turned = grad_all.T
        dk = [None] * blocks
        dv = [None] * blocks
        for t in range(blocks):
            at = slice(t * HALF, (t + 1) * HALF)
            query = q_ref[r, at, lanes]
            grad_out = grad_all[at]
            out = None
            dq = None
            for s in range(t + 1):
                of = slice(s * HALF, (s + 1) * HALF)
                key = k_ref[r, of, lanes]
                value = v_ref[r, of, lanes]
                mixing, scores = decayed(
                    [mm_nt(query, key), mm_nt(grad_out, value)], cum[at], row[:, of], s == t
                )
                o_new = mm(mixing, value)
                q_new = mm(scores, key)
                k_new = mm(query_turned[:, at], scores)
                v_new = mm(grad_turned[:, at], mixing)
                out = o_new if out is None else out + o_new
                dq = q_new if dq is None else dq + q_new
                dk[s] = k_new if dk[s] is None else dk[s] + k_new
                dv[s] = v_new if dv[s] is None else dv[s] + v_new
            out_ref[r, at, lanes] = out * opened[at]
            dq_ref[r, at, lanes] = dq
        for s in range(blocks):
            of = slice(s * HALF, (s + 1) * HALF)
            dk_buf[u, of, :] = dk[s].astype(BF16).T
            dv_buf[u, of, :] = dv[s].astype(BF16).T
        copies += [
            pltpu.make_async_copy(dk_buf.at[u], dk_hbm.at[r, :, lanes], sems.at[2 * u]),
            pltpu.make_async_copy(dv_buf.at[u], dv_hbm.at[r, :, lanes], sems.at[2 * u + 1]),
        ]
        copies[-2].start()
        copies[-1].start()
    for copy in copies:
        copy.wait()


def last_kernel(n, count, cols_ref, q_ref, grad_ref, po_ref, pdq_ref, keys_ref, values_ref, later_ref, *refs):
    got, refs = by_partner(refs[:n]), refs[n + 1 :]
    out_hbm, dq_hbm, dk_hbm, dv_hbm, start, out_buf, dq_buf, dk_buf, dv_buf, sems = refs
    part = DH // n
    block = H * part
    row = lax.axis_index("prompt")
    slots = q_ref.shape[1]
    tokens = keys_ref.shape[1]
    copies = []

    def send(a, b):
        copies.append(pltpu.make_async_copy(a, b, sems.at[len(copies)]))
        copies[-1].start()

    start[...] = jnp.zeros_like(start)
    for r in range(count + 1):
        for k in range(n):
            for h in range(H):
                of = pl.ds(pl.multiple_of(h * DH + lax.bitwise_xor(row, k) * part, part), part)
                rows = got[k][r * block + h * part : r * block + (h + 1) * part, :]
                start[r, of, h * DH : (h + 1) * DH] = rows
    factor = [
        jnp.exp(cols_ref[:tokens, 8 * count + h : 8 * count + h + 1] + later_ref[h : h + 1, 0:1]) for h in range(H)
    ]
    for buf, x in ((dk_buf, mm_nt(values_ref[0], start[count])), (dv_buf, mm(keys_ref[0], start[count]))):
        for h in range(H):
            lanes = slice(h * DH, (h + 1) * DH)
            buf[:, lanes] = (factor[h] * x[:, lanes]).astype(BF16)
    send(dk_buf, dk_hbm.at[0])
    send(dv_buf, dv_hbm.at[0])
    for r in range(count):
        for t in range(0, slots, HALF):
            at = slice(t, t + HALF)
            x = mm(q_ref[r, at, :], start[r])
            y = mm_nt(grad_ref[r, at, :], start[r])
            for h in range(H):
                lanes = slice(h * DH, (h + 1) * DH)
                carried = cols_ref[at, 8 * r + 2 + h : 8 * r + 3 + h]
                out_buf[r, at, lanes] = (po_ref[r, at, lanes] + carried * x[:, lanes]).astype(BF16)
                dq_buf[r, at, lanes] = (pdq_ref[r, at, lanes] + carried * y[:, lanes]).astype(BF16)
            send(out_buf.at[r, at], out_hbm.at[r, at])
            send(dq_buf.at[r, at], dq_hbm.at[r, at])
    for copy in copies:
        copy.wait()


def exchange(xs, axis):
    n = lax.axis_size(axis)
    return [xs[0]] + [lax.ppermute(xs[k], axis, [(s, s ^ k) for s in range(n)]) for k in range(n - 1, 0, -1)]


def by_partner(refs):
    return [refs[0], *refs[:0:-1]]


def shards(
    keys,
    values,
    prompt_gates,
    queries,
    resp_keys,
    resp_values,
    resp_gates,
    cotangent,
    group_ids,
    resp_lengths,
    loss_mask,
    advantages,
):
    n = lax.axis_size("prompt")
    chips = lax.axis_size("z")
    cores = lax.axis_size("core")
    responses, slots, width = queries.shape
    block = H * DH // n
    shape = jax.ShapeDtypeStruct

    outs = pl.pallas_call(
        lambda *refs: first_kernel(n, *refs),
        out_shape=[shape((block * (1 + responses) + 16, DH), BF16)] * n
        + [shape((slots, 128), F32), shape((responses, 8, slots), F32)]
        + [shape(queries.shape, BF16)] * 4,
        in_specs=[ANY] * 12,
        out_specs=[VMEM] * (n + 6),
        scratch_shapes=[
            pltpu.VMEM(keys.shape, BF16),
            pltpu.VMEM(values.shape, BF16),
            pltpu.VMEM(prompt_gates.shape, F32),
            pltpu.VMEM(resp_gates.shape, F32),
            pltpu.VMEM(loss_mask.shape, jnp.int32),
            pltpu.SMEM(group_ids.shape, jnp.int32),
            pltpu.SMEM(resp_lengths.shape, jnp.int32),
            pltpu.SMEM(advantages.shape, jnp.int32),
            pltpu.VMEM((H * (1 + responses), DH, DH), F32),
            pltpu.SemaphoreType.DMA((10 + 2 * responses,)),
        ],
        compiler_params=params(32),
        name="first",
    )(
        *[in_hbm(x) for x in (group_ids, resp_lengths, advantages, keys, values, prompt_gates, resp_gates)],
        *[in_hbm(x) for x in (loss_mask, queries, cotangent, resp_keys, resp_values)],
    )
    msgs, (cols, rows, queries, cotangent, resp_keys, resp_values) = outs[:n], outs[n:]

    like = shape(queries.shape, F32)
    like_out = shape(queries.shape, BF16)

    def sweep(units, before, token):
        outs = pl.pallas_call(
            lambda *refs: sweep_kernel(units, *refs),
            out_shape=[like, like, like_out, like_out, like_out, shape((8, 128), F32)],
            in_specs=[VMEM] * 6 + [ANY] * (1 + len(before)),
            out_specs=[VMEM, VMEM, VMEM, ANY, ANY, VMEM],
            scratch_shapes=[
                pltpu.VMEM((len(units), slots, DH), BF16),
                pltpu.VMEM((len(units), slots, DH), BF16),
                pltpu.SemaphoreType.DMA((2 * len(units),)),
            ],
            input_output_aliases={7 + k: k for k in range(len(before))},
            compiler_params=params(),
            name="sweep",
        )(cols, rows, queries, resp_keys, resp_values, cotangent, token, *before)
        return outs[:5], outs[5]

    units = [(r, h) for r in range(responses) for h in range(H)]
    got1 = exchange(msgs, "prompt")
    held, token = sweep(units[:2], [], cols)
    outs = pl.pallas_call(
        lambda *refs: second_kernel(n, chips, cores, *refs),
        out_shape=[shape(((1 + cores) * block, DH), BF16)] * chips + [shape((8, DH), F32)],
        in_specs=[VMEM] * n + [ANY],
        out_specs=[VMEM] * (chips + 1),
        scratch_shapes=[pltpu.VMEM((chips * cores, block, DH), F32)],
        compiler_params=params(),
        name="second",
    )(*got1, token)
    msgs, later = outs[:chips], outs[chips]
    got2 = exchange(msgs, "z")
    held, token = sweep(units[2:4], held, later)
    sent, kept = pl.pallas_call(
        lambda *refs: swap_kernel(chips, *refs),
        out_shape=[shape(((chips + 1) * block, DH), BF16)] * 2,
        in_specs=[VMEM] * chips + [ANY],
        out_specs=[VMEM, VMEM],
        compiler_params=params(),
        name="swap",
    )(*got2, token)
    swapped = exchange([kept, sent], "core")[1]
    held, token = sweep(units[4:5], held, kept)
    msgs = pl.pallas_call(
        lambda *refs: third_kernel(n, chips, *refs),
        out_shape=[shape(((responses + 1) * block, DH), BF16)] * n,
        in_specs=[VMEM] * (n + 2) + [ANY],
        out_specs=[VMEM] * n,
        compiler_params=params(),
        name="third",
    )(*got1, kept, swapped, token)
    got3 = exchange(msgs, "prompt")
    held, token = sweep(units[5:], held, msgs[0])
    partial_out, partial_dq, grad_out, resp_dk, resp_dv = held

    resp_out, resp_dq, prompt_dk, prompt_dv = pl.pallas_call(
        lambda *refs: last_kernel(n, responses, *refs),
        out_shape=[like_out, like_out, shape(keys.shape, BF16), shape(keys.shape, BF16)],
        in_specs=[VMEM] * (8 + n) + [ANY],
        out_specs=[ANY] * 4,
        scratch_shapes=[
            pltpu.VMEM((responses + 1, width, width), BF16),
            pltpu.VMEM(queries.shape, BF16),
            pltpu.VMEM(queries.shape, BF16),
            pltpu.VMEM(keys.shape[1:], BF16),
            pltpu.VMEM(keys.shape[1:], BF16),
            pltpu.SemaphoreType.DMA((2 + 2 * responses * (slots // HALF),)),
        ],
        compiler_params=params(),
        name="last",
    )(cols, queries, grad_out, partial_out, partial_dq, keys, values, later, *got3, token)
    return (resp_out, resp_dq, resp_dk, resp_dv, prompt_dk, prompt_dv)


def solution(mesh):
    n, count = mesh.shape["prompt"], mesh.shape["resp"]
    mesh = jax.sharding.Mesh(mesh.devices.reshape(n, count // 2, 2), ("prompt", "z", "core"))
    spread = P(("prompt", "z", "core"))
    three = P(("prompt", "z", "core"), None, None)
    two = P(("prompt", "z", "core"), None)
    prompt = P(("z", "core"), "prompt", None)
    return jax.shard_map(
        shards,
        mesh=mesh,
        in_specs=(
            prompt,
            prompt,
            P(("z", "core"), None, "prompt"),
            three,
            three,
            three,
            three,
            three,
            spread,
            two,
            two,
            spread,
        ),
        out_specs=(three, three, three, three, prompt, prompt),
        check_vma=False,
    )
```

```python
import jax
import jax.numpy as jnp
from jax import lax
from jax.experimental import pallas as pl
from jax.experimental.pallas import tpu as pltpu
from jax.sharding import PartitionSpec as P

H = 2
DH = 128
HALF = 256
LOG2E = 1.4426950408889634
F32 = jnp.float32
BF16 = jnp.bfloat16
NEVER = -1e30
VMEM = pl.BlockSpec(memory_space=pltpu.VMEM)
ANY = pl.BlockSpec(memory_space=pl.ANY)
SMEM = pl.BlockSpec(memory_space=pltpu.SMEM)


def params(mebibytes=16):
    return pltpu.CompilerParams(vmem_limit_bytes=mebibytes * 1024 * 1024)


def mm(a, b):
    return lax.dot_general(a, b, (((1,), (0,)), ((), ())), preferred_element_type=F32)


def mm_nt(a, b):
    return lax.dot_general(a, b, (((1,), (1,)), ((), ())), preferred_element_type=F32)


def mm_tn(a, b):
    return lax.dot_general(a, b, (((0,), (0,)), ((), ())), preferred_element_type=F32)


def in_hbm(x):
    return pltpu.with_memory_space_constraint(x, pltpu.HBM)


def three_terms(x):
    high = x.astype(BF16)
    rest = x - high.astype(F32)
    middle = rest.astype(BF16)
    return high, middle, (rest - middle.astype(F32)).astype(BF16)


def lane_cumsum(x):
    rows, width = x.shape
    ones = lax.broadcasted_iota(jnp.int32, (128, 128), 0) <= lax.broadcasted_iota(jnp.int32, (128, 128), 1)
    terms = jnp.concatenate(three_terms(x), axis=0)
    starts = range(0, width, 128)
    sums = mm(jnp.concatenate([terms[:, b : b + 128] for b in starts], axis=0), ones.astype(F32).astype(BF16))
    parts = []
    before = jnp.zeros((rows, 1), F32)
    for b in range(len(starts)):
        at = 3 * rows * b
        part = sums[at : at + rows] + sums[at + rows : at + 2 * rows] + sums[at + 2 * rows : at + 3 * rows]
        part = part + before
        before = part[:, 127:128]
        parts.append(part)
    return jnp.concatenate(parts, axis=1)


def first_kernel(
    n, ids_hbm, lens_hbm, adv_hbm, keys_hbm, values_hbm, pgates_hbm, gates_hbm, mask_hbm, q_hbm, c_hbm, k_hbm, v_hbm,
    *refs,
):
    msgs, (cols_ref, rows_ref, q, c, k_out, v_out) = refs[:n], refs[n : n + 6]
    keys, values, pgates, gates, mask, ids_ref, lens_ref, adv_ref, matrices, sems = refs[n + 6 :]
    pairs = [(pgates_hbm, pgates), (gates_hbm, gates), (mask_hbm, mask)]
    pairs += [(ids_hbm, ids_ref), (lens_hbm, lens_ref), (adv_hbm, adv_ref), (keys_hbm, keys), (values_hbm, values)]
    count = gates.shape[0]
    slots = gates.shape[2]
    tokens = keys.shape[1]
    for i in range(count):
        pairs += [(q_hbm.at[i], q.at[i]), (c_hbm.at[i], c.at[i])]
    pairs += [(k_hbm, k_out), (v_hbm, v_out)]
    copies = [pltpu.make_async_copy(a, b, sems.at[i]) for i, (a, b) in enumerate(pairs)]
    for copy in copies:
        copy.start()
    part = DH // n
    block = H * part
    targets = partners(n)

    def spread(at):
        for k in range(n):
            of = pl.ds(pl.multiple_of(targets[k] * part, part), part)
            msgs[k][at * part + (16 if at >= H else 0) : (at + 1) * part + (16 if at >= H else 0), :] = matrices[
                at, of, :
            ].astype(BF16)

    for copy in copies[:6]:
        copy.wait()
    piece = jnp.concatenate([pgates[0], jnp.zeros((H, slots - tokens), F32)], axis=1)
    gate_rows = [gates[i] for i in range(count)] + [piece, jnp.zeros((16 - H * (count + 1), slots), F32)]
    cum = lane_cumsum(jnp.concatenate(gate_rows, axis=0))
    carried = jnp.exp(cum)
    place = lax.broadcasted_iota(jnp.int32, (1, slots), 1)
    rows = []
    factors = []
    for i in range(count):
        weight = adv_ref[i].astype(F32) / 1024.0
        opened = jnp.where(place < lens_ref[0, i], 1.0, 0.0)
        live = mask[i : i + 1, :].astype(F32) * opened * weight
        rows += [cum[H * i : H * i + H], carried[H * i : H * i + H] * opened, live, opened, jnp.zeros((2, slots), F32)]
        factors.append(carried[H * i : H * i + H] * live)
    rows_ref[...] = jnp.concatenate(rows, axis=0).reshape(count, 8, slots)
    piece = cum[H * count : H * count + H]
    total = piece[:, -1:]
    suffix = total - piece
    rows += [suffix, jnp.zeros((128 - 8 * count - H, slots), F32)]
    cols_ref[...] = jnp.concatenate(rows, axis=0).T

    for copy in copies[6:8]:
        copy.wait()
    turned = keys[0].T
    later = jnp.exp(suffix[:, :tokens])
    for h in range(H):
        lanes = slice(h * DH, (h + 1) * DH)
        scaled = turned[lanes].astype(F32) * later[h : h + 1]
        high = scaled.astype(BF16)
        low = (scaled - high.astype(F32)).astype(BF16)
        both = mm(jnp.concatenate([high, low], axis=0), values[0, :, lanes])
        matrices[h] = both[:DH] + both[DH:]
        spread(h)
    notes = [jnp.broadcast_to(x[h : h + 1].astype(F32), (1, DH)) for x in three_terms(total) for h in range(H)]
    notes += [jnp.full((1, DH), ids_ref[i].astype(F32)) for i in range(count)]
    notes.append(jnp.zeros((16 - len(notes), DH), F32))
    notes = jnp.concatenate(notes, axis=0).astype(BF16)
    for k in range(n):
        msgs[k][block : block + 16, :] = notes

    for i in range(count):
        copies[8 + 2 * i].wait()
        turned = q[i].T
        copies[9 + 2 * i].wait()
        for h in range(H):
            lanes = slice(h * DH, (h + 1) * DH)
            scaled = (turned[lanes].astype(F32) * factors[i][h : h + 1]).astype(BF16)
            matrices[H * (1 + i) + h] = mm(scaled, c[i, :, lanes])
            spread(H * (1 + i) + h)
    for copy in copies[8 + 2 * count :]:
        copy.wait()


def noted_prompt(notes, i):
    return jnp.max(notes[3 * H + i : 3 * H + i + 1]).astype(jnp.int32)


def second_kernel(n, chips, cores, *refs):
    z_at = lax.axis_index("z")
    got, msgs, later_ref, sums = refs[:n], refs[n + 1 : n + 1 + chips], refs[-2], refs[-1]
    part = DH // n
    block = H * part
    responses = (got[0].shape[0] - block - 16) // block
    place = partners(n)
    notes = [got[k][block : block + 16, :].astype(F32) for k in range(n)]
    logs = [x[0:H] + x[H : 2 * H] + x[2 * H : 3 * H] for x in notes]
    final = jnp.zeros((block, DH), F32)
    for k in range(n):
        later = jnp.zeros_like(logs[0])
        for other in range(n):
            if other != k:
                later = later + jnp.where(place[other] > place[k], logs[other], 0.0)
        if k == 0:
            later_ref[...] = jnp.concatenate([later, jnp.zeros((8 - H, DH), F32)], axis=0)
        decay = jnp.exp(later)
        decay = [jnp.broadcast_to(decay[h : h + 1], (part, DH)) for h in range(H)]
        final = final + jnp.concatenate(decay, axis=0) * got[k][0:block, :].astype(F32)
    sums[...] = jnp.zeros_like(sums)
    for k in range(n):
        for i in range(responses):
            at = block * (1 + i) + 16
            sums[noted_prompt(notes[k], i)] += got[k][at : at + block, :].astype(F32)
    final = final.astype(BF16)
    for k in range(chips):
        z = lax.bitwise_xor(z_at, k)
        msgs[k][0:block, :] = final
        for c in range(cores):
            msgs[k][(1 + c) * block : (2 + c) * block, :] = sums[z * cores + c].astype(BF16)


def swap_kernel(chips, *refs):
    got, sent_ref, kept_ref = by_partner(refs[:chips]), refs[chips + 1], refs[chips + 2]
    block = got[0].shape[0] // 3
    totals = []
    for c in range(2):
        total = got[0][(1 + c) * block : (2 + c) * block, :].astype(F32)
        for k in range(1, chips):
            total = total + got[k][(1 + c) * block : (2 + c) * block, :].astype(F32)
        totals.append(total)
    for k in range(chips):
        final = got[k][0:block, :]
        sent_ref[k * block : (k + 1) * block, :] = final
        kept_ref[k * block : (k + 1) * block, :] = final
    low = lax.axis_index("core") == 0
    sent_ref[chips * block :, :] = jnp.where(low, totals[1], totals[0]).astype(BF16)
    kept_ref[chips * block :, :] = jnp.where(low, totals[0], totals[1]).astype(BF16)


def third_kernel(n, chips, *refs):
    z_at, core = lax.axis_index("z"), lax.axis_index("core")
    noted, kept_ref, got_ref, msgs = refs[:n], refs[n], refs[n + 1], refs[n + 3 :]
    block = H * DH // n
    responses = (noted[0].shape[0] - block - 16) // block
    total = kept_ref[chips * block :, :].astype(F32) + got_ref[chips * block :, :].astype(F32)
    total = total.astype(BF16)
    for k in range(n):
        notes = noted[k][block : block + 16, :].astype(F32)
        for i in range(responses):
            p = noted_prompt(notes, i)
            slot = lax.bitwise_xor(z_at, lax.div(p, 2))
            at = pl.ds(pl.multiple_of(slot * block, block), block)
            same = lax.rem(p, 2) == core
            state = jnp.where(same, kept_ref[at, :].astype(F32), got_ref[at, :].astype(F32))
            msgs[k][i * block : (i + 1) * block, :] = state.astype(BF16)
        msgs[k][responses * block :, :] = total


def sweep_kernel(units, cols_ref, rows_ref, q_ref, k_ref, v_ref, c_ref, *refs):
    out_ref, dq_ref, grad_ref, dk_ref, dv_ref, token_ref = refs[-6:]
    token_ref[...] = jnp.zeros_like(token_ref)
    quarter = HALF // 2
    causal = lax.broadcasted_iota(jnp.int32, (quarter, quarter), 0) >= lax.broadcasted_iota(
        jnp.int32, (quarter, quarter), 1
    )
    blank = jnp.zeros((quarter, quarter), BF16)
    blocks = q_ref.shape[1] // HALF

    def decayed(products, cum, row, diagonal):
        if not diagonal:
            decay = jnp.exp2(cum - row)
            return [(x * decay).astype(BF16) for x in products]
        first = jnp.exp2(jnp.where(causal, cum[:quarter] - row[:, :quarter], NEVER))
        left = jnp.exp2(cum[quarter:] - row[:, :quarter])
        right = jnp.exp2(jnp.where(causal, cum[quarter:] - row[:, quarter:], NEVER))
        results = []
        for x in products:
            upper = jnp.concatenate([(x[:quarter, :quarter] * first).astype(BF16), blank], axis=1)
            lower = [(x[quarter:, :quarter] * left).astype(BF16), (x[quarter:, quarter:] * right).astype(BF16)]
            results.append(jnp.concatenate([upper, jnp.concatenate(lower, axis=1)], axis=0))
        return results

    for r, h in units:
        lanes = slice(h * DH, (h + 1) * DH)
        cum = cols_ref[:, 8 * r + h : 8 * r + h + 1] * LOG2E
        row = rows_ref[r, h : h + 1, :] * LOG2E
        live = cols_ref[:, 8 * r + 4 : 8 * r + 5]
        opened = cols_ref[:, 8 * r + 5 : 8 * r + 6]
        grad_all = (c_ref[r, :, lanes].astype(F32) * live).astype(BF16)
        grad_ref[r, :, lanes] = grad_all
        query_turned = q_ref[r, :, lanes].T
        grad_turned = grad_all.T
        dk = [None] * blocks
        dv = [None] * blocks
        for t in range(blocks):
            at = slice(t * HALF, (t + 1) * HALF)
            query = q_ref[r, at, lanes]
            grad_out = grad_all[at]
            out = None
            dq = None
            for s in range(t + 1):
                of = slice(s * HALF, (s + 1) * HALF)
                key = k_ref[r, of, lanes]
                value = v_ref[r, of, lanes]
                mixing, scores = decayed(
                    [mm_nt(query, key), mm_nt(grad_out, value)], cum[at], row[:, of], s == t
                )
                o_new = mm(mixing, value)
                q_new = mm(scores, key)
                k_new = mm(query_turned[:, at], scores)
                v_new = mm(grad_turned[:, at], mixing)
                out = o_new if out is None else out + o_new
                dq = q_new if dq is None else dq + q_new
                dk[s] = k_new if dk[s] is None else dk[s] + k_new
                dv[s] = v_new if dv[s] is None else dv[s] + v_new
            out_ref[r, at, lanes] = out * opened[at]
            dq_ref[r, at, lanes] = dq
        for s in range(blocks):
            of = slice(s * HALF, (s + 1) * HALF)
            dk_ref[r, of, lanes] = dk[s].astype(BF16).T
            dv_ref[r, of, lanes] = dv[s].astype(BF16).T


def last_kernel(
    n, count, cols_ref, q_ref, grad_ref, po_ref, pdq_ref, rdk_ref, rdv_ref, keys_ref, values_ref, later_ref, *refs
):
    got, refs = refs[:n], refs[n + 1 :]
    out_hbm, dq_hbm, rdk_hbm, rdv_hbm, dk_hbm, dv_hbm, start, out_buf, dq_buf, dk_buf, dv_buf, sems = refs
    part = DH // n
    block = H * part
    place = partners(n)
    slots = q_ref.shape[1]
    tokens = keys_ref.shape[1]
    copies = []

    def send(a, b):
        copies.append(pltpu.make_async_copy(a, b, sems.at[len(copies)]))
        copies[-1].start()

    send(rdk_ref, rdk_hbm)
    send(rdv_ref, rdv_hbm)
    start[...] = jnp.zeros_like(start)
    for r in range(count + 1):
        for k in range(n):
            for h in range(H):
                of = pl.ds(pl.multiple_of(h * DH + place[k] * part, part), part)
                rows = got[k][r * block + h * part : r * block + (h + 1) * part, :]
                start[r, of, h * DH : (h + 1) * DH] = rows
    factor = [
        jnp.exp(cols_ref[:tokens, 8 * count + h : 8 * count + h + 1] + later_ref[h : h + 1, 0:1]) for h in range(H)
    ]
    for buf, x in ((dk_buf, mm_nt(values_ref[0], start[count])), (dv_buf, mm(keys_ref[0], start[count]))):
        for h in range(H):
            lanes = slice(h * DH, (h + 1) * DH)
            buf[:, lanes] = (factor[h] * x[:, lanes]).astype(BF16)
    send(dk_buf, dk_hbm.at[0])
    send(dv_buf, dv_hbm.at[0])
    for r in range(count):
        for t in range(0, slots, HALF):
            at = slice(t, t + HALF)
            x = mm(q_ref[r, at, :], start[r])
            y = mm_nt(grad_ref[r, at, :], start[r])
            for h in range(H):
                lanes = slice(h * DH, (h + 1) * DH)
                carried = cols_ref[at, 8 * r + 2 + h : 8 * r + 3 + h]
                out_buf[r, at, lanes] = (po_ref[r, at, lanes] + carried * x[:, lanes]).astype(BF16)
                dq_buf[r, at, lanes] = (pdq_ref[r, at, lanes] + carried * y[:, lanes]).astype(BF16)
            send(out_buf.at[r, at], out_hbm.at[r, at])
            send(dq_buf.at[r, at], dq_hbm.at[r, at])
    for copy in copies:
        copy.wait()


def steps(n):
    first = list(range(n - 1, 0, -1))
    return [0, *first], [0, *first[-1:], *first[:-1]]


def partners(n):
    me = lax.axis_index("prompt")
    low = lax.axis_index("core") == 0
    return [lax.bitwise_xor(me, jnp.where(low, a, b)) for a, b in zip(*steps(n))]


def exchange_prompt(xs):
    n = lax.axis_size("prompt")
    got = [xs[0]]
    for x, ks in zip(xs[1:], list(zip(*steps(n)))[1:]):
        pairs = [(2 * s + c, 2 * (s ^ ks[c]) + c) for s in range(n) for c in range(2)]
        got.append(lax.ppermute(x, ("prompt", "core"), pairs))
    return got


def exchange(xs, axis):
    n = lax.axis_size(axis)
    return [xs[0]] + [lax.ppermute(xs[k], axis, [(s, s ^ k) for s in range(n)]) for k in range(n - 1, 0, -1)]


def by_partner(refs):
    return [refs[0], *refs[:0:-1]]


def shards(
    keys,
    values,
    prompt_gates,
    queries,
    resp_keys,
    resp_values,
    resp_gates,
    cotangent,
    group_ids,
    resp_lengths,
    loss_mask,
    advantages,
):
    n = lax.axis_size("prompt")
    chips = lax.axis_size("z")
    cores = lax.axis_size("core")
    responses, slots, width = queries.shape
    block = H * DH // n
    shape = jax.ShapeDtypeStruct

    outs = pl.pallas_call(
        lambda *refs: first_kernel(n, *refs),
        out_shape=[shape((block * (1 + responses) + 16, DH), BF16)] * n
        + [shape((slots, 128), F32), shape((responses, 8, slots), F32)]
        + [shape(queries.shape, BF16)] * 4,
        in_specs=[ANY] * 12,
        out_specs=[VMEM] * (n + 6),
        scratch_shapes=[
            pltpu.VMEM(keys.shape, BF16),
            pltpu.VMEM(values.shape, BF16),
            pltpu.VMEM(prompt_gates.shape, F32),
            pltpu.VMEM(resp_gates.shape, F32),
            pltpu.VMEM(loss_mask.shape, jnp.int32),
            pltpu.SMEM(group_ids.shape, jnp.int32),
            pltpu.SMEM(resp_lengths.shape, jnp.int32),
            pltpu.SMEM(advantages.shape, jnp.int32),
            pltpu.VMEM((H * (1 + responses), DH, DH), F32),
            pltpu.SemaphoreType.DMA((10 + 2 * responses,)),
        ],
        compiler_params=params(32),
        name="first",
    )(
        *[in_hbm(x) for x in (group_ids, resp_lengths, advantages, keys, values, prompt_gates, resp_gates)],
        *[in_hbm(x) for x in (loss_mask, queries, cotangent, resp_keys, resp_values)],
    )
    msgs, (cols, rows, queries, cotangent, resp_keys, resp_values) = outs[:n], outs[n:]

    like = shape(queries.shape, F32)
    like_out = shape(queries.shape, BF16)

    def sweep(units, before, token):
        outs = pl.pallas_call(
            lambda *refs: sweep_kernel(units, *refs),
            out_shape=[like, like, like_out, like_out, like_out, shape((8, 128), F32)],
            in_specs=[VMEM] * 6 + [ANY] * (1 + len(before)),
            out_specs=[VMEM] * 6,
            input_output_aliases={7 + k: k for k in range(len(before))},
            compiler_params=params(),
            name="sweep",
        )(cols, rows, queries, resp_keys, resp_values, cotangent, token, *before)
        return outs[:5], outs[5]

    units = [(r, h) for r in range(responses) for h in range(H)]
    got1 = exchange_prompt(msgs)
    held, token = sweep(units[:2], [], cols)
    outs = pl.pallas_call(
        lambda *refs: second_kernel(n, chips, cores, *refs),
        out_shape=[shape(((1 + cores) * block, DH), BF16)] * chips + [shape((8, DH), F32)],
        in_specs=[VMEM] * n + [ANY],
        out_specs=[VMEM] * (chips + 1),
        scratch_shapes=[pltpu.VMEM((chips * cores, block, DH), F32)],
        compiler_params=params(),
        name="second",
    )(*got1, token)
    msgs, later = outs[:chips], outs[chips]
    got2 = exchange(msgs, "z")
    held, token = sweep(units[2:4], held, later)
    sent, kept = pl.pallas_call(
        lambda *refs: swap_kernel(chips, *refs),
        out_shape=[shape(((chips + 1) * block, DH), BF16)] * 2,
        in_specs=[VMEM] * chips + [ANY],
        out_specs=[VMEM, VMEM],
        compiler_params=params(),
        name="swap",
    )(*got2, token)
    swapped = exchange([kept, sent], "core")[1]
    held, token = sweep(units[4:5], held, kept)
    msgs = pl.pallas_call(
        lambda *refs: third_kernel(n, chips, *refs),
        out_shape=[shape(((responses + 1) * block, DH), BF16)] * n,
        in_specs=[VMEM] * (n + 2) + [ANY],
        out_specs=[VMEM] * n,
        compiler_params=params(),
        name="third",
    )(*got1, kept, swapped, token)
    got3 = exchange_prompt(msgs)
    held, token = sweep(units[5:], held, msgs[0])
    partial_out, partial_dq, grad_out, resp_dk, resp_dv = held

    resp_out, resp_dq, resp_dk, resp_dv, prompt_dk, prompt_dv = pl.pallas_call(
        lambda *refs: last_kernel(n, responses, *refs),
        out_shape=[like_out] * 4 + [shape(keys.shape, BF16)] * 2,
        in_specs=[VMEM] * (10 + n) + [ANY],
        out_specs=[ANY] * 6,
        scratch_shapes=[
            pltpu.VMEM((responses + 1, width, width), BF16),
            pltpu.VMEM(queries.shape, BF16),
            pltpu.VMEM(queries.shape, BF16),
            pltpu.VMEM(keys.shape[1:], BF16),
            pltpu.VMEM(keys.shape[1:], BF16),
            pltpu.SemaphoreType.DMA((4 + 2 * responses * (slots // HALF),)),
        ],
        compiler_params=params(),
        name="last",
    )(cols, queries, grad_out, partial_out, partial_dq, resp_dk, resp_dv, keys, values, later, *got3, token)
    return (resp_out, resp_dq, resp_dk, resp_dv, prompt_dk, prompt_dv)


def solution(mesh):
    n, count = mesh.shape["prompt"], mesh.shape["resp"]
    mesh = jax.sharding.Mesh(mesh.devices.reshape(n, count // 2, 2), ("prompt", "z", "core"))
    spread = P(("prompt", "z", "core"))
    three = P(("prompt", "z", "core"), None, None)
    two = P(("prompt", "z", "core"), None)
    prompt = P(("z", "core"), "prompt", None)
    return jax.shard_map(
        shards,
        mesh=mesh,
        in_specs=(
            prompt,
            prompt,
            P(("z", "core"), None, "prompt"),
            three,
            three,
            three,
            three,
            three,
            spread,
            two,
            two,
            spread,
        ),
        out_specs=(three, three, three, three, prompt, prompt),
        check_vma=False,
    )
```

```python
import jax
import jax.numpy as jnp
from jax import lax
from jax.experimental import pallas as pl
from jax.experimental.pallas import tpu as pltpu
from jax.sharding import PartitionSpec as P

H = 2
DH = 128
HALF = 256
LOG2E = 1.4426950408889634
F32 = jnp.float32
BF16 = jnp.bfloat16
NEVER = -1e30
VMEM = pl.BlockSpec(memory_space=pltpu.VMEM)
ANY = pl.BlockSpec(memory_space=pl.ANY)
SMEM = pl.BlockSpec(memory_space=pltpu.SMEM)


def params(mebibytes=16):
    return pltpu.CompilerParams(vmem_limit_bytes=mebibytes * 1024 * 1024)


def mm(a, b):
    return lax.dot_general(a, b, (((1,), (0,)), ((), ())), preferred_element_type=F32)


def mm_nt(a, b):
    return lax.dot_general(a, b, (((1,), (1,)), ((), ())), preferred_element_type=F32)


def mm_tn(a, b):
    return lax.dot_general(a, b, (((0,), (0,)), ((), ())), preferred_element_type=F32)


def in_hbm(x):
    return pltpu.with_memory_space_constraint(x, pltpu.HBM)


def three_terms(x):
    high = x.astype(BF16)
    rest = x - high.astype(F32)
    middle = rest.astype(BF16)
    return high, middle, (rest - middle.astype(F32)).astype(BF16)


def lane_cumsum(x):
    rows, width = x.shape
    ones = lax.broadcasted_iota(jnp.int32, (128, 128), 0) <= lax.broadcasted_iota(jnp.int32, (128, 128), 1)
    terms = jnp.concatenate(three_terms(x), axis=0)
    starts = range(0, width, 128)
    sums = mm(jnp.concatenate([terms[:, b : b + 128] for b in starts], axis=0), ones.astype(F32).astype(BF16))
    parts = []
    before = jnp.zeros((rows, 1), F32)
    for b in range(len(starts)):
        at = 3 * rows * b
        part = sums[at : at + rows] + sums[at + rows : at + 2 * rows] + sums[at + 2 * rows : at + 3 * rows]
        part = part + before
        before = part[:, 127:128]
        parts.append(part)
    return jnp.concatenate(parts, axis=1)


def first_kernel(
    n, ids_hbm, lens_hbm, adv_hbm, keys_hbm, values_hbm, pgates_hbm, gates_hbm, mask_hbm, q_hbm, c_hbm, k_hbm, v_hbm,
    *refs,
):
    msgs, (cols_ref, rows_ref, q, c, k_out, v_out) = refs[:n], refs[n : n + 6]
    keys, values, pgates, gates, mask, ids_ref, lens_ref, adv_ref, matrices, sems = refs[n + 6 :]
    pairs = [(pgates_hbm, pgates), (gates_hbm, gates), (mask_hbm, mask)]
    pairs += [(ids_hbm, ids_ref), (lens_hbm, lens_ref), (adv_hbm, adv_ref), (keys_hbm, keys), (values_hbm, values)]
    count = gates.shape[0]
    slots = gates.shape[2]
    tokens = keys.shape[1]
    for i in range(count):
        pairs += [(q_hbm.at[i], q.at[i]), (c_hbm.at[i], c.at[i])]
    pairs += [(k_hbm, k_out), (v_hbm, v_out)]
    copies = [pltpu.make_async_copy(a, b, sems.at[i]) for i, (a, b) in enumerate(pairs)]
    for copy in copies:
        copy.start()
    part = DH // n
    block = H * part
    targets = partners(n)

    def spread(at):
        for k in range(n):
            of = pl.ds(pl.multiple_of(targets[k] * part, part), part)
            msgs[k][at * part + (16 if at >= H else 0) : (at + 1) * part + (16 if at >= H else 0), :] = matrices[
                at, of, :
            ].astype(BF16)

    for copy in copies[:6]:
        copy.wait()
    piece = jnp.concatenate([pgates[0], jnp.zeros((H, slots - tokens), F32)], axis=1)
    gate_rows = [gates[i] for i in range(count)] + [piece, jnp.zeros((16 - H * (count + 1), slots), F32)]
    cum = lane_cumsum(jnp.concatenate(gate_rows, axis=0))
    carried = jnp.exp(cum)
    place = lax.broadcasted_iota(jnp.int32, (1, slots), 1)
    rows = []
    factors = []
    for i in range(count):
        weight = adv_ref[i].astype(F32) / 1024.0
        opened = jnp.where(place < lens_ref[0, i], 1.0, 0.0)
        live = mask[i : i + 1, :].astype(F32) * opened * weight
        rows += [cum[H * i : H * i + H], carried[H * i : H * i + H] * opened, live, opened, jnp.zeros((2, slots), F32)]
        factors.append(carried[H * i : H * i + H] * live)
    rows_ref[...] = jnp.concatenate(rows, axis=0).reshape(count, 8, slots)
    piece = cum[H * count : H * count + H]
    total = piece[:, -1:]
    suffix = total - piece
    rows += [suffix, jnp.zeros((128 - 8 * count - H, slots), F32)]
    cols_ref[...] = jnp.concatenate(rows, axis=0).T

    for copy in copies[6:8]:
        copy.wait()
    turned = keys[0].T
    later = jnp.exp(suffix[:, :tokens])
    for h in range(H):
        lanes = slice(h * DH, (h + 1) * DH)
        scaled = turned[lanes].astype(F32) * later[h : h + 1]
        high = scaled.astype(BF16)
        low = (scaled - high.astype(F32)).astype(BF16)
        both = mm(jnp.concatenate([high, low], axis=0), values[0, :, lanes])
        matrices[h] = both[:DH] + both[DH:]
        spread(h)
    notes = [jnp.broadcast_to(x[h : h + 1].astype(F32), (1, DH)) for x in three_terms(total) for h in range(H)]
    notes += [jnp.full((1, DH), ids_ref[i].astype(F32)) for i in range(count)]
    notes.append(jnp.zeros((16 - len(notes), DH), F32))
    notes = jnp.concatenate(notes, axis=0).astype(BF16)
    for k in range(n):
        msgs[k][block : block + 16, :] = notes

    for i in range(count):
        copies[8 + 2 * i].wait()
        turned = q[i].T
        copies[9 + 2 * i].wait()
        for h in range(H):
            lanes = slice(h * DH, (h + 1) * DH)
            scaled = (turned[lanes].astype(F32) * factors[i][h : h + 1]).astype(BF16)
            matrices[H * (1 + i) + h] = mm(scaled, c[i, :, lanes])
            spread(H * (1 + i) + h)
    for copy in copies[8 + 2 * count :]:
        copy.wait()


def noted_prompt(notes, i):
    return jnp.max(notes[3 * H + i : 3 * H + i + 1]).astype(jnp.int32)


def second_kernel(n, chips, cores, *refs):
    z_at = lax.axis_index("z")
    got, msgs, later_ref, sums = refs[:n], refs[n + 1 : n + 1 + chips], refs[-2], refs[-1]
    part = DH // n
    block = H * part
    responses = (got[0].shape[0] - block - 16) // block
    place = partners(n)
    notes = [got[k][block : block + 16, :].astype(F32) for k in range(n)]
    logs = [x[0:H] + x[H : 2 * H] + x[2 * H : 3 * H] for x in notes]
    final = jnp.zeros((block, DH), F32)
    for k in range(n):
        later = jnp.zeros_like(logs[0])
        for other in range(n):
            if other != k:
                later = later + jnp.where(place[other] > place[k], logs[other], 0.0)
        if k == 0:
            later_ref[...] = jnp.concatenate([later, jnp.zeros((8 - H, DH), F32)], axis=0)
        decay = jnp.exp(later)
        decay = [jnp.broadcast_to(decay[h : h + 1], (part, DH)) for h in range(H)]
        final = final + jnp.concatenate(decay, axis=0) * got[k][0:block, :].astype(F32)
    sums[...] = jnp.zeros_like(sums)
    for k in range(n):
        for i in range(responses):
            at = block * (1 + i) + 16
            sums[noted_prompt(notes[k], i)] += got[k][at : at + block, :].astype(F32)
    final = final.astype(BF16)
    for k in range(chips):
        z = lax.bitwise_xor(z_at, k)
        msgs[k][0:block, :] = final
        for c in range(cores):
            msgs[k][(1 + c) * block : (2 + c) * block, :] = sums[z * cores + c].astype(BF16)


def swap_kernel(chips, *refs):
    got, sent_ref, kept_ref = refs[:chips], refs[chips + 1], refs[chips + 2]
    block = got[0].shape[0] // 3
    totals = []
    for c in range(2):
        total = got[0][(1 + c) * block : (2 + c) * block, :].astype(F32)
        for k in range(1, chips):
            total = total + got[k][(1 + c) * block : (2 + c) * block, :].astype(F32)
        totals.append(total)
    for k in range(chips):
        final = got[k][0:block, :]
        sent_ref[k * block : (k + 1) * block, :] = final
        kept_ref[k * block : (k + 1) * block, :] = final
    low = lax.axis_index("core") == 0
    sent_ref[chips * block :, :] = jnp.where(low, totals[1], totals[0]).astype(BF16)
    kept_ref[chips * block :, :] = jnp.where(low, totals[0], totals[1]).astype(BF16)


def third_kernel(n, chips, *refs):
    z_at, core = lax.axis_index("z"), lax.axis_index("core")
    noted, kept_ref, got_ref, msgs = refs[:n], refs[n], refs[n + 1], refs[n + 3 :]
    block = H * DH // n
    responses = (noted[0].shape[0] - block - 16) // block
    total = kept_ref[chips * block :, :].astype(F32) + got_ref[chips * block :, :].astype(F32)
    total = total.astype(BF16)
    for k in range(n):
        notes = noted[k][block : block + 16, :].astype(F32)
        for i in range(responses):
            p = noted_prompt(notes, i)
            slot = lax.bitwise_xor(z_at, lax.div(p, 2))
            at = pl.ds(pl.multiple_of(slot * block, block), block)
            same = lax.rem(p, 2) == core
            state = jnp.where(same, kept_ref[at, :].astype(F32), got_ref[at, :].astype(F32))
            msgs[k][i * block : (i + 1) * block, :] = state.astype(BF16)
        msgs[k][responses * block :, :] = total


def sweep_kernel(units, done, cols_ref, rows_ref, q_ref, k_ref, v_ref, c_ref, *refs):
    writes = len(done) > 0
    if writes:
        *refs, dk_hbm, dv_hbm, sems = refs
    out_ref, dq_ref, query_ref, grad_ref, dk_ref, dv_ref, token_ref = refs[-7:]
    copies = []

    def send(r):
        for a, b in ((dk_ref, dk_hbm), (dv_ref, dv_hbm)):
            copies.append(pltpu.make_async_copy(a.at[r], b.at[r], sems.at[len(copies)]))
            copies[-1].start()

    for r in done:
        send(r)
    token_ref[...] = jnp.zeros_like(token_ref)
    quarter = HALF // 2
    causal = lax.broadcasted_iota(jnp.int32, (quarter, quarter), 0) >= lax.broadcasted_iota(
        jnp.int32, (quarter, quarter), 1
    )
    blank = jnp.zeros((quarter, quarter), BF16)
    blocks = q_ref.shape[1] // HALF

    def decayed(products, cum, row, diagonal):
        if not diagonal:
            decay = jnp.exp2(cum - row)
            return [(x * decay).astype(BF16) for x in products]
        first = jnp.exp2(jnp.where(causal, cum[:quarter] - row[:, :quarter], NEVER))
        left = jnp.exp2(cum[quarter:] - row[:, :quarter])
        right = jnp.exp2(jnp.where(causal, cum[quarter:] - row[:, quarter:], NEVER))
        results = []
        for x in products:
            upper = jnp.concatenate([(x[:quarter, :quarter] * first).astype(BF16), blank], axis=1)
            lower = [(x[quarter:, :quarter] * left).astype(BF16), (x[quarter:, quarter:] * right).astype(BF16)]
            results.append(jnp.concatenate([upper, jnp.concatenate(lower, axis=1)], axis=0))
        return results

    for r, h in units:
        lanes = slice(h * DH, (h + 1) * DH)
        cum = cols_ref[:, 8 * r + h : 8 * r + h + 1] * LOG2E
        row = rows_ref[r, h : h + 1, :] * LOG2E
        live = cols_ref[:, 8 * r + 4 : 8 * r + 5]
        opened = cols_ref[:, 8 * r + 5 : 8 * r + 6]
        grad_all = (c_ref[r, :, lanes].astype(F32) * live).astype(BF16)
        carried = cols_ref[:, 8 * r + 2 + h : 8 * r + 3 + h]
        query_ref[r, :, lanes] = (q_ref[r, :, lanes].astype(F32) * carried).astype(BF16)
        grad_ref[r, :, lanes] = (grad_all.astype(F32) * carried).astype(BF16)
        query_turned = q_ref[r, :, lanes].T
        grad_turned = grad_all.T
        dk = [None] * blocks
        dv = [None] * blocks
        for t in range(blocks):
            at = slice(t * HALF, (t + 1) * HALF)
            query = q_ref[r, at, lanes]
            grad_out = grad_all[at]
            out = None
            dq = None
            for s in range(t + 1):
                of = slice(s * HALF, (s + 1) * HALF)
                key = k_ref[r, of, lanes]
                value = v_ref[r, of, lanes]
                mixing, scores = decayed(
                    [mm_nt(query, key), mm_nt(grad_out, value)], cum[at], row[:, of], s == t
                )
                o_new = mm(mixing, value)
                q_new = mm(scores, key)
                k_new = mm(query_turned[:, at], scores)
                v_new = mm(grad_turned[:, at], mixing)
                out = o_new if out is None else out + o_new
                dq = q_new if dq is None else dq + q_new
                dk[s] = k_new if dk[s] is None else dk[s] + k_new
                dv[s] = v_new if dv[s] is None else dv[s] + v_new
            out_ref[r, at, lanes] = out * opened[at]
            dq_ref[r, at, lanes] = dq
        for s in range(blocks):
            of = slice(s * HALF, (s + 1) * HALF)
            dk_ref[r, of, lanes] = dk[s].astype(BF16).T
            dv_ref[r, of, lanes] = dv[s].astype(BF16).T
        if writes and h == H - 1:
            send(r)
    for copy in copies:
        copy.wait()


def last_kernel(
    n, count, cols_ref, q_ref, grad_ref, po_ref, pdq_ref, keys_ref, values_ref, later_ref, *refs
):
    got, refs = refs[:n], refs[n + 1 :]
    out_hbm, dq_hbm, dk_hbm, dv_hbm, start, out_buf, dq_buf, dk_buf, dv_buf, sems = refs
    part = DH // n
    block = H * part
    place = partners(n)
    slots = q_ref.shape[1]
    tokens = keys_ref.shape[1]
    copies = []

    def send(a, b):
        copies.append(pltpu.make_async_copy(a, b, sems.at[len(copies)]))
        copies[-1].start()

    start[...] = jnp.zeros_like(start)
    for r in range(count + 1):
        for k in range(n):
            for h in range(H):
                of = pl.ds(pl.multiple_of(h * DH + place[k] * part, part), part)
                rows = got[k][r * block + h * part : r * block + (h + 1) * part, :]
                start[r, of, h * DH : (h + 1) * DH] = rows
    factor = [
        jnp.exp(cols_ref[:tokens, 8 * count + h : 8 * count + h + 1] + later_ref[h : h + 1, 0:1]) for h in range(H)
    ]
    for buf, x in ((dk_buf, mm_nt(values_ref[0], start[count])), (dv_buf, mm(keys_ref[0], start[count]))):
        for h in range(H):
            lanes = slice(h * DH, (h + 1) * DH)
            buf[:, lanes] = (factor[h] * x[:, lanes]).astype(BF16)
    send(dk_buf, dk_hbm.at[0])
    send(dv_buf, dv_hbm.at[0])
    for r in range(count):
        for t in range(0, slots, HALF):
            at = slice(t, t + HALF)
            out_buf[r, at, :] = (po_ref[r, at, :] + mm(q_ref[r, at, :], start[r])).astype(BF16)
            dq_buf[r, at, :] = (pdq_ref[r, at, :] + mm_nt(grad_ref[r, at, :], start[r])).astype(BF16)
            send(out_buf.at[r, at], out_hbm.at[r, at])
            send(dq_buf.at[r, at], dq_hbm.at[r, at])
    for copy in copies:
        copy.wait()


def exchange(xs, axis):
    n = lax.axis_size(axis)
    return [xs[0]] + [lax.ppermute(xs[k], axis, [(s, s ^ k) for s in range(n)]) for k in range(1, n)]


def partners(n):
    me = lax.axis_index("prompt")
    return [lax.bitwise_xor(me, k) for k in range(n)]


def shards(
    keys,
    values,
    prompt_gates,
    queries,
    resp_keys,
    resp_values,
    resp_gates,
    cotangent,
    group_ids,
    resp_lengths,
    loss_mask,
    advantages,
):
    n = lax.axis_size("prompt")
    chips = lax.axis_size("z")
    cores = lax.axis_size("core")
    responses, slots, width = queries.shape
    block = H * DH // n
    shape = jax.ShapeDtypeStruct

    outs = pl.pallas_call(
        lambda *refs: first_kernel(n, *refs),
        out_shape=[shape((block * (1 + responses) + 16, DH), BF16)] * n
        + [shape((slots, 128), F32), shape((responses, 8, slots), F32)]
        + [shape(queries.shape, BF16)] * 4,
        in_specs=[ANY] * 12,
        out_specs=[VMEM] * (n + 6),
        scratch_shapes=[
            pltpu.VMEM(keys.shape, BF16),
            pltpu.VMEM(values.shape, BF16),
            pltpu.VMEM(prompt_gates.shape, F32),
            pltpu.VMEM(resp_gates.shape, F32),
            pltpu.VMEM(loss_mask.shape, jnp.int32),
            pltpu.SMEM(group_ids.shape, jnp.int32),
            pltpu.SMEM(resp_lengths.shape, jnp.int32),
            pltpu.SMEM(advantages.shape, jnp.int32),
            pltpu.VMEM((H * (1 + responses), DH, DH), F32),
            pltpu.SemaphoreType.DMA((10 + 2 * responses,)),
        ],
        compiler_params=params(32),
        name="first",
    )(
        *[in_hbm(x) for x in (group_ids, resp_lengths, advantages, keys, values, prompt_gates, resp_gates)],
        *[in_hbm(x) for x in (loss_mask, queries, cotangent, resp_keys, resp_values)],
    )
    msgs, (cols, rows, queries, cotangent, resp_keys, resp_values) = outs[:n], outs[n:]

    like = shape(queries.shape, F32)
    like_out = shape(queries.shape, BF16)

    def sweep(units, before, token, done=()):
        writes = len(done) > 0
        outs = pl.pallas_call(
            lambda *refs: sweep_kernel(units, done, *refs),
            out_shape=[like, like] + [like_out] * 4 + [shape((8, 128), F32)] + [like_out] * (2 * writes),
            in_specs=[VMEM] * 6 + [ANY] * (1 + len(before)),
            out_specs=[VMEM] * 7 + [ANY] * (2 * writes),
            scratch_shapes=[pltpu.SemaphoreType.DMA((2 * responses,))] * writes,
            input_output_aliases={7 + k: k for k in range(len(before))},
            compiler_params=params(),
            name="sweep",
        )(cols, rows, queries, resp_keys, resp_values, cotangent, token, *before)
        return (outs[:4] + outs[7:] if writes else outs[:6]), outs[6]

    units = [(r, h) for r in range(responses) for h in range(H)]
    got1 = exchange(msgs, "prompt")
    held, token = sweep(units[:3], [], cols)
    outs = pl.pallas_call(
        lambda *refs: second_kernel(n, chips, cores, *refs),
        out_shape=[shape(((1 + cores) * block, DH), BF16)] * chips + [shape((8, DH), F32)],
        in_specs=[VMEM] * n + [ANY],
        out_specs=[VMEM] * (chips + 1),
        scratch_shapes=[pltpu.VMEM((chips * cores, block, DH), F32)],
        compiler_params=params(),
        name="second",
    )(*got1, token)
    msgs, later = outs[:chips], outs[chips]
    got2 = exchange(msgs, "z")
    held, token = sweep(units[3:5], held, later)
    sent, kept = pl.pallas_call(
        lambda *refs: swap_kernel(chips, *refs),
        out_shape=[shape(((chips + 1) * block, DH), BF16)] * 2,
        in_specs=[VMEM] * chips + [ANY],
        out_specs=[VMEM, VMEM],
        compiler_params=params(),
        name="swap",
    )(*got2, token)
    swapped = exchange([kept, sent], "core")[1]
    held, token = sweep(units[5:6], held, kept)
    msgs = pl.pallas_call(
        lambda *refs: third_kernel(n, chips, *refs),
        out_shape=[shape(((responses + 1) * block, DH), BF16)] * n,
        in_specs=[VMEM] * (n + 2) + [ANY],
        out_specs=[VMEM] * n,
        compiler_params=params(),
        name="third",
    )(*got1, kept, swapped, token)
    got3 = exchange(msgs, "prompt")
    held, token = sweep(units[6:], held, msgs[0], range(responses - 1))
    partial_out, partial_dq, query, grad_out, resp_dk, resp_dv = held

    resp_out, resp_dq, prompt_dk, prompt_dv = pl.pallas_call(
        lambda *refs: last_kernel(n, responses, *refs),
        out_shape=[like_out] * 2 + [shape(keys.shape, BF16)] * 2,
        in_specs=[VMEM] * (8 + n) + [ANY],
        out_specs=[ANY] * 4,
        scratch_shapes=[
            pltpu.VMEM((responses + 1, width, width), BF16),
            pltpu.VMEM(queries.shape, BF16),
            pltpu.VMEM(queries.shape, BF16),
            pltpu.VMEM(keys.shape[1:], BF16),
            pltpu.VMEM(keys.shape[1:], BF16),
            pltpu.SemaphoreType.DMA((2 + 2 * responses * (slots // HALF),)),
        ],
        compiler_params=params(),
        name="last",
    )(cols, query, grad_out, partial_out, partial_dq, keys, values, later, *got3, token)
    return (resp_out, resp_dq, resp_dk, resp_dv, prompt_dk, prompt_dv)


def solution(mesh):
    n, count = mesh.shape["prompt"], mesh.shape["resp"]
    mesh = jax.sharding.Mesh(mesh.devices.reshape(n, count // 2, 2), ("prompt", "z", "core"))
    spread = P(("prompt", "z", "core"))
    three = P(("prompt", "z", "core"), None, None)
    two = P(("prompt", "z", "core"), None)
    prompt = P(("z", "core"), "prompt", None)
    return jax.shard_map(
        shards,
        mesh=mesh,
        in_specs=(
            prompt,
            prompt,
            P(("z", "core"), None, "prompt"),
            three,
            three,
            three,
            three,
            three,
            spread,
            two,
            two,
            spread,
        ),
        out_specs=(three, three, three, three, prompt, prompt),
        check_vma=False,
    )
```

```python
import jax
import jax.numpy as jnp
from jax import lax
from jax.experimental import pallas as pl
from jax.experimental.pallas import tpu as pltpu
from jax.sharding import PartitionSpec as P

H = 2
DH = 128
HALF = 256
LOG2E = 1.4426950408889634
F32 = jnp.float32
BF16 = jnp.bfloat16
NEVER = -1e30
VMEM = pl.BlockSpec(memory_space=pltpu.VMEM)
ANY = pl.BlockSpec(memory_space=pl.ANY)
SMEM = pl.BlockSpec(memory_space=pltpu.SMEM)


def params(mebibytes=16):
    return pltpu.CompilerParams(vmem_limit_bytes=mebibytes * 1024 * 1024)


def mm(a, b):
    return lax.dot_general(a, b, (((1,), (0,)), ((), ())), preferred_element_type=F32)


def mm_nt(a, b):
    return lax.dot_general(a, b, (((1,), (1,)), ((), ())), preferred_element_type=F32)


def mm_tn(a, b):
    return lax.dot_general(a, b, (((0,), (0,)), ((), ())), preferred_element_type=F32)


def to_columns(rows):
    return jnp.concatenate([rows, jnp.zeros((128 - rows.shape[0], rows.shape[1]), F32)], axis=0).T


def in_hbm(x):
    return pltpu.with_memory_space_constraint(x, pltpu.HBM)


def three_terms(x):
    high = x.astype(BF16)
    rest = x - high.astype(F32)
    middle = rest.astype(BF16)
    return high, middle, (rest - middle.astype(F32)).astype(BF16)


def lane_cumsum(x):
    rows, width = x.shape
    ones = lax.broadcasted_iota(jnp.int32, (128, 128), 0) <= lax.broadcasted_iota(jnp.int32, (128, 128), 1)
    terms = jnp.concatenate(three_terms(x), axis=0)
    starts = range(0, width, 128)
    sums = mm(jnp.concatenate([terms[:, b : b + 128] for b in starts], axis=0), ones.astype(F32).astype(BF16))
    parts = []
    before = jnp.zeros((rows, 1), F32)
    for b in range(len(starts)):
        at = 3 * rows * b
        part = sums[at : at + rows] + sums[at + rows : at + 2 * rows] + sums[at + 2 * rows : at + 3 * rows]
        part = part + before
        before = part[:, 127:128]
        parts.append(part)
    return jnp.concatenate(parts, axis=1)


def first_kernel(
    n, ids_hbm, lens_hbm, adv_hbm, keys_hbm, values_hbm, pgates_hbm, gates_hbm, mask_hbm, q_hbm, c_hbm, k_hbm, v_hbm,
    *refs,
):
    msgs, (rows_ref, q, c, k_out, v_out) = refs[:n], refs[n : n + 5]
    keys, values, pgates, gates, mask, ids_ref, lens_ref, adv_ref, matrices, sems = refs[n + 5 :]
    pairs = [(pgates_hbm, pgates), (gates_hbm, gates), (mask_hbm, mask)]
    pairs += [(ids_hbm, ids_ref), (lens_hbm, lens_ref), (adv_hbm, adv_ref), (keys_hbm, keys), (values_hbm, values)]
    count = gates.shape[0]
    slots = gates.shape[2]
    tokens = keys.shape[1]
    for i in range(count):
        pairs += [(q_hbm.at[i], q.at[i]), (c_hbm.at[i], c.at[i])]
    pairs += [(k_hbm, k_out), (v_hbm, v_out)]
    copies = [pltpu.make_async_copy(a, b, sems.at[i]) for i, (a, b) in enumerate(pairs)]
    for copy in copies:
        copy.start()
    part = DH // n
    block = H * part
    targets = partners(n)

    def spread(at):
        for k in range(n):
            of = pl.ds(pl.multiple_of(targets[k] * part, part), part)
            msgs[k][at * part + (16 if at >= H else 0) : (at + 1) * part + (16 if at >= H else 0), :] = matrices[
                at, of, :
            ].astype(BF16)

    for copy in copies[:6]:
        copy.wait()
    piece = jnp.concatenate([pgates[0], jnp.zeros((H, slots - tokens), F32)], axis=1)
    gate_rows = [gates[i] for i in range(count)] + [piece, jnp.zeros((16 - H * (count + 1), slots), F32)]
    cum = lane_cumsum(jnp.concatenate(gate_rows, axis=0))
    carried = jnp.exp(cum)
    place = lax.broadcasted_iota(jnp.int32, (1, slots), 1)
    rows = []
    factors = []
    for i in range(count):
        weight = adv_ref[i].astype(F32) / 1024.0
        opened = jnp.where(place < lens_ref[0, i], 1.0, 0.0)
        live = mask[i : i + 1, :].astype(F32) * opened * weight
        rows += [cum[H * i : H * i + H], carried[H * i : H * i + H] * opened, live, opened, jnp.zeros((2, slots), F32)]
        factors.append(carried[H * i : H * i + H] * live)
    piece = cum[H * count : H * count + H]
    total = piece[:, -1:]
    suffix = total - piece
    rows += [suffix, jnp.zeros((8 - H, slots), F32)]
    rows_ref[...] = jnp.concatenate(rows, axis=0)

    for copy in copies[6:8]:
        copy.wait()
    turned = keys[0].T
    later = jnp.exp(suffix[:, :tokens])
    for h in range(H):
        lanes = slice(h * DH, (h + 1) * DH)
        scaled = turned[lanes].astype(F32) * later[h : h + 1]
        high = scaled.astype(BF16)
        low = (scaled - high.astype(F32)).astype(BF16)
        both = mm(jnp.concatenate([high, low], axis=0), values[0, :, lanes])
        matrices[h] = both[:DH] + both[DH:]
        spread(h)
    notes = [jnp.broadcast_to(x[h : h + 1].astype(F32), (1, DH)) for x in three_terms(total) for h in range(H)]
    notes += [jnp.full((1, DH), ids_ref[i].astype(F32)) for i in range(count)]
    notes.append(jnp.zeros((16 - len(notes), DH), F32))
    notes = jnp.concatenate(notes, axis=0).astype(BF16)
    for k in range(n):
        msgs[k][block : block + 16, :] = notes

    for i in range(count):
        copies[8 + 2 * i].wait()
        turned = q[i].T
        copies[9 + 2 * i].wait()
        for h in range(H):
            lanes = slice(h * DH, (h + 1) * DH)
            scaled = (turned[lanes].astype(F32) * factors[i][h : h + 1]).astype(BF16)
            matrices[H * (1 + i) + h] = mm(scaled, c[i, :, lanes])
            spread(H * (1 + i) + h)
    for copy in copies[8 + 2 * count :]:
        copy.wait()


def noted_prompt(notes, i):
    return jnp.max(notes[3 * H + i : 3 * H + i + 1]).astype(jnp.int32)


def second_kernel(n, chips, cores, *refs):
    z_at = lax.axis_index("z")
    got, msgs, later_ref, sums = far_first(refs[:n]), refs[n + 1 : n + 1 + chips], refs[-2], refs[-1]
    part = DH // n
    block = H * part
    responses = (got[0].shape[0] - block - 16) // block
    place = partners(n)
    notes = [got[k][block : block + 16, :].astype(F32) for k in range(n)]
    logs = [x[0:H] + x[H : 2 * H] + x[2 * H : 3 * H] for x in notes]
    final = jnp.zeros((block, DH), F32)
    for k in range(n):
        later = jnp.zeros_like(logs[0])
        for other in range(n):
            if other != k:
                later = later + jnp.where(place[other] > place[k], logs[other], 0.0)
        if k == 0:
            later_ref[...] = jnp.concatenate([later, jnp.zeros((8 - H, DH), F32)], axis=0)
        decay = jnp.exp(later)
        decay = [jnp.broadcast_to(decay[h : h + 1], (part, DH)) for h in range(H)]
        final = final + jnp.concatenate(decay, axis=0) * got[k][0:block, :].astype(F32)
    sums[...] = jnp.zeros_like(sums)
    for k in range(n):
        for i in range(responses):
            at = block * (1 + i) + 16
            sums[noted_prompt(notes[k], i)] += got[k][at : at + block, :].astype(F32)
    final = final.astype(BF16)
    for k in range(chips):
        z = lax.bitwise_xor(z_at, k)
        msgs[k][0:block, :] = final
        for c in range(cores):
            msgs[k][(1 + c) * block : (2 + c) * block, :] = sums[z * cores + c].astype(BF16)


def swap_kernel(chips, *refs):
    got, sent_ref, kept_ref = far_first(refs[:chips]), refs[chips + 1], refs[chips + 2]
    block = got[0].shape[0] // 3
    totals = []
    for c in range(2):
        total = got[0][(1 + c) * block : (2 + c) * block, :].astype(F32)
        for k in range(1, chips):
            total = total + got[k][(1 + c) * block : (2 + c) * block, :].astype(F32)
        totals.append(total)
    for k in range(chips):
        final = got[k][0:block, :]
        sent_ref[k * block : (k + 1) * block, :] = final
        kept_ref[k * block : (k + 1) * block, :] = final
    low = lax.axis_index("core") == 0
    sent_ref[chips * block :, :] = jnp.where(low, totals[1], totals[0]).astype(BF16)
    kept_ref[chips * block :, :] = jnp.where(low, totals[0], totals[1]).astype(BF16)


def third_kernel(n, chips, *refs):
    z_at, core = lax.axis_index("z"), lax.axis_index("core")
    noted, kept_ref, got_ref, msgs = far_first(refs[:n]), refs[n], refs[n + 1], refs[n + 3 :]
    block = H * DH // n
    responses = (noted[0].shape[0] - block - 16) // block
    total = kept_ref[chips * block :, :].astype(F32) + got_ref[chips * block :, :].astype(F32)
    total = total.astype(BF16)
    for k in range(n):
        notes = noted[k][block : block + 16, :].astype(F32)
        for i in range(responses):
            p = noted_prompt(notes, i)
            slot = lax.bitwise_xor(z_at, lax.div(p, 2))
            at = pl.ds(pl.multiple_of(slot * block, block), block)
            same = lax.rem(p, 2) == core
            state = jnp.where(same, kept_ref[at, :].astype(F32), got_ref[at, :].astype(F32))
            msgs[k][i * block : (i + 1) * block, :] = state.astype(BF16)
        msgs[k][responses * block :, :] = total


def sweep_kernel(units, done, rows_ref, q_ref, k_ref, v_ref, c_ref, cols_ref, *refs):
    writes = len(done) > 0
    if writes:
        *refs, dk_hbm, dv_hbm, sems = refs
    out_ref, dq_ref, query_ref, grad_ref, dk_ref, dv_ref, token_ref = refs[-7:]
    if cols_ref is None:
        cols_ref = refs[0]
        cols_ref[...] = to_columns(rows_ref[...])
    copies = []

    def send(r):
        for a, b in ((dk_ref, dk_hbm), (dv_ref, dv_hbm)):
            copies.append(pltpu.make_async_copy(a.at[r], b.at[r], sems.at[len(copies)]))
            copies[-1].start()

    for r in done:
        send(r)
    token_ref[...] = jnp.zeros_like(token_ref)
    quarter = HALF // 2
    causal = lax.broadcasted_iota(jnp.int32, (quarter, quarter), 0) >= lax.broadcasted_iota(
        jnp.int32, (quarter, quarter), 1
    )
    blank = jnp.zeros((quarter, quarter), BF16)
    blocks = q_ref.shape[1] // HALF

    def decayed(products, cum, row, diagonal):
        if not diagonal:
            decay = jnp.exp2(cum - row)
            return [(x * decay).astype(BF16) for x in products]
        first = jnp.exp2(jnp.where(causal, cum[:quarter] - row[:, :quarter], NEVER))
        left = jnp.exp2(cum[quarter:] - row[:, :quarter])
        right = jnp.exp2(jnp.where(causal, cum[quarter:] - row[:, quarter:], NEVER))
        results = []
        for x in products:
            upper = jnp.concatenate([(x[:quarter, :quarter] * first).astype(BF16), blank], axis=1)
            lower = [(x[quarter:, :quarter] * left).astype(BF16), (x[quarter:, quarter:] * right).astype(BF16)]
            results.append(jnp.concatenate([upper, jnp.concatenate(lower, axis=1)], axis=0))
        return results

    for r, h in units:
        lanes = slice(h * DH, (h + 1) * DH)
        cum = cols_ref[:, 8 * r + h : 8 * r + h + 1] * LOG2E
        row = rows_ref[8 * r + h : 8 * r + h + 1, :] * LOG2E
        live = cols_ref[:, 8 * r + 4 : 8 * r + 5]
        opened = cols_ref[:, 8 * r + 5 : 8 * r + 6]
        grad_all = (c_ref[r, :, lanes].astype(F32) * live).astype(BF16)
        carried = cols_ref[:, 8 * r + 2 + h : 8 * r + 3 + h]
        query_ref[r, :, lanes] = (q_ref[r, :, lanes].astype(F32) * carried).astype(BF16)
        grad_ref[r, :, lanes] = (grad_all.astype(F32) * carried).astype(BF16)
        query_turned = q_ref[r, :, lanes].T
        grad_turned = grad_all.T
        dk = [None] * blocks
        dv = [None] * blocks
        for t in range(blocks):
            at = slice(t * HALF, (t + 1) * HALF)
            query = q_ref[r, at, lanes]
            grad_out = grad_all[at]
            out = None
            dq = None
            for s in range(t + 1):
                of = slice(s * HALF, (s + 1) * HALF)
                key = k_ref[r, of, lanes]
                value = v_ref[r, of, lanes]
                mixing, scores = decayed(
                    [mm_nt(query, key), mm_nt(grad_out, value)], cum[at], row[:, of], s == t
                )
                o_new = mm(mixing, value)
                q_new = mm(scores, key)
                k_new = mm(query_turned[:, at], scores)
                v_new = mm(grad_turned[:, at], mixing)
                out = o_new if out is None else out + o_new
                dq = q_new if dq is None else dq + q_new
                dk[s] = k_new if dk[s] is None else dk[s] + k_new
                dv[s] = v_new if dv[s] is None else dv[s] + v_new
            out_ref[r, at, lanes] = out * opened[at]
            dq_ref[r, at, lanes] = dq
        for s in range(blocks):
            of = slice(s * HALF, (s + 1) * HALF)
            dk_ref[r, of, lanes] = dk[s].astype(BF16).T
            dv_ref[r, of, lanes] = dv[s].astype(BF16).T
        if writes and h == H - 1:
            send(r)
    for copy in copies:
        copy.wait()


def last_kernel(
    n, count, cols_ref, q_ref, grad_ref, po_ref, pdq_ref, keys_ref, values_ref, later_ref, *refs
):
    got, refs = refs[:n], refs[n + 1 :]
    out_hbm, dq_hbm, dk_hbm, dv_hbm, start, out_buf, dq_buf, dk_buf, dv_buf, sems = refs
    part = DH // n
    block = H * part
    place = partners(n)
    slots = q_ref.shape[1]
    tokens = keys_ref.shape[1]
    copies = []

    def send(a, b):
        copies.append(pltpu.make_async_copy(a, b, sems.at[len(copies)]))
        copies[-1].start()

    start[...] = jnp.zeros_like(start)
    for r in range(count + 1):
        for k in range(n):
            for h in range(H):
                of = pl.ds(pl.multiple_of(h * DH + place[k] * part, part), part)
                rows = got[k][r * block + h * part : r * block + (h + 1) * part, :]
                start[r, of, h * DH : (h + 1) * DH] = rows
    factor = [
        jnp.exp(cols_ref[:tokens, 8 * count + h : 8 * count + h + 1] + later_ref[h : h + 1, 0:1]) for h in range(H)
    ]
    for buf, x in ((dk_buf, mm_nt(values_ref[0], start[count])), (dv_buf, mm(keys_ref[0], start[count]))):
        for h in range(H):
            lanes = slice(h * DH, (h + 1) * DH)
            buf[:, lanes] = (factor[h] * x[:, lanes]).astype(BF16)
    send(dk_buf, dk_hbm.at[0])
    send(dv_buf, dv_hbm.at[0])
    for r in range(count):
        for t in range(0, slots, HALF):
            at = slice(t, t + HALF)
            out_buf[r, at, :] = (po_ref[r, at, :] + mm(q_ref[r, at, :], start[r])).astype(BF16)
            dq_buf[r, at, :] = (pdq_ref[r, at, :] + mm_nt(grad_ref[r, at, :], start[r])).astype(BF16)
            send(out_buf.at[r, at], out_hbm.at[r, at])
            send(dq_buf.at[r, at], dq_hbm.at[r, at])
    for copy in copies:
        copy.wait()


def exchange(xs, axis):
    n = lax.axis_size(axis)
    return [xs[0]] + [lax.ppermute(xs[k], axis, [(s, s ^ k) for s in range(n)]) for k in range(1, n)]


def far_first(refs):
    return [refs[0], *refs[:0:-1]]


def partners(n):
    me = lax.axis_index("prompt")
    return [lax.bitwise_xor(me, k) for k in range(n)]


def shards(
    keys,
    values,
    prompt_gates,
    queries,
    resp_keys,
    resp_values,
    resp_gates,
    cotangent,
    group_ids,
    resp_lengths,
    loss_mask,
    advantages,
):
    n = lax.axis_size("prompt")
    chips = lax.axis_size("z")
    cores = lax.axis_size("core")
    responses, slots, width = queries.shape
    block = H * DH // n
    shape = jax.ShapeDtypeStruct

    outs = pl.pallas_call(
        lambda *refs: first_kernel(n, *refs),
        out_shape=[shape((block * (1 + responses) + 16, DH), BF16)] * n
        + [shape((8 * (responses + 1), slots), F32)]
        + [shape(queries.shape, BF16)] * 4,
        in_specs=[ANY] * 12,
        out_specs=[VMEM] * (n + 5),
        scratch_shapes=[
            pltpu.VMEM(keys.shape, BF16),
            pltpu.VMEM(values.shape, BF16),
            pltpu.VMEM(prompt_gates.shape, F32),
            pltpu.VMEM(resp_gates.shape, F32),
            pltpu.VMEM(loss_mask.shape, jnp.int32),
            pltpu.SMEM(group_ids.shape, jnp.int32),
            pltpu.SMEM(resp_lengths.shape, jnp.int32),
            pltpu.SMEM(advantages.shape, jnp.int32),
            pltpu.VMEM((H * (1 + responses), DH, DH), F32),
            pltpu.SemaphoreType.DMA((10 + 2 * responses,)),
        ],
        compiler_params=params(32),
        name="first",
    )(
        *[in_hbm(x) for x in (group_ids, resp_lengths, advantages, keys, values, prompt_gates, resp_gates)],
        *[in_hbm(x) for x in (loss_mask, queries, cotangent, resp_keys, resp_values)],
    )
    msgs, (rows, queries, cotangent, resp_keys, resp_values) = outs[:n], outs[n:]

    like = shape(queries.shape, F32)
    like_out = shape(queries.shape, BF16)

    held_shapes = [like, like] + [like_out] * 4 + [shape((8, 128), F32)]

    def first_sweep(units):
        outs = pl.pallas_call(
            lambda *refs: sweep_kernel(units, (), *refs[:5], None, *refs[5:]),
            out_shape=[shape((slots, 128), F32)] + held_shapes,
            in_specs=[VMEM] * 5,
            out_specs=[VMEM] * 8,
            compiler_params=params(),
            name="sweep",
        )(rows, queries, resp_keys, resp_values, cotangent)
        return outs[0], outs[1:7], outs[7]

    def sweep(units, before, token, done=()):
        writes = len(done) > 0
        outs = pl.pallas_call(
            lambda *refs: sweep_kernel(units, done, *refs),
            out_shape=held_shapes + [like_out] * (2 * writes),
            in_specs=[VMEM] * 6 + [ANY] * 7,
            out_specs=[VMEM] * 7 + [ANY] * (2 * writes),
            scratch_shapes=[pltpu.SemaphoreType.DMA((2 * responses,))] * writes,
            input_output_aliases={7 + k: k for k in range(6)},
            compiler_params=params(),
            name="sweep",
        )(rows, queries, resp_keys, resp_values, cotangent, cols, token, *before)
        return (outs[:4] + outs[7:] if writes else outs[:6]), outs[6]

    units = [(r, h) for r in range(responses) for h in range(H)]
    got1 = far_first(exchange(msgs, "prompt"))
    cols, held, token = first_sweep(units[:3])
    outs = pl.pallas_call(
        lambda *refs: second_kernel(n, chips, cores, *refs),
        out_shape=[shape(((1 + cores) * block, DH), BF16)] * chips + [shape((8, DH), F32)],
        in_specs=[VMEM] * n + [ANY],
        out_specs=[VMEM] * (chips + 1),
        scratch_shapes=[pltpu.VMEM((chips * cores, block, DH), F32)],
        compiler_params=params(),
        name="second",
    )(*got1, token)
    msgs, later = outs[:chips], outs[chips]
    got2 = far_first(exchange(msgs, "z"))
    held, token = sweep(units[3:5], held, later)
    sent, kept = pl.pallas_call(
        lambda *refs: swap_kernel(chips, *refs),
        out_shape=[shape(((chips + 1) * block, DH), BF16)] * 2,
        in_specs=[VMEM] * chips + [ANY],
        out_specs=[VMEM, VMEM],
        compiler_params=params(),
        name="swap",
    )(*got2, token)
    swapped = exchange([kept, sent], "core")[1]
    held, token = sweep(units[5:6], held, kept)
    msgs = pl.pallas_call(
        lambda *refs: third_kernel(n, chips, *refs),
        out_shape=[shape(((responses + 1) * block, DH), BF16)] * n,
        in_specs=[VMEM] * (n + 2) + [ANY],
        out_specs=[VMEM] * n,
        compiler_params=params(),
        name="third",
    )(*got1, kept, swapped, token)
    got3 = exchange(msgs, "prompt")
    held, token = sweep(units[6:], held, msgs[0], range(responses - 1))
    partial_out, partial_dq, query, grad_out, resp_dk, resp_dv = held

    resp_out, resp_dq, prompt_dk, prompt_dv = pl.pallas_call(
        lambda *refs: last_kernel(n, responses, *refs),
        out_shape=[like_out] * 2 + [shape(keys.shape, BF16)] * 2,
        in_specs=[VMEM] * (8 + n) + [ANY],
        out_specs=[ANY] * 4,
        scratch_shapes=[
            pltpu.VMEM((responses + 1, width, width), BF16),
            pltpu.VMEM(queries.shape, BF16),
            pltpu.VMEM(queries.shape, BF16),
            pltpu.VMEM(keys.shape[1:], BF16),
            pltpu.VMEM(keys.shape[1:], BF16),
            pltpu.SemaphoreType.DMA((2 + 2 * responses * (slots // HALF),)),
        ],
        compiler_params=params(),
        name="last",
    )(cols, query, grad_out, partial_out, partial_dq, keys, values, later, *got3, token)
    return (resp_out, resp_dq, resp_dk, resp_dv, prompt_dk, prompt_dv)


def solution(mesh):
    n, count = mesh.shape["prompt"], mesh.shape["resp"]
    mesh = jax.sharding.Mesh(mesh.devices.reshape(n, count // 2, 2), ("prompt", "z", "core"))
    spread = P(("prompt", "z", "core"))
    three = P(("prompt", "z", "core"), None, None)
    two = P(("prompt", "z", "core"), None)
    prompt = P(("z", "core"), "prompt", None)
    return jax.shard_map(
        shards,
        mesh=mesh,
        in_specs=(
            prompt,
            prompt,
            P(("z", "core"), None, "prompt"),
            three,
            three,
            three,
            three,
            three,
            spread,
            two,
            two,
            spread,
        ),
        out_specs=(three, three, three, three, prompt, prompt),
        check_vma=False,
    )
```

```python
import jax
import jax.numpy as jnp
from jax import lax
from jax.experimental import pallas as pl
from jax.experimental.pallas import tpu as pltpu
from jax.sharding import PartitionSpec as P

H = 2
DH = 128
HALF = 256
LOG2E = 1.4426950408889634
F32 = jnp.float32
BF16 = jnp.bfloat16
NEVER = -1e30
VMEM = pl.BlockSpec(memory_space=pltpu.VMEM)
ANY = pl.BlockSpec(memory_space=pl.ANY)
SMEM = pl.BlockSpec(memory_space=pltpu.SMEM)


def params(mebibytes=16):
    return pltpu.CompilerParams(vmem_limit_bytes=mebibytes * 1024 * 1024)


def mm(a, b):
    return lax.dot_general(a, b, (((1,), (0,)), ((), ())), preferred_element_type=F32)


def mm_nt(a, b):
    return lax.dot_general(a, b, (((1,), (1,)), ((), ())), preferred_element_type=F32)


def mm_tn(a, b):
    return lax.dot_general(a, b, (((0,), (0,)), ((), ())), preferred_element_type=F32)


def to_columns(rows):
    return jnp.concatenate([rows, jnp.zeros((128 - rows.shape[0], rows.shape[1]), F32)], axis=0).T


def in_hbm(x):
    return pltpu.with_memory_space_constraint(x, pltpu.HBM)


def three_terms(x):
    high = x.astype(BF16)
    rest = x - high.astype(F32)
    middle = rest.astype(BF16)
    return high, middle, (rest - middle.astype(F32)).astype(BF16)


def lane_cumsum(x):
    rows, width = x.shape
    ones = lax.broadcasted_iota(jnp.int32, (128, 128), 0) <= lax.broadcasted_iota(jnp.int32, (128, 128), 1)
    terms = jnp.concatenate(three_terms(x), axis=0)
    starts = range(0, width, 128)
    sums = mm(jnp.concatenate([terms[:, b : b + 128] for b in starts], axis=0), ones.astype(F32).astype(BF16))
    parts = []
    before = jnp.zeros((rows, 1), F32)
    for b in range(len(starts)):
        at = 3 * rows * b
        part = sums[at : at + rows] + sums[at + rows : at + 2 * rows] + sums[at + 2 * rows : at + 3 * rows]
        part = part + before
        before = part[:, 127:128]
        parts.append(part)
    return jnp.concatenate(parts, axis=1)


def first_kernel(
    n, ids_hbm, lens_hbm, adv_hbm, keys_hbm, values_hbm, pgates_hbm, gates_hbm, mask_hbm, q_hbm, c_hbm, k_hbm, v_hbm,
    *refs,
):
    msgs, (rows_ref, q, c, k_out, v_out) = refs[:n], refs[n : n + 5]
    keys, values, pgates, gates, mask, ids_ref, lens_ref, adv_ref, matrices, sems = refs[n + 5 :]
    pairs = [(pgates_hbm, pgates), (gates_hbm, gates), (mask_hbm, mask)]
    pairs += [(ids_hbm, ids_ref), (lens_hbm, lens_ref), (adv_hbm, adv_ref), (keys_hbm, keys), (q_hbm, q)]
    pairs += [(values_hbm, values)]
    count = gates.shape[0]
    slots = gates.shape[2]
    tokens = keys.shape[1]
    pairs += [(c_hbm.at[i], c.at[i]) for i in range(count)] + [(k_hbm, k_out), (v_hbm, v_out)]
    copies = [pltpu.make_async_copy(a, b, sems.at[i]) for i, (a, b) in enumerate(pairs)]
    for copy in copies:
        copy.start()
    part = DH // n
    block = H * part
    targets = partners(n)

    def spread(at):
        for k in range(n):
            of = pl.ds(pl.multiple_of(targets[k] * part, part), part)
            msgs[k][at * part + (16 if at >= H else 0) : (at + 1) * part + (16 if at >= H else 0), :] = matrices[
                at, of, :
            ].astype(BF16)

    for copy in copies[:8]:
        copy.wait()
    turned_keys = keys[0].T
    turned = [q[i].T for i in range(count)]
    piece = jnp.concatenate([pgates[0], jnp.zeros((H, slots - tokens), F32)], axis=1)
    gate_rows = [gates[i] for i in range(count)] + [piece, jnp.zeros((16 - H * (count + 1), slots), F32)]
    cum = lane_cumsum(jnp.concatenate(gate_rows, axis=0))
    carried = jnp.exp(cum)
    place = lax.broadcasted_iota(jnp.int32, (1, slots), 1)
    rows = []
    factors = []
    for i in range(count):
        weight = adv_ref[i].astype(F32) / 1024.0
        opened = jnp.where(place < lens_ref[0, i], 1.0, 0.0)
        live = mask[i : i + 1, :].astype(F32) * opened * weight
        rows += [cum[H * i : H * i + H], carried[H * i : H * i + H] * opened, live, opened, jnp.zeros((2, slots), F32)]
        factors.append(carried[H * i : H * i + H] * live)
    piece = cum[H * count : H * count + H]
    total = piece[:, -1:]
    suffix = total - piece
    rows += [suffix, jnp.zeros((8 - H, slots), F32)]
    rows_ref[...] = jnp.concatenate(rows, axis=0)

    copies[8].wait()
    later = jnp.exp(suffix[:, :tokens])
    for h in range(H):
        lanes = slice(h * DH, (h + 1) * DH)
        scaled = turned_keys[lanes].astype(F32) * later[h : h + 1]
        high = scaled.astype(BF16)
        low = (scaled - high.astype(F32)).astype(BF16)
        both = mm(jnp.concatenate([high, low], axis=0), values[0, :, lanes])
        matrices[h] = both[:DH] + both[DH:]
        spread(h)
    notes = [jnp.broadcast_to(x[h : h + 1].astype(F32), (1, DH)) for x in three_terms(total) for h in range(H)]
    notes += [jnp.full((1, DH), ids_ref[i].astype(F32)) for i in range(count)]
    notes.append(jnp.zeros((16 - len(notes), DH), F32))
    notes = jnp.concatenate(notes, axis=0).astype(BF16)
    for k in range(n):
        msgs[k][block : block + 16, :] = notes

    for i in range(count):
        copies[9 + i].wait()
        for h in range(H):
            lanes = slice(h * DH, (h + 1) * DH)
            scaled = (turned[i][lanes].astype(F32) * factors[i][h : h + 1]).astype(BF16)
            matrices[H * (1 + i) + h] = mm(scaled, c[i, :, lanes])
            spread(H * (1 + i) + h)
    for copy in copies[9 + count :]:
        copy.wait()


def noted_prompt(notes, i):
    return jnp.max(notes[3 * H + i : 3 * H + i + 1]).astype(jnp.int32)


def second_kernel(n, chips, cores, *refs):
    z_at = lax.axis_index("z")
    got, msgs, later_ref, sums = far_first(refs[:n]), refs[n + 1 : n + 1 + chips], refs[-2], refs[-1]
    part = DH // n
    block = H * part
    responses = (got[0].shape[0] - block - 16) // block
    place = partners(n)
    notes = [got[k][block : block + 16, :].astype(F32) for k in range(n)]
    logs = [x[0:H] + x[H : 2 * H] + x[2 * H : 3 * H] for x in notes]
    final = jnp.zeros((block, DH), F32)
    for k in range(n):
        later = jnp.zeros_like(logs[0])
        for other in range(n):
            if other != k:
                later = later + jnp.where(place[other] > place[k], logs[other], 0.0)
        if k == 0:
            later_ref[...] = jnp.concatenate([later, jnp.zeros((8 - H, DH), F32)], axis=0)
        decay = jnp.exp(later)
        decay = [jnp.broadcast_to(decay[h : h + 1], (part, DH)) for h in range(H)]
        final = final + jnp.concatenate(decay, axis=0) * got[k][0:block, :].astype(F32)
    sums[...] = jnp.zeros_like(sums)
    for k in range(n):
        for i in range(responses):
            at = block * (1 + i) + 16
            sums[noted_prompt(notes[k], i)] += got[k][at : at + block, :].astype(F32)
    final = final.astype(BF16)
    for k in range(chips):
        z = lax.rem(z_at + k, chips)
        msgs[k][0:block, :] = final
        for c in range(cores):
            msgs[k][(1 + c) * block : (2 + c) * block, :] = sums[z * cores + c].astype(BF16)


def swap_kernel(chips, *refs):
    got, sent_ref, kept_ref = refs[:chips], refs[chips + 1], refs[chips + 2]
    block = got[0].shape[0] // 3
    totals = []
    for c in range(2):
        total = got[0][(1 + c) * block : (2 + c) * block, :].astype(F32)
        for k in range(1, chips):
            total = total + got[k][(1 + c) * block : (2 + c) * block, :].astype(F32)
        totals.append(total)
    for k in range(chips):
        final = got[k][0:block, :]
        sent_ref[k * block : (k + 1) * block, :] = final
        kept_ref[k * block : (k + 1) * block, :] = final
    low = lax.axis_index("core") == 0
    sent_ref[chips * block :, :] = jnp.where(low, totals[1], totals[0]).astype(BF16)
    kept_ref[chips * block :, :] = jnp.where(low, totals[0], totals[1]).astype(BF16)


def third_kernel(n, chips, *refs):
    z_at, core = lax.axis_index("z"), lax.axis_index("core")
    noted, kept_ref, got_ref, msgs = far_first(refs[:n]), refs[n], refs[n + 1], refs[n + 3 :]
    block = H * DH // n
    responses = (noted[0].shape[0] - block - 16) // block
    total = kept_ref[chips * block :, :].astype(F32) + got_ref[chips * block :, :].astype(F32)
    total = total.astype(BF16)
    for k in range(n):
        notes = noted[k][block : block + 16, :].astype(F32)
        for i in range(responses):
            p = noted_prompt(notes, i)
            slot = lax.rem(z_at + chips - lax.div(p, 2), chips)
            at = pl.ds(pl.multiple_of(slot * block, block), block)
            same = lax.rem(p, 2) == core
            state = jnp.where(same, kept_ref[at, :].astype(F32), got_ref[at, :].astype(F32))
            msgs[k][i * block : (i + 1) * block, :] = state.astype(BF16)
        msgs[k][responses * block :, :] = total


def sweep_kernel(units, done, rows_ref, q_ref, k_ref, v_ref, c_ref, cols_ref, *refs):
    writes = len(done) > 0
    if writes:
        *refs, dk_hbm, dv_hbm, sems = refs
    out_ref, dq_ref, query_ref, grad_ref, dk_ref, dv_ref, token_ref = refs[-7:]
    if cols_ref is None:
        cols_ref = refs[0]
        cols_ref[...] = to_columns(rows_ref[...])
    copies = []

    def send(r):
        for a, b in ((dk_ref, dk_hbm), (dv_ref, dv_hbm)):
            copies.append(pltpu.make_async_copy(a.at[r], b.at[r], sems.at[len(copies)]))
            copies[-1].start()

    for r in done:
        send(r)
    token_ref[...] = jnp.zeros_like(token_ref)
    quarter = HALF // 2
    causal = lax.broadcasted_iota(jnp.int32, (quarter, quarter), 0) >= lax.broadcasted_iota(
        jnp.int32, (quarter, quarter), 1
    )
    blank = jnp.zeros((quarter, quarter), BF16)
    blocks = q_ref.shape[1] // HALF

    def decayed(products, cum, row, diagonal):
        if not diagonal:
            decay = jnp.exp2(cum - row)
            return [(x * decay).astype(BF16) for x in products]
        first = jnp.exp2(jnp.where(causal, cum[:quarter] - row[:, :quarter], NEVER))
        left = jnp.exp2(cum[quarter:] - row[:, :quarter])
        right = jnp.exp2(jnp.where(causal, cum[quarter:] - row[:, quarter:], NEVER))
        results = []
        for x in products:
            upper = jnp.concatenate([(x[:quarter, :quarter] * first).astype(BF16), blank], axis=1)
            lower = [(x[quarter:, :quarter] * left).astype(BF16), (x[quarter:, quarter:] * right).astype(BF16)]
            results.append(jnp.concatenate([upper, jnp.concatenate(lower, axis=1)], axis=0))
        return results

    for r, h in units:
        lanes = slice(h * DH, (h + 1) * DH)
        cum = cols_ref[:, 8 * r + h : 8 * r + h + 1] * LOG2E
        row = rows_ref[8 * r + h : 8 * r + h + 1, :] * LOG2E
        live = cols_ref[:, 8 * r + 4 : 8 * r + 5]
        opened = cols_ref[:, 8 * r + 5 : 8 * r + 6]
        grad_all = (c_ref[r, :, lanes].astype(F32) * live).astype(BF16)
        carried = cols_ref[:, 8 * r + 2 + h : 8 * r + 3 + h]
        query_ref[r, :, lanes] = (q_ref[r, :, lanes].astype(F32) * carried).astype(BF16)
        grad_ref[r, :, lanes] = (grad_all.astype(F32) * carried).astype(BF16)
        query_turned = q_ref[r, :, lanes].T
        grad_turned = grad_all.T
        dk = [None] * blocks
        dv = [None] * blocks
        for t in range(blocks):
            at = slice(t * HALF, (t + 1) * HALF)
            query = q_ref[r, at, lanes]
            grad_out = grad_all[at]
            out = None
            dq = None
            for s in range(t + 1):
                of = slice(s * HALF, (s + 1) * HALF)
                key = k_ref[r, of, lanes]
                value = v_ref[r, of, lanes]
                mixing, scores = decayed(
                    [mm_nt(query, key), mm_nt(grad_out, value)], cum[at], row[:, of], s == t
                )
                o_new = mm(mixing, value)
                q_new = mm(scores, key)
                k_new = mm(query_turned[:, at], scores)
                v_new = mm(grad_turned[:, at], mixing)
                out = o_new if out is None else out + o_new
                dq = q_new if dq is None else dq + q_new
                dk[s] = k_new if dk[s] is None else dk[s] + k_new
                dv[s] = v_new if dv[s] is None else dv[s] + v_new
            out_ref[r, at, lanes] = out * opened[at]
            dq_ref[r, at, lanes] = dq
        for s in range(blocks):
            of = slice(s * HALF, (s + 1) * HALF)
            dk_ref[r, of, lanes] = dk[s].astype(BF16).T
            dv_ref[r, of, lanes] = dv[s].astype(BF16).T
        if writes and h == H - 1:
            send(r)
    for copy in copies:
        copy.wait()


def last_kernel(
    n, count, cols_ref, q_ref, grad_ref, po_ref, pdq_ref, keys_ref, values_ref, later_ref, *refs
):
    got, refs = refs[:n], refs[n + 1 :]
    out_hbm, dq_hbm, dk_hbm, dv_hbm, start, out_buf, dq_buf, dk_buf, dv_buf, sems = refs
    part = DH // n
    block = H * part
    place = partners(n)
    slots = q_ref.shape[1]
    tokens = keys_ref.shape[1]
    copies = []

    def send(a, b):
        copies.append(pltpu.make_async_copy(a, b, sems.at[len(copies)]))
        copies[-1].start()

    start[...] = jnp.zeros_like(start)
    for r in range(count + 1):
        for k in range(n):
            for h in range(H):
                of = pl.ds(pl.multiple_of(h * DH + place[k] * part, part), part)
                rows = got[k][r * block + h * part : r * block + (h + 1) * part, :]
                start[r, of, h * DH : (h + 1) * DH] = rows
    factor = [
        jnp.exp(cols_ref[:tokens, 8 * count + h : 8 * count + h + 1] + later_ref[h : h + 1, 0:1]) for h in range(H)
    ]
    for buf, x in ((dk_buf, mm_nt(values_ref[0], start[count])), (dv_buf, mm(keys_ref[0], start[count]))):
        for h in range(H):
            lanes = slice(h * DH, (h + 1) * DH)
            buf[:, lanes] = (factor[h] * x[:, lanes]).astype(BF16)
    send(dk_buf, dk_hbm.at[0])
    send(dv_buf, dv_hbm.at[0])
    for r in range(count):
        for t in range(0, slots, HALF):
            at = slice(t, t + HALF)
            out_buf[r, at, :] = (po_ref[r, at, :] + mm(q_ref[r, at, :], start[r])).astype(BF16)
            dq_buf[r, at, :] = (pdq_ref[r, at, :] + mm_nt(grad_ref[r, at, :], start[r])).astype(BF16)
            send(out_buf.at[r, at], out_hbm.at[r, at])
            send(dq_buf.at[r, at], dq_hbm.at[r, at])
    for copy in copies:
        copy.wait()


def exchange(xs, axis):
    n = lax.axis_size(axis)
    return [xs[0]] + [lax.ppermute(xs[k], axis, [(s, s ^ k) for s in range(n)]) for k in range(1, n)]


def exchange_ring(xs, axis):
    n = lax.axis_size(axis)
    return [xs[0]] + [lax.ppermute(xs[k], axis, [(s, (s + k) % n) for s in range(n)]) for k in range(1, n)]


def far_first(refs):
    return [refs[0], *refs[:0:-1]]


def partners(n):
    me = lax.axis_index("prompt")
    return [lax.bitwise_xor(me, k) for k in range(n)]


def shards(
    keys,
    values,
    prompt_gates,
    queries,
    resp_keys,
    resp_values,
    resp_gates,
    cotangent,
    group_ids,
    resp_lengths,
    loss_mask,
    advantages,
):
    n = lax.axis_size("prompt")
    chips = lax.axis_size("z")
    cores = lax.axis_size("core")
    responses, slots, width = queries.shape
    block = H * DH // n
    shape = jax.ShapeDtypeStruct

    outs = pl.pallas_call(
        lambda *refs: first_kernel(n, *refs),
        out_shape=[shape((block * (1 + responses) + 16, DH), BF16)] * n
        + [shape((8 * (responses + 1), slots), F32)]
        + [shape(queries.shape, BF16)] * 4,
        in_specs=[ANY] * 12,
        out_specs=[VMEM] * (n + 5),
        scratch_shapes=[
            pltpu.VMEM(keys.shape, BF16),
            pltpu.VMEM(values.shape, BF16),
            pltpu.VMEM(prompt_gates.shape, F32),
            pltpu.VMEM(resp_gates.shape, F32),
            pltpu.VMEM(loss_mask.shape, jnp.int32),
            pltpu.SMEM(group_ids.shape, jnp.int32),
            pltpu.SMEM(resp_lengths.shape, jnp.int32),
            pltpu.SMEM(advantages.shape, jnp.int32),
            pltpu.VMEM((H * (1 + responses), DH, DH), F32),
            pltpu.SemaphoreType.DMA((11 + responses,)),
        ],
        compiler_params=params(32),
        name="first",
    )(
        *[in_hbm(x) for x in (group_ids, resp_lengths, advantages, keys, values, prompt_gates, resp_gates)],
        *[in_hbm(x) for x in (loss_mask, queries, cotangent, resp_keys, resp_values)],
    )
    msgs, (rows, queries, cotangent, resp_keys, resp_values) = outs[:n], outs[n:]

    like = shape(queries.shape, F32)
    like_out = shape(queries.shape, BF16)

    held_shapes = [like, like] + [like_out] * 4 + [shape((8, 128), F32)]

    def first_sweep(units):
        outs = pl.pallas_call(
            lambda *refs: sweep_kernel(units, (), *refs[:5], None, *refs[5:]),
            out_shape=[shape((slots, 128), F32)] + held_shapes,
            in_specs=[VMEM] * 5,
            out_specs=[VMEM] * 8,
            compiler_params=params(),
            name="sweep",
        )(rows, queries, resp_keys, resp_values, cotangent)
        return outs[0], outs[1:7], outs[7]

    def sweep(units, before, token, done=()):
        writes = len(done) > 0
        outs = pl.pallas_call(
            lambda *refs: sweep_kernel(units, done, *refs),
            out_shape=held_shapes + [like_out] * (2 * writes),
            in_specs=[VMEM] * 6 + [ANY] * 7,
            out_specs=[VMEM] * 7 + [ANY] * (2 * writes),
            scratch_shapes=[pltpu.SemaphoreType.DMA((2 * responses,))] * writes,
            input_output_aliases={7 + k: k for k in range(6)},
            compiler_params=params(),
            name="sweep",
        )(rows, queries, resp_keys, resp_values, cotangent, cols, token, *before)
        return (outs[:4] + outs[7:] if writes else outs[:6]), outs[6]

    units = [(r, h) for r in range(responses) for h in range(H)]
    got1 = far_first(exchange(msgs, "prompt"))
    cols, held, token = first_sweep(units[:3])
    outs = pl.pallas_call(
        lambda *refs: second_kernel(n, chips, cores, *refs),
        out_shape=[shape(((1 + cores) * block, DH), BF16)] * chips + [shape((8, DH), F32)],
        in_specs=[VMEM] * n + [ANY],
        out_specs=[VMEM] * (chips + 1),
        scratch_shapes=[pltpu.VMEM((chips * cores, block, DH), F32)],
        compiler_params=params(),
        name="second",
    )(*got1, token)
    msgs, later = outs[:chips], outs[chips]
    got2 = exchange_ring(msgs, "z")
    held, token = sweep(units[3:5], held, later)
    sent, kept = pl.pallas_call(
        lambda *refs: swap_kernel(chips, *refs),
        out_shape=[shape(((chips + 1) * block, DH), BF16)] * 2,
        in_specs=[VMEM] * chips + [ANY],
        out_specs=[VMEM, VMEM],
        compiler_params=params(),
        name="swap",
    )(*got2, token)
    swapped = exchange([kept, sent], "core")[1]
    held, token = sweep(units[5:6], held, kept)
    msgs = pl.pallas_call(
        lambda *refs: third_kernel(n, chips, *refs),
        out_shape=[shape(((responses + 1) * block, DH), BF16)] * n,
        in_specs=[VMEM] * (n + 2) + [ANY],
        out_specs=[VMEM] * n,
        compiler_params=params(),
        name="third",
    )(*got1, kept, swapped, token)
    got3 = exchange(msgs, "prompt")
    held, token = sweep(units[6:], held, msgs[0], range(responses - 1))
    partial_out, partial_dq, query, grad_out, resp_dk, resp_dv = held

    resp_out, resp_dq, prompt_dk, prompt_dv = pl.pallas_call(
        lambda *refs: last_kernel(n, responses, *refs),
        out_shape=[like_out] * 2 + [shape(keys.shape, BF16)] * 2,
        in_specs=[VMEM] * (8 + n) + [ANY],
        out_specs=[ANY] * 4,
        scratch_shapes=[
            pltpu.VMEM((responses + 1, width, width), BF16),
            pltpu.VMEM(queries.shape, BF16),
            pltpu.VMEM(queries.shape, BF16),
            pltpu.VMEM(keys.shape[1:], BF16),
            pltpu.VMEM(keys.shape[1:], BF16),
            pltpu.SemaphoreType.DMA((2 + 2 * responses * (slots // HALF),)),
        ],
        compiler_params=params(),
        name="last",
    )(cols, query, grad_out, partial_out, partial_dq, keys, values, later, *got3, token)
    return (resp_out, resp_dq, resp_dk, resp_dv, prompt_dk, prompt_dv)


def solution(mesh):
    n, count = mesh.shape["prompt"], mesh.shape["resp"]
    mesh = jax.sharding.Mesh(mesh.devices.reshape(n, count // 2, 2), ("prompt", "z", "core"))
    spread = P(("prompt", "z", "core"))
    three = P(("prompt", "z", "core"), None, None)
    two = P(("prompt", "z", "core"), None)
    prompt = P(("z", "core"), "prompt", None)
    return jax.shard_map(
        shards,
        mesh=mesh,
        in_specs=(
            prompt,
            prompt,
            P(("z", "core"), None, "prompt"),
            three,
            three,
            three,
            three,
            three,
            spread,
            two,
            two,
            spread,
        ),
        out_specs=(three, three, three, three, prompt, prompt),
        check_vma=False,
    )
```

```python
import jax
import jax.numpy as jnp
from jax import lax
from jax.experimental import pallas as pl
from jax.experimental.pallas import tpu as pltpu
from jax.sharding import PartitionSpec as P

H = 2
DH = 128
HALF = 256
LOG2E = 1.4426950408889634
F32 = jnp.float32
BF16 = jnp.bfloat16
NEVER = -1e30
VMEM = pl.BlockSpec(memory_space=pltpu.VMEM)
ANY = pl.BlockSpec(memory_space=pl.ANY)
SMEM = pl.BlockSpec(memory_space=pltpu.SMEM)


def params(mebibytes=16):
    return pltpu.CompilerParams(vmem_limit_bytes=mebibytes * 1024 * 1024)


def mm(a, b):
    return lax.dot_general(a, b, (((1,), (0,)), ((), ())), preferred_element_type=F32)


def mm_nt(a, b):
    return lax.dot_general(a, b, (((1,), (1,)), ((), ())), preferred_element_type=F32)


def mm_tn(a, b):
    return lax.dot_general(a, b, (((0,), (0,)), ((), ())), preferred_element_type=F32)


def to_columns(rows):
    return jnp.concatenate([rows, jnp.zeros((128 - rows.shape[0], rows.shape[1]), F32)], axis=0).T


def in_hbm(x):
    return pltpu.with_memory_space_constraint(x, pltpu.HBM)


def turn(x):
    size = x.shape[1]
    same = lax.broadcasted_iota(jnp.int32, (size, size), 0) == lax.broadcasted_iota(jnp.int32, (size, size), 1)
    return mm_nt(same.astype(F32).astype(BF16), x)


def three_terms(x):
    high = x.astype(BF16)
    rest = x - high.astype(F32)
    middle = rest.astype(BF16)
    return high, middle, (rest - middle.astype(F32)).astype(BF16)


def lane_cumsum(x):
    rows, width = x.shape
    ones = lax.broadcasted_iota(jnp.int32, (128, 128), 0) <= lax.broadcasted_iota(jnp.int32, (128, 128), 1)
    terms = jnp.concatenate(three_terms(x), axis=0)
    starts = range(0, width, 128)
    sums = mm(jnp.concatenate([terms[:, b : b + 128] for b in starts], axis=0), ones.astype(F32).astype(BF16))
    parts = []
    before = jnp.zeros((rows, 1), F32)
    for b in range(len(starts)):
        at = 3 * rows * b
        part = sums[at : at + rows] + sums[at + rows : at + 2 * rows] + sums[at + 2 * rows : at + 3 * rows]
        part = part + before
        before = part[:, 127:128]
        parts.append(part)
    return jnp.concatenate(parts, axis=1)


def first_kernel(
    n, ids_hbm, lens_hbm, adv_hbm, keys_hbm, values_hbm, pgates_hbm, gates_hbm, mask_hbm, q_hbm, c_hbm, k_hbm, v_hbm,
    *refs,
):
    msgs, (rows_ref, q, c, k_out, v_out) = refs[:n], refs[n : n + 5]
    keys, values, pgates, gates, mask, ids_ref, lens_ref, adv_ref, matrices, sems = refs[n + 5 :]
    pairs = [(pgates_hbm, pgates), (gates_hbm, gates), (mask_hbm, mask)]
    pairs += [(ids_hbm, ids_ref), (lens_hbm, lens_ref), (adv_hbm, adv_ref), (keys_hbm, keys), (values_hbm, values)]
    count = gates.shape[0]
    slots = gates.shape[2]
    tokens = keys.shape[1]
    for i in range(count):
        pairs += [(q_hbm.at[i], q.at[i]), (c_hbm.at[i], c.at[i])]
    pairs += [(k_hbm, k_out), (v_hbm, v_out)]
    copies = [pltpu.make_async_copy(a, b, sems.at[i]) for i, (a, b) in enumerate(pairs)]
    for copy in copies:
        copy.start()
    part = DH // n
    block = H * part
    targets = partners(n)

    def spread(at):
        for k in range(n):
            of = pl.ds(pl.multiple_of(targets[k] * part, part), part)
            msgs[k][at * part + (16 if at >= H else 0) : (at + 1) * part + (16 if at >= H else 0), :] = matrices[
                at, of, :
            ].astype(BF16)

    for copy in copies[:6]:
        copy.wait()
    piece = jnp.concatenate([pgates[0], jnp.zeros((H, slots - tokens), F32)], axis=1)
    gate_rows = [gates[i] for i in range(count)] + [piece, jnp.zeros((16 - H * (count + 1), slots), F32)]
    cum = lane_cumsum(jnp.concatenate(gate_rows, axis=0))
    carried = jnp.exp(cum)
    place = lax.broadcasted_iota(jnp.int32, (1, slots), 1)
    rows = []
    factors = []
    for i in range(count):
        weight = adv_ref[i].astype(F32) / 1024.0
        opened = jnp.where(place < lens_ref[0, i], 1.0, 0.0)
        live = mask[i : i + 1, :].astype(F32) * opened * weight
        rows += [cum[H * i : H * i + H], carried[H * i : H * i + H] * opened, live, opened, jnp.zeros((2, slots), F32)]
        factors.append(carried[H * i : H * i + H] * live)
    piece = cum[H * count : H * count + H]
    total = piece[:, -1:]
    suffix = total - piece
    rows += [suffix, jnp.zeros((8 - H, slots), F32)]
    rows_ref[...] = jnp.concatenate(rows, axis=0)

    for copy in copies[6:8]:
        copy.wait()
    turned = turn(keys[0])
    later = jnp.exp(suffix[:, :tokens])
    for h in range(H):
        lanes = slice(h * DH, (h + 1) * DH)
        scaled = turned[lanes] * later[h : h + 1]
        high = scaled.astype(BF16)
        low = (scaled - high.astype(F32)).astype(BF16)
        both = mm(jnp.concatenate([high, low], axis=0), values[0, :, lanes])
        matrices[h] = both[:DH] + both[DH:]
        spread(h)
    notes = [jnp.broadcast_to(x[h : h + 1].astype(F32), (1, DH)) for x in three_terms(total) for h in range(H)]
    notes += [jnp.full((1, DH), ids_ref[i].astype(F32)) for i in range(count)]
    notes.append(jnp.zeros((16 - len(notes), DH), F32))
    notes = jnp.concatenate(notes, axis=0).astype(BF16)
    for k in range(n):
        msgs[k][block : block + 16, :] = notes

    for i in range(count):
        copies[8 + 2 * i].wait()
        turned = turn(q[i])
        copies[9 + 2 * i].wait()
        for h in range(H):
            lanes = slice(h * DH, (h + 1) * DH)
            scaled = (turned[lanes] * factors[i][h : h + 1]).astype(BF16)
            matrices[H * (1 + i) + h] = mm(scaled, c[i, :, lanes])
            spread(H * (1 + i) + h)
    for copy in copies[8 + 2 * count :]:
        copy.wait()


def noted_prompt(notes, i):
    return jnp.max(notes[3 * H + i : 3 * H + i + 1]).astype(jnp.int32)


def second_kernel(n, chips, cores, *refs):
    z_at = lax.axis_index("z")
    got, msgs, later_ref, sums = far_first(refs[:n]), refs[n + 1 : n + 1 + chips], refs[-2], refs[-1]
    part = DH // n
    block = H * part
    responses = (got[0].shape[0] - block - 16) // block
    place = partners(n)
    notes = [got[k][block : block + 16, :].astype(F32) for k in range(n)]
    logs = [x[0:H] + x[H : 2 * H] + x[2 * H : 3 * H] for x in notes]
    final = jnp.zeros((block, DH), F32)
    for k in range(n):
        later = jnp.zeros_like(logs[0])
        for other in range(n):
            if other != k:
                later = later + jnp.where(place[other] > place[k], logs[other], 0.0)
        if k == 0:
            later_ref[...] = jnp.concatenate([later, jnp.zeros((8 - H, DH), F32)], axis=0)
        decay = jnp.exp(later)
        decay = [jnp.broadcast_to(decay[h : h + 1], (part, DH)) for h in range(H)]
        final = final + jnp.concatenate(decay, axis=0) * got[k][0:block, :].astype(F32)
    sums[...] = jnp.zeros_like(sums)
    for k in range(n):
        for i in range(responses):
            at = block * (1 + i) + 16
            sums[noted_prompt(notes[k], i)] += got[k][at : at + block, :].astype(F32)
    final = final.astype(BF16)
    for k in range(chips):
        z = lax.rem(z_at + k, chips)
        msgs[k][0:block, :] = final
        for c in range(cores):
            msgs[k][(1 + c) * block : (2 + c) * block, :] = sums[z * cores + c].astype(BF16)


def swap_kernel(chips, *refs):
    got, sent_ref, kept_ref = refs[:chips], refs[chips + 1], refs[chips + 2]
    block = got[0].shape[0] // 3
    totals = []
    for c in range(2):
        total = got[0][(1 + c) * block : (2 + c) * block, :].astype(F32)
        for k in range(1, chips):
            total = total + got[k][(1 + c) * block : (2 + c) * block, :].astype(F32)
        totals.append(total)
    for k in range(chips):
        final = got[k][0:block, :]
        sent_ref[k * block : (k + 1) * block, :] = final
        kept_ref[k * block : (k + 1) * block, :] = final
    low = lax.axis_index("core") == 0
    sent_ref[chips * block :, :] = jnp.where(low, totals[1], totals[0]).astype(BF16)
    kept_ref[chips * block :, :] = jnp.where(low, totals[0], totals[1]).astype(BF16)


def third_kernel(n, chips, *refs):
    z_at, core = lax.axis_index("z"), lax.axis_index("core")
    noted, kept_ref, got_ref, msgs = far_first(refs[:n]), refs[n], refs[n + 1], refs[n + 3 :]
    block = H * DH // n
    responses = (noted[0].shape[0] - block - 16) // block
    total = kept_ref[chips * block :, :].astype(F32) + got_ref[chips * block :, :].astype(F32)
    total = total.astype(BF16)
    for k in range(n):
        notes = noted[k][block : block + 16, :].astype(F32)
        for i in range(responses):
            p = noted_prompt(notes, i)
            slot = lax.rem(z_at + chips - lax.div(p, 2), chips)
            at = pl.ds(pl.multiple_of(slot * block, block), block)
            same = lax.rem(p, 2) == core
            state = jnp.where(same, kept_ref[at, :].astype(F32), got_ref[at, :].astype(F32))
            msgs[k][i * block : (i + 1) * block, :] = state.astype(BF16)
        msgs[k][responses * block :, :] = total


def sweep_kernel(units, done, rows_ref, q_ref, k_ref, v_ref, c_ref, cols_ref, *refs):
    writes = len(done) > 0
    if writes:
        *refs, dk_hbm, dv_hbm, sems = refs
    out_ref, dq_ref, query_ref, grad_ref, dk_ref, dv_ref, token_ref = refs[-7:]
    if cols_ref is None:
        cols_ref = refs[0]
        cols_ref[...] = to_columns(rows_ref[...])
    copies = []

    def send(r):
        for a, b in ((dk_ref, dk_hbm), (dv_ref, dv_hbm)):
            copies.append(pltpu.make_async_copy(a.at[r], b.at[r], sems.at[len(copies)]))
            copies[-1].start()

    for r in done:
        send(r)
    token_ref[...] = jnp.zeros_like(token_ref)
    quarter = HALF // 2
    causal = lax.broadcasted_iota(jnp.int32, (quarter, quarter), 0) >= lax.broadcasted_iota(
        jnp.int32, (quarter, quarter), 1
    )
    blank = jnp.zeros((quarter, quarter), BF16)
    blocks = q_ref.shape[1] // HALF

    def decayed(products, cum, row, diagonal):
        if not diagonal:
            decay = jnp.exp2(cum - row)
            return [(x * decay).astype(BF16) for x in products]
        first = jnp.exp2(jnp.where(causal, cum[:quarter] - row[:, :quarter], NEVER))
        left = jnp.exp2(cum[quarter:] - row[:, :quarter])
        right = jnp.exp2(jnp.where(causal, cum[quarter:] - row[:, quarter:], NEVER))
        results = []
        for x in products:
            upper = jnp.concatenate([(x[:quarter, :quarter] * first).astype(BF16), blank], axis=1)
            lower = [(x[quarter:, :quarter] * left).astype(BF16), (x[quarter:, quarter:] * right).astype(BF16)]
            results.append(jnp.concatenate([upper, jnp.concatenate(lower, axis=1)], axis=0))
        return results

    for r, h in units:
        lanes = slice(h * DH, (h + 1) * DH)
        cum = cols_ref[:, 8 * r + h : 8 * r + h + 1] * LOG2E
        row = rows_ref[8 * r + h : 8 * r + h + 1, :] * LOG2E
        live = cols_ref[:, 8 * r + 4 : 8 * r + 5]
        opened = cols_ref[:, 8 * r + 5 : 8 * r + 6]
        grad_all = (c_ref[r, :, lanes].astype(F32) * live).astype(BF16)
        carried = cols_ref[:, 8 * r + 2 + h : 8 * r + 3 + h]
        query_ref[r, :, lanes] = (q_ref[r, :, lanes].astype(F32) * carried).astype(BF16)
        grad_ref[r, :, lanes] = (grad_all.astype(F32) * carried).astype(BF16)
        query_turned = q_ref[r, :, lanes].T
        grad_turned = grad_all.T
        dk = [None] * blocks
        dv = [None] * blocks
        for t in range(blocks):
            at = slice(t * HALF, (t + 1) * HALF)
            query = q_ref[r, at, lanes]
            grad_out = grad_all[at]
            out = None
            dq = None
            for s in range(t + 1):
                of = slice(s * HALF, (s + 1) * HALF)
                key = k_ref[r, of, lanes]
                value = v_ref[r, of, lanes]
                mixing, scores = decayed(
                    [mm_nt(query, key), mm_nt(grad_out, value)], cum[at], row[:, of], s == t
                )
                o_new = mm(mixing, value)
                q_new = mm(scores, key)
                k_new = mm(query_turned[:, at], scores)
                v_new = mm(grad_turned[:, at], mixing)
                out = o_new if out is None else out + o_new
                dq = q_new if dq is None else dq + q_new
                dk[s] = k_new if dk[s] is None else dk[s] + k_new
                dv[s] = v_new if dv[s] is None else dv[s] + v_new
            out_ref[r, at, lanes] = out * opened[at]
            dq_ref[r, at, lanes] = dq
        for s in range(blocks):
            of = slice(s * HALF, (s + 1) * HALF)
            dk_ref[r, of, lanes] = dk[s].astype(BF16).T
            dv_ref[r, of, lanes] = dv[s].astype(BF16).T
        if writes and h == H - 1:
            send(r)
    for copy in copies:
        copy.wait()


def last_kernel(
    n, count, cols_ref, q_ref, grad_ref, po_ref, pdq_ref, keys_ref, values_ref, later_ref, *refs
):
    got, refs = refs[:n], refs[n + 1 :]
    out_hbm, dq_hbm, dk_hbm, dv_hbm, start, out_buf, dq_buf, dk_buf, dv_buf, sems = refs
    part = DH // n
    block = H * part
    place = partners(n)
    slots = q_ref.shape[1]
    tokens = keys_ref.shape[1]
    copies = []

    def send(a, b):
        copies.append(pltpu.make_async_copy(a, b, sems.at[len(copies)]))
        copies[-1].start()

    start[...] = jnp.zeros_like(start)
    for r in range(count + 1):
        for k in range(n):
            for h in range(H):
                of = pl.ds(pl.multiple_of(h * DH + place[k] * part, part), part)
                rows = got[k][r * block + h * part : r * block + (h + 1) * part, :]
                start[r, of, h * DH : (h + 1) * DH] = rows
    factor = [
        jnp.exp(cols_ref[:tokens, 8 * count + h : 8 * count + h + 1] + later_ref[h : h + 1, 0:1]) for h in range(H)
    ]
    for buf, x in ((dk_buf, mm_nt(values_ref[0], start[count])), (dv_buf, mm(keys_ref[0], start[count]))):
        for h in range(H):
            lanes = slice(h * DH, (h + 1) * DH)
            buf[:, lanes] = (factor[h] * x[:, lanes]).astype(BF16)
    send(dk_buf, dk_hbm.at[0])
    send(dv_buf, dv_hbm.at[0])
    for r in range(count):
        for t in range(0, slots, HALF):
            at = slice(t, t + HALF)
            out_buf[r, at, :] = (po_ref[r, at, :] + mm(q_ref[r, at, :], start[r])).astype(BF16)
            dq_buf[r, at, :] = (pdq_ref[r, at, :] + mm_nt(grad_ref[r, at, :], start[r])).astype(BF16)
            send(out_buf.at[r, at], out_hbm.at[r, at])
            send(dq_buf.at[r, at], dq_hbm.at[r, at])
    for copy in copies:
        copy.wait()


def exchange(xs, axis):
    n = lax.axis_size(axis)
    return [xs[0]] + [lax.ppermute(xs[k], axis, [(s, s ^ k) for s in range(n)]) for k in range(1, n)]


def exchange_ring(xs, axis):
    n = lax.axis_size(axis)
    return [xs[0]] + [lax.ppermute(xs[k], axis, [(s, (s + k) % n) for s in range(n)]) for k in range(1, n)]


def far_first(refs):
    return [refs[0], *refs[:0:-1]]


def partners(n):
    me = lax.axis_index("prompt")
    return [lax.bitwise_xor(me, k) for k in range(n)]


def shards(
    keys,
    values,
    prompt_gates,
    queries,
    resp_keys,
    resp_values,
    resp_gates,
    cotangent,
    group_ids,
    resp_lengths,
    loss_mask,
    advantages,
):
    n = lax.axis_size("prompt")
    chips = lax.axis_size("z")
    cores = lax.axis_size("core")
    responses, slots, width = queries.shape
    block = H * DH // n
    shape = jax.ShapeDtypeStruct

    outs = pl.pallas_call(
        lambda *refs: first_kernel(n, *refs),
        out_shape=[shape((block * (1 + responses) + 16, DH), BF16)] * n
        + [shape((8 * (responses + 1), slots), F32)]
        + [shape(queries.shape, BF16)] * 4,
        in_specs=[ANY] * 12,
        out_specs=[VMEM] * (n + 5),
        scratch_shapes=[
            pltpu.VMEM(keys.shape, BF16),
            pltpu.VMEM(values.shape, BF16),
            pltpu.VMEM(prompt_gates.shape, F32),
            pltpu.VMEM(resp_gates.shape, F32),
            pltpu.VMEM(loss_mask.shape, jnp.int32),
            pltpu.SMEM(group_ids.shape, jnp.int32),
            pltpu.SMEM(resp_lengths.shape, jnp.int32),
            pltpu.SMEM(advantages.shape, jnp.int32),
            pltpu.VMEM((H * (1 + responses), DH, DH), F32),
            pltpu.SemaphoreType.DMA((10 + 2 * responses,)),
        ],
        compiler_params=params(32),
        name="first",
    )(
        *[in_hbm(x) for x in (group_ids, resp_lengths, advantages, keys, values, prompt_gates, resp_gates)],
        *[in_hbm(x) for x in (loss_mask, queries, cotangent, resp_keys, resp_values)],
    )
    msgs, (rows, queries, cotangent, resp_keys, resp_values) = outs[:n], outs[n:]

    like = shape(queries.shape, F32)
    like_out = shape(queries.shape, BF16)

    held_shapes = [like, like] + [like_out] * 4 + [shape((8, 128), F32)]

    def first_sweep(units):
        outs = pl.pallas_call(
            lambda *refs: sweep_kernel(units, (), *refs[:5], None, *refs[5:]),
            out_shape=[shape((slots, 128), F32)] + held_shapes,
            in_specs=[VMEM] * 5,
            out_specs=[VMEM] * 8,
            compiler_params=params(),
            name="sweep",
        )(rows, queries, resp_keys, resp_values, cotangent)
        return outs[0], outs[1:7], outs[7]

    def sweep(units, before, token, done=()):
        writes = len(done) > 0
        outs = pl.pallas_call(
            lambda *refs: sweep_kernel(units, done, *refs),
            out_shape=held_shapes + [like_out] * (2 * writes),
            in_specs=[VMEM] * 6 + [ANY] * 7,
            out_specs=[VMEM] * 7 + [ANY] * (2 * writes),
            scratch_shapes=[pltpu.SemaphoreType.DMA((2 * responses,))] * writes,
            input_output_aliases={7 + k: k for k in range(6)},
            compiler_params=params(),
            name="sweep",
        )(rows, queries, resp_keys, resp_values, cotangent, cols, token, *before)
        return (outs[:4] + outs[7:] if writes else outs[:6]), outs[6]

    units = [(r, h) for r in range(responses) for h in range(H)]
    got1 = far_first(exchange(msgs, "prompt"))
    cols, held, token = first_sweep(units[:3])
    outs = pl.pallas_call(
        lambda *refs: second_kernel(n, chips, cores, *refs),
        out_shape=[shape(((1 + cores) * block, DH), BF16)] * chips + [shape((8, DH), F32)],
        in_specs=[VMEM] * n + [ANY],
        out_specs=[VMEM] * (chips + 1),
        scratch_shapes=[pltpu.VMEM((chips * cores, block, DH), F32)],
        compiler_params=params(),
        name="second",
    )(*got1, token)
    msgs, later = outs[:chips], outs[chips]
    got2 = exchange_ring(msgs, "z")
    held, token = sweep(units[3:5], held, later)
    sent, kept = pl.pallas_call(
        lambda *refs: swap_kernel(chips, *refs),
        out_shape=[shape(((chips + 1) * block, DH), BF16)] * 2,
        in_specs=[VMEM] * chips + [ANY],
        out_specs=[VMEM, VMEM],
        compiler_params=params(),
        name="swap",
    )(*got2, token)
    swapped = exchange([kept, sent], "core")[1]
    held, token = sweep(units[5:6], held, kept)
    msgs = pl.pallas_call(
        lambda *refs: third_kernel(n, chips, *refs),
        out_shape=[shape(((responses + 1) * block, DH), BF16)] * n,
        in_specs=[VMEM] * (n + 2) + [ANY],
        out_specs=[VMEM] * n,
        compiler_params=params(),
        name="third",
    )(*got1, kept, swapped, token)
    got3 = exchange(msgs, "prompt")
    held, token = sweep(units[6:], held, msgs[0], range(responses - 1))
    partial_out, partial_dq, query, grad_out, resp_dk, resp_dv = held

    resp_out, resp_dq, prompt_dk, prompt_dv = pl.pallas_call(
        lambda *refs: last_kernel(n, responses, *refs),
        out_shape=[like_out] * 2 + [shape(keys.shape, BF16)] * 2,
        in_specs=[VMEM] * (8 + n) + [ANY],
        out_specs=[ANY] * 4,
        scratch_shapes=[
            pltpu.VMEM((responses + 1, width, width), BF16),
            pltpu.VMEM(queries.shape, BF16),
            pltpu.VMEM(queries.shape, BF16),
            pltpu.VMEM(keys.shape[1:], BF16),
            pltpu.VMEM(keys.shape[1:], BF16),
            pltpu.SemaphoreType.DMA((2 + 2 * responses * (slots // HALF),)),
        ],
        compiler_params=params(),
        name="last",
    )(cols, query, grad_out, partial_out, partial_dq, keys, values, later, *got3, token)
    return (resp_out, resp_dq, resp_dk, resp_dv, prompt_dk, prompt_dv)


def solution(mesh):
    n, count = mesh.shape["prompt"], mesh.shape["resp"]
    mesh = jax.sharding.Mesh(mesh.devices.reshape(n, count // 2, 2), ("prompt", "z", "core"))
    spread = P(("prompt", "z", "core"))
    three = P(("prompt", "z", "core"), None, None)
    two = P(("prompt", "z", "core"), None)
    prompt = P(("z", "core"), "prompt", None)
    return jax.shard_map(
        shards,
        mesh=mesh,
        in_specs=(
            prompt,
            prompt,
            P(("z", "core"), None, "prompt"),
            three,
            three,
            three,
            three,
            three,
            spread,
            two,
            two,
            spread,
        ),
        out_specs=(three, three, three, three, prompt, prompt),
        check_vma=False,
    )
```

```python
import jax
import jax.numpy as jnp
from jax import lax
from jax.experimental import pallas as pl
from jax.experimental.pallas import tpu as pltpu
from jax.sharding import PartitionSpec as P

H = 2
DH = 128
HALF = 256
LOG2E = 1.4426950408889634
F32 = jnp.float32
BF16 = jnp.bfloat16
NEVER = -1e30
VMEM = pl.BlockSpec(memory_space=pltpu.VMEM)
ANY = pl.BlockSpec(memory_space=pl.ANY)
SMEM = pl.BlockSpec(memory_space=pltpu.SMEM)


def params(mebibytes=16):
    return pltpu.CompilerParams(vmem_limit_bytes=mebibytes * 1024 * 1024)


def mm(a, b):
    return lax.dot_general(a, b, (((1,), (0,)), ((), ())), preferred_element_type=F32)


def mm_nt(a, b):
    return lax.dot_general(a, b, (((1,), (1,)), ((), ())), preferred_element_type=F32)


def mm_tn(a, b):
    return lax.dot_general(a, b, (((0,), (0,)), ((), ())), preferred_element_type=F32)


def to_columns(rows):
    return jnp.concatenate([rows, jnp.zeros((128 - rows.shape[0], rows.shape[1]), F32)], axis=0).T


def in_hbm(x):
    return pltpu.with_memory_space_constraint(x, pltpu.HBM)


def three_terms(x):
    high = x.astype(BF16)
    rest = x - high.astype(F32)
    middle = rest.astype(BF16)
    return high, middle, (rest - middle.astype(F32)).astype(BF16)


def lane_cumsum(x):
    rows, width = x.shape
    ones = lax.broadcasted_iota(jnp.int32, (128, 128), 0) <= lax.broadcasted_iota(jnp.int32, (128, 128), 1)
    terms = jnp.concatenate(three_terms(x), axis=0)
    starts = range(0, width, 128)
    sums = mm(jnp.concatenate([terms[:, b : b + 128] for b in starts], axis=0), ones.astype(F32).astype(BF16))
    parts = []
    before = jnp.zeros((rows, 1), F32)
    for b in range(len(starts)):
        at = 3 * rows * b
        part = sums[at : at + rows] + sums[at + rows : at + 2 * rows] + sums[at + 2 * rows : at + 3 * rows]
        part = part + before
        before = part[:, 127:128]
        parts.append(part)
    return jnp.concatenate(parts, axis=1)


def first_kernel(
    n, ids_hbm, lens_hbm, adv_hbm, keys_hbm, values_hbm, pgates_hbm, gates_hbm, mask_hbm, q_hbm, c_hbm, k_hbm, v_hbm,
    *refs,
):
    msgs, (rows_ref, q, c, k_out, v_out) = refs[:n], refs[n : n + 5]
    keys, values, pgates, gates, mask, ids_ref, lens_ref, adv_ref, matrices, sems = refs[n + 5 :]
    pairs = [(pgates_hbm, pgates), (gates_hbm, gates), (mask_hbm, mask)]
    pairs += [(ids_hbm, ids_ref), (lens_hbm, lens_ref), (adv_hbm, adv_ref), (keys_hbm, keys), (values_hbm, values)]
    pairs += [(q_hbm, q), (c_hbm, c), (k_hbm, k_out), (v_hbm, v_out)]
    copies = [pltpu.make_async_copy(a, b, sems.at[i]) for i, (a, b) in enumerate(pairs)]
    for copy in copies[:10]:
        copy.start()
    count = gates.shape[0]
    slots = gates.shape[2]
    tokens = keys.shape[1]
    part = DH // n
    block = H * part
    targets = partners(n)

    def spread(at):
        for k in range(n):
            of = pl.ds(pl.multiple_of(targets[k] * part, part), part)
            msgs[k][at * part + (16 if at >= H else 0) : (at + 1) * part + (16 if at >= H else 0), :] = matrices[
                at, of, :
            ].astype(BF16)

    for copy in copies[:6]:
        copy.wait()
    for copy in copies[10:]:
        copy.start()
    piece = jnp.concatenate([pgates[0], jnp.zeros((H, slots - tokens), F32)], axis=1)
    gate_rows = [gates[i] for i in range(count)] + [piece, jnp.zeros((16 - H * (count + 1), slots), F32)]
    cum = lane_cumsum(jnp.concatenate(gate_rows, axis=0))
    carried = jnp.exp(cum)
    place = lax.broadcasted_iota(jnp.int32, (1, slots), 1)
    rows = []
    factors = []
    for i in range(count):
        weight = adv_ref[i].astype(F32) / 1024.0
        opened = jnp.where(place < lens_ref[0, i], 1.0, 0.0)
        live = mask[i : i + 1, :].astype(F32) * opened * weight
        rows += [cum[H * i : H * i + H], carried[H * i : H * i + H] * opened, live, opened, jnp.zeros((2, slots), F32)]
        factors.append(carried[H * i : H * i + H] * live)
    piece = cum[H * count : H * count + H]
    total = piece[:, -1:]
    suffix = total - piece
    rows += [suffix, jnp.zeros((8 - H, slots), F32)]
    rows_ref[...] = jnp.concatenate(rows, axis=0)

    copies[6].wait()
    copies[7].wait()
    turned = keys[0].T
    later = jnp.exp(suffix[:, :tokens])
    for h in range(H):
        lanes = slice(h * DH, (h + 1) * DH)
        scaled = turned[lanes].astype(F32) * later[h : h + 1]
        high = scaled.astype(BF16)
        low = (scaled - high.astype(F32)).astype(BF16)
        both = mm(jnp.concatenate([high, low], axis=0), values[0, :, lanes])
        matrices[h] = both[:DH] + both[DH:]
        spread(h)
    notes = [jnp.broadcast_to(x[h : h + 1].astype(F32), (1, DH)) for x in three_terms(total) for h in range(H)]
    notes += [jnp.full((1, DH), ids_ref[i].astype(F32)) for i in range(count)]
    notes.append(jnp.zeros((16 - len(notes), DH), F32))
    notes = jnp.concatenate(notes, axis=0).astype(BF16)
    for k in range(n):
        msgs[k][block : block + 16, :] = notes

    copies[8].wait()
    copies[9].wait()
    for i in range(count):
        turned = q[i].T
        for h in range(H):
            lanes = slice(h * DH, (h + 1) * DH)
            scaled = (turned[lanes].astype(F32) * factors[i][h : h + 1]).astype(BF16)
            matrices[H * (1 + i) + h] = mm(scaled, c[i, :, lanes])
            spread(H * (1 + i) + h)
    for copy in copies[10:]:
        copy.wait()


def noted_prompt(notes, i):
    return jnp.max(notes[3 * H + i : 3 * H + i + 1]).astype(jnp.int32)


def second_kernel(n, chips, cores, *refs):
    z_at = lax.axis_index("z")
    got, msgs, later_ref, sums = far_first(refs[:n]), refs[n + 1 : n + 1 + chips], refs[-2], refs[-1]
    part = DH // n
    block = H * part
    responses = (got[0].shape[0] - block - 16) // block
    place = partners(n)
    notes = [got[k][block : block + 16, :].astype(F32) for k in range(n)]
    logs = [x[0:H] + x[H : 2 * H] + x[2 * H : 3 * H] for x in notes]
    final = jnp.zeros((block, DH), F32)
    for k in range(n):
        later = jnp.zeros_like(logs[0])
        for other in range(n):
            if other != k:
                later = later + jnp.where(place[other] > place[k], logs[other], 0.0)
        if k == 0:
            later_ref[...] = jnp.concatenate([later, jnp.zeros((8 - H, DH), F32)], axis=0)
        decay = jnp.exp(later)
        decay = [jnp.broadcast_to(decay[h : h + 1], (part, DH)) for h in range(H)]
        final = final + jnp.concatenate(decay, axis=0) * got[k][0:block, :].astype(F32)
    sums[...] = jnp.zeros_like(sums)
    for k in range(n):
        for i in range(responses):
            at = block * (1 + i) + 16
            sums[noted_prompt(notes[k], i)] += got[k][at : at + block, :].astype(F32)
    final = final.astype(BF16)
    for k in range(chips):
        z = lax.rem(z_at + k, chips)
        msgs[k][0:block, :] = final
        for c in range(cores):
            msgs[k][(1 + c) * block : (2 + c) * block, :] = sums[z * cores + c].astype(BF16)


def swap_kernel(chips, *refs):
    got, sent_ref, kept_ref = refs[:chips], refs[chips + 1], refs[chips + 2]
    block = got[0].shape[0] // 3
    totals = []
    for c in range(2):
        total = got[0][(1 + c) * block : (2 + c) * block, :].astype(F32)
        for k in range(1, chips):
            total = total + got[k][(1 + c) * block : (2 + c) * block, :].astype(F32)
        totals.append(total)
    for k in range(chips):
        final = got[k][0:block, :]
        sent_ref[k * block : (k + 1) * block, :] = final
        kept_ref[k * block : (k + 1) * block, :] = final
    low = lax.axis_index("core") == 0
    sent_ref[chips * block :, :] = jnp.where(low, totals[1], totals[0]).astype(BF16)
    kept_ref[chips * block :, :] = jnp.where(low, totals[0], totals[1]).astype(BF16)


def third_kernel(n, chips, *refs):
    z_at, core = lax.axis_index("z"), lax.axis_index("core")
    noted, kept_ref, got_ref, msgs = far_first(refs[:n]), refs[n], refs[n + 1], refs[n + 3 :]
    block = H * DH // n
    responses = (noted[0].shape[0] - block - 16) // block
    total = kept_ref[chips * block :, :].astype(F32) + got_ref[chips * block :, :].astype(F32)
    total = total.astype(BF16)
    for k in range(n):
        notes = noted[k][block : block + 16, :].astype(F32)
        for i in range(responses):
            p = noted_prompt(notes, i)
            slot = lax.rem(z_at + chips - lax.div(p, 2), chips)
            at = pl.ds(pl.multiple_of(slot * block, block), block)
            same = lax.rem(p, 2) == core
            state = jnp.where(same, kept_ref[at, :].astype(F32), got_ref[at, :].astype(F32))
            msgs[k][i * block : (i + 1) * block, :] = state.astype(BF16)
        msgs[k][responses * block :, :] = total


def sweep_kernel(units, done, rows_ref, q_ref, k_ref, v_ref, c_ref, cols_ref, *refs):
    writes = len(done) > 0
    if writes:
        *refs, dk_hbm, dv_hbm, sems = refs
    out_ref, dq_ref, query_ref, grad_ref, dk_ref, dv_ref, token_ref = refs[-7:]
    if cols_ref is None:
        cols_ref = refs[0]
        cols_ref[...] = to_columns(rows_ref[...])
    copies = []

    def send(r):
        for a, b in ((dk_ref, dk_hbm), (dv_ref, dv_hbm)):
            copies.append(pltpu.make_async_copy(a.at[r], b.at[r], sems.at[len(copies)]))
            copies[-1].start()

    for r in done:
        send(r)
    token_ref[...] = jnp.zeros_like(token_ref)
    quarter = HALF // 2
    causal = lax.broadcasted_iota(jnp.int32, (quarter, quarter), 0) >= lax.broadcasted_iota(
        jnp.int32, (quarter, quarter), 1
    )
    blank = jnp.zeros((quarter, quarter), BF16)
    blocks = q_ref.shape[1] // HALF

    def decayed(products, cum, row, diagonal):
        if not diagonal:
            decay = jnp.exp2(cum - row)
            return [(x * decay).astype(BF16) for x in products]
        first = jnp.exp2(jnp.where(causal, cum[:quarter] - row[:, :quarter], NEVER))
        left = jnp.exp2(cum[quarter:] - row[:, :quarter])
        right = jnp.exp2(jnp.where(causal, cum[quarter:] - row[:, quarter:], NEVER))
        results = []
        for x in products:
            upper = jnp.concatenate([(x[:quarter, :quarter] * first).astype(BF16), blank], axis=1)
            lower = [(x[quarter:, :quarter] * left).astype(BF16), (x[quarter:, quarter:] * right).astype(BF16)]
            results.append(jnp.concatenate([upper, jnp.concatenate(lower, axis=1)], axis=0))
        return results

    for r, h in units:
        lanes = slice(h * DH, (h + 1) * DH)
        cum = cols_ref[:, 8 * r + h : 8 * r + h + 1] * LOG2E
        row = rows_ref[8 * r + h : 8 * r + h + 1, :] * LOG2E
        live = cols_ref[:, 8 * r + 4 : 8 * r + 5]
        opened = cols_ref[:, 8 * r + 5 : 8 * r + 6]
        grad_all = (c_ref[r, :, lanes].astype(F32) * live).astype(BF16)
        carried = cols_ref[:, 8 * r + 2 + h : 8 * r + 3 + h]
        query_ref[r, :, lanes] = (q_ref[r, :, lanes].astype(F32) * carried).astype(BF16)
        grad_ref[r, :, lanes] = (grad_all.astype(F32) * carried).astype(BF16)
        query_turned = q_ref[r, :, lanes].T
        grad_turned = grad_all.T
        dk = [None] * blocks
        dv = [None] * blocks
        for t in range(blocks):
            at = slice(t * HALF, (t + 1) * HALF)
            query = q_ref[r, at, lanes]
            grad_out = grad_all[at]
            out = None
            dq = None
            for s in range(t + 1):
                of = slice(s * HALF, (s + 1) * HALF)
                key = k_ref[r, of, lanes]
                value = v_ref[r, of, lanes]
                mixing, scores = decayed(
                    [mm_nt(query, key), mm_nt(grad_out, value)], cum[at], row[:, of], s == t
                )
                o_new = mm(mixing, value)
                q_new = mm(scores, key)
                k_new = mm(query_turned[:, at], scores)
                v_new = mm(grad_turned[:, at], mixing)
                out = o_new if out is None else out + o_new
                dq = q_new if dq is None else dq + q_new
                dk[s] = k_new if dk[s] is None else dk[s] + k_new
                dv[s] = v_new if dv[s] is None else dv[s] + v_new
            out_ref[r, at, lanes] = out * opened[at]
            dq_ref[r, at, lanes] = dq
        for s in range(blocks):
            of = slice(s * HALF, (s + 1) * HALF)
            dk_ref[r, of, lanes] = dk[s].astype(BF16).T
            dv_ref[r, of, lanes] = dv[s].astype(BF16).T
        if writes and h == H - 1:
            send(r)
    for copy in copies:
        copy.wait()


def last_kernel(
    n, count, cols_ref, q_ref, grad_ref, po_ref, pdq_ref, keys_ref, values_ref, later_ref, *refs
):
    got, refs = refs[:n], refs[n + 1 :]
    out_hbm, dq_hbm, dk_hbm, dv_hbm, start, out_buf, dq_buf, dk_buf, dv_buf, sems = refs
    part = DH // n
    block = H * part
    place = partners(n)
    slots = q_ref.shape[1]
    tokens = keys_ref.shape[1]
    copies = []

    def send(a, b):
        copies.append(pltpu.make_async_copy(a, b, sems.at[len(copies)]))
        copies[-1].start()

    start[...] = jnp.zeros_like(start)
    for r in range(count + 1):
        for k in range(n):
            for h in range(H):
                of = pl.ds(pl.multiple_of(h * DH + place[k] * part, part), part)
                rows = got[k][r * block + h * part : r * block + (h + 1) * part, :]
                start[r, of, h * DH : (h + 1) * DH] = rows
    factor = [
        jnp.exp(cols_ref[:tokens, 8 * count + h : 8 * count + h + 1] + later_ref[h : h + 1, 0:1]) for h in range(H)
    ]
    for buf, x in ((dk_buf, mm_nt(values_ref[0], start[count])), (dv_buf, mm(keys_ref[0], start[count]))):
        for h in range(H):
            lanes = slice(h * DH, (h + 1) * DH)
            buf[:, lanes] = (factor[h] * x[:, lanes]).astype(BF16)
    send(dk_buf, dk_hbm.at[0])
    send(dv_buf, dv_hbm.at[0])
    for r in range(count):
        for t in range(0, slots, HALF):
            at = slice(t, t + HALF)
            out_buf[r, at, :] = (po_ref[r, at, :] + mm(q_ref[r, at, :], start[r])).astype(BF16)
            dq_buf[r, at, :] = (pdq_ref[r, at, :] + mm_nt(grad_ref[r, at, :], start[r])).astype(BF16)
        send(out_buf.at[r], out_hbm.at[r])
        send(dq_buf.at[r], dq_hbm.at[r])
    for copy in copies:
        copy.wait()


def exchange(xs, axis):
    n = lax.axis_size(axis)
    return [xs[0]] + [lax.ppermute(xs[k], axis, [(s, s ^ k) for s in range(n)]) for k in range(1, n)]


def exchange_ring(xs, axis):
    n = lax.axis_size(axis)
    return [xs[0]] + [lax.ppermute(xs[k], axis, [(s, (s + k) % n) for s in range(n)]) for k in range(1, n)]


def far_first(refs):
    return [refs[0], *refs[:0:-1]]


def partners(n):
    me = lax.axis_index("prompt")
    return [lax.bitwise_xor(me, k) for k in range(n)]


def shards(
    keys,
    values,
    prompt_gates,
    queries,
    resp_keys,
    resp_values,
    resp_gates,
    cotangent,
    group_ids,
    resp_lengths,
    loss_mask,
    advantages,
):
    n = lax.axis_size("prompt")
    chips = lax.axis_size("z")
    cores = lax.axis_size("core")
    responses, slots, width = queries.shape
    block = H * DH // n
    shape = jax.ShapeDtypeStruct

    outs = pl.pallas_call(
        lambda *refs: first_kernel(n, *refs),
        out_shape=[shape((block * (1 + responses) + 16, DH), BF16)] * n
        + [shape((8 * (responses + 1), slots), F32)]
        + [shape(queries.shape, BF16)] * 4,
        in_specs=[ANY] * 12,
        out_specs=[VMEM] * (n + 5),
        scratch_shapes=[
            pltpu.VMEM(keys.shape, BF16),
            pltpu.VMEM(values.shape, BF16),
            pltpu.VMEM(prompt_gates.shape, F32),
            pltpu.VMEM(resp_gates.shape, F32),
            pltpu.VMEM(loss_mask.shape, jnp.int32),
            pltpu.SMEM(group_ids.shape, jnp.int32),
            pltpu.SMEM(resp_lengths.shape, jnp.int32),
            pltpu.SMEM(advantages.shape, jnp.int32),
            pltpu.VMEM((H * (1 + responses), DH, DH), F32),
            pltpu.SemaphoreType.DMA((12,)),
        ],
        compiler_params=params(32),
        name="first",
    )(
        *[in_hbm(x) for x in (group_ids, resp_lengths, advantages, keys, values, prompt_gates, resp_gates)],
        *[in_hbm(x) for x in (loss_mask, queries, cotangent, resp_keys, resp_values)],
    )
    msgs, (rows, queries, cotangent, resp_keys, resp_values) = outs[:n], outs[n:]

    like = shape(queries.shape, F32)
    like_out = shape(queries.shape, BF16)

    held_shapes = [like, like] + [like_out] * 4 + [shape((8, 128), F32)]

    def first_sweep(units):
        outs = pl.pallas_call(
            lambda *refs: sweep_kernel(units, (), *refs[:5], None, *refs[5:]),
            out_shape=[shape((slots, 128), F32)] + held_shapes,
            in_specs=[VMEM] * 5,
            out_specs=[VMEM] * 8,
            compiler_params=params(),
            name="sweep",
        )(rows, queries, resp_keys, resp_values, cotangent)
        return outs[0], outs[1:7], outs[7]

    def sweep(units, before, token, done=()):
        writes = len(done) > 0
        outs = pl.pallas_call(
            lambda *refs: sweep_kernel(units, done, *refs),
            out_shape=held_shapes + [like_out] * (2 * writes),
            in_specs=[VMEM] * 6 + [ANY] * 7,
            out_specs=[VMEM] * 7 + [ANY] * (2 * writes),
            scratch_shapes=[pltpu.SemaphoreType.DMA((2 * responses,))] * writes,
            input_output_aliases={7 + k: k for k in range(6)},
            compiler_params=params(),
            name="sweep",
        )(rows, queries, resp_keys, resp_values, cotangent, cols, token, *before)
        return (outs[:4] + outs[7:] if writes else outs[:6]), outs[6]

    units = [(r, h) for r in range(responses) for h in range(H)]
    got1 = far_first(exchange(msgs, "prompt"))
    cols, held, token = first_sweep(units[:3])
    outs = pl.pallas_call(
        lambda *refs: second_kernel(n, chips, cores, *refs),
        out_shape=[shape(((1 + cores) * block, DH), BF16)] * chips + [shape((8, DH), F32)],
        in_specs=[VMEM] * n + [ANY],
        out_specs=[VMEM] * (chips + 1),
        scratch_shapes=[pltpu.VMEM((chips * cores, block, DH), F32)],
        compiler_params=params(),
        name="second",
    )(*got1, token)
    msgs, later = outs[:chips], outs[chips]
    got2 = exchange_ring(msgs, "z")
    held, token = sweep(units[3:5], held, later)
    sent, kept = pl.pallas_call(
        lambda *refs: swap_kernel(chips, *refs),
        out_shape=[shape(((chips + 1) * block, DH), BF16)] * 2,
        in_specs=[VMEM] * chips + [ANY],
        out_specs=[VMEM, VMEM],
        compiler_params=params(),
        name="swap",
    )(*got2, token)
    swapped = exchange([kept, sent], "core")[1]
    held, token = sweep(units[5:6], held, kept)
    msgs = pl.pallas_call(
        lambda *refs: third_kernel(n, chips, *refs),
        out_shape=[shape(((responses + 1) * block, DH), BF16)] * n,
        in_specs=[VMEM] * (n + 2) + [ANY],
        out_specs=[VMEM] * n,
        compiler_params=params(),
        name="third",
    )(*got1, kept, swapped, token)
    got3 = exchange(msgs, "prompt")
    held, token = sweep(units[6:], held, msgs[0], range(responses - 1))
    partial_out, partial_dq, query, grad_out, resp_dk, resp_dv = held

    resp_out, resp_dq, prompt_dk, prompt_dv = pl.pallas_call(
        lambda *refs: last_kernel(n, responses, *refs),
        out_shape=[like_out] * 2 + [shape(keys.shape, BF16)] * 2,
        in_specs=[VMEM] * (8 + n) + [ANY],
        out_specs=[ANY] * 4,
        scratch_shapes=[
            pltpu.VMEM((responses + 1, width, width), BF16),
            pltpu.VMEM(queries.shape, BF16),
            pltpu.VMEM(queries.shape, BF16),
            pltpu.VMEM(keys.shape[1:], BF16),
            pltpu.VMEM(keys.shape[1:], BF16),
            pltpu.SemaphoreType.DMA((2 + 2 * responses,)),
        ],
        compiler_params=params(),
        name="last",
    )(cols, query, grad_out, partial_out, partial_dq, keys, values, later, *got3, token)
    return (resp_out, resp_dq, resp_dk, resp_dv, prompt_dk, prompt_dv)


def solution(mesh):
    n, count = mesh.shape["prompt"], mesh.shape["resp"]
    mesh = jax.sharding.Mesh(mesh.devices.reshape(n, count // 2, 2), ("prompt", "z", "core"))
    spread = P(("prompt", "z", "core"))
    three = P(("prompt", "z", "core"), None, None)
    two = P(("prompt", "z", "core"), None)
    prompt = P(("z", "core"), "prompt", None)
    return jax.shard_map(
        shards,
        mesh=mesh,
        in_specs=(
            prompt,
            prompt,
            P(("z", "core"), None, "prompt"),
            three,
            three,
            three,
            three,
            three,
            spread,
            two,
            two,
            spread,
        ),
        out_specs=(three, three, three, three, prompt, prompt),
        check_vma=False,
    )
```

```python
import jax
import jax.numpy as jnp
from jax import lax
from jax.experimental import pallas as pl
from jax.experimental.pallas import tpu as pltpu
from jax.sharding import PartitionSpec as P

H = 2
DH = 128
HALF = 256
LOG2E = 1.4426950408889634
F32 = jnp.float32
BF16 = jnp.bfloat16
NEVER = -1e30
VMEM = pl.BlockSpec(memory_space=pltpu.VMEM)
ANY = pl.BlockSpec(memory_space=pl.ANY)
SMEM = pl.BlockSpec(memory_space=pltpu.SMEM)


def params(mebibytes=16):
    return pltpu.CompilerParams(vmem_limit_bytes=mebibytes * 1024 * 1024)


def mm(a, b):
    return lax.dot_general(a, b, (((1,), (0,)), ((), ())), preferred_element_type=F32)


def mm_nt(a, b):
    return lax.dot_general(a, b, (((1,), (1,)), ((), ())), preferred_element_type=F32)


def mm_tn(a, b):
    return lax.dot_general(a, b, (((0,), (0,)), ((), ())), preferred_element_type=F32)


def to_columns(rows):
    return jnp.concatenate([rows, jnp.zeros((128 - rows.shape[0], rows.shape[1]), F32)], axis=0).T


def in_hbm(x):
    return pltpu.with_memory_space_constraint(x, pltpu.HBM)


def three_terms(x):
    high = x.astype(BF16)
    rest = x - high.astype(F32)
    middle = rest.astype(BF16)
    return high, middle, (rest - middle.astype(F32)).astype(BF16)


def lane_cumsum(x):
    rows, width = x.shape
    ones = lax.broadcasted_iota(jnp.int32, (128, 128), 0) <= lax.broadcasted_iota(jnp.int32, (128, 128), 1)
    terms = jnp.concatenate(three_terms(x), axis=0)
    starts = range(0, width, 128)
    sums = mm(jnp.concatenate([terms[:, b : b + 128] for b in starts], axis=0), ones.astype(F32).astype(BF16))
    parts = []
    before = jnp.zeros((rows, 1), F32)
    for b in range(len(starts)):
        at = 3 * rows * b
        part = sums[at : at + rows] + sums[at + rows : at + 2 * rows] + sums[at + 2 * rows : at + 3 * rows]
        part = part + before
        before = part[:, 127:128]
        parts.append(part)
    return jnp.concatenate(parts, axis=1)


def first_kernel(
    n, ids_hbm, lens_hbm, adv_hbm, keys_hbm, values_hbm, pgates_hbm, gates_hbm, mask_hbm, q_hbm, c_hbm, k_hbm, v_hbm,
    *refs,
):
    msgs, (rows_ref, q, c, k_out, v_out) = refs[:n], refs[n : n + 5]
    keys, values, pgates, gates, mask, ids_ref, lens_ref, adv_ref, matrices, sems = refs[n + 5 :]
    pairs = [(pgates_hbm, pgates), (gates_hbm, gates), (mask_hbm, mask)]
    pairs += [(ids_hbm, ids_ref), (lens_hbm, lens_ref), (adv_hbm, adv_ref), (keys_hbm, keys), (values_hbm, values)]
    pairs += [(q_hbm, q), (c_hbm, c), (k_hbm, k_out), (v_hbm, v_out)]
    copies = [pltpu.make_async_copy(a, b, sems.at[i]) for i, (a, b) in enumerate(pairs)]
    for copy in copies[:10]:
        copy.start()
    count = gates.shape[0]
    slots = gates.shape[2]
    tokens = keys.shape[1]
    part = DH // n
    block = H * part
    targets = partners(n)

    def spread(at):
        for k in range(n):
            of = pl.ds(pl.multiple_of(targets[k] * part, part), part)
            msgs[k][at * part + (16 if at >= H else 0) : (at + 1) * part + (16 if at >= H else 0), :] = matrices[
                at, of, :
            ].astype(BF16)

    for copy in copies[:6]:
        copy.wait()
    for copy in copies[10:]:
        copy.start()
    piece = jnp.concatenate([pgates[0], jnp.zeros((H, slots - tokens), F32)], axis=1)
    gate_rows = [gates[i] for i in range(count)] + [piece, jnp.zeros((16 - H * (count + 1), slots), F32)]
    cum = lane_cumsum(jnp.concatenate(gate_rows, axis=0))
    carried = jnp.exp(cum)
    place = lax.broadcasted_iota(jnp.int32, (1, slots), 1)
    rows = []
    factors = []
    for i in range(count):
        weight = adv_ref[i].astype(F32) / 1024.0
        opened = jnp.where(place < lens_ref[0, i], 1.0, 0.0)
        live = mask[i : i + 1, :].astype(F32) * opened * weight
        rows += [cum[H * i : H * i + H], carried[H * i : H * i + H] * opened, live, opened, jnp.zeros((2, slots), F32)]
        factors.append(carried[H * i : H * i + H] * live)
    piece = cum[H * count : H * count + H]
    total = piece[:, -1:]
    suffix = total - piece
    rows += [suffix, jnp.zeros((8 - H, slots), F32)]
    rows_ref[...] = jnp.concatenate(rows, axis=0)

    copies[6].wait()
    copies[7].wait()
    turned = keys[0].T
    later = jnp.exp(suffix[:, :tokens])
    scaled = [turned[h * DH : (h + 1) * DH].astype(F32) * later[h : h + 1] for h in range(H)]
    high = [x.astype(BF16) for x in scaled]
    low = [(x - y.astype(F32)).astype(BF16) for x, y in zip(scaled, high)]
    both = mm(jnp.concatenate(high + low, axis=0), values[0])
    for h in range(H):
        lanes = slice(h * DH, (h + 1) * DH)
        matrices[h] = both[h * DH : (h + 1) * DH, lanes] + both[(H + h) * DH : (H + h + 1) * DH, lanes]
        spread(h)
    notes = [jnp.broadcast_to(x[h : h + 1].astype(F32), (1, DH)) for x in three_terms(total) for h in range(H)]
    notes += [jnp.full((1, DH), ids_ref[i].astype(F32)) for i in range(count)]
    notes.append(jnp.zeros((16 - len(notes), DH), F32))
    notes = jnp.concatenate(notes, axis=0).astype(BF16)
    for k in range(n):
        msgs[k][block : block + 16, :] = notes

    copies[8].wait()
    copies[9].wait()
    for i in range(count):
        turned = q[i].T
        scaled = [turned[h * DH : (h + 1) * DH].astype(F32) * factors[i][h : h + 1] for h in range(H)]
        grads = mm(jnp.concatenate(scaled, axis=0).astype(BF16), c[i])
        for h in range(H):
            lanes = slice(h * DH, (h + 1) * DH)
            matrices[H * (1 + i) + h] = grads[lanes, lanes]
            spread(H * (1 + i) + h)
    for copy in copies[10:]:
        copy.wait()


def noted_prompt(notes, i):
    return jnp.max(notes[3 * H + i : 3 * H + i + 1]).astype(jnp.int32)


def second_kernel(n, chips, cores, *refs):
    z_at = lax.axis_index("z")
    got, msgs, later_ref, sums = by_partner(refs[:n]), refs[n + 1 : n + 1 + chips], refs[-2], refs[-1]
    part = DH // n
    block = H * part
    responses = (got[0].shape[0] - block - 16) // block
    place = partners(n)
    notes = [got[k][block : block + 16, :].astype(F32) for k in range(n)]
    logs = [x[0:H] + x[H : 2 * H] + x[2 * H : 3 * H] for x in notes]
    final = jnp.zeros((block, DH), F32)
    for k in range(n):
        later = jnp.zeros_like(logs[0])
        for other in range(n):
            if other != k:
                later = later + jnp.where(place[other] > place[k], logs[other], 0.0)
        if k == 0:
            later_ref[...] = jnp.concatenate([later, jnp.zeros((8 - H, DH), F32)], axis=0)
        decay = jnp.exp(later)
        decay = [jnp.broadcast_to(decay[h : h + 1], (part, DH)) for h in range(H)]
        final = final + jnp.concatenate(decay, axis=0) * got[k][0:block, :].astype(F32)
    sums[...] = jnp.zeros_like(sums)
    for k in range(n):
        for i in range(responses):
            at = block * (1 + i) + 16
            sums[noted_prompt(notes[k], i)] += got[k][at : at + block, :].astype(F32)
    final = final.astype(BF16)
    for k in range(chips):
        z = lax.rem(z_at + k, chips)
        msgs[k][0:block, :] = final
        for c in range(cores):
            msgs[k][(1 + c) * block : (2 + c) * block, :] = sums[z * cores + c].astype(BF16)


def swap_kernel(chips, *refs):
    got, sent_ref, kept_ref = refs[:chips], refs[chips + 1], refs[chips + 2]
    block = got[0].shape[0] // 3
    totals = []
    for c in range(2):
        total = got[0][(1 + c) * block : (2 + c) * block, :].astype(F32)
        for k in range(1, chips):
            total = total + got[k][(1 + c) * block : (2 + c) * block, :].astype(F32)
        totals.append(total)
    for k in range(chips):
        final = got[k][0:block, :]
        sent_ref[k * block : (k + 1) * block, :] = final
        kept_ref[k * block : (k + 1) * block, :] = final
    low = lax.axis_index("core") == 0
    sent_ref[chips * block :, :] = jnp.where(low, totals[1], totals[0]).astype(BF16)
    kept_ref[chips * block :, :] = jnp.where(low, totals[0], totals[1]).astype(BF16)


def third_kernel(n, chips, *refs):
    z_at, core = lax.axis_index("z"), lax.axis_index("core")
    noted, kept_ref, got_ref, msgs = by_partner(refs[:n]), refs[n], refs[n + 1], refs[n + 3 :]
    block = H * DH // n
    responses = (noted[0].shape[0] - block - 16) // block
    total = kept_ref[chips * block :, :].astype(F32) + got_ref[chips * block :, :].astype(F32)
    total = total.astype(BF16)
    for k in range(n):
        notes = noted[k][block : block + 16, :].astype(F32)
        for i in range(responses):
            p = noted_prompt(notes, i)
            slot = lax.rem(z_at + chips - lax.div(p, 2), chips)
            at = pl.ds(pl.multiple_of(slot * block, block), block)
            same = lax.rem(p, 2) == core
            state = jnp.where(same, kept_ref[at, :].astype(F32), got_ref[at, :].astype(F32))
            msgs[k][i * block : (i + 1) * block, :] = state.astype(BF16)
        msgs[k][responses * block :, :] = total


def sweep_kernel(units, done, rows_ref, q_ref, k_ref, v_ref, c_ref, cols_ref, *refs):
    writes = len(done) > 0
    if writes:
        *refs, dk_hbm, dv_hbm, sems = refs
    out_ref, dq_ref, query_ref, grad_ref, dk_ref, dv_ref, token_ref = refs[-7:]
    if cols_ref is None:
        cols_ref = refs[0]
        cols_ref[...] = to_columns(rows_ref[...])
    copies = []

    def send(r):
        for a, b in ((dk_ref, dk_hbm), (dv_ref, dv_hbm)):
            copies.append(pltpu.make_async_copy(a.at[r], b.at[r], sems.at[len(copies)]))
            copies[-1].start()

    for r in done:
        send(r)
    token_ref[...] = jnp.zeros_like(token_ref)
    quarter = HALF // 2
    causal = lax.broadcasted_iota(jnp.int32, (quarter, quarter), 0) >= lax.broadcasted_iota(
        jnp.int32, (quarter, quarter), 1
    )
    blank = jnp.zeros((quarter, quarter), BF16)
    blocks = q_ref.shape[1] // HALF

    def decayed(products, cum, row, diagonal):
        if not diagonal:
            decay = jnp.exp2(cum - row)
            return [(x * decay).astype(BF16) for x in products]
        first = jnp.exp2(jnp.where(causal, cum[:quarter] - row[:, :quarter], NEVER))
        left = jnp.exp2(cum[quarter:] - row[:, :quarter])
        right = jnp.exp2(jnp.where(causal, cum[quarter:] - row[:, quarter:], NEVER))
        results = []
        for x in products:
            upper = jnp.concatenate([(x[:quarter, :quarter] * first).astype(BF16), blank], axis=1)
            lower = [(x[quarter:, :quarter] * left).astype(BF16), (x[quarter:, quarter:] * right).astype(BF16)]
            results.append(jnp.concatenate([upper, jnp.concatenate(lower, axis=1)], axis=0))
        return results

    for r, h in units:
        lanes = slice(h * DH, (h + 1) * DH)
        cum = cols_ref[:, 8 * r + h : 8 * r + h + 1] * LOG2E
        row = rows_ref[8 * r + h : 8 * r + h + 1, :] * LOG2E
        live = cols_ref[:, 8 * r + 4 : 8 * r + 5]
        opened = cols_ref[:, 8 * r + 5 : 8 * r + 6]
        grad_all = (c_ref[r, :, lanes].astype(F32) * live).astype(BF16)
        carried = cols_ref[:, 8 * r + 2 + h : 8 * r + 3 + h]
        query_ref[r, :, lanes] = (q_ref[r, :, lanes].astype(F32) * carried).astype(BF16)
        grad_ref[r, :, lanes] = (grad_all.astype(F32) * carried).astype(BF16)
        query_turned = q_ref[r, :, lanes].T
        grad_turned = grad_all.T
        dk = [None] * blocks
        dv = [None] * blocks
        for t in range(blocks):
            at = slice(t * HALF, (t + 1) * HALF)
            query = q_ref[r, at, lanes]
            grad_out = grad_all[at]
            out = None
            dq = None
            for s in range(t + 1):
                of = slice(s * HALF, (s + 1) * HALF)
                key = k_ref[r, of, lanes]
                value = v_ref[r, of, lanes]
                mixing, scores = decayed(
                    [mm_nt(query, key), mm_nt(grad_out, value)], cum[at], row[:, of], s == t
                )
                o_new = mm(mixing, value)
                q_new = mm(scores, key)
                k_new = mm(query_turned[:, at], scores)
                v_new = mm(grad_turned[:, at], mixing)
                out = o_new if out is None else out + o_new
                dq = q_new if dq is None else dq + q_new
                dk[s] = k_new if dk[s] is None else dk[s] + k_new
                dv[s] = v_new if dv[s] is None else dv[s] + v_new
            out_ref[r, at, lanes] = out * opened[at]
            dq_ref[r, at, lanes] = dq
        for s in range(blocks):
            of = slice(s * HALF, (s + 1) * HALF)
            dk_ref[r, of, lanes] = dk[s].astype(BF16).T
            dv_ref[r, of, lanes] = dv[s].astype(BF16).T
        if writes and h == H - 1:
            send(r)
    for copy in copies:
        copy.wait()


def last_kernel(
    n, count, cols_ref, q_ref, grad_ref, po_ref, pdq_ref, keys_ref, values_ref, later_ref, *refs
):
    got, refs = by_partner(refs[:n]), refs[n + 1 :]
    out_hbm, dq_hbm, dk_hbm, dv_hbm, start, out_buf, dq_buf, dk_buf, dv_buf, sems = refs
    part = DH // n
    block = H * part
    place = partners(n)
    slots = q_ref.shape[1]
    tokens = keys_ref.shape[1]
    copies = []

    def send(a, b):
        copies.append(pltpu.make_async_copy(a, b, sems.at[len(copies)]))
        copies[-1].start()

    start[...] = jnp.zeros_like(start)
    for r in range(count + 1):
        for k in range(n):
            for h in range(H):
                of = pl.ds(pl.multiple_of(h * DH + place[k] * part, part), part)
                rows = got[k][r * block + h * part : r * block + (h + 1) * part, :]
                start[r, of, h * DH : (h + 1) * DH] = rows
    factor = [
        jnp.exp(cols_ref[:tokens, 8 * count + h : 8 * count + h + 1] + later_ref[h : h + 1, 0:1]) for h in range(H)
    ]
    for buf, x in ((dk_buf, mm_nt(values_ref[0], start[count])), (dv_buf, mm(keys_ref[0], start[count]))):
        for h in range(H):
            lanes = slice(h * DH, (h + 1) * DH)
            buf[:, lanes] = (factor[h] * x[:, lanes]).astype(BF16)
    send(dk_buf, dk_hbm.at[0])
    send(dv_buf, dv_hbm.at[0])
    for r in range(count):
        for t in range(0, slots, HALF):
            at = slice(t, t + HALF)
            out_buf[r, at, :] = (po_ref[r, at, :] + mm(q_ref[r, at, :], start[r])).astype(BF16)
            dq_buf[r, at, :] = (pdq_ref[r, at, :] + mm_nt(grad_ref[r, at, :], start[r])).astype(BF16)
        send(out_buf.at[r], out_hbm.at[r])
        send(dq_buf.at[r], dq_hbm.at[r])
    for copy in copies:
        copy.wait()


def exchange(xs, axis):
    n = lax.axis_size(axis)
    return [xs[0]] + [lax.ppermute(xs[k], axis, [(s, s ^ k) for s in range(n)]) for k in range(1, n)]


def exchange_ring(xs, axis):
    n = lax.axis_size(axis)
    return [xs[0]] + [lax.ppermute(xs[k], axis, [(s, (s + k) % n) for s in range(n)]) for k in range(1, n)]


def order(n):
    return [0, *sorted(range(1, n), key=lambda k: (k % 2, -k))]


def taken(xs):
    return [xs[k] for k in order(len(xs))]


def by_partner(refs):
    return [refs[order(len(refs)).index(k)] for k in range(len(refs))]


def partners(n):
    me = lax.axis_index("prompt")
    return [lax.bitwise_xor(me, k) for k in range(n)]


def shards(
    keys,
    values,
    prompt_gates,
    queries,
    resp_keys,
    resp_values,
    resp_gates,
    cotangent,
    group_ids,
    resp_lengths,
    loss_mask,
    advantages,
):
    n = lax.axis_size("prompt")
    chips = lax.axis_size("z")
    cores = lax.axis_size("core")
    responses, slots, width = queries.shape
    block = H * DH // n
    shape = jax.ShapeDtypeStruct

    outs = pl.pallas_call(
        lambda *refs: first_kernel(n, *refs),
        out_shape=[shape((block * (1 + responses) + 16, DH), BF16)] * n
        + [shape((8 * (responses + 1), slots), F32)]
        + [shape(queries.shape, BF16)] * 4,
        in_specs=[ANY] * 12,
        out_specs=[VMEM] * (n + 5),
        scratch_shapes=[
            pltpu.VMEM(keys.shape, BF16),
            pltpu.VMEM(values.shape, BF16),
            pltpu.VMEM(prompt_gates.shape, F32),
            pltpu.VMEM(resp_gates.shape, F32),
            pltpu.VMEM(loss_mask.shape, jnp.int32),
            pltpu.SMEM(group_ids.shape, jnp.int32),
            pltpu.SMEM(resp_lengths.shape, jnp.int32),
            pltpu.SMEM(advantages.shape, jnp.int32),
            pltpu.VMEM((H * (1 + responses), DH, DH), F32),
            pltpu.SemaphoreType.DMA((12,)),
        ],
        compiler_params=params(32),
        name="first",
    )(
        *[in_hbm(x) for x in (group_ids, resp_lengths, advantages, keys, values, prompt_gates, resp_gates)],
        *[in_hbm(x) for x in (loss_mask, queries, cotangent, resp_keys, resp_values)],
    )
    msgs, (rows, queries, cotangent, resp_keys, resp_values) = outs[:n], outs[n:]

    like = shape(queries.shape, F32)
    like_out = shape(queries.shape, BF16)

    held_shapes = [like, like] + [like_out] * 4 + [shape((8, 128), F32)]

    def first_sweep(units):
        outs = pl.pallas_call(
            lambda *refs: sweep_kernel(units, (), *refs[:5], None, *refs[5:]),
            out_shape=[shape((slots, 128), F32)] + held_shapes,
            in_specs=[VMEM] * 5,
            out_specs=[VMEM] * 8,
            compiler_params=params(),
            name="sweep",
        )(rows, queries, resp_keys, resp_values, cotangent)
        return outs[0], outs[1:7], outs[7]

    def sweep(units, before, token, done=()):
        writes = len(done) > 0
        outs = pl.pallas_call(
            lambda *refs: sweep_kernel(units, done, *refs),
            out_shape=held_shapes + [like_out] * (2 * writes),
            in_specs=[VMEM] * 6 + [ANY] * 7,
            out_specs=[VMEM] * 7 + [ANY] * (2 * writes),
            scratch_shapes=[pltpu.SemaphoreType.DMA((2 * responses,))] * writes,
            input_output_aliases={7 + k: k for k in range(6)},
            compiler_params=params(),
            name="sweep",
        )(rows, queries, resp_keys, resp_values, cotangent, cols, token, *before)
        return (outs[:4] + outs[7:] if writes else outs[:6]), outs[6]

    units = [(r, h) for r in range(responses) for h in range(H)]
    got1 = taken(exchange(msgs, "prompt"))
    cols, held, token = first_sweep(units[:3])
    outs = pl.pallas_call(
        lambda *refs: second_kernel(n, chips, cores, *refs),
        out_shape=[shape(((1 + cores) * block, DH), BF16)] * chips + [shape((8, DH), F32)],
        in_specs=[VMEM] * n + [ANY],
        out_specs=[VMEM] * (chips + 1),
        scratch_shapes=[pltpu.VMEM((chips * cores, block, DH), F32)],
        compiler_params=params(),
        name="second",
    )(*got1, token)
    msgs, later = outs[:chips], outs[chips]
    got2 = exchange_ring(msgs, "z")
    held, token = sweep(units[3:5], held, later)
    sent, kept = pl.pallas_call(
        lambda *refs: swap_kernel(chips, *refs),
        out_shape=[shape(((chips + 1) * block, DH), BF16)] * 2,
        in_specs=[VMEM] * chips + [ANY],
        out_specs=[VMEM, VMEM],
        compiler_params=params(),
        name="swap",
    )(*got2, token)
    swapped = exchange([kept, sent], "core")[1]
    held, token = sweep(units[5:6], held, kept)
    msgs = pl.pallas_call(
        lambda *refs: third_kernel(n, chips, *refs),
        out_shape=[shape(((responses + 1) * block, DH), BF16)] * n,
        in_specs=[VMEM] * (n + 2) + [ANY],
        out_specs=[VMEM] * n,
        compiler_params=params(),
        name="third",
    )(*got1, kept, swapped, token)
    got3 = taken(exchange(msgs, "prompt"))
    held, token = sweep(units[6:], held, msgs[0], range(responses - 1))
    partial_out, partial_dq, query, grad_out, resp_dk, resp_dv = held

    resp_out, resp_dq, prompt_dk, prompt_dv = pl.pallas_call(
        lambda *refs: last_kernel(n, responses, *refs),
        out_shape=[like_out] * 2 + [shape(keys.shape, BF16)] * 2,
        in_specs=[VMEM] * (8 + n) + [ANY],
        out_specs=[ANY] * 4,
        scratch_shapes=[
            pltpu.VMEM((responses + 1, width, width), BF16),
            pltpu.VMEM(queries.shape, BF16),
            pltpu.VMEM(queries.shape, BF16),
            pltpu.VMEM(keys.shape[1:], BF16),
            pltpu.VMEM(keys.shape[1:], BF16),
            pltpu.SemaphoreType.DMA((2 + 2 * responses,)),
        ],
        compiler_params=params(),
        name="last",
    )(cols, query, grad_out, partial_out, partial_dq, keys, values, later, *got3, token)
    return (resp_out, resp_dq, resp_dk, resp_dv, prompt_dk, prompt_dv)


def solution(mesh):
    n, count = mesh.shape["prompt"], mesh.shape["resp"]
    mesh = jax.sharding.Mesh(mesh.devices.reshape(n, count // 2, 2), ("prompt", "z", "core"))
    spread = P(("prompt", "z", "core"))
    three = P(("prompt", "z", "core"), None, None)
    two = P(("prompt", "z", "core"), None)
    prompt = P(("z", "core"), "prompt", None)
    return jax.shard_map(
        shards,
        mesh=mesh,
        in_specs=(
            prompt,
            prompt,
            P(("z", "core"), None, "prompt"),
            three,
            three,
            three,
            three,
            three,
            spread,
            two,
            two,
            spread,
        ),
        out_specs=(three, three, three, three, prompt, prompt),
        check_vma=False,
    )
```

```python
import jax
import jax.numpy as jnp
from jax import lax
from jax.experimental import pallas as pl
from jax.experimental.pallas import tpu as pltpu
from jax.sharding import PartitionSpec as P

H = 2
DH = 128
HALF = 256
LOG2E = 1.4426950408889634
F32 = jnp.float32
BF16 = jnp.bfloat16
NEVER = -1e30
VMEM = pl.BlockSpec(memory_space=pltpu.VMEM)
ANY = pl.BlockSpec(memory_space=pl.ANY)
SMEM = pl.BlockSpec(memory_space=pltpu.SMEM)


def params(mebibytes=16):
    return pltpu.CompilerParams(vmem_limit_bytes=mebibytes * 1024 * 1024)


def mm(a, b):
    return lax.dot_general(a, b, (((1,), (0,)), ((), ())), preferred_element_type=F32)


def mm_nt(a, b):
    return lax.dot_general(a, b, (((1,), (1,)), ((), ())), preferred_element_type=F32)


def mm_tn(a, b):
    return lax.dot_general(a, b, (((0,), (0,)), ((), ())), preferred_element_type=F32)


def to_columns(rows):
    return jnp.concatenate([rows, jnp.zeros((128 - rows.shape[0], rows.shape[1]), F32)], axis=0).T


def in_hbm(x):
    return pltpu.with_memory_space_constraint(x, pltpu.HBM)


def three_terms(x):
    high = x.astype(BF16)
    rest = x - high.astype(F32)
    middle = rest.astype(BF16)
    return high, middle, (rest - middle.astype(F32)).astype(BF16)


def lane_cumsum(x):
    rows, width = x.shape
    ones = lax.broadcasted_iota(jnp.int32, (128, 128), 0) <= lax.broadcasted_iota(jnp.int32, (128, 128), 1)
    terms = jnp.concatenate(three_terms(x), axis=0)
    starts = range(0, width, 128)
    sums = mm(jnp.concatenate([terms[:, b : b + 128] for b in starts], axis=0), ones.astype(F32).astype(BF16))
    parts = []
    before = jnp.zeros((rows, 1), F32)
    for b in range(len(starts)):
        at = 3 * rows * b
        part = sums[at : at + rows] + sums[at + rows : at + 2 * rows] + sums[at + 2 * rows : at + 3 * rows]
        part = part + before
        before = part[:, 127:128]
        parts.append(part)
    return jnp.concatenate(parts, axis=1)


def first_kernel(
    n, ids_hbm, lens_hbm, adv_hbm, keys_hbm, values_hbm, pgates_hbm, gates_hbm, mask_hbm, q_hbm, c_hbm, k_hbm, v_hbm,
    *refs,
):
    msgs, (rows_ref, q, c, k_out, v_out) = refs[:n], refs[n : n + 5]
    keys, values, pgates, gates, mask, ids_ref, lens_ref, adv_ref, matrices, sems = refs[n + 5 :]
    pairs = [(pgates_hbm, pgates), (gates_hbm, gates), (mask_hbm, mask)]
    pairs += [(ids_hbm, ids_ref), (lens_hbm, lens_ref), (adv_hbm, adv_ref), (keys_hbm, keys), (values_hbm, values)]
    pairs += [(q_hbm, q), (c_hbm, c), (k_hbm, k_out), (v_hbm, v_out)]
    copies = [pltpu.make_async_copy(a, b, sems.at[i]) for i, (a, b) in enumerate(pairs)]
    for copy in copies[:10]:
        copy.start()
    count = gates.shape[0]
    slots = gates.shape[2]
    tokens = keys.shape[1]
    part = DH // n
    block = H * part
    targets = partners(n)

    def spread(at):
        for k in range(n):
            of = pl.ds(pl.multiple_of(targets[k] * part, part), part)
            msgs[k][at * part + (16 if at >= H else 0) : (at + 1) * part + (16 if at >= H else 0), :] = matrices[
                at, of, :
            ].astype(BF16)

    for copy in copies[:6]:
        copy.wait()
    for copy in copies[10:]:
        copy.start()
    piece = jnp.concatenate([pgates[0], jnp.zeros((H, slots - tokens), F32)], axis=1)
    gate_rows = [gates[i] for i in range(count)] + [piece, jnp.zeros((16 - H * (count + 1), slots), F32)]
    cum = lane_cumsum(jnp.concatenate(gate_rows, axis=0))
    carried = jnp.exp(cum)
    place = lax.broadcasted_iota(jnp.int32, (1, slots), 1)
    rows = []
    factors = []
    for i in range(count):
        weight = adv_ref[i].astype(F32) / 1024.0
        opened = jnp.where(place < lens_ref[0, i], 1.0, 0.0)
        live = mask[i : i + 1, :].astype(F32) * opened * weight
        rows += [cum[H * i : H * i + H], carried[H * i : H * i + H] * opened, live, opened, jnp.zeros((2, slots), F32)]
        factors.append(carried[H * i : H * i + H] * live)
    piece = cum[H * count : H * count + H]
    total = piece[:, -1:]
    suffix = total - piece
    rows += [suffix, jnp.zeros((8 - H, slots), F32)]
    rows_ref[...] = jnp.concatenate(rows, axis=0)

    copies[6].wait()
    copies[7].wait()
    turned = keys[0].T
    later = jnp.exp(suffix[:, :tokens])
    for h in range(H):
        lanes = slice(h * DH, (h + 1) * DH)
        scaled = turned[lanes].astype(F32) * later[h : h + 1]
        high = scaled.astype(BF16)
        low = (scaled - high.astype(F32)).astype(BF16)
        both = mm(jnp.concatenate([high, low], axis=0), values[0, :, lanes])
        matrices[h] = both[:DH] + both[DH:]
        spread(h)
    notes = [jnp.broadcast_to(x[h : h + 1].astype(F32), (1, DH)) for x in three_terms(total) for h in range(H)]
    notes += [jnp.full((1, DH), ids_ref[i].astype(F32)) for i in range(count)]
    notes.append(jnp.zeros((16 - len(notes), DH), F32))
    notes = jnp.concatenate(notes, axis=0).astype(BF16)
    for k in range(n):
        msgs[k][block : block + 16, :] = notes

    copies[8].wait()
    copies[9].wait()
    for i in range(count):
        turned = q[i].T
        for h in range(H):
            lanes = slice(h * DH, (h + 1) * DH)
            scaled = (turned[lanes].astype(F32) * factors[i][h : h + 1]).astype(BF16)
            matrices[H * (1 + i) + h] = mm(scaled, c[i, :, lanes])
            spread(H * (1 + i) + h)
    for copy in copies[10:]:
        copy.wait()


def noted_prompt(notes, i):
    return jnp.max(notes[3 * H + i : 3 * H + i + 1]).astype(jnp.int32)


def second_kernel(n, chips, cores, *refs):
    z_at = lax.axis_index("z")
    got, msgs, later_ref, sums = far_first(refs[:n]), refs[n + 1 : n + 1 + chips], refs[-2], refs[-1]
    part = DH // n
    block = H * part
    responses = (got[0].shape[0] - block - 16) // block
    place = partners(n)
    notes = [got[k][block : block + 16, :].astype(F32) for k in range(n)]
    logs = [x[0:H] + x[H : 2 * H] + x[2 * H : 3 * H] for x in notes]
    final = jnp.zeros((block, DH), F32)
    for k in range(n):
        later = jnp.zeros_like(logs[0])
        for other in range(n):
            if other != k:
                later = later + jnp.where(place[other] > place[k], logs[other], 0.0)
        if k == 0:
            later_ref[...] = jnp.concatenate([later, jnp.zeros((8 - H, DH), F32)], axis=0)
        decay = jnp.exp(later)
        decay = [jnp.broadcast_to(decay[h : h + 1], (part, DH)) for h in range(H)]
        final = final + jnp.concatenate(decay, axis=0) * got[k][0:block, :].astype(F32)
    sums[...] = jnp.zeros_like(sums)
    for k in range(n):
        for i in range(responses):
            at = block * (1 + i) + 16
            sums[noted_prompt(notes[k], i)] += got[k][at : at + block, :].astype(F32)
    final = final.astype(BF16)
    for k in range(chips):
        z = lax.rem(z_at + k, chips)
        msgs[k][0:block, :] = final
        for c in range(cores):
            msgs[k][(1 + c) * block : (2 + c) * block, :] = sums[z * cores + c].astype(BF16)


def swap_kernel(chips, *refs):
    got, sent_ref, kept_ref = [refs[middle_first(chips).index(k)] for k in range(chips)], refs[chips + 1], refs[chips + 2]
    block = got[0].shape[0] // 3
    totals = []
    for c in range(2):
        total = got[0][(1 + c) * block : (2 + c) * block, :].astype(F32)
        for k in range(1, chips):
            total = total + got[k][(1 + c) * block : (2 + c) * block, :].astype(F32)
        totals.append(total)
    for k in range(chips):
        final = got[k][0:block, :]
        sent_ref[k * block : (k + 1) * block, :] = final
        kept_ref[k * block : (k + 1) * block, :] = final
    low = lax.axis_index("core") == 0
    sent_ref[chips * block :, :] = jnp.where(low, totals[1], totals[0]).astype(BF16)
    kept_ref[chips * block :, :] = jnp.where(low, totals[0], totals[1]).astype(BF16)


def third_kernel(n, chips, *refs):
    z_at, core = lax.axis_index("z"), lax.axis_index("core")
    noted, kept_ref, got_ref, msgs = far_first(refs[:n]), refs[n], refs[n + 1], refs[n + 3 :]
    block = H * DH // n
    responses = (noted[0].shape[0] - block - 16) // block
    total = kept_ref[chips * block :, :].astype(F32) + got_ref[chips * block :, :].astype(F32)
    total = total.astype(BF16)
    for k in range(n):
        notes = noted[k][block : block + 16, :].astype(F32)
        for i in range(responses):
            p = noted_prompt(notes, i)
            slot = lax.rem(z_at + chips - lax.div(p, 2), chips)
            at = pl.ds(pl.multiple_of(slot * block, block), block)
            same = lax.rem(p, 2) == core
            state = jnp.where(same, kept_ref[at, :].astype(F32), got_ref[at, :].astype(F32))
            msgs[k][i * block : (i + 1) * block, :] = state.astype(BF16)
        msgs[k][responses * block :, :] = total


def sweep_kernel(units, done, rows_ref, q_ref, k_ref, v_ref, c_ref, cols_ref, *refs):
    writes = len(done) > 0
    if writes:
        *refs, dk_hbm, dv_hbm, sems = refs
    out_ref, dq_ref, query_ref, grad_ref, dk_ref, dv_ref, token_ref = refs[-7:]
    if cols_ref is None:
        cols_ref = refs[0]
        cols_ref[...] = to_columns(rows_ref[...])
    copies = []

    def send(r):
        for a, b in ((dk_ref, dk_hbm), (dv_ref, dv_hbm)):
            copies.append(pltpu.make_async_copy(a.at[r], b.at[r], sems.at[len(copies)]))
            copies[-1].start()

    for r in done:
        send(r)
    token_ref[...] = jnp.zeros_like(token_ref)
    quarter = HALF // 2
    causal = lax.broadcasted_iota(jnp.int32, (quarter, quarter), 0) >= lax.broadcasted_iota(
        jnp.int32, (quarter, quarter), 1
    )
    blank = jnp.zeros((quarter, quarter), BF16)
    blocks = q_ref.shape[1] // HALF

    def decayed(products, cum, row, diagonal):
        if not diagonal:
            decay = jnp.exp2(cum - row)
            return [(x * decay).astype(BF16) for x in products]
        first = jnp.exp2(jnp.where(causal, cum[:quarter] - row[:, :quarter], NEVER))
        left = jnp.exp2(cum[quarter:] - row[:, :quarter])
        right = jnp.exp2(jnp.where(causal, cum[quarter:] - row[:, quarter:], NEVER))
        results = []
        for x in products:
            upper = jnp.concatenate([(x[:quarter, :quarter] * first).astype(BF16), blank], axis=1)
            lower = [(x[quarter:, :quarter] * left).astype(BF16), (x[quarter:, quarter:] * right).astype(BF16)]
            results.append(jnp.concatenate([upper, jnp.concatenate(lower, axis=1)], axis=0))
        return results

    for r, h in units:
        lanes = slice(h * DH, (h + 1) * DH)
        cum = cols_ref[:, 8 * r + h : 8 * r + h + 1] * LOG2E
        row = rows_ref[8 * r + h : 8 * r + h + 1, :] * LOG2E
        live = cols_ref[:, 8 * r + 4 : 8 * r + 5]
        opened = cols_ref[:, 8 * r + 5 : 8 * r + 6]
        grad_all = (c_ref[r, :, lanes].astype(F32) * live).astype(BF16)
        carried = cols_ref[:, 8 * r + 2 + h : 8 * r + 3 + h]
        query_ref[r, :, lanes] = (q_ref[r, :, lanes].astype(F32) * carried).astype(BF16)
        grad_ref[r, :, lanes] = (grad_all.astype(F32) * carried).astype(BF16)
        query_turned = q_ref[r, :, lanes].T
        grad_turned = grad_all.T
        dk = [None] * blocks
        dv = [None] * blocks
        for t in range(blocks):
            at = slice(t * HALF, (t + 1) * HALF)
            query = q_ref[r, at, lanes]
            grad_out = grad_all[at]
            out = None
            dq = None
            for s in range(t + 1):
                of = slice(s * HALF, (s + 1) * HALF)
                key = k_ref[r, of, lanes]
                value = v_ref[r, of, lanes]
                mixing, scores = decayed(
                    [mm_nt(query, key), mm_nt(grad_out, value)], cum[at], row[:, of], s == t
                )
                o_new = mm(mixing, value)
                q_new = mm(scores, key)
                k_new = mm(query_turned[:, at], scores)
                v_new = mm(grad_turned[:, at], mixing)
                out = o_new if out is None else out + o_new
                dq = q_new if dq is None else dq + q_new
                dk[s] = k_new if dk[s] is None else dk[s] + k_new
                dv[s] = v_new if dv[s] is None else dv[s] + v_new
            out_ref[r, at, lanes] = out * opened[at]
            dq_ref[r, at, lanes] = dq
        for s in range(blocks):
            of = slice(s * HALF, (s + 1) * HALF)
            dk_ref[r, of, lanes] = dk[s].astype(BF16).T
            dv_ref[r, of, lanes] = dv[s].astype(BF16).T
        if writes and h == H - 1:
            send(r)
    for copy in copies:
        copy.wait()


def last_kernel(
    n, count, cols_ref, q_ref, grad_ref, po_ref, pdq_ref, keys_ref, values_ref, later_ref, *refs
):
    got, refs = refs[:n], refs[n + 1 :]
    out_hbm, dq_hbm, dk_hbm, dv_hbm, start, out_buf, dq_buf, dk_buf, dv_buf, sems = refs
    part = DH // n
    block = H * part
    place = partners(n)
    tokens = keys_ref.shape[1]
    copies = []

    def send(a, b):
        copies.append(pltpu.make_async_copy(a, b, sems.at[len(copies)]))
        copies[-1].start()

    start[...] = jnp.zeros_like(start)
    for r in range(count + 1):
        for k in range(n):
            for h in range(H):
                of = pl.ds(pl.multiple_of(h * DH + place[k] * part, part), part)
                rows = got[k][r * block + h * part : r * block + (h + 1) * part, :]
                start[r, of, h * DH : (h + 1) * DH] = rows
    factor = [
        jnp.exp(cols_ref[:tokens, 8 * count + h : 8 * count + h + 1] + later_ref[h : h + 1, 0:1]) for h in range(H)
    ]
    for buf, x in ((dk_buf, mm_nt(values_ref[0], start[count])), (dv_buf, mm(keys_ref[0], start[count]))):
        for h in range(H):
            lanes = slice(h * DH, (h + 1) * DH)
            buf[:, lanes] = (factor[h] * x[:, lanes]).astype(BF16)
    send(dk_buf, dk_hbm.at[0])
    send(dv_buf, dv_hbm.at[0])
    for r in range(count):
        out_buf[r] = (po_ref[r] + mm(q_ref[r], start[r])).astype(BF16)
        dq_buf[r] = (pdq_ref[r] + mm_nt(grad_ref[r], start[r])).astype(BF16)
        send(out_buf.at[r], out_hbm.at[r])
        send(dq_buf.at[r], dq_hbm.at[r])
    for copy in copies:
        copy.wait()


def exchange(xs, axis):
    n = lax.axis_size(axis)
    return [xs[0]] + [lax.ppermute(xs[k], axis, [(s, s ^ k) for s in range(n)]) for k in range(1, n)]


def exchange_ring(xs, axis):
    n = lax.axis_size(axis)
    return [xs[0]] + [lax.ppermute(xs[k], axis, [(s, (s + k) % n) for s in range(n)]) for k in range(1, n)]


def middle_first(n):
    return [0, *sorted(range(1, n), key=lambda k: (-min(k, n - k), k))]


def far_first(refs):
    return [refs[0], *refs[:0:-1]]


def partners(n):
    me = lax.axis_index("prompt")
    return [lax.bitwise_xor(me, k) for k in range(n)]


def shards(
    keys,
    values,
    prompt_gates,
    queries,
    resp_keys,
    resp_values,
    resp_gates,
    cotangent,
    group_ids,
    resp_lengths,
    loss_mask,
    advantages,
):
    n = lax.axis_size("prompt")
    chips = lax.axis_size("z")
    cores = lax.axis_size("core")
    responses, slots, width = queries.shape
    block = H * DH // n
    shape = jax.ShapeDtypeStruct

    outs = pl.pallas_call(
        lambda *refs: first_kernel(n, *refs),
        out_shape=[shape((block * (1 + responses) + 16, DH), BF16)] * n
        + [shape((8 * (responses + 1), slots), F32)]
        + [shape(queries.shape, BF16)] * 4,
        in_specs=[ANY] * 12,
        out_specs=[VMEM] * (n + 5),
        scratch_shapes=[
            pltpu.VMEM(keys.shape, BF16),
            pltpu.VMEM(values.shape, BF16),
            pltpu.VMEM(prompt_gates.shape, F32),
            pltpu.VMEM(resp_gates.shape, F32),
            pltpu.VMEM(loss_mask.shape, jnp.int32),
            pltpu.SMEM(group_ids.shape, jnp.int32),
            pltpu.SMEM(resp_lengths.shape, jnp.int32),
            pltpu.SMEM(advantages.shape, jnp.int32),
            pltpu.VMEM((H * (1 + responses), DH, DH), F32),
            pltpu.SemaphoreType.DMA((12,)),
        ],
        compiler_params=params(32),
        name="first",
    )(
        *[in_hbm(x) for x in (group_ids, resp_lengths, advantages, keys, values, prompt_gates, resp_gates)],
        *[in_hbm(x) for x in (loss_mask, queries, cotangent, resp_keys, resp_values)],
    )
    msgs, (rows, queries, cotangent, resp_keys, resp_values) = outs[:n], outs[n:]

    like = shape(queries.shape, F32)
    like_out = shape(queries.shape, BF16)

    held_shapes = [like, like] + [like_out] * 4 + [shape((8, 128), F32)]

    def first_sweep(units):
        outs = pl.pallas_call(
            lambda *refs: sweep_kernel(units, (), *refs[:5], None, *refs[5:]),
            out_shape=[shape((slots, 128), F32)] + held_shapes,
            in_specs=[VMEM] * 5,
            out_specs=[VMEM] * 8,
            compiler_params=params(),
            name="sweep",
        )(rows, queries, resp_keys, resp_values, cotangent)
        return outs[0], outs[1:7], outs[7]

    def sweep(units, before, token, done=()):
        writes = len(done) > 0
        outs = pl.pallas_call(
            lambda *refs: sweep_kernel(units, done, *refs),
            out_shape=held_shapes + [like_out] * (2 * writes),
            in_specs=[VMEM] * 6 + [ANY] * 7,
            out_specs=[VMEM] * 7 + [ANY] * (2 * writes),
            scratch_shapes=[pltpu.SemaphoreType.DMA((2 * responses,))] * writes,
            input_output_aliases={7 + k: k for k in range(6)},
            compiler_params=params(),
            name="sweep",
        )(rows, queries, resp_keys, resp_values, cotangent, cols, token, *before)
        return (outs[:4] + outs[7:] if writes else outs[:6]), outs[6]

    units = [(r, h) for r in range(responses) for h in range(H)]
    got1 = far_first(exchange(msgs, "prompt"))
    cols, held, token = first_sweep(units[:3])
    outs = pl.pallas_call(
        lambda *refs: second_kernel(n, chips, cores, *refs),
        out_shape=[shape(((1 + cores) * block, DH), BF16)] * chips + [shape((8, DH), F32)],
        in_specs=[VMEM] * n + [ANY],
        out_specs=[VMEM] * (chips + 1),
        scratch_shapes=[pltpu.VMEM((chips * cores, block, DH), F32)],
        compiler_params=params(),
        name="second",
    )(*got1, token)
    msgs, later = outs[:chips], outs[chips]
    got2 = exchange_ring(msgs, "z")
    got2 = [got2[k] for k in middle_first(chips)]
    held, token = sweep(units[3:5], held, later)
    sent, kept = pl.pallas_call(
        lambda *refs: swap_kernel(chips, *refs),
        out_shape=[shape(((chips + 1) * block, DH), BF16)] * 2,
        in_specs=[VMEM] * chips + [ANY],
        out_specs=[VMEM, VMEM],
        compiler_params=params(),
        name="swap",
    )(*got2, token)
    swapped = exchange([kept, sent], "core")[1]
    held, token = sweep(units[5:6], held, kept)
    msgs = pl.pallas_call(
        lambda *refs: third_kernel(n, chips, *refs),
        out_shape=[shape(((responses + 1) * block, DH), BF16)] * n,
        in_specs=[VMEM] * (n + 2) + [ANY],
        out_specs=[VMEM] * n,
        compiler_params=params(),
        name="third",
    )(*got1, kept, swapped, token)
    got3 = exchange(msgs, "prompt")
    held, token = sweep(units[6:], held, msgs[0], range(responses - 1))
    partial_out, partial_dq, query, grad_out, resp_dk, resp_dv = held

    resp_out, resp_dq, prompt_dk, prompt_dv = pl.pallas_call(
        lambda *refs: last_kernel(n, responses, *refs),
        out_shape=[like_out] * 2 + [shape(keys.shape, BF16)] * 2,
        in_specs=[VMEM] * (8 + n) + [ANY],
        out_specs=[ANY] * 4,
        scratch_shapes=[
            pltpu.VMEM((responses + 1, width, width), BF16),
            pltpu.VMEM(queries.shape, BF16),
            pltpu.VMEM(queries.shape, BF16),
            pltpu.VMEM(keys.shape[1:], BF16),
            pltpu.VMEM(keys.shape[1:], BF16),
            pltpu.SemaphoreType.DMA((2 + 2 * responses,)),
        ],
        compiler_params=params(),
        name="last",
    )(cols, query, grad_out, partial_out, partial_dq, keys, values, later, *got3, token)
    return (resp_out, resp_dq, resp_dk, resp_dv, prompt_dk, prompt_dv)


def solution(mesh):
    n, count = mesh.shape["prompt"], mesh.shape["resp"]
    mesh = jax.sharding.Mesh(mesh.devices.reshape(n, count // 2, 2), ("prompt", "z", "core"))
    spread = P(("prompt", "z", "core"))
    three = P(("prompt", "z", "core"), None, None)
    two = P(("prompt", "z", "core"), None)
    prompt = P(("z", "core"), "prompt", None)
    return jax.shard_map(
        shards,
        mesh=mesh,
        in_specs=(
            prompt,
            prompt,
            P(("z", "core"), None, "prompt"),
            three,
            three,
            three,
            three,
            three,
            spread,
            two,
            two,
            spread,
        ),
        out_specs=(three, three, three, three, prompt, prompt),
        check_vma=False,
    )
```

```python
import jax
import jax.numpy as jnp
from jax import lax
from jax.experimental import pallas as pl
from jax.experimental.pallas import tpu as pltpu
from jax.sharding import PartitionSpec as P

H = 2
DH = 128
HALF = 256
LOG2E = 1.4426950408889634
F32 = jnp.float32
BF16 = jnp.bfloat16
NEVER = -1e30
VMEM = pl.BlockSpec(memory_space=pltpu.VMEM)
ANY = pl.BlockSpec(memory_space=pl.ANY)
SMEM = pl.BlockSpec(memory_space=pltpu.SMEM)


def params(mebibytes=16):
    return pltpu.CompilerParams(vmem_limit_bytes=mebibytes * 1024 * 1024)


def mm(a, b):
    return lax.dot_general(a, b, (((1,), (0,)), ((), ())), preferred_element_type=F32)


def mm_nt(a, b):
    return lax.dot_general(a, b, (((1,), (1,)), ((), ())), preferred_element_type=F32)


def mm_tn(a, b):
    return lax.dot_general(a, b, (((0,), (0,)), ((), ())), preferred_element_type=F32)


def to_columns(rows):
    return jnp.concatenate([rows, jnp.zeros((128 - rows.shape[0], rows.shape[1]), F32)], axis=0).T


def in_hbm(x):
    return pltpu.with_memory_space_constraint(x, pltpu.HBM)


def three_terms(x):
    high = x.astype(BF16)
    rest = x - high.astype(F32)
    middle = rest.astype(BF16)
    return high, middle, (rest - middle.astype(F32)).astype(BF16)


def lane_cumsum(x):
    rows, width = x.shape
    ones = lax.broadcasted_iota(jnp.int32, (128, 128), 0) <= lax.broadcasted_iota(jnp.int32, (128, 128), 1)
    terms = jnp.concatenate(three_terms(x), axis=0)
    starts = range(0, width, 128)
    sums = mm(jnp.concatenate([terms[:, b : b + 128] for b in starts], axis=0), ones.astype(F32).astype(BF16))
    parts = []
    before = jnp.zeros((rows, 1), F32)
    for b in range(len(starts)):
        at = 3 * rows * b
        part = sums[at : at + rows] + sums[at + rows : at + 2 * rows] + sums[at + 2 * rows : at + 3 * rows]
        part = part + before
        before = part[:, 127:128]
        parts.append(part)
    return jnp.concatenate(parts, axis=1)


def first_kernel(
    n, ids_hbm, lens_hbm, adv_hbm, keys_hbm, values_hbm, pgates_hbm, gates_hbm, mask_hbm, q_hbm, c_hbm, k_hbm, v_hbm,
    *refs,
):
    msgs, (rows_ref, q, c, k_out, v_out) = refs[:n], refs[n : n + 5]
    keys, values, pgates, gates, mask, ids_ref, lens_ref, adv_ref, matrices, sems = refs[n + 5 :]
    pairs = [(pgates_hbm, pgates), (gates_hbm, gates), (lens_hbm, lens_ref), (adv_hbm, adv_ref), (mask_hbm, mask)]
    pairs += [(keys_hbm, keys), (values_hbm, values), (q_hbm, q), (c_hbm, c), (ids_hbm, ids_ref)]
    pairs += [(k_hbm, k_out), (v_hbm, v_out)]
    copies = [pltpu.make_async_copy(a, b, sems.at[i]) for i, (a, b) in enumerate(pairs)]
    for copy in copies[:10]:
        copy.start()
    count = gates.shape[0]
    slots = gates.shape[2]
    tokens = keys.shape[1]
    part = DH // n
    block = H * part
    targets = partners(n)

    def spread(at):
        for k in range(n):
            of = pl.ds(pl.multiple_of(targets[k] * part, part), part)
            msgs[k][at * part + (16 if at >= H else 0) : (at + 1) * part + (16 if at >= H else 0), :] = matrices[
                at, of, :
            ].astype(BF16)

    for copy in copies[10:]:
        copy.start()
    copies[0].wait()
    copies[1].wait()
    piece = jnp.concatenate([pgates[0], jnp.zeros((H, slots - tokens), F32)], axis=1)
    gate_rows = [gates[i] for i in range(count)] + [piece, jnp.zeros((16 - H * (count + 1), slots), F32)]
    cum = lane_cumsum(jnp.concatenate(gate_rows, axis=0))
    carried = jnp.exp(cum)
    place = lax.broadcasted_iota(jnp.int32, (1, slots), 1)
    for copy in copies[2:5]:
        copy.wait()
    rows = []
    factors = []
    for i in range(count):
        weight = adv_ref[i].astype(F32) / 1024.0
        opened = jnp.where(place < lens_ref[0, i], 1.0, 0.0)
        live = mask[i : i + 1, :].astype(F32) * opened * weight
        rows += [cum[H * i : H * i + H], carried[H * i : H * i + H] * opened, live, opened, jnp.zeros((2, slots), F32)]
        factors.append(carried[H * i : H * i + H] * live)
    piece = cum[H * count : H * count + H]
    total = piece[:, -1:]
    suffix = total - piece
    rows += [suffix, jnp.zeros((8 - H, slots), F32)]
    rows_ref[...] = jnp.concatenate(rows, axis=0)

    copies[5].wait()
    copies[6].wait()
    turned = keys[0].T
    later = jnp.exp(suffix[:, :tokens])
    for h in range(H):
        lanes = slice(h * DH, (h + 1) * DH)
        scaled = turned[lanes].astype(F32) * later[h : h + 1]
        high = scaled.astype(BF16)
        low = (scaled - high.astype(F32)).astype(BF16)
        both = mm(jnp.concatenate([high, low], axis=0), values[0, :, lanes])
        matrices[h] = both[:DH] + both[DH:]
        spread(h)
    copies[7].wait()
    copies[8].wait()
    for i in range(count):
        turned = q[i].T
        for h in range(H):
            lanes = slice(h * DH, (h + 1) * DH)
            scaled = (turned[lanes].astype(F32) * factors[i][h : h + 1]).astype(BF16)
            matrices[H * (1 + i) + h] = mm(scaled, c[i, :, lanes])
            spread(H * (1 + i) + h)
    copies[9].wait()
    notes = [jnp.broadcast_to(x[h : h + 1].astype(F32), (1, DH)) for x in three_terms(total) for h in range(H)]
    notes += [jnp.full((1, DH), ids_ref[i].astype(F32)) for i in range(count)]
    notes.append(jnp.zeros((16 - len(notes), DH), F32))
    notes = jnp.concatenate(notes, axis=0).astype(BF16)
    for k in range(n):
        msgs[k][block : block + 16, :] = notes
    for copy in copies[10:]:
        copy.wait()


def noted_prompt(notes, i):
    return jnp.max(notes[3 * H + i : 3 * H + i + 1]).astype(jnp.int32)


def second_kernel(n, chips, cores, *refs):
    z_at = lax.axis_index("z")
    got, msgs, later_ref, sums = far_first(refs[:n]), refs[n + 1 : n + 1 + chips], refs[-2], refs[-1]
    part = DH // n
    block = H * part
    responses = (got[0].shape[0] - block - 16) // block
    place = partners(n)
    notes = [got[k][block : block + 16, :].astype(F32) for k in range(n)]
    logs = [x[0:H] + x[H : 2 * H] + x[2 * H : 3 * H] for x in notes]
    final = jnp.zeros((block, DH), F32)
    for k in range(n):
        later = jnp.zeros_like(logs[0])
        for other in range(n):
            if other != k:
                later = later + jnp.where(place[other] > place[k], logs[other], 0.0)
        if k == 0:
            later_ref[...] = jnp.concatenate([later, jnp.zeros((8 - H, DH), F32)], axis=0)
        decay = jnp.exp(later)
        decay = [jnp.broadcast_to(decay[h : h + 1], (part, DH)) for h in range(H)]
        final = final + jnp.concatenate(decay, axis=0) * got[k][0:block, :].astype(F32)
    sums[...] = jnp.zeros_like(sums)
    for k in range(n):
        for i in range(responses):
            at = block * (1 + i) + 16
            sums[noted_prompt(notes[k], i)] += got[k][at : at + block, :].astype(F32)
    final = final.astype(BF16)
    for k in range(chips):
        z = lax.rem(z_at + k, chips)
        msgs[k][0:block, :] = final
        for c in range(cores):
            msgs[k][(1 + c) * block : (2 + c) * block, :] = sums[z * cores + c].astype(BF16)


def swap_kernel(chips, *refs):
    got, sent_ref, kept_ref = refs[:chips], refs[chips + 1], refs[chips + 2]
    block = got[0].shape[0] // 3
    totals = []
    for c in range(2):
        total = got[0][(1 + c) * block : (2 + c) * block, :].astype(F32)
        for k in range(1, chips):
            total = total + got[k][(1 + c) * block : (2 + c) * block, :].astype(F32)
        totals.append(total)
    for k in range(chips):
        final = got[k][0:block, :]
        sent_ref[k * block : (k + 1) * block, :] = final
        kept_ref[k * block : (k + 1) * block, :] = final
    low = lax.axis_index("core") == 0
    sent_ref[chips * block :, :] = jnp.where(low, totals[1], totals[0]).astype(BF16)
    kept_ref[chips * block :, :] = jnp.where(low, totals[0], totals[1]).astype(BF16)


def third_kernel(n, chips, *refs):
    z_at, core = lax.axis_index("z"), lax.axis_index("core")
    noted, kept_ref, got_ref, msgs = far_first(refs[:n]), refs[n], refs[n + 1], refs[n + 3 :]
    block = H * DH // n
    responses = (noted[0].shape[0] - block - 16) // block
    total = kept_ref[chips * block :, :].astype(F32) + got_ref[chips * block :, :].astype(F32)
    total = total.astype(BF16)
    for k in range(n):
        notes = noted[k][block : block + 16, :].astype(F32)
        for i in range(responses):
            p = noted_prompt(notes, i)
            slot = lax.rem(z_at + chips - lax.div(p, 2), chips)
            at = pl.ds(pl.multiple_of(slot * block, block), block)
            same = lax.rem(p, 2) == core
            state = jnp.where(same, kept_ref[at, :].astype(F32), got_ref[at, :].astype(F32))
            msgs[k][i * block : (i + 1) * block, :] = state.astype(BF16)
        msgs[k][responses * block :, :] = total


def sweep_kernel(units, done, rows_ref, q_ref, k_ref, v_ref, c_ref, cols_ref, *refs):
    writes = len(done) > 0
    if writes:
        *refs, dk_hbm, dv_hbm, sems = refs
    out_ref, dq_ref, query_ref, grad_ref, dk_ref, dv_ref, token_ref = refs[-7:]
    if cols_ref is None:
        cols_ref = refs[0]
        cols_ref[...] = to_columns(rows_ref[...])
    copies = []

    def send(r):
        for a, b in ((dk_ref, dk_hbm), (dv_ref, dv_hbm)):
            copies.append(pltpu.make_async_copy(a.at[r], b.at[r], sems.at[len(copies)]))
            copies[-1].start()

    for r in done:
        send(r)
    token_ref[...] = jnp.zeros_like(token_ref)
    quarter = HALF // 2
    causal = lax.broadcasted_iota(jnp.int32, (quarter, quarter), 0) >= lax.broadcasted_iota(
        jnp.int32, (quarter, quarter), 1
    )
    blank = jnp.zeros((quarter, quarter), BF16)
    blocks = q_ref.shape[1] // HALF

    def decayed(products, cum, row, diagonal):
        if not diagonal:
            decay = jnp.exp2(cum - row)
            return [(x * decay).astype(BF16) for x in products]
        first = jnp.exp2(jnp.where(causal, cum[:quarter] - row[:, :quarter], NEVER))
        left = jnp.exp2(cum[quarter:] - row[:, :quarter])
        right = jnp.exp2(jnp.where(causal, cum[quarter:] - row[:, quarter:], NEVER))
        results = []
        for x in products:
            upper = jnp.concatenate([(x[:quarter, :quarter] * first).astype(BF16), blank], axis=1)
            lower = [(x[quarter:, :quarter] * left).astype(BF16), (x[quarter:, quarter:] * right).astype(BF16)]
            results.append(jnp.concatenate([upper, jnp.concatenate(lower, axis=1)], axis=0))
        return results

    for r, h in units:
        lanes = slice(h * DH, (h + 1) * DH)
        cum = cols_ref[:, 8 * r + h : 8 * r + h + 1] * LOG2E
        row = rows_ref[8 * r + h : 8 * r + h + 1, :] * LOG2E
        live = cols_ref[:, 8 * r + 4 : 8 * r + 5]
        opened = cols_ref[:, 8 * r + 5 : 8 * r + 6]
        grad_all = (c_ref[r, :, lanes].astype(F32) * live).astype(BF16)
        carried = cols_ref[:, 8 * r + 2 + h : 8 * r + 3 + h]
        query_ref[r, :, lanes] = (q_ref[r, :, lanes].astype(F32) * carried).astype(BF16)
        grad_ref[r, :, lanes] = (grad_all.astype(F32) * carried).astype(BF16)
        query_turned = q_ref[r, :, lanes].T
        grad_turned = grad_all.T
        dk = [None] * blocks
        dv = [None] * blocks
        for t in range(blocks):
            at = slice(t * HALF, (t + 1) * HALF)
            query = q_ref[r, at, lanes]
            grad_out = grad_all[at]
            out = None
            dq = None
            for s in range(t + 1):
                of = slice(s * HALF, (s + 1) * HALF)
                key = k_ref[r, of, lanes]
                value = v_ref[r, of, lanes]
                mixing, scores = decayed(
                    [mm_nt(query, key), mm_nt(grad_out, value)], cum[at], row[:, of], s == t
                )
                o_new = mm(mixing, value)
                q_new = mm(scores, key)
                k_new = mm(query_turned[:, at], scores)
                v_new = mm(grad_turned[:, at], mixing)
                out = o_new if out is None else out + o_new
                dq = q_new if dq is None else dq + q_new
                dk[s] = k_new if dk[s] is None else dk[s] + k_new
                dv[s] = v_new if dv[s] is None else dv[s] + v_new
            out_ref[r, at, lanes] = out * opened[at]
            dq_ref[r, at, lanes] = dq
        for s in range(blocks):
            of = slice(s * HALF, (s + 1) * HALF)
            dk_ref[r, of, lanes] = dk[s].astype(BF16).T
            dv_ref[r, of, lanes] = dv[s].astype(BF16).T
        if writes and h == H - 1:
            send(r)
    for copy in copies:
        copy.wait()


def last_kernel(
    n, count, cols_ref, q_ref, grad_ref, po_ref, pdq_ref, keys_ref, values_ref, later_ref, *refs
):
    got, refs = refs[:n], refs[n + 1 :]
    out_hbm, dq_hbm, dk_hbm, dv_hbm, start, out_buf, dq_buf, dk_buf, dv_buf, sems = refs
    part = DH // n
    block = H * part
    place = partners(n)
    slots = q_ref.shape[1]
    tokens = keys_ref.shape[1]
    copies = []

    def send(a, b):
        copies.append(pltpu.make_async_copy(a, b, sems.at[len(copies)]))
        copies[-1].start()

    start[...] = jnp.zeros_like(start)
    for r in range(count + 1):
        for k in range(n):
            for h in range(H):
                of = pl.ds(pl.multiple_of(h * DH + place[k] * part, part), part)
                rows = got[k][r * block + h * part : r * block + (h + 1) * part, :]
                start[r, of, h * DH : (h + 1) * DH] = rows
    for r in range(count):
        for t in range(0, slots, HALF):
            at = slice(t, t + HALF)
            out_buf[r, at, :] = (po_ref[r, at, :] + mm(q_ref[r, at, :], start[r])).astype(BF16)
            dq_buf[r, at, :] = (pdq_ref[r, at, :] + mm_nt(grad_ref[r, at, :], start[r])).astype(BF16)
        send(out_buf.at[r], out_hbm.at[r])
        send(dq_buf.at[r], dq_hbm.at[r])
    factor = [
        jnp.exp(cols_ref[:tokens, 8 * count + h : 8 * count + h + 1] + later_ref[h : h + 1, 0:1]) for h in range(H)
    ]
    for buf, x in ((dk_buf, mm_nt(values_ref[0], start[count])), (dv_buf, mm(keys_ref[0], start[count]))):
        for h in range(H):
            lanes = slice(h * DH, (h + 1) * DH)
            buf[:, lanes] = (factor[h] * x[:, lanes]).astype(BF16)
    send(dk_buf, dk_hbm.at[0])
    send(dv_buf, dv_hbm.at[0])
    for copy in copies:
        copy.wait()


def exchange(xs, axis):
    n = lax.axis_size(axis)
    return [xs[0]] + [lax.ppermute(xs[k], axis, [(s, s ^ k) for s in range(n)]) for k in range(1, n)]


def exchange_ring(xs, axis):
    n = lax.axis_size(axis)
    return [xs[0]] + [lax.ppermute(xs[k], axis, [(s, (s + k) % n) for s in range(n)]) for k in range(1, n)]


def far_first(refs):
    return [refs[0], *refs[:0:-1]]


def partners(n):
    me = lax.axis_index("prompt")
    return [lax.bitwise_xor(me, k) for k in range(n)]


def shards(
    keys,
    values,
    prompt_gates,
    queries,
    resp_keys,
    resp_values,
    resp_gates,
    cotangent,
    group_ids,
    resp_lengths,
    loss_mask,
    advantages,
):
    n = lax.axis_size("prompt")
    chips = lax.axis_size("z")
    cores = lax.axis_size("core")
    responses, slots, width = queries.shape
    block = H * DH // n
    shape = jax.ShapeDtypeStruct

    outs = pl.pallas_call(
        lambda *refs: first_kernel(n, *refs),
        out_shape=[shape((block * (1 + responses) + 16, DH), BF16)] * n
        + [shape((8 * (responses + 1), slots), F32)]
        + [shape(queries.shape, BF16)] * 4,
        in_specs=[ANY] * 12,
        out_specs=[VMEM] * (n + 5),
        scratch_shapes=[
            pltpu.VMEM(keys.shape, BF16),
            pltpu.VMEM(values.shape, BF16),
            pltpu.VMEM(prompt_gates.shape, F32),
            pltpu.VMEM(resp_gates.shape, F32),
            pltpu.VMEM(loss_mask.shape, jnp.int32),
            pltpu.SMEM(group_ids.shape, jnp.int32),
            pltpu.SMEM(resp_lengths.shape, jnp.int32),
            pltpu.SMEM(advantages.shape, jnp.int32),
            pltpu.VMEM((H * (1 + responses), DH, DH), F32),
            pltpu.SemaphoreType.DMA((12,)),
        ],
        compiler_params=params(32),
        name="first",
    )(
        *[in_hbm(x) for x in (group_ids, resp_lengths, advantages, keys, values, prompt_gates, resp_gates)],
        *[in_hbm(x) for x in (loss_mask, queries, cotangent, resp_keys, resp_values)],
    )
    msgs, (rows, queries, cotangent, resp_keys, resp_values) = outs[:n], outs[n:]

    like = shape(queries.shape, F32)
    like_out = shape(queries.shape, BF16)

    held_shapes = [like, like] + [like_out] * 4 + [shape((8, 128), F32)]

    def first_sweep(units):
        outs = pl.pallas_call(
            lambda *refs: sweep_kernel(units, (), *refs[:5], None, *refs[5:]),
            out_shape=[shape((slots, 128), F32)] + held_shapes,
            in_specs=[VMEM] * 5,
            out_specs=[VMEM] * 8,
            compiler_params=params(),
            name="sweep",
        )(rows, queries, resp_keys, resp_values, cotangent)
        return outs[0], outs[1:7], outs[7]

    def sweep(units, before, token, done=()):
        writes = len(done) > 0
        outs = pl.pallas_call(
            lambda *refs: sweep_kernel(units, done, *refs),
            out_shape=held_shapes + [like_out] * (2 * writes),
            in_specs=[VMEM] * 6 + [ANY] * 7,
            out_specs=[VMEM] * 7 + [ANY] * (2 * writes),
            scratch_shapes=[pltpu.SemaphoreType.DMA((2 * responses,))] * writes,
            input_output_aliases={7 + k: k for k in range(6)},
            compiler_params=params(),
            name="sweep",
        )(rows, queries, resp_keys, resp_values, cotangent, cols, token, *before)
        return (outs[:4] + outs[7:] if writes else outs[:6]), outs[6]

    units = [(r, h) for r in range(responses) for h in range(H)]
    got1 = far_first(exchange(msgs, "prompt"))
    cols, held, token = first_sweep(units[:3])
    outs = pl.pallas_call(
        lambda *refs: second_kernel(n, chips, cores, *refs),
        out_shape=[shape(((1 + cores) * block, DH), BF16)] * chips + [shape((8, DH), F32)],
        in_specs=[VMEM] * n + [ANY],
        out_specs=[VMEM] * (chips + 1),
        scratch_shapes=[pltpu.VMEM((chips * cores, block, DH), F32)],
        compiler_params=params(),
        name="second",
    )(*got1, token)
    msgs, later = outs[:chips], outs[chips]
    got2 = exchange_ring(msgs, "z")
    held, token = sweep(units[3:5], held, later)
    sent, kept = pl.pallas_call(
        lambda *refs: swap_kernel(chips, *refs),
        out_shape=[shape(((chips + 1) * block, DH), BF16)] * 2,
        in_specs=[VMEM] * chips + [ANY],
        out_specs=[VMEM, VMEM],
        compiler_params=params(),
        name="swap",
    )(*got2, token)
    swapped = exchange([kept, sent], "core")[1]
    held, token = sweep(units[5:6], held, kept)
    msgs = pl.pallas_call(
        lambda *refs: third_kernel(n, chips, *refs),
        out_shape=[shape(((responses + 1) * block, DH), BF16)] * n,
        in_specs=[VMEM] * (n + 2) + [ANY],
        out_specs=[VMEM] * n,
        compiler_params=params(),
        name="third",
    )(*got1, kept, swapped, token)
    got3 = exchange(msgs, "prompt")
    held, token = sweep(units[6:], held, msgs[0], range(responses - 1))
    partial_out, partial_dq, query, grad_out, resp_dk, resp_dv = held

    resp_out, resp_dq, prompt_dk, prompt_dv = pl.pallas_call(
        lambda *refs: last_kernel(n, responses, *refs),
        out_shape=[like_out] * 2 + [shape(keys.shape, BF16)] * 2,
        in_specs=[VMEM] * (8 + n) + [ANY],
        out_specs=[ANY] * 4,
        scratch_shapes=[
            pltpu.VMEM((responses + 1, width, width), BF16),
            pltpu.VMEM(queries.shape, BF16),
            pltpu.VMEM(queries.shape, BF16),
            pltpu.VMEM(keys.shape[1:], BF16),
            pltpu.VMEM(keys.shape[1:], BF16),
            pltpu.SemaphoreType.DMA((2 + 2 * responses,)),
        ],
        compiler_params=params(),
        name="last",
    )(cols, query, grad_out, partial_out, partial_dq, keys, values, later, *got3, token)
    return (resp_out, resp_dq, resp_dk, resp_dv, prompt_dk, prompt_dv)


def solution(mesh):
    n, count = mesh.shape["prompt"], mesh.shape["resp"]
    mesh = jax.sharding.Mesh(mesh.devices.reshape(n, count // 2, 2), ("prompt", "z", "core"))
    spread = P(("prompt", "z", "core"))
    three = P(("prompt", "z", "core"), None, None)
    two = P(("prompt", "z", "core"), None)
    prompt = P(("z", "core"), "prompt", None)
    return jax.shard_map(
        shards,
        mesh=mesh,
        in_specs=(
            prompt,
            prompt,
            P(("z", "core"), None, "prompt"),
            three,
            three,
            three,
            three,
            three,
            spread,
            two,
            two,
            spread,
        ),
        out_specs=(three, three, three, three, prompt, prompt),
        check_vma=False,
    )
```

```python
import jax
import jax.numpy as jnp
from jax import lax
from jax.experimental import pallas as pl
from jax.experimental.pallas import tpu as pltpu
from jax.sharding import PartitionSpec as P

H = 2
DH = 128
HALF = 256
LOG2E = 1.4426950408889634
F32 = jnp.float32
BF16 = jnp.bfloat16
NEVER = -1e30
VMEM = pl.BlockSpec(memory_space=pltpu.VMEM)
ANY = pl.BlockSpec(memory_space=pl.ANY)
SMEM = pl.BlockSpec(memory_space=pltpu.SMEM)


def params(mebibytes=16):
    return pltpu.CompilerParams(vmem_limit_bytes=mebibytes * 1024 * 1024)


def mm(a, b):
    return lax.dot_general(a, b, (((1,), (0,)), ((), ())), preferred_element_type=F32)


def mm_nt(a, b):
    return lax.dot_general(a, b, (((1,), (1,)), ((), ())), preferred_element_type=F32)


def mm_tn(a, b):
    return lax.dot_general(a, b, (((0,), (0,)), ((), ())), preferred_element_type=F32)


def to_columns(rows):
    return jnp.concatenate([rows, jnp.zeros((128 - rows.shape[0], rows.shape[1]), F32)], axis=0).T


def in_hbm(x):
    return pltpu.with_memory_space_constraint(x, pltpu.HBM)


def three_terms(x):
    high = x.astype(BF16)
    rest = x - high.astype(F32)
    middle = rest.astype(BF16)
    return high, middle, (rest - middle.astype(F32)).astype(BF16)


def lane_cumsum(x):
    rows, width = x.shape
    ones = lax.broadcasted_iota(jnp.int32, (128, 128), 0) <= lax.broadcasted_iota(jnp.int32, (128, 128), 1)
    terms = jnp.concatenate(three_terms(x), axis=0)
    starts = range(0, width, 128)
    sums = mm(jnp.concatenate([terms[:, b : b + 128] for b in starts], axis=0), ones.astype(F32).astype(BF16))
    parts = []
    before = jnp.zeros((rows, 1), F32)
    for b in range(len(starts)):
        at = 3 * rows * b
        part = sums[at : at + rows] + sums[at + rows : at + 2 * rows] + sums[at + 2 * rows : at + 3 * rows]
        part = part + before
        before = part[:, 127:128]
        parts.append(part)
    return jnp.concatenate(parts, axis=1)


def first_kernel(
    n, ids_hbm, lens_hbm, adv_hbm, keys_hbm, values_hbm, pgates_hbm, gates_hbm, mask_hbm, q_hbm, c_hbm, k_hbm, v_hbm,
    *refs,
):
    msgs, (rows_ref, q, c, k_out, v_out) = refs[:n], refs[n : n + 5]
    keys, values, pgates, gates, mask, ids_ref, lens_ref, adv_ref, matrices, sems = refs[n + 5 :]
    pairs = [(pgates_hbm, pgates), (gates_hbm, gates), (lens_hbm, lens_ref), (adv_hbm, adv_ref), (mask_hbm, mask)]
    pairs += [(keys_hbm, keys), (values_hbm, values), (q_hbm, q), (c_hbm, c), (ids_hbm, ids_ref)]
    pairs += [(k_hbm, k_out), (v_hbm, v_out)]
    copies = [pltpu.make_async_copy(a, b, sems.at[i]) for i, (a, b) in enumerate(pairs)]
    for copy in copies[:10]:
        copy.start()
    count = gates.shape[0]
    slots = gates.shape[2]
    tokens = keys.shape[1]
    part = DH // n
    block = H * part
    targets = partners(n)

    def spread(at):
        for k in range(n):
            of = pl.ds(pl.multiple_of(targets[k] * part, part), part)
            msgs[k][at * part + (16 if at >= H else 0) : (at + 1) * part + (16 if at >= H else 0), :] = matrices[
                at, of, :
            ].astype(BF16)

    copies[0].wait()
    copies[1].wait()
    for copy in copies[10:]:
        copy.start()
    piece = jnp.concatenate([pgates[0], jnp.zeros((H, slots - tokens), F32)], axis=1)
    gate_rows = [gates[i] for i in range(count)] + [piece, jnp.zeros((16 - H * (count + 1), slots), F32)]
    cum = lane_cumsum(jnp.concatenate(gate_rows, axis=0))
    carried = jnp.exp(cum)
    place = lax.broadcasted_iota(jnp.int32, (1, slots), 1)
    for copy in copies[2:5]:
        copy.wait()
    rows = []
    factors = []
    for i in range(count):
        weight = adv_ref[i].astype(F32) / 1024.0
        opened = jnp.where(place < lens_ref[0, i], 1.0, 0.0)
        live = mask[i : i + 1, :].astype(F32) * opened * weight
        rows += [cum[H * i : H * i + H], carried[H * i : H * i + H] * opened, live, opened, jnp.zeros((2, slots), F32)]
        factors.append(carried[H * i : H * i + H] * live)
    piece = cum[H * count : H * count + H]
    total = piece[:, -1:]
    suffix = total - piece
    rows += [suffix, jnp.zeros((8 - H, slots), F32)]
    rows_ref[...] = jnp.concatenate(rows, axis=0)

    copies[5].wait()
    copies[6].wait()
    turned = keys[0].T
    later = jnp.exp(suffix[:, :tokens])
    for h in range(H):
        lanes = slice(h * DH, (h + 1) * DH)
        scaled = turned[lanes].astype(F32) * later[h : h + 1]
        high = scaled.astype(BF16)
        low = (scaled - high.astype(F32)).astype(BF16)
        both = mm(jnp.concatenate([high, low], axis=0), values[0, :, lanes])
        matrices[h] = both[:DH] + both[DH:]
        spread(h)
    copies[7].wait()
    copies[8].wait()
    for i in range(count):
        turned = q[i].T
        for h in range(H):
            lanes = slice(h * DH, (h + 1) * DH)
            scaled = (turned[lanes].astype(F32) * factors[i][h : h + 1]).astype(BF16)
            matrices[H * (1 + i) + h] = mm(scaled, c[i, :, lanes])
            spread(H * (1 + i) + h)
    copies[9].wait()
    notes = [jnp.broadcast_to(x[h : h + 1].astype(F32), (1, DH)) for x in three_terms(total) for h in range(H)]
    notes += [jnp.full((1, DH), ids_ref[i].astype(F32)) for i in range(count)]
    notes.append(jnp.zeros((16 - len(notes), DH), F32))
    notes = jnp.concatenate(notes, axis=0).astype(BF16)
    for k in range(n):
        msgs[k][block : block + 16, :] = notes
    for copy in copies[10:]:
        copy.wait()


def noted_prompt(notes, i):
    return jnp.max(notes[3 * H + i : 3 * H + i + 1]).astype(jnp.int32)


def second_kernel(n, chips, cores, *refs):
    z_at = lax.axis_index("z")
    got, msgs, later_ref, sums = far_first(refs[:n]), refs[n + 1 : n + 1 + chips], refs[-2], refs[-1]
    part = DH // n
    block = H * part
    responses = (got[0].shape[0] - block - 16) // block
    place = partners(n)
    notes = [got[k][block : block + 16, :].astype(F32) for k in range(n)]
    logs = [x[0:H] + x[H : 2 * H] + x[2 * H : 3 * H] for x in notes]
    final = jnp.zeros((block, DH), F32)
    for k in range(n):
        later = jnp.zeros_like(logs[0])
        for other in range(n):
            if other != k:
                later = later + jnp.where(place[other] > place[k], logs[other], 0.0)
        if k == 0:
            later_ref[...] = jnp.concatenate([later, jnp.zeros((8 - H, DH), F32)], axis=0)
        decay = jnp.exp(later)
        decay = [jnp.broadcast_to(decay[h : h + 1], (part, DH)) for h in range(H)]
        final = final + jnp.concatenate(decay, axis=0) * got[k][0:block, :].astype(F32)
    sums[...] = jnp.zeros_like(sums)
    for k in range(n):
        for i in range(responses):
            at = block * (1 + i) + 16
            sums[noted_prompt(notes[k], i)] += got[k][at : at + block, :].astype(F32)
    final = final.astype(BF16)
    for k in range(chips):
        z = lax.rem(z_at + k, chips)
        msgs[k][0:block, :] = final
        for c in range(cores):
            msgs[k][(1 + c) * block : (2 + c) * block, :] = sums[z * cores + c].astype(BF16)


def swap_kernel(chips, *refs):
    got, sent_ref, kept_ref = refs[:chips], refs[chips + 1], refs[chips + 2]
    block = got[0].shape[0] // 3
    totals = []
    for c in range(2):
        total = got[0][(1 + c) * block : (2 + c) * block, :].astype(F32)
        for k in range(1, chips):
            total = total + got[k][(1 + c) * block : (2 + c) * block, :].astype(F32)
        totals.append(total)
    for k in range(chips):
        final = got[k][0:block, :]
        sent_ref[k * block : (k + 1) * block, :] = final
        kept_ref[k * block : (k + 1) * block, :] = final
    low = lax.axis_index("core") == 0
    sent_ref[chips * block :, :] = jnp.where(low, totals[1], totals[0]).astype(BF16)
    kept_ref[chips * block :, :] = jnp.where(low, totals[0], totals[1]).astype(BF16)


def third_kernel(n, chips, *refs):
    z_at, core = lax.axis_index("z"), lax.axis_index("core")
    noted, kept_ref, got_ref, msgs = far_first(refs[:n]), refs[n], refs[n + 1], refs[n + 3 :]
    block = H * DH // n
    responses = (noted[0].shape[0] - block - 16) // block
    total = kept_ref[chips * block :, :].astype(F32) + got_ref[chips * block :, :].astype(F32)
    total = total.astype(BF16)
    for k in range(n):
        notes = noted[k][block : block + 16, :].astype(F32)
        for i in range(responses):
            p = noted_prompt(notes, i)
            slot = lax.rem(z_at + chips - lax.div(p, 2), chips)
            at = pl.ds(pl.multiple_of(slot * block, block), block)
            same = lax.rem(p, 2) == core
            state = jnp.where(same, kept_ref[at, :].astype(F32), got_ref[at, :].astype(F32))
            msgs[k][i * block : (i + 1) * block, :] = state.astype(BF16)
        msgs[k][responses * block :, :] = total


def sweep_kernel(units, done, rows_ref, q_ref, k_ref, v_ref, c_ref, cols_ref, *refs):
    writes = len(done) > 0
    if writes:
        *refs, dk_hbm, dv_hbm, sems = refs
    out_ref, dq_ref, query_ref, grad_ref, dk_ref, dv_ref, token_ref = refs[-7:]
    if cols_ref is None:
        cols_ref = refs[0]
        cols_ref[...] = to_columns(rows_ref[...])
    copies = []

    def send(r):
        for a, b in ((dk_ref, dk_hbm), (dv_ref, dv_hbm)):
            copies.append(pltpu.make_async_copy(a.at[r], b.at[r], sems.at[len(copies)]))
            copies[-1].start()

    for r in done:
        send(r)
    token_ref[...] = jnp.zeros_like(token_ref)
    quarter = HALF // 2
    causal = lax.broadcasted_iota(jnp.int32, (quarter, quarter), 0) >= lax.broadcasted_iota(
        jnp.int32, (quarter, quarter), 1
    )
    blank = jnp.zeros((quarter, quarter), BF16)
    blocks = q_ref.shape[1] // HALF

    def decayed(products, cum, row, diagonal):
        if not diagonal:
            decay = jnp.exp2(cum - row)
            return [(x * decay).astype(BF16) for x in products]
        first = jnp.exp2(jnp.where(causal, cum[:quarter] - row[:, :quarter], NEVER))
        left = jnp.exp2(cum[quarter:] - row[:, :quarter])
        right = jnp.exp2(jnp.where(causal, cum[quarter:] - row[:, quarter:], NEVER))
        results = []
        for x in products:
            upper = jnp.concatenate([(x[:quarter, :quarter] * first).astype(BF16), blank], axis=1)
            lower = [(x[quarter:, :quarter] * left).astype(BF16), (x[quarter:, quarter:] * right).astype(BF16)]
            results.append(jnp.concatenate([upper, jnp.concatenate(lower, axis=1)], axis=0))
        return results

    for r, h in units:
        lanes = slice(h * DH, (h + 1) * DH)
        cum = cols_ref[:, 8 * r + h : 8 * r + h + 1] * LOG2E
        row = rows_ref[8 * r + h : 8 * r + h + 1, :] * LOG2E
        live = cols_ref[:, 8 * r + 4 : 8 * r + 5]
        opened = cols_ref[:, 8 * r + 5 : 8 * r + 6]
        grad_all = (c_ref[r, :, lanes].astype(F32) * live).astype(BF16)
        carried = cols_ref[:, 8 * r + 2 + h : 8 * r + 3 + h]
        query_ref[r, :, lanes] = (q_ref[r, :, lanes].astype(F32) * carried).astype(BF16)
        grad_ref[r, :, lanes] = (grad_all.astype(F32) * carried).astype(BF16)
        query_turned = q_ref[r, :, lanes].T
        grad_turned = grad_all.T
        dk = [None] * blocks
        dv = [None] * blocks
        for t in range(blocks):
            at = slice(t * HALF, (t + 1) * HALF)
            query = q_ref[r, at, lanes]
            grad_out = grad_all[at]
            out = None
            dq = None
            for s in range(t + 1):
                of = slice(s * HALF, (s + 1) * HALF)
                key = k_ref[r, of, lanes]
                value = v_ref[r, of, lanes]
                mixing, scores = decayed(
                    [mm_nt(query, key), mm_nt(grad_out, value)], cum[at], row[:, of], s == t
                )
                o_new = mm(mixing, value)
                q_new = mm(scores, key)
                k_new = mm(query_turned[:, at], scores)
                v_new = mm(grad_turned[:, at], mixing)
                out = o_new if out is None else out + o_new
                dq = q_new if dq is None else dq + q_new
                dk[s] = k_new if dk[s] is None else dk[s] + k_new
                dv[s] = v_new if dv[s] is None else dv[s] + v_new
            out_ref[r, at, lanes] = out * opened[at]
            dq_ref[r, at, lanes] = dq
        for s in range(blocks):
            of = slice(s * HALF, (s + 1) * HALF)
            dk_ref[r, of, lanes] = dk[s].astype(BF16).T
            dv_ref[r, of, lanes] = dv[s].astype(BF16).T
        if writes and h == H - 1:
            send(r)
    for copy in copies:
        copy.wait()


def last_kernel(
    n, count, cols_ref, q_ref, grad_ref, po_ref, pdq_ref, keys_ref, values_ref, later_ref, *refs
):
    got, refs = refs[:n], refs[n + 1 :]
    out_hbm, dq_hbm, dk_hbm, dv_hbm, start, turned, out_buf, dq_buf, dk_buf, dv_buf, sems = refs
    part = DH // n
    block = H * part
    place = partners(n)
    slots = q_ref.shape[1]
    tokens = keys_ref.shape[1]
    copies = []

    def send(a, b):
        copies.append(pltpu.make_async_copy(a, b, sems.at[len(copies)]))
        copies[-1].start()

    start[...] = jnp.zeros_like(start)
    turned[...] = jnp.zeros_like(turned)
    for r in range(count + 1):
        for h in range(H):
            lanes = slice(h * DH, (h + 1) * DH)
            for k in range(n):
                of = pl.ds(pl.multiple_of(h * DH + place[k] * part, part), part)
                start[r, of, lanes] = got[k][r * block + h * part : r * block + (h + 1) * part, :]
            turned[r, lanes, lanes] = start[r, lanes, lanes].T
    for r in range(count):
        for t in range(0, slots, HALF):
            at = slice(t, t + HALF)
            out_buf[r, at, :] = (po_ref[r, at, :] + mm(q_ref[r, at, :], start[r])).astype(BF16)
            dq_buf[r, at, :] = (pdq_ref[r, at, :] + mm(grad_ref[r, at, :], turned[r])).astype(BF16)
        send(out_buf.at[r], out_hbm.at[r])
        send(dq_buf.at[r], dq_hbm.at[r])
    factor = [
        jnp.exp(cols_ref[:tokens, 8 * count + h : 8 * count + h + 1] + later_ref[h : h + 1, 0:1]) for h in range(H)
    ]
    for buf, x in ((dk_buf, mm(values_ref[0], turned[count])), (dv_buf, mm(keys_ref[0], start[count]))):
        for h in range(H):
            lanes = slice(h * DH, (h + 1) * DH)
            buf[:, lanes] = (factor[h] * x[:, lanes]).astype(BF16)
    send(dk_buf, dk_hbm.at[0])
    send(dv_buf, dv_hbm.at[0])
    for copy in copies:
        copy.wait()


def exchange(xs, axis):
    n = lax.axis_size(axis)
    return [xs[0]] + [lax.ppermute(xs[k], axis, [(s, s ^ k) for s in range(n)]) for k in range(1, n)]


def exchange_ring(xs, axis):
    n = lax.axis_size(axis)
    return [xs[0]] + [lax.ppermute(xs[k], axis, [(s, (s + k) % n) for s in range(n)]) for k in range(1, n)]


def far_first(refs):
    return [refs[0], *refs[:0:-1]]


def partners(n):
    me = lax.axis_index("prompt")
    return [lax.bitwise_xor(me, k) for k in range(n)]


def shards(
    keys,
    values,
    prompt_gates,
    queries,
    resp_keys,
    resp_values,
    resp_gates,
    cotangent,
    group_ids,
    resp_lengths,
    loss_mask,
    advantages,
):
    n = lax.axis_size("prompt")
    chips = lax.axis_size("z")
    cores = lax.axis_size("core")
    responses, slots, width = queries.shape
    block = H * DH // n
    shape = jax.ShapeDtypeStruct

    outs = pl.pallas_call(
        lambda *refs: first_kernel(n, *refs),
        out_shape=[shape((block * (1 + responses) + 16, DH), BF16)] * n
        + [shape((8 * (responses + 1), slots), F32)]
        + [shape(queries.shape, BF16)] * 4,
        in_specs=[ANY] * 12,
        out_specs=[VMEM] * (n + 5),
        scratch_shapes=[
            pltpu.VMEM(keys.shape, BF16),
            pltpu.VMEM(values.shape, BF16),
            pltpu.VMEM(prompt_gates.shape, F32),
            pltpu.VMEM(resp_gates.shape, F32),
            pltpu.VMEM(loss_mask.shape, jnp.int32),
            pltpu.SMEM(group_ids.shape, jnp.int32),
            pltpu.SMEM(resp_lengths.shape, jnp.int32),
            pltpu.SMEM(advantages.shape, jnp.int32),
            pltpu.VMEM((H * (1 + responses), DH, DH), F32),
            pltpu.SemaphoreType.DMA((12,)),
        ],
        compiler_params=params(32),
        name="first",
    )(
        *[in_hbm(x) for x in (group_ids, resp_lengths, advantages, keys, values, prompt_gates, resp_gates)],
        *[in_hbm(x) for x in (loss_mask, queries, cotangent, resp_keys, resp_values)],
    )
    msgs, (rows, queries, cotangent, resp_keys, resp_values) = outs[:n], outs[n:]

    like = shape(queries.shape, F32)
    like_out = shape(queries.shape, BF16)

    held_shapes = [like, like] + [like_out] * 4 + [shape((8, 128), F32)]

    def first_sweep(units):
        outs = pl.pallas_call(
            lambda *refs: sweep_kernel(units, (), *refs[:5], None, *refs[5:]),
            out_shape=[shape((slots, 128), F32)] + held_shapes,
            in_specs=[VMEM] * 5,
            out_specs=[VMEM] * 8,
            compiler_params=params(),
            name="sweep",
        )(rows, queries, resp_keys, resp_values, cotangent)
        return outs[0], outs[1:7], outs[7]

    def sweep(units, before, token, done=()):
        writes = len(done) > 0
        outs = pl.pallas_call(
            lambda *refs: sweep_kernel(units, done, *refs),
            out_shape=held_shapes + [like_out] * (2 * writes),
            in_specs=[VMEM] * 6 + [ANY] * 7,
            out_specs=[VMEM] * 7 + [ANY] * (2 * writes),
            scratch_shapes=[pltpu.SemaphoreType.DMA((2 * responses,))] * writes,
            input_output_aliases={7 + k: k for k in range(6)},
            compiler_params=params(),
            name="sweep",
        )(rows, queries, resp_keys, resp_values, cotangent, cols, token, *before)
        return (outs[:4] + outs[7:] if writes else outs[:6]), outs[6]

    units = [(r, h) for r in range(responses) for h in range(H)]
    got1 = far_first(exchange(msgs, "prompt"))
    cols, held, token = first_sweep(units[:3])
    outs = pl.pallas_call(
        lambda *refs: second_kernel(n, chips, cores, *refs),
        out_shape=[shape(((1 + cores) * block, DH), BF16)] * chips + [shape((8, DH), F32)],
        in_specs=[VMEM] * n + [ANY],
        out_specs=[VMEM] * (chips + 1),
        scratch_shapes=[pltpu.VMEM((chips * cores, block, DH), F32)],
        compiler_params=params(),
        name="second",
    )(*got1, token)
    msgs, later = outs[:chips], outs[chips]
    got2 = exchange_ring(msgs, "z")
    held, token = sweep(units[3:5], held, later)
    sent, kept = pl.pallas_call(
        lambda *refs: swap_kernel(chips, *refs),
        out_shape=[shape(((chips + 1) * block, DH), BF16)] * 2,
        in_specs=[VMEM] * chips + [ANY],
        out_specs=[VMEM, VMEM],
        compiler_params=params(),
        name="swap",
    )(*got2, token)
    swapped = exchange([kept, sent], "core")[1]
    held, token = sweep(units[5:6], held, kept)
    msgs = pl.pallas_call(
        lambda *refs: third_kernel(n, chips, *refs),
        out_shape=[shape(((responses + 1) * block, DH), BF16)] * n,
        in_specs=[VMEM] * (n + 2) + [ANY],
        out_specs=[VMEM] * n,
        compiler_params=params(),
        name="third",
    )(*got1, kept, swapped, token)
    got3 = exchange(msgs, "prompt")
    held, token = sweep(units[6:], held, msgs[0], range(responses - 1))
    partial_out, partial_dq, query, grad_out, resp_dk, resp_dv = held

    resp_out, resp_dq, prompt_dk, prompt_dv = pl.pallas_call(
        lambda *refs: last_kernel(n, responses, *refs),
        out_shape=[like_out] * 2 + [shape(keys.shape, BF16)] * 2,
        in_specs=[VMEM] * (8 + n) + [ANY],
        out_specs=[ANY] * 4,
        scratch_shapes=[
            pltpu.VMEM((responses + 1, width, width), BF16),
            pltpu.VMEM((responses + 1, width, width), BF16),
            pltpu.VMEM(queries.shape, BF16),
            pltpu.VMEM(queries.shape, BF16),
            pltpu.VMEM(keys.shape[1:], BF16),
            pltpu.VMEM(keys.shape[1:], BF16),
            pltpu.SemaphoreType.DMA((2 + 2 * responses,)),
        ],
        compiler_params=params(),
        name="last",
    )(cols, query, grad_out, partial_out, partial_dq, keys, values, later, *got3, token)
    return (resp_out, resp_dq, resp_dk, resp_dv, prompt_dk, prompt_dv)


def solution(mesh):
    n, count = mesh.shape["prompt"], mesh.shape["resp"]
    mesh = jax.sharding.Mesh(mesh.devices.reshape(n, count // 2, 2), ("prompt", "z", "core"))
    spread = P(("prompt", "z", "core"))
    three = P(("prompt", "z", "core"), None, None)
    two = P(("prompt", "z", "core"), None)
    prompt = P(("z", "core"), "prompt", None)
    return jax.shard_map(
        shards,
        mesh=mesh,
        in_specs=(
            prompt,
            prompt,
            P(("z", "core"), None, "prompt"),
            three,
            three,
            three,
            three,
            three,
            spread,
            two,
            two,
            spread,
        ),
        out_specs=(three, three, three, three, prompt, prompt),
        check_vma=False,
    )
```

```python
import jax
import jax.numpy as jnp
from jax import lax
from jax.experimental import pallas as pl
from jax.experimental.pallas import tpu as pltpu
from jax.sharding import PartitionSpec as P

H = 2
DH = 128
HALF = 256
LOG2E = 1.4426950408889634
F32 = jnp.float32
BF16 = jnp.bfloat16
NEVER = -1e30
VMEM = pl.BlockSpec(memory_space=pltpu.VMEM)
ANY = pl.BlockSpec(memory_space=pl.ANY)
SMEM = pl.BlockSpec(memory_space=pltpu.SMEM)


def params(mebibytes=16):
    return pltpu.CompilerParams(vmem_limit_bytes=mebibytes * 1024 * 1024)


def mm(a, b):
    return lax.dot_general(a, b, (((1,), (0,)), ((), ())), preferred_element_type=F32)


def mm_nt(a, b):
    return lax.dot_general(a, b, (((1,), (1,)), ((), ())), preferred_element_type=F32)


def mm_tn(a, b):
    return lax.dot_general(a, b, (((0,), (0,)), ((), ())), preferred_element_type=F32)


def to_columns(rows):
    return jnp.concatenate([rows, jnp.zeros((128 - rows.shape[0], rows.shape[1]), F32)], axis=0).T


def in_hbm(x):
    return pltpu.with_memory_space_constraint(x, pltpu.HBM)


def three_terms(x):
    high = x.astype(BF16)
    rest = x - high.astype(F32)
    middle = rest.astype(BF16)
    return high, middle, (rest - middle.astype(F32)).astype(BF16)


def lane_cumsum(x):
    rows, width = x.shape
    ones = lax.broadcasted_iota(jnp.int32, (128, 128), 0) <= lax.broadcasted_iota(jnp.int32, (128, 128), 1)
    terms = jnp.concatenate(three_terms(x), axis=0)
    starts = range(0, width, 128)
    sums = mm(jnp.concatenate([terms[:, b : b + 128] for b in starts], axis=0), ones.astype(F32).astype(BF16))
    parts = []
    before = jnp.zeros((rows, 1), F32)
    for b in range(len(starts)):
        at = 3 * rows * b
        part = sums[at : at + rows] + sums[at + rows : at + 2 * rows] + sums[at + 2 * rows : at + 3 * rows]
        part = part + before
        before = part[:, 127:128]
        parts.append(part)
    return jnp.concatenate(parts, axis=1)


def first_kernel(
    n, ids_hbm, lens_hbm, adv_hbm, keys_hbm, values_hbm, pgates_hbm, gates_hbm, mask_hbm, q_hbm, c_hbm,
    *refs,
):
    msgs, (rows_ref, q, c) = refs[:n], refs[n : n + 3]
    keys, values, pgates, gates, mask, ids_ref, lens_ref, adv_ref, matrices, sems = refs[n + 3 :]
    pairs = [(pgates_hbm, pgates), (gates_hbm, gates), (lens_hbm, lens_ref), (adv_hbm, adv_ref), (mask_hbm, mask)]
    pairs += [(keys_hbm, keys), (values_hbm, values), (q_hbm, q), (c_hbm, c), (ids_hbm, ids_ref)]
    copies = [pltpu.make_async_copy(a, b, sems.at[i]) for i, (a, b) in enumerate(pairs)]
    for copy in copies:
        copy.start()
    count = gates.shape[0]
    slots = gates.shape[2]
    tokens = keys.shape[1]
    part = DH // n
    block = H * part
    targets = partners(n)

    def spread(at):
        for k in range(n):
            of = pl.ds(pl.multiple_of(targets[k] * part, part), part)
            msgs[k][at * part + (16 if at >= H else 0) : (at + 1) * part + (16 if at >= H else 0), :] = matrices[
                at, of, :
            ].astype(BF16)

    copies[0].wait()
    copies[1].wait()
    piece = jnp.concatenate([pgates[0], jnp.zeros((H, slots - tokens), F32)], axis=1)
    gate_rows = [gates[i] for i in range(count)] + [piece, jnp.zeros((16 - H * (count + 1), slots), F32)]
    cum = lane_cumsum(jnp.concatenate(gate_rows, axis=0))
    carried = jnp.exp(cum)
    place = lax.broadcasted_iota(jnp.int32, (1, slots), 1)
    for copy in copies[2:5]:
        copy.wait()
    rows = []
    factors = []
    for i in range(count):
        weight = adv_ref[i].astype(F32) / 1024.0
        opened = jnp.where(place < lens_ref[0, i], 1.0, 0.0)
        live = mask[i : i + 1, :].astype(F32) * opened * weight
        rows += [cum[H * i : H * i + H], carried[H * i : H * i + H] * opened, live, opened, jnp.zeros((2, slots), F32)]
        factors.append(carried[H * i : H * i + H] * live)
    piece = cum[H * count : H * count + H]
    total = piece[:, -1:]
    suffix = total - piece
    rows += [suffix, jnp.zeros((8 - H, slots), F32)]
    rows_ref[...] = jnp.concatenate(rows, axis=0)

    copies[5].wait()
    copies[6].wait()
    turned = keys[0].T
    later = jnp.exp(suffix[:, :tokens])
    for h in range(H):
        lanes = slice(h * DH, (h + 1) * DH)
        scaled = turned[lanes].astype(F32) * later[h : h + 1]
        high = scaled.astype(BF16)
        low = (scaled - high.astype(F32)).astype(BF16)
        both = mm(jnp.concatenate([high, low], axis=0), values[0, :, lanes])
        matrices[h] = both[:DH] + both[DH:]
        spread(h)
    copies[7].wait()
    copies[8].wait()
    for i in range(count):
        turned = q[i].T
        for h in range(H):
            lanes = slice(h * DH, (h + 1) * DH)
            scaled = (turned[lanes].astype(F32) * factors[i][h : h + 1]).astype(BF16)
            matrices[H * (1 + i) + h] = mm(scaled, c[i, :, lanes])
            spread(H * (1 + i) + h)
    copies[9].wait()
    notes = [jnp.broadcast_to(x[h : h + 1].astype(F32), (1, DH)) for x in three_terms(total) for h in range(H)]
    notes += [jnp.full((1, DH), ids_ref[i].astype(F32)) for i in range(count)]
    notes.append(jnp.zeros((16 - len(notes), DH), F32))
    notes = jnp.concatenate(notes, axis=0).astype(BF16)
    for k in range(n):
        msgs[k][block : block + 16, :] = notes


def noted_prompt(notes, i):
    return jnp.max(notes[3 * H + i : 3 * H + i + 1]).astype(jnp.int32)


def second_kernel(n, chips, cores, *refs):
    z_at = lax.axis_index("z")
    got, msgs, later_ref, sums = far_first(refs[:n]), refs[n + 1 : n + 1 + chips], refs[-2], refs[-1]
    part = DH // n
    block = H * part
    responses = (got[0].shape[0] - block - 16) // block
    place = partners(n)
    notes = [got[k][block : block + 16, :].astype(F32) for k in range(n)]
    logs = [x[0:H] + x[H : 2 * H] + x[2 * H : 3 * H] for x in notes]
    final = jnp.zeros((block, DH), F32)
    for k in range(n):
        later = jnp.zeros_like(logs[0])
        for other in range(n):
            if other != k:
                later = later + jnp.where(place[other] > place[k], logs[other], 0.0)
        if k == 0:
            later_ref[...] = jnp.concatenate([later, jnp.zeros((8 - H, DH), F32)], axis=0)
        decay = jnp.exp(later)
        decay = [jnp.broadcast_to(decay[h : h + 1], (part, DH)) for h in range(H)]
        final = final + jnp.concatenate(decay, axis=0) * got[k][0:block, :].astype(F32)
    sums[...] = jnp.zeros_like(sums)
    for k in range(n):
        for i in range(responses):
            at = block * (1 + i) + 16
            sums[noted_prompt(notes[k], i)] += got[k][at : at + block, :].astype(F32)
    final = final.astype(BF16)
    for k in range(chips):
        z = lax.rem(z_at + k, chips)
        msgs[k][0:block, :] = final
        for c in range(cores):
            msgs[k][(1 + c) * block : (2 + c) * block, :] = sums[z * cores + c].astype(BF16)


def swap_kernel(chips, *refs):
    got, sent_ref, kept_ref = refs[:chips], refs[chips + 1], refs[chips + 2]
    block = got[0].shape[0] // 3
    totals = []
    for c in range(2):
        total = got[0][(1 + c) * block : (2 + c) * block, :].astype(F32)
        for k in range(1, chips):
            total = total + got[k][(1 + c) * block : (2 + c) * block, :].astype(F32)
        totals.append(total)
    for k in range(chips):
        final = got[k][0:block, :]
        sent_ref[k * block : (k + 1) * block, :] = final
        kept_ref[k * block : (k + 1) * block, :] = final
    low = lax.axis_index("core") == 0
    sent_ref[chips * block :, :] = jnp.where(low, totals[1], totals[0]).astype(BF16)
    kept_ref[chips * block :, :] = jnp.where(low, totals[0], totals[1]).astype(BF16)


def third_kernel(n, chips, *refs):
    z_at, core = lax.axis_index("z"), lax.axis_index("core")
    noted, kept_ref, got_ref, msgs = far_first(refs[:n]), refs[n], refs[n + 1], refs[n + 3 :]
    block = H * DH // n
    responses = (noted[0].shape[0] - block - 16) // block
    total = kept_ref[chips * block :, :].astype(F32) + got_ref[chips * block :, :].astype(F32)
    total = total.astype(BF16)
    for k in range(n):
        notes = noted[k][block : block + 16, :].astype(F32)
        for i in range(responses):
            p = noted_prompt(notes, i)
            slot = lax.rem(z_at + chips - lax.div(p, 2), chips)
            at = pl.ds(pl.multiple_of(slot * block, block), block)
            same = lax.rem(p, 2) == core
            state = jnp.where(same, kept_ref[at, :].astype(F32), got_ref[at, :].astype(F32))
            msgs[k][i * block : (i + 1) * block, :] = state.astype(BF16)
        msgs[k][responses * block :, :] = total


def sweep_kernel(units, done, rows_ref, q_ref, k_ref, v_ref, c_ref, cols_ref, *refs):
    writes = len(done) > 0
    if writes:
        *refs, dk_hbm, dv_hbm, sems = refs
    out_ref, dq_ref, query_ref, grad_ref, dk_ref, dv_ref, token_ref = refs[-7:]
    if cols_ref is None:
        cols_ref = refs[0]
        cols_ref[...] = to_columns(rows_ref[...])
    copies = []

    def send(r):
        for a, b in ((dk_ref, dk_hbm), (dv_ref, dv_hbm)):
            copies.append(pltpu.make_async_copy(a.at[r], b.at[r], sems.at[len(copies)]))
            copies[-1].start()

    for r in done:
        send(r)
    token_ref[...] = jnp.zeros_like(token_ref)
    quarter = HALF // 2
    causal = lax.broadcasted_iota(jnp.int32, (quarter, quarter), 0) >= lax.broadcasted_iota(
        jnp.int32, (quarter, quarter), 1
    )
    blank = jnp.zeros((quarter, quarter), BF16)
    blocks = q_ref.shape[1] // HALF

    def decayed(products, cum, row, diagonal):
        if not diagonal:
            decay = jnp.exp2(cum - row)
            return [(x * decay).astype(BF16) for x in products]
        first = jnp.exp2(jnp.where(causal, cum[:quarter] - row[:, :quarter], NEVER))
        left = jnp.exp2(cum[quarter:] - row[:, :quarter])
        right = jnp.exp2(jnp.where(causal, cum[quarter:] - row[:, quarter:], NEVER))
        results = []
        for x in products:
            upper = jnp.concatenate([(x[:quarter, :quarter] * first).astype(BF16), blank], axis=1)
            lower = [(x[quarter:, :quarter] * left).astype(BF16), (x[quarter:, quarter:] * right).astype(BF16)]
            results.append(jnp.concatenate([upper, jnp.concatenate(lower, axis=1)], axis=0))
        return results

    for r, h in units:
        lanes = slice(h * DH, (h + 1) * DH)
        cum = cols_ref[:, 8 * r + h : 8 * r + h + 1] * LOG2E
        row = rows_ref[8 * r + h : 8 * r + h + 1, :] * LOG2E
        live = cols_ref[:, 8 * r + 4 : 8 * r + 5]
        opened = cols_ref[:, 8 * r + 5 : 8 * r + 6]
        grad_all = (c_ref[r, :, lanes].astype(F32) * live).astype(BF16)
        carried = cols_ref[:, 8 * r + 2 + h : 8 * r + 3 + h]
        query_ref[r, :, lanes] = (q_ref[r, :, lanes].astype(F32) * carried).astype(BF16)
        grad_ref[r, :, lanes] = (grad_all.astype(F32) * carried).astype(BF16)
        query_turned = q_ref[r, :, lanes].T
        grad_turned = grad_all.T
        dk = [None] * blocks
        dv = [None] * blocks
        for t in range(blocks):
            at = slice(t * HALF, (t + 1) * HALF)
            query = q_ref[r, at, lanes]
            grad_out = grad_all[at]
            out = None
            dq = None
            for s in range(t + 1):
                of = slice(s * HALF, (s + 1) * HALF)
                key = k_ref[r, of, lanes]
                value = v_ref[r, of, lanes]
                mixing, scores = decayed(
                    [mm_nt(query, key), mm_nt(grad_out, value)], cum[at], row[:, of], s == t
                )
                o_new = mm(mixing, value)
                q_new = mm(scores, key)
                k_new = mm(query_turned[:, at], scores)
                v_new = mm(grad_turned[:, at], mixing)
                out = o_new if out is None else out + o_new
                dq = q_new if dq is None else dq + q_new
                dk[s] = k_new if dk[s] is None else dk[s] + k_new
                dv[s] = v_new if dv[s] is None else dv[s] + v_new
            out_ref[r, at, lanes] = out * opened[at]
            dq_ref[r, at, lanes] = dq
        for s in range(blocks):
            of = slice(s * HALF, (s + 1) * HALF)
            dk_ref[r, of, lanes] = dk[s].astype(BF16).T
            dv_ref[r, of, lanes] = dv[s].astype(BF16).T
        if writes and h == H - 1:
            send(r)
    for copy in copies:
        copy.wait()


def last_kernel(
    n, count, cols_ref, q_ref, grad_ref, po_ref, pdq_ref, keys_ref, values_ref, later_ref, *refs
):
    got, refs = refs[:n], refs[n + 1 :]
    out_hbm, dq_hbm, dk_hbm, dv_hbm, start, out_buf, dq_buf, dk_buf, dv_buf, sems = refs
    part = DH // n
    block = H * part
    place = partners(n)
    slots = q_ref.shape[1]
    tokens = keys_ref.shape[1]
    copies = []

    def send(a, b):
        copies.append(pltpu.make_async_copy(a, b, sems.at[len(copies)]))
        copies[-1].start()

    start[...] = jnp.zeros_like(start)
    for r in range(count + 1):
        for k in range(n):
            for h in range(H):
                of = pl.ds(pl.multiple_of(h * DH + place[k] * part, part), part)
                rows = got[k][r * block + h * part : r * block + (h + 1) * part, :]
                start[r, of, h * DH : (h + 1) * DH] = rows
    for r in range(count):
        for t in range(0, slots, HALF):
            at = slice(t, t + HALF)
            out_buf[r, at, :] = (po_ref[r, at, :] + mm(q_ref[r, at, :], start[r])).astype(BF16)
            dq_buf[r, at, :] = (pdq_ref[r, at, :] + mm_nt(grad_ref[r, at, :], start[r])).astype(BF16)
        send(out_buf.at[r], out_hbm.at[r])
        send(dq_buf.at[r], dq_hbm.at[r])
    factor = [
        jnp.exp(cols_ref[:tokens, 8 * count + h : 8 * count + h + 1] + later_ref[h : h + 1, 0:1]) for h in range(H)
    ]
    for buf, x in ((dk_buf, mm_nt(values_ref[0], start[count])), (dv_buf, mm(keys_ref[0], start[count]))):
        for h in range(H):
            lanes = slice(h * DH, (h + 1) * DH)
            buf[:, lanes] = (factor[h] * x[:, lanes]).astype(BF16)
    send(dk_buf, dk_hbm.at[0])
    send(dv_buf, dv_hbm.at[0])
    for copy in copies:
        copy.wait()


def exchange(xs, axis):
    n = lax.axis_size(axis)
    return [xs[0]] + [lax.ppermute(xs[k], axis, [(s, s ^ k) for s in range(n)]) for k in range(1, n)]


def exchange_ring(xs, axis):
    n = lax.axis_size(axis)
    return [xs[0]] + [lax.ppermute(xs[k], axis, [(s, (s + k) % n) for s in range(n)]) for k in range(1, n)]


def far_first(refs):
    return [refs[0], *refs[:0:-1]]


def partners(n):
    me = lax.axis_index("prompt")
    return [lax.bitwise_xor(me, k) for k in range(n)]


def shards(
    keys,
    values,
    prompt_gates,
    queries,
    resp_keys,
    resp_values,
    resp_gates,
    cotangent,
    group_ids,
    resp_lengths,
    loss_mask,
    advantages,
):
    n = lax.axis_size("prompt")
    chips = lax.axis_size("z")
    cores = lax.axis_size("core")
    responses, slots, width = queries.shape
    block = H * DH // n
    shape = jax.ShapeDtypeStruct

    outs = pl.pallas_call(
        lambda *refs: first_kernel(n, *refs),
        out_shape=[shape((block * (1 + responses) + 16, DH), BF16)] * n
        + [shape((8 * (responses + 1), slots), F32)]
        + [shape(queries.shape, BF16)] * 2,
        in_specs=[ANY] * 10,
        out_specs=[VMEM] * (n + 3),
        scratch_shapes=[
            pltpu.VMEM(keys.shape, BF16),
            pltpu.VMEM(values.shape, BF16),
            pltpu.VMEM(prompt_gates.shape, F32),
            pltpu.VMEM(resp_gates.shape, F32),
            pltpu.VMEM(loss_mask.shape, jnp.int32),
            pltpu.SMEM(group_ids.shape, jnp.int32),
            pltpu.SMEM(resp_lengths.shape, jnp.int32),
            pltpu.SMEM(advantages.shape, jnp.int32),
            pltpu.VMEM((H * (1 + responses), DH, DH), F32),
            pltpu.SemaphoreType.DMA((10,)),
        ],
        compiler_params=params(32),
        name="first",
    )(
        *[in_hbm(x) for x in (group_ids, resp_lengths, advantages, keys, values, prompt_gates, resp_gates)],
        *[in_hbm(x) for x in (loss_mask, queries, cotangent)],
    )
    msgs, (rows, queries, cotangent) = outs[:n], outs[n:]

    like = shape(queries.shape, F32)
    like_out = shape(queries.shape, BF16)

    held_shapes = [like, like] + [like_out] * 4 + [shape((8, 128), F32)]

    def first_sweep(units):
        outs = pl.pallas_call(
            lambda *refs: sweep_kernel(units, (), *refs[:5], None, *refs[5:]),
            out_shape=[shape((slots, 128), F32)] + held_shapes,
            in_specs=[VMEM] * 5,
            out_specs=[VMEM] * 8,
            compiler_params=params(),
            name="sweep",
        )(rows, queries, resp_keys, resp_values, cotangent)
        return outs[0], outs[1:7], outs[7]

    def sweep(units, before, token, done=()):
        writes = len(done) > 0
        outs = pl.pallas_call(
            lambda *refs: sweep_kernel(units, done, *refs),
            out_shape=held_shapes + [like_out] * (2 * writes),
            in_specs=[VMEM] * 6 + [ANY] * 7,
            out_specs=[VMEM] * 7 + [ANY] * (2 * writes),
            scratch_shapes=[pltpu.SemaphoreType.DMA((2 * responses,))] * writes,
            input_output_aliases={7 + k: k for k in range(6)},
            compiler_params=params(),
            name="sweep",
        )(rows, queries, resp_keys, resp_values, cotangent, cols, token, *before)
        return (outs[:4] + outs[7:] if writes else outs[:6]), outs[6]

    units = [(r, h) for r in range(responses) for h in range(H)]
    got1 = far_first(exchange(msgs, "prompt"))
    cols, held, token = first_sweep(units[:3])
    outs = pl.pallas_call(
        lambda *refs: second_kernel(n, chips, cores, *refs),
        out_shape=[shape(((1 + cores) * block, DH), BF16)] * chips + [shape((8, DH), F32)],
        in_specs=[VMEM] * n + [ANY],
        out_specs=[VMEM] * (chips + 1),
        scratch_shapes=[pltpu.VMEM((chips * cores, block, DH), F32)],
        compiler_params=params(),
        name="second",
    )(*got1, token)
    msgs, later = outs[:chips], outs[chips]
    got2 = exchange_ring(msgs, "z")
    held, token = sweep(units[3:5], held, later)
    sent, kept = pl.pallas_call(
        lambda *refs: swap_kernel(chips, *refs),
        out_shape=[shape(((chips + 1) * block, DH), BF16)] * 2,
        in_specs=[VMEM] * chips + [ANY],
        out_specs=[VMEM, VMEM],
        compiler_params=params(),
        name="swap",
    )(*got2, token)
    swapped = exchange([kept, sent], "core")[1]
    held, token = sweep(units[5:6], held, kept)
    msgs = pl.pallas_call(
        lambda *refs: third_kernel(n, chips, *refs),
        out_shape=[shape(((responses + 1) * block, DH), BF16)] * n,
        in_specs=[VMEM] * (n + 2) + [ANY],
        out_specs=[VMEM] * n,
        compiler_params=params(),
        name="third",
    )(*got1, kept, swapped, token)
    got3 = exchange(msgs, "prompt")
    held, token = sweep(units[6:], held, msgs[0], range(responses - 1))
    partial_out, partial_dq, query, grad_out, resp_dk, resp_dv = held

    resp_out, resp_dq, prompt_dk, prompt_dv = pl.pallas_call(
        lambda *refs: last_kernel(n, responses, *refs),
        out_shape=[like_out] * 2 + [shape(keys.shape, BF16)] * 2,
        in_specs=[VMEM] * (8 + n) + [ANY],
        out_specs=[ANY] * 4,
        scratch_shapes=[
            pltpu.VMEM((responses + 1, width, width), BF16),
            pltpu.VMEM(queries.shape, BF16),
            pltpu.VMEM(queries.shape, BF16),
            pltpu.VMEM(keys.shape[1:], BF16),
            pltpu.VMEM(keys.shape[1:], BF16),
            pltpu.SemaphoreType.DMA((2 + 2 * responses,)),
        ],
        compiler_params=params(),
        name="last",
    )(cols, query, grad_out, partial_out, partial_dq, keys, values, later, *got3, token)
    return (resp_out, resp_dq, resp_dk, resp_dv, prompt_dk, prompt_dv)


def solution(mesh):
    n, count = mesh.shape["prompt"], mesh.shape["resp"]
    mesh = jax.sharding.Mesh(mesh.devices.reshape(n, count // 2, 2), ("prompt", "z", "core"))
    spread = P(("prompt", "z", "core"))
    three = P(("prompt", "z", "core"), None, None)
    two = P(("prompt", "z", "core"), None)
    prompt = P(("z", "core"), "prompt", None)
    return jax.shard_map(
        shards,
        mesh=mesh,
        in_specs=(
            prompt,
            prompt,
            P(("z", "core"), None, "prompt"),
            three,
            three,
            three,
            three,
            three,
            spread,
            two,
            two,
            spread,
        ),
        out_specs=(three, three, three, three, prompt, prompt),
        check_vma=False,
    )
```

```python
import jax
import jax.numpy as jnp
from jax import lax
from jax.experimental import pallas as pl
from jax.experimental.pallas import tpu as pltpu
from jax.sharding import PartitionSpec as P

H = 2
DH = 128
HALF = 256
LOG2E = 1.4426950408889634
F32 = jnp.float32
BF16 = jnp.bfloat16
NEVER = -1e30
VMEM = pl.BlockSpec(memory_space=pltpu.VMEM)
ANY = pl.BlockSpec(memory_space=pl.ANY)
SMEM = pl.BlockSpec(memory_space=pltpu.SMEM)


def params(mebibytes=16):
    return pltpu.CompilerParams(vmem_limit_bytes=mebibytes * 1024 * 1024)


def mm(a, b):
    return lax.dot_general(a, b, (((1,), (0,)), ((), ())), preferred_element_type=F32)


def mm_nt(a, b):
    return lax.dot_general(a, b, (((1,), (1,)), ((), ())), preferred_element_type=F32)


def mm_tn(a, b):
    return lax.dot_general(a, b, (((0,), (0,)), ((), ())), preferred_element_type=F32)


def to_columns(rows):
    return jnp.concatenate([rows, jnp.zeros((128 - rows.shape[0], rows.shape[1]), F32)], axis=0).T


def in_hbm(x):
    return pltpu.with_memory_space_constraint(x, pltpu.HBM)


def three_terms(x):
    high = x.astype(BF16)
    rest = x - high.astype(F32)
    middle = rest.astype(BF16)
    return high, middle, (rest - middle.astype(F32)).astype(BF16)


def lane_cumsum(x):
    rows, width = x.shape
    ones = lax.broadcasted_iota(jnp.int32, (128, 128), 0) <= lax.broadcasted_iota(jnp.int32, (128, 128), 1)
    terms = jnp.concatenate(three_terms(x), axis=0)
    starts = range(0, width, 128)
    sums = mm(jnp.concatenate([terms[:, b : b + 128] for b in starts], axis=0), ones.astype(F32).astype(BF16))
    parts = []
    before = jnp.zeros((rows, 1), F32)
    for b in range(len(starts)):
        at = 3 * rows * b
        part = sums[at : at + rows] + sums[at + rows : at + 2 * rows] + sums[at + 2 * rows : at + 3 * rows]
        part = part + before
        before = part[:, 127:128]
        parts.append(part)
    return jnp.concatenate(parts, axis=1)


def first_kernel(
    n, ids_hbm, lens_hbm, adv_hbm, keys_hbm, values_hbm, pgates_hbm, gates_hbm, mask_hbm, q_hbm, c_hbm,
    *refs,
):
    msgs, (rows_ref, q, c) = refs[:n], refs[n : n + 3]
    keys, values, pgates, gates, mask, ids_ref, lens_ref, adv_ref, matrices, sems = refs[n + 3 :]
    pairs = [(pgates_hbm, pgates), (gates_hbm, gates), (lens_hbm, lens_ref), (adv_hbm, adv_ref), (mask_hbm, mask)]
    pairs += [(keys_hbm, keys), (values_hbm, values), (q_hbm, q), (c_hbm, c), (ids_hbm, ids_ref)]
    copies = [pltpu.make_async_copy(a, b, sems.at[i]) for i, (a, b) in enumerate(pairs)]
    for copy in copies:
        copy.start()
    count = gates.shape[0]
    slots = gates.shape[2]
    tokens = keys.shape[1]
    part = DH // n
    block = H * part
    targets = partners(n)

    def spread(at):
        for k in range(n):
            of = pl.ds(pl.multiple_of(targets[k] * part, part), part)
            msgs[k][at * part + (16 if at >= H else 0) : (at + 1) * part + (16 if at >= H else 0), :] = matrices[
                at, of, :
            ].astype(BF16)

    copies[0].wait()
    copies[1].wait()
    piece = jnp.concatenate([pgates[0], jnp.zeros((H, slots - tokens), F32)], axis=1)
    gate_rows = [gates[i] for i in range(count)] + [piece, jnp.zeros((16 - H * (count + 1), slots), F32)]
    cum = lane_cumsum(jnp.concatenate(gate_rows, axis=0))
    carried = jnp.exp(cum)
    place = lax.broadcasted_iota(jnp.int32, (1, slots), 1)
    for copy in copies[2:5]:
        copy.wait()
    rows = []
    factors = []
    for i in range(count):
        weight = adv_ref[i].astype(F32) / 1024.0
        opened = jnp.where(place < lens_ref[0, i], 1.0, 0.0)
        live = mask[i : i + 1, :].astype(F32) * opened * weight
        rows += [cum[H * i : H * i + H], carried[H * i : H * i + H] * opened, live, opened, jnp.zeros((2, slots), F32)]
        factors.append(carried[H * i : H * i + H] * live)
    piece = cum[H * count : H * count + H]
    total = piece[:, -1:]
    suffix = total - piece
    rows += [suffix, jnp.zeros((8 - H, slots), F32)]
    rows_ref[...] = jnp.concatenate(rows, axis=0)

    copies[5].wait()
    copies[6].wait()
    turned = keys[0].T
    later = jnp.exp(suffix[:, :tokens])
    for h in range(H):
        lanes = slice(h * DH, (h + 1) * DH)
        scaled = turned[lanes].astype(F32) * later[h : h + 1]
        high = scaled.astype(BF16)
        low = (scaled - high.astype(F32)).astype(BF16)
        both = mm(jnp.concatenate([high, low], axis=0), values[0, :, lanes])
        matrices[h] = both[:DH] + both[DH:]
        spread(h)
    copies[7].wait()
    copies[8].wait()
    for i in range(count):
        turned = q[i].T
        for h in range(H):
            lanes = slice(h * DH, (h + 1) * DH)
            scaled = (turned[lanes].astype(F32) * factors[i][h : h + 1]).astype(BF16)
            matrices[H * (1 + i) + h] = mm(scaled, c[i, :, lanes])
            spread(H * (1 + i) + h)
    copies[9].wait()
    notes = [jnp.broadcast_to(x[h : h + 1].astype(F32), (1, DH)) for x in three_terms(total) for h in range(H)]
    notes += [jnp.full((1, DH), ids_ref[i].astype(F32)) for i in range(count)]
    notes.append(jnp.zeros((16 - len(notes), DH), F32))
    notes = jnp.concatenate(notes, axis=0).astype(BF16)
    for k in range(n):
        msgs[k][block : block + 16, :] = notes


def noted_prompt(notes, i):
    return jnp.max(notes[3 * H + i : 3 * H + i + 1]).astype(jnp.int32)


def second_kernel(n, chips, cores, *refs):
    z_at = lax.axis_index("z")
    got, msgs, later_ref, sums = far_first(refs[:n]), refs[n + 1 : n + 1 + chips], refs[-2], refs[-1]
    part = DH // n
    block = H * part
    responses = (got[0].shape[0] - block - 16) // block
    place = partners(n)
    notes = [got[k][block : block + 16, :].astype(F32) for k in range(n)]
    logs = [x[0:H] + x[H : 2 * H] + x[2 * H : 3 * H] for x in notes]
    final = jnp.zeros((block, DH), F32)
    for k in range(n):
        later = jnp.zeros_like(logs[0])
        for other in range(n):
            if other != k:
                later = later + jnp.where(place[other] > place[k], logs[other], 0.0)
        if k == 0:
            later_ref[...] = jnp.concatenate([later, jnp.zeros((8 - H, DH), F32)], axis=0)
        decay = jnp.exp(later)
        decay = [jnp.broadcast_to(decay[h : h + 1], (part, DH)) for h in range(H)]
        final = final + jnp.concatenate(decay, axis=0) * got[k][0:block, :].astype(F32)
    sums[...] = jnp.zeros_like(sums)
    for k in range(n):
        for i in range(responses):
            at = block * (1 + i) + 16
            sums[noted_prompt(notes[k], i)] += got[k][at : at + block, :].astype(F32)
    final = final.astype(BF16)
    for k in range(chips):
        z = lax.rem(z_at + k, chips)
        msgs[k][0:block, :] = final
        for c in range(cores):
            msgs[k][(1 + c) * block : (2 + c) * block, :] = sums[z * cores + c].astype(BF16)


def swap_kernel(chips, *refs):
    got, sent_ref, kept_ref = refs[:chips], refs[chips + 1], refs[chips + 2]
    block = got[0].shape[0] // 3
    totals = []
    for c in range(2):
        total = got[0][(1 + c) * block : (2 + c) * block, :].astype(F32)
        for k in range(1, chips):
            total = total + got[k][(1 + c) * block : (2 + c) * block, :].astype(F32)
        totals.append(total)
    for k in range(chips):
        final = got[k][0:block, :]
        sent_ref[k * block : (k + 1) * block, :] = final
        kept_ref[k * block : (k + 1) * block, :] = final
    low = lax.axis_index("core") == 0
    sent_ref[chips * block :, :] = jnp.where(low, totals[1], totals[0]).astype(BF16)
    kept_ref[chips * block :, :] = jnp.where(low, totals[0], totals[1]).astype(BF16)


def third_kernel(n, chips, *refs):
    z_at, core = lax.axis_index("z"), lax.axis_index("core")
    noted, kept_ref, got_ref, msgs = far_first(refs[:n]), refs[n], refs[n + 1], refs[n + 3 :]
    block = H * DH // n
    responses = (noted[0].shape[0] - block - 16) // block
    total = kept_ref[chips * block :, :].astype(F32) + got_ref[chips * block :, :].astype(F32)
    total = total.astype(BF16)
    for k in range(n):
        notes = noted[k][block : block + 16, :].astype(F32)
        for i in range(responses):
            p = noted_prompt(notes, i)
            slot = lax.rem(z_at + chips - lax.div(p, 2), chips)
            at = pl.ds(pl.multiple_of(slot * block, block), block)
            same = lax.rem(p, 2) == core
            state = jnp.where(same, kept_ref[at, :].astype(F32), got_ref[at, :].astype(F32))
            msgs[k][i * block : (i + 1) * block, :] = state.astype(BF16)
        msgs[k][responses * block :, :] = total


def sweep_kernel(units, done, rows_ref, q_ref, k_ref, v_ref, c_ref, cols_ref, *refs):
    writes = len(done) > 0
    if writes:
        *refs, dk_hbm, dv_hbm, sems = refs
    out_ref, dq_ref, query_ref, grad_ref, dk_ref, dv_ref, token_ref = refs[-7:]
    fetches = []
    if cols_ref is None:
        cols_ref, k_vmem, v_vmem = refs[:3]
        sems = refs[-8]
        for r in range(k_ref.shape[0]):
            for a, b in ((k_ref, k_vmem), (v_ref, v_vmem)):
                fetches.append(pltpu.make_async_copy(a.at[r], b.at[r], sems.at[len(fetches)]))
                fetches[-1].start()
        cols_ref[...] = to_columns(rows_ref[...])
        k_ref, v_ref = k_vmem, v_vmem
        for fetch in fetches[:2]:
            fetch.wait()
    copies = []

    def send(r):
        for a, b in ((dk_ref, dk_hbm), (dv_ref, dv_hbm)):
            copies.append(pltpu.make_async_copy(a.at[r], b.at[r], sems.at[len(copies)]))
            copies[-1].start()

    for r in done:
        send(r)
    token_ref[...] = jnp.zeros_like(token_ref)
    quarter = HALF // 2
    causal = lax.broadcasted_iota(jnp.int32, (quarter, quarter), 0) >= lax.broadcasted_iota(
        jnp.int32, (quarter, quarter), 1
    )
    blank = jnp.zeros((quarter, quarter), BF16)
    blocks = q_ref.shape[1] // HALF

    def decayed(products, cum, row, diagonal):
        if not diagonal:
            decay = jnp.exp2(cum - row)
            return [(x * decay).astype(BF16) for x in products]
        first = jnp.exp2(jnp.where(causal, cum[:quarter] - row[:, :quarter], NEVER))
        left = jnp.exp2(cum[quarter:] - row[:, :quarter])
        right = jnp.exp2(jnp.where(causal, cum[quarter:] - row[:, quarter:], NEVER))
        results = []
        for x in products:
            upper = jnp.concatenate([(x[:quarter, :quarter] * first).astype(BF16), blank], axis=1)
            lower = [(x[quarter:, :quarter] * left).astype(BF16), (x[quarter:, quarter:] * right).astype(BF16)]
            results.append(jnp.concatenate([upper, jnp.concatenate(lower, axis=1)], axis=0))
        return results

    for r, h in units:
        lanes = slice(h * DH, (h + 1) * DH)
        cum = cols_ref[:, 8 * r + h : 8 * r + h + 1] * LOG2E
        row = rows_ref[8 * r + h : 8 * r + h + 1, :] * LOG2E
        live = cols_ref[:, 8 * r + 4 : 8 * r + 5]
        opened = cols_ref[:, 8 * r + 5 : 8 * r + 6]
        grad_all = (c_ref[r, :, lanes].astype(F32) * live).astype(BF16)
        carried = cols_ref[:, 8 * r + 2 + h : 8 * r + 3 + h]
        query_ref[r, :, lanes] = (q_ref[r, :, lanes].astype(F32) * carried).astype(BF16)
        grad_ref[r, :, lanes] = (grad_all.astype(F32) * carried).astype(BF16)
        query_turned = q_ref[r, :, lanes].T
        grad_turned = grad_all.T
        dk = [None] * blocks
        dv = [None] * blocks
        for t in range(blocks):
            at = slice(t * HALF, (t + 1) * HALF)
            query = q_ref[r, at, lanes]
            grad_out = grad_all[at]
            out = None
            dq = None
            for s in range(t + 1):
                of = slice(s * HALF, (s + 1) * HALF)
                key = k_ref[r, of, lanes]
                value = v_ref[r, of, lanes]
                mixing, scores = decayed(
                    [mm_nt(query, key), mm_nt(grad_out, value)], cum[at], row[:, of], s == t
                )
                o_new = mm(mixing, value)
                q_new = mm(scores, key)
                k_new = mm(query_turned[:, at], scores)
                v_new = mm(grad_turned[:, at], mixing)
                out = o_new if out is None else out + o_new
                dq = q_new if dq is None else dq + q_new
                dk[s] = k_new if dk[s] is None else dk[s] + k_new
                dv[s] = v_new if dv[s] is None else dv[s] + v_new
            out_ref[r, at, lanes] = out * opened[at]
            dq_ref[r, at, lanes] = dq
        for s in range(blocks):
            of = slice(s * HALF, (s + 1) * HALF)
            dk_ref[r, of, lanes] = dk[s].astype(BF16).T
            dv_ref[r, of, lanes] = dv[s].astype(BF16).T
        if writes and h == H - 1:
            send(r)
    for copy in copies + fetches[2:]:
        copy.wait()


def last_kernel(
    n, count, cols_ref, q_ref, grad_ref, po_ref, pdq_ref, keys_ref, values_ref, later_ref, *refs
):
    got, refs = refs[:n], refs[n + 1 :]
    out_hbm, dq_hbm, dk_hbm, dv_hbm, start, out_buf, dq_buf, dk_buf, dv_buf, sems = refs
    part = DH // n
    block = H * part
    place = partners(n)
    slots = q_ref.shape[1]
    tokens = keys_ref.shape[1]
    copies = []

    def send(a, b):
        copies.append(pltpu.make_async_copy(a, b, sems.at[len(copies)]))
        copies[-1].start()

    start[...] = jnp.zeros_like(start)
    for r in range(count + 1):
        for k in range(n):
            for h in range(H):
                of = pl.ds(pl.multiple_of(h * DH + place[k] * part, part), part)
                rows = got[k][r * block + h * part : r * block + (h + 1) * part, :]
                start[r, of, h * DH : (h + 1) * DH] = rows
    for r in range(count):
        for t in range(0, slots, HALF):
            at = slice(t, t + HALF)
            out_buf[r, at, :] = (po_ref[r, at, :] + mm(q_ref[r, at, :], start[r])).astype(BF16)
            dq_buf[r, at, :] = (pdq_ref[r, at, :] + mm_nt(grad_ref[r, at, :], start[r])).astype(BF16)
        send(out_buf.at[r], out_hbm.at[r])
        send(dq_buf.at[r], dq_hbm.at[r])
    factor = [
        jnp.exp(cols_ref[:tokens, 8 * count + h : 8 * count + h + 1] + later_ref[h : h + 1, 0:1]) for h in range(H)
    ]
    for buf, x in ((dk_buf, mm_nt(values_ref[0], start[count])), (dv_buf, mm(keys_ref[0], start[count]))):
        for h in range(H):
            lanes = slice(h * DH, (h + 1) * DH)
            buf[:, lanes] = (factor[h] * x[:, lanes]).astype(BF16)
    send(dk_buf, dk_hbm.at[0])
    send(dv_buf, dv_hbm.at[0])
    for copy in copies:
        copy.wait()


def exchange(xs, axis):
    n = lax.axis_size(axis)
    return [xs[0]] + [lax.ppermute(xs[k], axis, [(s, s ^ k) for s in range(n)]) for k in range(1, n)]


def exchange_ring(xs, axis):
    n = lax.axis_size(axis)
    return [xs[0]] + [lax.ppermute(xs[k], axis, [(s, (s + k) % n) for s in range(n)]) for k in range(1, n)]


def far_first(refs):
    return [refs[0], *refs[:0:-1]]


def partners(n):
    me = lax.axis_index("prompt")
    return [lax.bitwise_xor(me, k) for k in range(n)]


def shards(
    keys,
    values,
    prompt_gates,
    queries,
    resp_keys,
    resp_values,
    resp_gates,
    cotangent,
    group_ids,
    resp_lengths,
    loss_mask,
    advantages,
):
    n = lax.axis_size("prompt")
    chips = lax.axis_size("z")
    cores = lax.axis_size("core")
    responses, slots, width = queries.shape
    block = H * DH // n
    shape = jax.ShapeDtypeStruct

    outs = pl.pallas_call(
        lambda *refs: first_kernel(n, *refs),
        out_shape=[shape((block * (1 + responses) + 16, DH), BF16)] * n
        + [shape((8 * (responses + 1), slots), F32)]
        + [shape(queries.shape, BF16)] * 2,
        in_specs=[ANY] * 10,
        out_specs=[VMEM] * (n + 3),
        scratch_shapes=[
            pltpu.VMEM(keys.shape, BF16),
            pltpu.VMEM(values.shape, BF16),
            pltpu.VMEM(prompt_gates.shape, F32),
            pltpu.VMEM(resp_gates.shape, F32),
            pltpu.VMEM(loss_mask.shape, jnp.int32),
            pltpu.SMEM(group_ids.shape, jnp.int32),
            pltpu.SMEM(resp_lengths.shape, jnp.int32),
            pltpu.SMEM(advantages.shape, jnp.int32),
            pltpu.VMEM((H * (1 + responses), DH, DH), F32),
            pltpu.SemaphoreType.DMA((10,)),
        ],
        compiler_params=params(32),
        name="first",
    )(
        *[in_hbm(x) for x in (group_ids, resp_lengths, advantages, keys, values, prompt_gates, resp_gates)],
        *[in_hbm(x) for x in (loss_mask, queries, cotangent)],
    )
    msgs, (rows, queries, cotangent) = outs[:n], outs[n:]

    like = shape(queries.shape, F32)
    like_out = shape(queries.shape, BF16)

    held_shapes = [like, like] + [like_out] * 4 + [shape((8, 128), F32)]

    def first_sweep(units):
        outs = pl.pallas_call(
            lambda *refs: sweep_kernel(units, (), *refs[:5], None, *refs[5:8], refs[-1], *refs[8:-1]),
            out_shape=[shape((slots, 128), F32), like_out, like_out] + held_shapes,
            in_specs=[VMEM, VMEM, ANY, ANY, VMEM],
            out_specs=[VMEM] * 10,
            scratch_shapes=[pltpu.SemaphoreType.DMA((2 * responses,))],
            compiler_params=params(),
            name="sweep",
        )(rows, queries, in_hbm(resp_keys), in_hbm(resp_values), cotangent)
        return outs[0], outs[1], outs[2], outs[3:9], outs[9]

    def sweep(units, before, token, done=()):
        writes = len(done) > 0
        outs = pl.pallas_call(
            lambda *refs: sweep_kernel(units, done, *refs),
            out_shape=held_shapes + [like_out] * (2 * writes),
            in_specs=[VMEM] * 6 + [ANY] * 7,
            out_specs=[VMEM] * 7 + [ANY] * (2 * writes),
            scratch_shapes=[pltpu.SemaphoreType.DMA((2 * responses,))] * writes,
            input_output_aliases={7 + k: k for k in range(6)},
            compiler_params=params(),
            name="sweep",
        )(rows, queries, resp_keys, resp_values, cotangent, cols, token, *before)
        return (outs[:4] + outs[7:] if writes else outs[:6]), outs[6]

    units = [(r, h) for r in range(responses) for h in range(H)]
    got1 = far_first(exchange(msgs, "prompt"))
    cols, resp_keys, resp_values, held, token = first_sweep(units[:2])
    outs = pl.pallas_call(
        lambda *refs: second_kernel(n, chips, cores, *refs),
        out_shape=[shape(((1 + cores) * block, DH), BF16)] * chips + [shape((8, DH), F32)],
        in_specs=[VMEM] * n + [ANY],
        out_specs=[VMEM] * (chips + 1),
        scratch_shapes=[pltpu.VMEM((chips * cores, block, DH), F32)],
        compiler_params=params(),
        name="second",
    )(*got1, token)
    msgs, later = outs[:chips], outs[chips]
    got2 = exchange_ring(msgs, "z")
    held, token = sweep(units[2:5], held, later)
    sent, kept = pl.pallas_call(
        lambda *refs: swap_kernel(chips, *refs),
        out_shape=[shape(((chips + 1) * block, DH), BF16)] * 2,
        in_specs=[VMEM] * chips + [ANY],
        out_specs=[VMEM, VMEM],
        compiler_params=params(),
        name="swap",
    )(*got2, token)
    swapped = exchange([kept, sent], "core")[1]
    held, token = sweep(units[5:6], held, kept)
    msgs = pl.pallas_call(
        lambda *refs: third_kernel(n, chips, *refs),
        out_shape=[shape(((responses + 1) * block, DH), BF16)] * n,
        in_specs=[VMEM] * (n + 2) + [ANY],
        out_specs=[VMEM] * n,
        compiler_params=params(),
        name="third",
    )(*got1, kept, swapped, token)
    got3 = exchange(msgs, "prompt")
    held, token = sweep(units[6:], held, msgs[0], range(responses - 1))
    partial_out, partial_dq, query, grad_out, resp_dk, resp_dv = held

    resp_out, resp_dq, prompt_dk, prompt_dv = pl.pallas_call(
        lambda *refs: last_kernel(n, responses, *refs),
        out_shape=[like_out] * 2 + [shape(keys.shape, BF16)] * 2,
        in_specs=[VMEM] * (8 + n) + [ANY],
        out_specs=[ANY] * 4,
        scratch_shapes=[
            pltpu.VMEM((responses + 1, width, width), BF16),
            pltpu.VMEM(queries.shape, BF16),
            pltpu.VMEM(queries.shape, BF16),
            pltpu.VMEM(keys.shape[1:], BF16),
            pltpu.VMEM(keys.shape[1:], BF16),
            pltpu.SemaphoreType.DMA((2 + 2 * responses,)),
        ],
        compiler_params=params(),
        name="last",
    )(cols, query, grad_out, partial_out, partial_dq, keys, values, later, *got3, token)
    return (resp_out, resp_dq, resp_dk, resp_dv, prompt_dk, prompt_dv)


def solution(mesh):
    n, count = mesh.shape["prompt"], mesh.shape["resp"]
    mesh = jax.sharding.Mesh(mesh.devices.reshape(n, count // 2, 2), ("prompt", "z", "core"))
    spread = P(("prompt", "z", "core"))
    three = P(("prompt", "z", "core"), None, None)
    two = P(("prompt", "z", "core"), None)
    prompt = P(("z", "core"), "prompt", None)
    return jax.shard_map(
        shards,
        mesh=mesh,
        in_specs=(
            prompt,
            prompt,
            P(("z", "core"), None, "prompt"),
            three,
            three,
            three,
            three,
            three,
            spread,
            two,
            two,
            spread,
        ),
        out_specs=(three, three, three, three, prompt, prompt),
        check_vma=False,
    )
```

```python
import jax
import jax.numpy as jnp
from jax import lax
from jax.experimental import pallas as pl
from jax.experimental.pallas import tpu as pltpu
from jax.sharding import PartitionSpec as P

H = 2
DH = 128
HALF = 256
LOG2E = 1.4426950408889634
F32 = jnp.float32
BF16 = jnp.bfloat16
NEVER = -1e30
VMEM = pl.BlockSpec(memory_space=pltpu.VMEM)
ANY = pl.BlockSpec(memory_space=pl.ANY)
SMEM = pl.BlockSpec(memory_space=pltpu.SMEM)


def params(mebibytes=16):
    return pltpu.CompilerParams(vmem_limit_bytes=mebibytes * 1024 * 1024)


def mm(a, b):
    return lax.dot_general(a, b, (((1,), (0,)), ((), ())), preferred_element_type=F32)


def mm_nt(a, b):
    return lax.dot_general(a, b, (((1,), (1,)), ((), ())), preferred_element_type=F32)


def mm_tn(a, b):
    return lax.dot_general(a, b, (((0,), (0,)), ((), ())), preferred_element_type=F32)


def to_columns(rows):
    return jnp.concatenate([rows, jnp.zeros((128 - rows.shape[0], rows.shape[1]), F32)], axis=0).T


def in_hbm(x):
    return pltpu.with_memory_space_constraint(x, pltpu.HBM)


def three_terms(x):
    high = x.astype(BF16)
    rest = x - high.astype(F32)
    middle = rest.astype(BF16)
    return high, middle, (rest - middle.astype(F32)).astype(BF16)


def lane_cumsum(x):
    rows, width = x.shape
    ones = lax.broadcasted_iota(jnp.int32, (128, 128), 0) <= lax.broadcasted_iota(jnp.int32, (128, 128), 1)
    terms = jnp.concatenate(three_terms(x), axis=0)
    starts = range(0, width, 128)
    sums = mm(jnp.concatenate([terms[:, b : b + 128] for b in starts], axis=0), ones.astype(F32).astype(BF16))
    parts = []
    before = jnp.zeros((rows, 1), F32)
    for b in range(len(starts)):
        at = 3 * rows * b
        part = sums[at : at + rows] + sums[at + rows : at + 2 * rows] + sums[at + 2 * rows : at + 3 * rows]
        part = part + before
        before = part[:, 127:128]
        parts.append(part)
    return jnp.concatenate(parts, axis=1)


def first_kernel(
    n, ids_hbm, lens_hbm, adv_hbm, keys_hbm, values_hbm, pgates_hbm, gates_hbm, mask_hbm, q_hbm, c_hbm,
    *refs,
):
    msgs, (rows_ref, q, c) = refs[:n], refs[n : n + 3]
    keys, values, pgates, gates, mask, ids_ref, lens_ref, adv_ref, matrices, sems = refs[n + 3 :]
    pairs = [(pgates_hbm, pgates), (gates_hbm, gates), (lens_hbm, lens_ref), (adv_hbm, adv_ref), (mask_hbm, mask)]
    pairs += [(keys_hbm, keys), (values_hbm, values), (q_hbm, q), (c_hbm, c), (ids_hbm, ids_ref)]
    copies = [pltpu.make_async_copy(a, b, sems.at[i]) for i, (a, b) in enumerate(pairs)]
    for copy in copies:
        copy.start()
    count = gates.shape[0]
    slots = gates.shape[2]
    tokens = keys.shape[1]
    part = DH // n
    block = H * part
    targets = partners(n)

    def spread(at):
        for k in range(n):
            of = pl.ds(pl.multiple_of(targets[k] * part, part), part)
            msgs[k][at * part + (16 if at >= H else 0) : (at + 1) * part + (16 if at >= H else 0), :] = matrices[
                at, of, :
            ].astype(BF16)

    copies[0].wait()
    copies[1].wait()
    piece = jnp.concatenate([pgates[0], jnp.zeros((H, slots - tokens), F32)], axis=1)
    gate_rows = [gates[i] for i in range(count)] + [piece, jnp.zeros((16 - H * (count + 1), slots), F32)]
    cum = lane_cumsum(jnp.concatenate(gate_rows, axis=0))
    carried = jnp.exp(cum)
    place = lax.broadcasted_iota(jnp.int32, (1, slots), 1)
    for copy in copies[2:5]:
        copy.wait()
    rows = []
    factors = []
    for i in range(count):
        weight = adv_ref[i].astype(F32) / 1024.0
        opened = jnp.where(place < lens_ref[0, i], 1.0, 0.0)
        live = mask[i : i + 1, :].astype(F32) * opened * weight
        rows += [cum[H * i : H * i + H], carried[H * i : H * i + H] * opened, live, opened, jnp.zeros((2, slots), F32)]
        factors.append(carried[H * i : H * i + H] * live)
    piece = cum[H * count : H * count + H]
    total = piece[:, -1:]
    suffix = total - piece
    rows += [suffix, jnp.zeros((8 - H, slots), F32)]
    rows_ref[...] = jnp.concatenate(rows, axis=0)

    for copy in copies[5:]:
        copy.wait()
    turned = keys[0].T
    later = jnp.exp(suffix[:, :tokens])
    for h in range(H):
        lanes = slice(h * DH, (h + 1) * DH)
        scaled = turned[lanes].astype(F32) * later[h : h + 1]
        high = scaled.astype(BF16)
        low = (scaled - high.astype(F32)).astype(BF16)
        both = mm(jnp.concatenate([high, low], axis=0), values[0, :, lanes])
        matrices[h] = both[:DH] + both[DH:]
        spread(h)
    for i in range(count):
        turned = q[i].T
        for h in range(H):
            lanes = slice(h * DH, (h + 1) * DH)
            scaled = (turned[lanes].astype(F32) * factors[i][h : h + 1]).astype(BF16)
            matrices[H * (1 + i) + h] = mm(scaled, c[i, :, lanes])
            spread(H * (1 + i) + h)
    notes = [jnp.broadcast_to(x[h : h + 1].astype(F32), (1, DH)) for x in three_terms(total) for h in range(H)]
    notes += [jnp.full((1, DH), ids_ref[i].astype(F32)) for i in range(count)]
    notes.append(jnp.zeros((16 - len(notes), DH), F32))
    notes = jnp.concatenate(notes, axis=0).astype(BF16)
    for k in range(n):
        msgs[k][block : block + 16, :] = notes


def noted_prompt(notes, i):
    return jnp.max(notes[3 * H + i : 3 * H + i + 1]).astype(jnp.int32)


def second_kernel(n, chips, cores, *refs):
    z_at = lax.axis_index("z")
    got, msgs, later_ref, sums = far_first(refs[:n]), refs[n + 1 : n + 1 + chips], refs[-2], refs[-1]
    part = DH // n
    block = H * part
    responses = (got[0].shape[0] - block - 16) // block
    place = partners(n)
    notes = [got[k][block : block + 16, :].astype(F32) for k in range(n)]
    logs = [x[0:H] + x[H : 2 * H] + x[2 * H : 3 * H] for x in notes]
    final = jnp.zeros((block, DH), F32)
    for k in range(n):
        later = jnp.zeros_like(logs[0])
        for other in range(n):
            if other != k:
                later = later + jnp.where(place[other] > place[k], logs[other], 0.0)
        if k == 0:
            later_ref[...] = jnp.concatenate([later, jnp.zeros((8 - H, DH), F32)], axis=0)
        decay = jnp.exp(later)
        decay = [jnp.broadcast_to(decay[h : h + 1], (part, DH)) for h in range(H)]
        final = final + jnp.concatenate(decay, axis=0) * got[k][0:block, :].astype(F32)
    sums[...] = jnp.zeros_like(sums)
    for k in range(n):
        for i in range(responses):
            at = block * (1 + i) + 16
            sums[noted_prompt(notes[k], i)] += got[k][at : at + block, :].astype(F32)
    final = final.astype(BF16)
    for k in range(chips):
        z = lax.rem(z_at + k, chips)
        msgs[k][0:block, :] = final
        for c in range(cores):
            msgs[k][(1 + c) * block : (2 + c) * block, :] = sums[z * cores + c].astype(BF16)


def swap_kernel(chips, *refs):
    got, sent_ref, kept_ref = refs[:chips], refs[chips + 1], refs[chips + 2]
    block = got[0].shape[0] // 3
    totals = []
    for c in range(2):
        total = got[0][(1 + c) * block : (2 + c) * block, :].astype(F32)
        for k in range(1, chips):
            total = total + got[k][(1 + c) * block : (2 + c) * block, :].astype(F32)
        totals.append(total)
    for k in range(chips):
        final = got[k][0:block, :]
        sent_ref[k * block : (k + 1) * block, :] = final
        kept_ref[k * block : (k + 1) * block, :] = final
    low = lax.axis_index("core") == 0
    sent_ref[chips * block :, :] = jnp.where(low, totals[1], totals[0]).astype(BF16)
    kept_ref[chips * block :, :] = jnp.where(low, totals[0], totals[1]).astype(BF16)


def third_kernel(n, chips, *refs):
    z_at, core = lax.axis_index("z"), lax.axis_index("core")
    noted, kept_ref, got_ref, msgs = far_first(refs[:n]), refs[n], refs[n + 1], refs[n + 3 :]
    block = H * DH // n
    responses = (noted[0].shape[0] - block - 16) // block
    total = kept_ref[chips * block :, :].astype(F32) + got_ref[chips * block :, :].astype(F32)
    total = total.astype(BF16)
    for k in range(n):
        notes = noted[k][block : block + 16, :].astype(F32)
        for i in range(responses):
            p = noted_prompt(notes, i)
            slot = lax.rem(z_at + chips - lax.div(p, 2), chips)
            at = pl.ds(pl.multiple_of(slot * block, block), block)
            same = lax.rem(p, 2) == core
            state = jnp.where(same, kept_ref[at, :].astype(F32), got_ref[at, :].astype(F32))
            msgs[k][i * block : (i + 1) * block, :] = state.astype(BF16)
        msgs[k][responses * block :, :] = total


def sweep_kernel(units, done, rows_ref, q_ref, k_ref, v_ref, c_ref, cols_ref, *refs):
    writes = len(done) > 0
    if writes:
        *refs, dk_hbm, dv_hbm, sems = refs
    out_ref, dq_ref, query_ref, grad_ref, dk_ref, dv_ref, token_ref = refs[-7:]
    fetches = []
    if cols_ref is None:
        cols_ref, k_vmem, v_vmem = refs[:3]
        sems = refs[-8]
        for r in range(k_ref.shape[0]):
            for a, b in ((k_ref, k_vmem), (v_ref, v_vmem)):
                fetches.append(pltpu.make_async_copy(a.at[r], b.at[r], sems.at[len(fetches)]))
                fetches[-1].start()
        cols_ref[...] = to_columns(rows_ref[...])
        k_ref, v_ref = k_vmem, v_vmem
        for fetch in fetches[:2]:
            fetch.wait()
    copies = []

    def send(r):
        for a, b in ((dk_ref, dk_hbm), (dv_ref, dv_hbm)):
            copies.append(pltpu.make_async_copy(a.at[r], b.at[r], sems.at[len(copies)]))
            copies[-1].start()

    for r in done:
        send(r)
    token_ref[...] = jnp.zeros_like(token_ref)
    quarter = HALF // 2
    causal = lax.broadcasted_iota(jnp.int32, (quarter, quarter), 0) >= lax.broadcasted_iota(
        jnp.int32, (quarter, quarter), 1
    )
    blank = jnp.zeros((quarter, quarter), BF16)
    blocks = q_ref.shape[1] // HALF

    def decayed(products, cum, row, diagonal):
        if not diagonal:
            decay = jnp.exp2(cum - row)
            return [(x * decay).astype(BF16) for x in products]
        first = jnp.exp2(jnp.where(causal, cum[:quarter] - row[:, :quarter], NEVER))
        left = jnp.exp2(cum[quarter:] - row[:, :quarter])
        right = jnp.exp2(jnp.where(causal, cum[quarter:] - row[:, quarter:], NEVER))
        results = []
        for x in products:
            upper = jnp.concatenate([(x[:quarter, :quarter] * first).astype(BF16), blank], axis=1)
            lower = [(x[quarter:, :quarter] * left).astype(BF16), (x[quarter:, quarter:] * right).astype(BF16)]
            results.append(jnp.concatenate([upper, jnp.concatenate(lower, axis=1)], axis=0))
        return results

    for r, h in units:
        lanes = slice(h * DH, (h + 1) * DH)
        cum = cols_ref[:, 8 * r + h : 8 * r + h + 1] * LOG2E
        row = rows_ref[8 * r + h : 8 * r + h + 1, :] * LOG2E
        live = cols_ref[:, 8 * r + 4 : 8 * r + 5]
        opened = cols_ref[:, 8 * r + 5 : 8 * r + 6]
        grad_all = (c_ref[r, :, lanes].astype(F32) * live).astype(BF16)
        carried = cols_ref[:, 8 * r + 2 + h : 8 * r + 3 + h]
        query_ref[r, :, lanes] = (q_ref[r, :, lanes].astype(F32) * carried).astype(BF16)
        grad_ref[r, :, lanes] = (grad_all.astype(F32) * carried).astype(BF16)
        query_turned = q_ref[r, :, lanes].T
        grad_turned = grad_all.T
        dk = [None] * blocks
        dv = [None] * blocks
        for t in range(blocks):
            at = slice(t * HALF, (t + 1) * HALF)
            query = q_ref[r, at, lanes]
            grad_out = grad_all[at]
            out = None
            dq = None
            for s in range(t + 1):
                of = slice(s * HALF, (s + 1) * HALF)
                key = k_ref[r, of, lanes]
                value = v_ref[r, of, lanes]
                mixing, scores = decayed(
                    [mm_nt(query, key), mm_nt(grad_out, value)], cum[at], row[:, of], s == t
                )
                o_new = mm(mixing, value)
                q_new = mm(scores, key)
                k_new = mm(query_turned[:, at], scores)
                v_new = mm(grad_turned[:, at], mixing)
                out = o_new if out is None else out + o_new
                dq = q_new if dq is None else dq + q_new
                dk[s] = k_new if dk[s] is None else dk[s] + k_new
                dv[s] = v_new if dv[s] is None else dv[s] + v_new
            out_ref[r, at, lanes] = out * opened[at]
            dq_ref[r, at, lanes] = dq
        for s in range(blocks):
            of = slice(s * HALF, (s + 1) * HALF)
            dk_ref[r, of, lanes] = dk[s].astype(BF16).T
            dv_ref[r, of, lanes] = dv[s].astype(BF16).T
        if writes and h == H - 1:
            send(r)
    for copy in copies + fetches[2:]:
        copy.wait()


def last_kernel(
    n, count, cols_ref, q_ref, grad_ref, po_ref, pdq_ref, keys_ref, values_ref, later_ref, *refs
):
    got, refs = refs[:n], refs[n + 1 :]
    out_hbm, dq_hbm, dk_hbm, dv_hbm, start, out_buf, dq_buf, dk_buf, dv_buf, sems = refs
    part = DH // n
    block = H * part
    place = partners(n)
    slots = q_ref.shape[1]
    tokens = keys_ref.shape[1]
    copies = []

    def send(a, b):
        copies.append(pltpu.make_async_copy(a, b, sems.at[len(copies)]))
        copies[-1].start()

    start[...] = jnp.zeros_like(start)
    for r in range(count + 1):
        for k in range(n):
            for h in range(H):
                of = pl.ds(pl.multiple_of(h * DH + place[k] * part, part), part)
                rows = got[k][r * block + h * part : r * block + (h + 1) * part, :]
                start[r, of, h * DH : (h + 1) * DH] = rows
    for r in range(count):
        for t in range(0, slots, HALF):
            at = slice(t, t + HALF)
            out_buf[r, at, :] = (po_ref[r, at, :] + mm(q_ref[r, at, :], start[r])).astype(BF16)
            dq_buf[r, at, :] = (pdq_ref[r, at, :] + mm_nt(grad_ref[r, at, :], start[r])).astype(BF16)
        for ready in ([r - 1] if r > 0 else []) + ([r] if r == count - 1 else []):
            send(out_buf.at[ready], out_hbm.at[ready])
            send(dq_buf.at[ready], dq_hbm.at[ready])
    factor = [
        jnp.exp(cols_ref[:tokens, 8 * count + h : 8 * count + h + 1] + later_ref[h : h + 1, 0:1]) for h in range(H)
    ]
    for buf, x in ((dk_buf, mm_nt(values_ref[0], start[count])), (dv_buf, mm(keys_ref[0], start[count]))):
        for h in range(H):
            lanes = slice(h * DH, (h + 1) * DH)
            buf[:, lanes] = (factor[h] * x[:, lanes]).astype(BF16)
    send(dk_buf, dk_hbm.at[0])
    send(dv_buf, dv_hbm.at[0])
    for copy in copies:
        copy.wait()


def exchange(xs, axis):
    n = lax.axis_size(axis)
    return [xs[0]] + [lax.ppermute(xs[k], axis, [(s, s ^ k) for s in range(n)]) for k in range(1, n)]


def exchange_ring(xs, axis):
    n = lax.axis_size(axis)
    return [xs[0]] + [lax.ppermute(xs[k], axis, [(s, (s + k) % n) for s in range(n)]) for k in range(1, n)]


def far_first(refs):
    return [refs[0], *refs[:0:-1]]


def partners(n):
    me = lax.axis_index("prompt")
    return [lax.bitwise_xor(me, k) for k in range(n)]


def shards(
    keys,
    values,
    prompt_gates,
    queries,
    resp_keys,
    resp_values,
    resp_gates,
    cotangent,
    group_ids,
    resp_lengths,
    loss_mask,
    advantages,
):
    n = lax.axis_size("prompt")
    chips = lax.axis_size("z")
    cores = lax.axis_size("core")
    responses, slots, width = queries.shape
    block = H * DH // n
    shape = jax.ShapeDtypeStruct

    outs = pl.pallas_call(
        lambda *refs: first_kernel(n, *refs),
        out_shape=[shape((block * (1 + responses) + 16, DH), BF16)] * n
        + [shape((8 * (responses + 1), slots), F32)]
        + [shape(queries.shape, BF16)] * 2,
        in_specs=[ANY] * 10,
        out_specs=[VMEM] * (n + 3),
        scratch_shapes=[
            pltpu.VMEM(keys.shape, BF16),
            pltpu.VMEM(values.shape, BF16),
            pltpu.VMEM(prompt_gates.shape, F32),
            pltpu.VMEM(resp_gates.shape, F32),
            pltpu.VMEM(loss_mask.shape, jnp.int32),
            pltpu.SMEM(group_ids.shape, jnp.int32),
            pltpu.SMEM(resp_lengths.shape, jnp.int32),
            pltpu.SMEM(advantages.shape, jnp.int32),
            pltpu.VMEM((H * (1 + responses), DH, DH), F32),
            pltpu.SemaphoreType.DMA((10,)),
        ],
        compiler_params=params(32),
        name="first",
    )(
        *[in_hbm(x) for x in (group_ids, resp_lengths, advantages, keys, values, prompt_gates, resp_gates)],
        *[in_hbm(x) for x in (loss_mask, queries, cotangent)],
    )
    msgs, (rows, queries, cotangent) = outs[:n], outs[n:]

    like = shape(queries.shape, F32)
    like_out = shape(queries.shape, BF16)

    held_shapes = [like, like] + [like_out] * 4 + [shape((8, 128), F32)]

    def first_sweep(units):
        outs = pl.pallas_call(
            lambda *refs: sweep_kernel(units, (), *refs[:5], None, *refs[5:8], refs[-1], *refs[8:-1]),
            out_shape=[shape((slots, 128), F32), like_out, like_out] + held_shapes,
            in_specs=[VMEM, VMEM, ANY, ANY, VMEM],
            out_specs=[VMEM] * 10,
            scratch_shapes=[pltpu.SemaphoreType.DMA((2 * responses,))],
            compiler_params=params(),
            name="sweep",
        )(rows, queries, in_hbm(resp_keys), in_hbm(resp_values), cotangent)
        return outs[0], outs[1], outs[2], outs[3:9], outs[9]

    def sweep(units, before, token, done=()):
        writes = len(done) > 0
        outs = pl.pallas_call(
            lambda *refs: sweep_kernel(units, done, *refs),
            out_shape=held_shapes + [like_out] * (2 * writes),
            in_specs=[VMEM] * 6 + [ANY] * 7,
            out_specs=[VMEM] * 7 + [ANY] * (2 * writes),
            scratch_shapes=[pltpu.SemaphoreType.DMA((2 * responses,))] * writes,
            input_output_aliases={7 + k: k for k in range(6)},
            compiler_params=params(),
            name="sweep",
        )(rows, queries, resp_keys, resp_values, cotangent, cols, token, *before)
        return (outs[:4] + outs[7:] if writes else outs[:6]), outs[6]

    units = [(r, h) for r in range(responses) for h in range(H)]
    got1 = far_first(exchange(msgs, "prompt"))
    cols, resp_keys, resp_values, held, token = first_sweep(units[:2])
    outs = pl.pallas_call(
        lambda *refs: second_kernel(n, chips, cores, *refs),
        out_shape=[shape(((1 + cores) * block, DH), BF16)] * chips + [shape((8, DH), F32)],
        in_specs=[VMEM] * n + [ANY],
        out_specs=[VMEM] * (chips + 1),
        scratch_shapes=[pltpu.VMEM((chips * cores, block, DH), F32)],
        compiler_params=params(),
        name="second",
    )(*got1, token)
    msgs, later = outs[:chips], outs[chips]
    got2 = exchange_ring(msgs, "z")
    held, token = sweep(units[2:5], held, later)
    sent, kept = pl.pallas_call(
        lambda *refs: swap_kernel(chips, *refs),
        out_shape=[shape(((chips + 1) * block, DH), BF16)] * 2,
        in_specs=[VMEM] * chips + [ANY],
        out_specs=[VMEM, VMEM],
        compiler_params=params(),
        name="swap",
    )(*got2, token)
    swapped = exchange([kept, sent], "core")[1]
    held, token = sweep(units[5:6], held, kept)
    msgs = pl.pallas_call(
        lambda *refs: third_kernel(n, chips, *refs),
        out_shape=[shape(((responses + 1) * block, DH), BF16)] * n,
        in_specs=[VMEM] * (n + 2) + [ANY],
        out_specs=[VMEM] * n,
        compiler_params=params(),
        name="third",
    )(*got1, kept, swapped, token)
    got3 = exchange(msgs, "prompt")
    held, token = sweep(units[6:], held, msgs[0], range(responses - 1))
    partial_out, partial_dq, query, grad_out, resp_dk, resp_dv = held

    resp_out, resp_dq, prompt_dk, prompt_dv = pl.pallas_call(
        lambda *refs: last_kernel(n, responses, *refs),
        out_shape=[like_out] * 2 + [shape(keys.shape, BF16)] * 2,
        in_specs=[VMEM] * (8 + n) + [ANY],
        out_specs=[ANY] * 4,
        scratch_shapes=[
            pltpu.VMEM((responses + 1, width, width), BF16),
            pltpu.VMEM(queries.shape, BF16),
            pltpu.VMEM(queries.shape, BF16),
            pltpu.VMEM(keys.shape[1:], BF16),
            pltpu.VMEM(keys.shape[1:], BF16),
            pltpu.SemaphoreType.DMA((2 + 2 * responses,)),
        ],
        compiler_params=params(),
        name="last",
    )(cols, query, grad_out, partial_out, partial_dq, keys, values, later, *got3, token)
    return (resp_out, resp_dq, resp_dk, resp_dv, prompt_dk, prompt_dv)


def solution(mesh):
    n, count = mesh.shape["prompt"], mesh.shape["resp"]
    mesh = jax.sharding.Mesh(mesh.devices.reshape(n, count // 2, 2), ("prompt", "z", "core"))
    spread = P(("prompt", "z", "core"))
    three = P(("prompt", "z", "core"), None, None)
    two = P(("prompt", "z", "core"), None)
    prompt = P(("z", "core"), "prompt", None)
    return jax.shard_map(
        shards,
        mesh=mesh,
        in_specs=(
            prompt,
            prompt,
            P(("z", "core"), None, "prompt"),
            three,
            three,
            three,
            three,
            three,
            spread,
            two,
            two,
            spread,
        ),
        out_specs=(three, three, three, three, prompt, prompt),
        check_vma=False,
    )
```

```python
import jax
import jax.numpy as jnp
from jax import lax
from jax.experimental import pallas as pl
from jax.experimental.pallas import tpu as pltpu
from jax.sharding import PartitionSpec as P

H = 2
DH = 128
HALF = 256
LOG2E = 1.4426950408889634
F32 = jnp.float32
BF16 = jnp.bfloat16
NEVER = -1e30
VMEM = pl.BlockSpec(memory_space=pltpu.VMEM)
ANY = pl.BlockSpec(memory_space=pl.ANY)
SMEM = pl.BlockSpec(memory_space=pltpu.SMEM)


def params(mebibytes=16):
    return pltpu.CompilerParams(vmem_limit_bytes=mebibytes * 1024 * 1024)


def mm(a, b):
    return lax.dot_general(a, b, (((1,), (0,)), ((), ())), preferred_element_type=F32)


def mm_nt(a, b):
    return lax.dot_general(a, b, (((1,), (1,)), ((), ())), preferred_element_type=F32)


def mm_tn(a, b):
    return lax.dot_general(a, b, (((0,), (0,)), ((), ())), preferred_element_type=F32)


def to_columns(rows):
    return jnp.concatenate([rows, jnp.zeros((128 - rows.shape[0], rows.shape[1]), F32)], axis=0).T


def in_hbm(x):
    return pltpu.with_memory_space_constraint(x, pltpu.HBM)


def three_terms(x):
    high = x.astype(BF16)
    rest = x - high.astype(F32)
    middle = rest.astype(BF16)
    return high, middle, (rest - middle.astype(F32)).astype(BF16)


def lane_cumsum(x):
    rows, width = x.shape
    ones = lax.broadcasted_iota(jnp.int32, (128, 128), 0) <= lax.broadcasted_iota(jnp.int32, (128, 128), 1)
    terms = jnp.concatenate(three_terms(x), axis=0)
    starts = range(0, width, 128)
    sums = mm(jnp.concatenate([terms[:, b : b + 128] for b in starts], axis=0), ones.astype(F32).astype(BF16))
    parts = []
    before = jnp.zeros((rows, 1), F32)
    for b in range(len(starts)):
        at = 3 * rows * b
        part = sums[at : at + rows] + sums[at + rows : at + 2 * rows] + sums[at + 2 * rows : at + 3 * rows]
        part = part + before
        before = part[:, 127:128]
        parts.append(part)
    return jnp.concatenate(parts, axis=1)


def first_kernel(
    n, ids_hbm, lens_hbm, adv_hbm, keys_hbm, values_hbm, pgates_hbm, gates_hbm, mask_hbm, q_hbm, c_hbm,
    *refs,
):
    msgs, (rows_ref, q, c) = refs[:n], refs[n : n + 3]
    keys, values, pgates, gates, mask, ids_ref, lens_ref, adv_ref, matrices, sems = refs[n + 3 :]
    pairs = [(pgates_hbm, pgates), (gates_hbm, gates), (lens_hbm, lens_ref), (adv_hbm, adv_ref), (mask_hbm, mask)]
    pairs += [(keys_hbm, keys), (values_hbm, values), (q_hbm, q), (c_hbm, c), (ids_hbm, ids_ref)]
    copies = [pltpu.make_async_copy(a, b, sems.at[i]) for i, (a, b) in enumerate(pairs)]
    for copy in copies:
        copy.start()
    count = gates.shape[0]
    slots = gates.shape[2]
    tokens = keys.shape[1]
    part = DH // n
    block = H * part
    targets = partners(n)

    def spread(at):
        for k in range(n):
            of = pl.ds(pl.multiple_of(targets[k] * part, part), part)
            msgs[k][at * part + (16 if at >= H else 0) : (at + 1) * part + (16 if at >= H else 0), :] = matrices[
                at, of, :
            ].astype(BF16)

    copies[0].wait()
    copies[1].wait()
    piece = jnp.concatenate([pgates[0], jnp.zeros((H, slots - tokens), F32)], axis=1)
    gate_rows = [gates[i] for i in range(count)] + [piece, jnp.zeros((16 - H * (count + 1), slots), F32)]
    cum = lane_cumsum(jnp.concatenate(gate_rows, axis=0))
    carried = jnp.exp(cum)
    place = lax.broadcasted_iota(jnp.int32, (1, slots), 1)
    for copy in copies[2:5]:
        copy.wait()
    rows = []
    factors = []
    for i in range(count):
        weight = adv_ref[i].astype(F32) / 1024.0
        opened = jnp.where(place < lens_ref[0, i], 1.0, 0.0)
        live = mask[i : i + 1, :].astype(F32) * opened * weight
        rows += [cum[H * i : H * i + H], carried[H * i : H * i + H] * opened, live, opened, jnp.zeros((2, slots), F32)]
        factors.append(carried[H * i : H * i + H] * live)
    piece = cum[H * count : H * count + H]
    total = piece[:, -1:]
    suffix = total - piece
    rows += [suffix, jnp.zeros((8 - H, slots), F32)]
    rows_ref[...] = jnp.concatenate(rows, axis=0)

    copies[5].wait()
    copies[6].wait()
    turned = keys[0].T
    later = jnp.exp(suffix[:, :tokens])
    for h in range(H):
        lanes = slice(h * DH, (h + 1) * DH)
        scaled = turned[lanes].astype(F32) * later[h : h + 1]
        high = scaled.astype(BF16)
        low = (scaled - high.astype(F32)).astype(BF16)
        both = mm(jnp.concatenate([high, low], axis=0), values[0, :, lanes])
        matrices[h] = both[:DH] + both[DH:]
        spread(h)
    copies[7].wait()
    copies[8].wait()
    for i in range(count):
        turned = q[i].T
        for h in range(H):
            lanes = slice(h * DH, (h + 1) * DH)
            scaled = (turned[lanes].astype(F32) * factors[i][h : h + 1]).astype(BF16)
            matrices[H * (1 + i) + h] = mm(scaled, c[i, :, lanes])
            spread(H * (1 + i) + h)
    copies[9].wait()
    notes = [jnp.broadcast_to(x[h : h + 1].astype(F32), (1, DH)) for x in three_terms(total) for h in range(H)]
    notes += [jnp.full((1, DH), ids_ref[i].astype(F32)) for i in range(count)]
    notes.append(jnp.zeros((16 - len(notes), DH), F32))
    notes = jnp.concatenate(notes, axis=0).astype(BF16)
    for k in range(n):
        msgs[k][block : block + 16, :] = notes


def noted_prompt(notes, i):
    return jnp.max(notes[3 * H + i : 3 * H + i + 1]).astype(jnp.int32)


def second_kernel(n, chips, cores, *refs):
    z_at = lax.axis_index("z")
    got, msgs, later_ref, sums = far_first(refs[:n]), refs[n + 1 : n + 1 + chips], refs[-2], refs[-1]
    part = DH // n
    block = H * part
    responses = (got[0].shape[0] - block - 16) // block
    place = partners(n)
    notes = [got[k][block : block + 16, :].astype(F32) for k in range(n)]
    logs = [x[0:H] + x[H : 2 * H] + x[2 * H : 3 * H] for x in notes]
    final = jnp.zeros((block, DH), F32)
    for k in range(n):
        later = jnp.zeros_like(logs[0])
        for other in range(n):
            if other != k:
                later = later + jnp.where(place[other] > place[k], logs[other], 0.0)
        if k == 0:
            later_ref[...] = jnp.concatenate([later, jnp.zeros((8 - H, DH), F32)], axis=0)
        decay = jnp.exp(later)
        decay = [jnp.broadcast_to(decay[h : h + 1], (part, DH)) for h in range(H)]
        final = final + jnp.concatenate(decay, axis=0) * got[k][0:block, :].astype(F32)
    sums[...] = jnp.zeros_like(sums)
    for k in range(n):
        for i in range(responses):
            at = block * (1 + i) + 16
            sums[noted_prompt(notes[k], i)] += got[k][at : at + block, :].astype(F32)
    final = final.astype(BF16)
    for k in range(chips):
        z = lax.rem(z_at + k, chips)
        msgs[k][0:block, :] = final
        for c in range(cores):
            msgs[k][(1 + c) * block : (2 + c) * block, :] = sums[z * cores + c].astype(BF16)


def swap_kernel(chips, *refs):
    got, sent_ref, kept_ref = refs[:chips], refs[chips + 1], refs[chips + 2]
    block = got[0].shape[0] // 3
    totals = []
    for c in range(2):
        total = got[0][(1 + c) * block : (2 + c) * block, :].astype(F32)
        for k in range(1, chips):
            total = total + got[k][(1 + c) * block : (2 + c) * block, :].astype(F32)
        totals.append(total)
    for k in range(chips):
        final = got[k][0:block, :]
        sent_ref[k * block : (k + 1) * block, :] = final
        kept_ref[k * block : (k + 1) * block, :] = final
    low = lax.axis_index("core") == 0
    sent_ref[chips * block :, :] = jnp.where(low, totals[1], totals[0]).astype(BF16)
    kept_ref[chips * block :, :] = jnp.where(low, totals[0], totals[1]).astype(BF16)


def third_kernel(n, chips, *refs):
    z_at, core = lax.axis_index("z"), lax.axis_index("core")
    noted, kept_ref, got_ref, msgs = far_first(refs[:n]), refs[n], refs[n + 1], refs[n + 3 :]
    block = H * DH // n
    responses = (noted[0].shape[0] - block - 16) // block
    total = kept_ref[chips * block :, :].astype(F32) + got_ref[chips * block :, :].astype(F32)
    total = total.astype(BF16)
    for k in range(n):
        notes = noted[k][block : block + 16, :].astype(F32)
        for i in range(responses):
            p = noted_prompt(notes, i)
            slot = lax.rem(z_at + chips - lax.div(p, 2), chips)
            at = pl.ds(pl.multiple_of(slot * block, block), block)
            same = lax.rem(p, 2) == core
            state = jnp.where(same, kept_ref[at, :].astype(F32), got_ref[at, :].astype(F32))
            msgs[k][i * block : (i + 1) * block, :] = state.astype(BF16)
        msgs[k][responses * block :, :] = total


def sweep_kernel(units, done, rows_ref, q_ref, k_ref, v_ref, c_ref, cols_ref, *refs):
    writes = len(done) > 0
    if writes:
        *refs, dk_hbm, dv_hbm, sems = refs
    out_ref, dq_ref, query_ref, grad_ref, dk_ref, dv_ref, token_ref = refs[-7:]
    fetches = []
    if cols_ref is None:
        cols_ref, k_vmem, v_vmem = refs[:3]
        sems = refs[-8]
        for r in range(k_ref.shape[0]):
            for a, b in ((k_ref, k_vmem), (v_ref, v_vmem)):
                fetches.append(pltpu.make_async_copy(a.at[r], b.at[r], sems.at[len(fetches)]))
                fetches[-1].start()
        cols_ref[...] = to_columns(rows_ref[...])
        k_ref, v_ref = k_vmem, v_vmem
        for fetch in fetches[:2]:
            fetch.wait()
    copies = []

    def send(r):
        for a, b in ((dk_ref, dk_hbm), (dv_ref, dv_hbm)):
            copies.append(pltpu.make_async_copy(a.at[r], b.at[r], sems.at[len(copies)]))
            copies[-1].start()

    for r in done:
        send(r)
    token_ref[...] = jnp.zeros_like(token_ref)
    quarter = HALF // 2
    causal = lax.broadcasted_iota(jnp.int32, (quarter, quarter), 0) >= lax.broadcasted_iota(
        jnp.int32, (quarter, quarter), 1
    )
    blank = jnp.zeros((quarter, quarter), BF16)
    blocks = q_ref.shape[1] // HALF

    def decayed(products, cum, row, diagonal):
        if not diagonal:
            decay = jnp.exp2(cum - row)
            return [(x * decay).astype(BF16) for x in products]
        first = jnp.exp2(jnp.where(causal, cum[:quarter] - row[:, :quarter], NEVER))
        left = jnp.exp2(cum[quarter:] - row[:, :quarter])
        right = jnp.exp2(jnp.where(causal, cum[quarter:] - row[:, quarter:], NEVER))
        results = []
        for x in products:
            upper = jnp.concatenate([(x[:quarter, :quarter] * first).astype(BF16), blank], axis=1)
            lower = [(x[quarter:, :quarter] * left).astype(BF16), (x[quarter:, quarter:] * right).astype(BF16)]
            results.append(jnp.concatenate([upper, jnp.concatenate(lower, axis=1)], axis=0))
        return results

    for r, h in units:
        lanes = slice(h * DH, (h + 1) * DH)
        cum = cols_ref[:, 8 * r + h : 8 * r + h + 1] * LOG2E
        row = rows_ref[8 * r + h : 8 * r + h + 1, :] * LOG2E
        live = cols_ref[:, 8 * r + 4 : 8 * r + 5]
        opened = cols_ref[:, 8 * r + 5 : 8 * r + 6]
        grad_all = (c_ref[r, :, lanes].astype(F32) * live).astype(BF16)
        carried = cols_ref[:, 8 * r + 2 + h : 8 * r + 3 + h]
        query_ref[r, :, lanes] = (q_ref[r, :, lanes].astype(F32) * carried).astype(BF16)
        grad_ref[r, :, lanes] = (grad_all.astype(F32) * carried).astype(BF16)
        query_turned = q_ref[r, :, lanes].T
        grad_turned = grad_all.T
        dk = [None] * blocks
        dv = [None] * blocks
        for t in range(blocks):
            at = slice(t * HALF, (t + 1) * HALF)
            query = q_ref[r, at, lanes]
            grad_out = grad_all[at]
            out = None
            dq = None
            for s in range(t + 1):
                of = slice(s * HALF, (s + 1) * HALF)
                key = k_ref[r, of, lanes]
                value = v_ref[r, of, lanes]
                mixing, scores = decayed(
                    [mm_nt(query, key), mm_nt(grad_out, value)], cum[at], row[:, of], s == t
                )
                o_new = mm(mixing, value)
                q_new = mm(scores, key)
                k_new = mm(query_turned[:, at], scores)
                v_new = mm(grad_turned[:, at], mixing)
                out = o_new if out is None else out + o_new
                dq = q_new if dq is None else dq + q_new
                dk[s] = k_new if dk[s] is None else dk[s] + k_new
                dv[s] = v_new if dv[s] is None else dv[s] + v_new
            out_ref[r, at, lanes] = out * opened[at]
            dq_ref[r, at, lanes] = dq
        for s in range(blocks):
            of = slice(s * HALF, (s + 1) * HALF)
            dk_ref[r, of, lanes] = dk[s].astype(BF16).T
            dv_ref[r, of, lanes] = dv[s].astype(BF16).T
        if writes and h == H - 1:
            send(r)
    for copy in copies + fetches[2:]:
        copy.wait()


def last_kernel(
    n, count, cols_ref, q_ref, grad_ref, po_ref, pdq_ref, keys_ref, values_ref, later_ref, *refs
):
    got, refs = refs[:n], refs[n + 1 :]
    out_hbm, dq_hbm, dk_hbm, dv_hbm, start, out_buf, dq_buf, dk_buf, dv_buf, sems = refs
    part = DH // n
    block = H * part
    place = partners(n)
    slots = q_ref.shape[1]
    tokens = keys_ref.shape[1]
    copies = []

    def send(a, b):
        copies.append(pltpu.make_async_copy(a, b, sems.at[len(copies)]))
        copies[-1].start()

    start[...] = jnp.zeros_like(start)
    for r in range(count + 1):
        for k in range(n):
            for h in range(H):
                of = pl.ds(pl.multiple_of(h * DH + place[k] * part, part), part)
                rows = got[k][r * block + h * part : r * block + (h + 1) * part, :]
                start[r, of, h * DH : (h + 1) * DH] = rows
    for r in range(count):
        for t in range(0, slots, HALF):
            at = slice(t, t + HALF)
            out_buf[r, at, :] = (po_ref[r, at, :] + mm(q_ref[r, at, :], start[r])).astype(BF16)
            send(out_buf.at[r, at], out_hbm.at[r, at])
            dq_buf[r, at, :] = (pdq_ref[r, at, :] + mm_nt(grad_ref[r, at, :], start[r])).astype(BF16)
            send(dq_buf.at[r, at], dq_hbm.at[r, at])
    factor = [
        jnp.exp(cols_ref[:tokens, 8 * count + h : 8 * count + h + 1] + later_ref[h : h + 1, 0:1]) for h in range(H)
    ]
    for buf, x in ((dk_buf, mm_nt(values_ref[0], start[count])), (dv_buf, mm(keys_ref[0], start[count]))):
        for h in range(H):
            lanes = slice(h * DH, (h + 1) * DH)
            buf[:, lanes] = (factor[h] * x[:, lanes]).astype(BF16)
    send(dk_buf, dk_hbm.at[0])
    send(dv_buf, dv_hbm.at[0])
    for copy in copies:
        copy.wait()


def exchange(xs, axis):
    n = lax.axis_size(axis)
    return [xs[0]] + [lax.ppermute(xs[k], axis, [(s, s ^ k) for s in range(n)]) for k in range(1, n)]


def exchange_ring(xs, axis):
    n = lax.axis_size(axis)
    return [xs[0]] + [lax.ppermute(xs[k], axis, [(s, (s + k) % n) for s in range(n)]) for k in range(1, n)]


def far_first(refs):
    return [refs[0], *refs[:0:-1]]


def partners(n):
    me = lax.axis_index("prompt")
    return [lax.bitwise_xor(me, k) for k in range(n)]


def shards(
    keys,
    values,
    prompt_gates,
    queries,
    resp_keys,
    resp_values,
    resp_gates,
    cotangent,
    group_ids,
    resp_lengths,
    loss_mask,
    advantages,
):
    n = lax.axis_size("prompt")
    chips = lax.axis_size("z")
    cores = lax.axis_size("core")
    responses, slots, width = queries.shape
    block = H * DH // n
    shape = jax.ShapeDtypeStruct

    outs = pl.pallas_call(
        lambda *refs: first_kernel(n, *refs),
        out_shape=[shape((block * (1 + responses) + 16, DH), BF16)] * n
        + [shape((8 * (responses + 1), slots), F32)]
        + [shape(queries.shape, BF16)] * 2,
        in_specs=[ANY] * 10,
        out_specs=[VMEM] * (n + 3),
        scratch_shapes=[
            pltpu.VMEM(keys.shape, BF16),
            pltpu.VMEM(values.shape, BF16),
            pltpu.VMEM(prompt_gates.shape, F32),
            pltpu.VMEM(resp_gates.shape, F32),
            pltpu.VMEM(loss_mask.shape, jnp.int32),
            pltpu.SMEM(group_ids.shape, jnp.int32),
            pltpu.SMEM(resp_lengths.shape, jnp.int32),
            pltpu.SMEM(advantages.shape, jnp.int32),
            pltpu.VMEM((H * (1 + responses), DH, DH), F32),
            pltpu.SemaphoreType.DMA((10,)),
        ],
        compiler_params=params(32),
        name="first",
    )(
        *[in_hbm(x) for x in (group_ids, resp_lengths, advantages, keys, values, prompt_gates, resp_gates)],
        *[in_hbm(x) for x in (loss_mask, queries, cotangent)],
    )
    msgs, (rows, queries, cotangent) = outs[:n], outs[n:]

    like = shape(queries.shape, F32)
    like_out = shape(queries.shape, BF16)

    held_shapes = [like, like] + [like_out] * 4 + [shape((8, 128), F32)]

    def first_sweep(units):
        outs = pl.pallas_call(
            lambda *refs: sweep_kernel(units, (), *refs[:5], None, *refs[5:8], refs[-1], *refs[8:-1]),
            out_shape=[shape((slots, 128), F32), like_out, like_out] + held_shapes,
            in_specs=[VMEM, VMEM, ANY, ANY, VMEM],
            out_specs=[VMEM] * 10,
            scratch_shapes=[pltpu.SemaphoreType.DMA((2 * responses,))],
            compiler_params=params(),
            name="sweep",
        )(rows, queries, in_hbm(resp_keys), in_hbm(resp_values), cotangent)
        return outs[0], outs[1], outs[2], outs[3:9], outs[9]

    def sweep(units, before, token, done=()):
        writes = len(done) > 0
        outs = pl.pallas_call(
            lambda *refs: sweep_kernel(units, done, *refs),
            out_shape=held_shapes + [like_out] * (2 * writes),
            in_specs=[VMEM] * 6 + [ANY] * 7,
            out_specs=[VMEM] * 7 + [ANY] * (2 * writes),
            scratch_shapes=[pltpu.SemaphoreType.DMA((2 * responses,))] * writes,
            input_output_aliases={7 + k: k for k in range(6)},
            compiler_params=params(),
            name="sweep",
        )(rows, queries, resp_keys, resp_values, cotangent, cols, token, *before)
        return (outs[:4] + outs[7:] if writes else outs[:6]), outs[6]

    units = [(r, h) for r in range(responses) for h in range(H)]
    got1 = far_first(exchange(msgs, "prompt"))
    cols, resp_keys, resp_values, held, token = first_sweep(units[:2])
    outs = pl.pallas_call(
        lambda *refs: second_kernel(n, chips, cores, *refs),
        out_shape=[shape(((1 + cores) * block, DH), BF16)] * chips + [shape((8, DH), F32)],
        in_specs=[VMEM] * n + [ANY],
        out_specs=[VMEM] * (chips + 1),
        scratch_shapes=[pltpu.VMEM((chips * cores, block, DH), F32)],
        compiler_params=params(),
        name="second",
    )(*got1, token)
    msgs, later = outs[:chips], outs[chips]
    got2 = exchange_ring(msgs, "z")
    held, token = sweep(units[2:5], held, later)
    sent, kept = pl.pallas_call(
        lambda *refs: swap_kernel(chips, *refs),
        out_shape=[shape(((chips + 1) * block, DH), BF16)] * 2,
        in_specs=[VMEM] * chips + [ANY],
        out_specs=[VMEM, VMEM],
        compiler_params=params(),
        name="swap",
    )(*got2, token)
    swapped = exchange([kept, sent], "core")[1]
    held, token = sweep(units[5:6], held, kept)
    msgs = pl.pallas_call(
        lambda *refs: third_kernel(n, chips, *refs),
        out_shape=[shape(((responses + 1) * block, DH), BF16)] * n,
        in_specs=[VMEM] * (n + 2) + [ANY],
        out_specs=[VMEM] * n,
        compiler_params=params(),
        name="third",
    )(*got1, kept, swapped, token)
    got3 = exchange(msgs, "prompt")
    held, token = sweep(units[6:], held, msgs[0], range(responses - 1))
    partial_out, partial_dq, query, grad_out, resp_dk, resp_dv = held

    resp_out, resp_dq, prompt_dk, prompt_dv = pl.pallas_call(
        lambda *refs: last_kernel(n, responses, *refs),
        out_shape=[like_out] * 2 + [shape(keys.shape, BF16)] * 2,
        in_specs=[VMEM] * (8 + n) + [ANY],
        out_specs=[ANY] * 4,
        scratch_shapes=[
            pltpu.VMEM((responses + 1, width, width), BF16),
            pltpu.VMEM(queries.shape, BF16),
            pltpu.VMEM(queries.shape, BF16),
            pltpu.VMEM(keys.shape[1:], BF16),
            pltpu.VMEM(keys.shape[1:], BF16),
            pltpu.SemaphoreType.DMA((2 + 2 * responses * (slots // HALF),)),
        ],
        compiler_params=params(),
        name="last",
    )(cols, query, grad_out, partial_out, partial_dq, keys, values, later, *got3, token)
    return (resp_out, resp_dq, resp_dk, resp_dv, prompt_dk, prompt_dv)


def solution(mesh):
    n, count = mesh.shape["prompt"], mesh.shape["resp"]
    mesh = jax.sharding.Mesh(mesh.devices.reshape(n, count // 2, 2), ("prompt", "z", "core"))
    spread = P(("prompt", "z", "core"))
    three = P(("prompt", "z", "core"), None, None)
    two = P(("prompt", "z", "core"), None)
    prompt = P(("z", "core"), "prompt", None)
    return jax.shard_map(
        shards,
        mesh=mesh,
        in_specs=(
            prompt,
            prompt,
            P(("z", "core"), None, "prompt"),
            three,
            three,
            three,
            three,
            three,
            spread,
            two,
            two,
            spread,
        ),
        out_specs=(three, three, three, three, prompt, prompt),
        check_vma=False,
    )
```

```python
import jax
import jax.numpy as jnp
from jax import lax
from jax.experimental import pallas as pl
from jax.experimental.pallas import tpu as pltpu
from jax.sharding import PartitionSpec as P

H = 2
DH = 128
HALF = 256
LOG2E = 1.4426950408889634
F32 = jnp.float32
BF16 = jnp.bfloat16
NEVER = -1e30
VMEM = pl.BlockSpec(memory_space=pltpu.VMEM)
ANY = pl.BlockSpec(memory_space=pl.ANY)
SMEM = pl.BlockSpec(memory_space=pltpu.SMEM)


def params(mebibytes=16):
    return pltpu.CompilerParams(vmem_limit_bytes=mebibytes * 1024 * 1024)


def mm(a, b):
    return lax.dot_general(a, b, (((1,), (0,)), ((), ())), preferred_element_type=F32)


def mm_nt(a, b):
    return lax.dot_general(a, b, (((1,), (1,)), ((), ())), preferred_element_type=F32)


def mm_tn(a, b):
    return lax.dot_general(a, b, (((0,), (0,)), ((), ())), preferred_element_type=F32)


def to_columns(rows):
    return jnp.concatenate([rows, jnp.zeros((128 - rows.shape[0], rows.shape[1]), F32)], axis=0).T


def in_hbm(x):
    return pltpu.with_memory_space_constraint(x, pltpu.HBM)


def three_terms(x):
    high = x.astype(BF16)
    rest = x - high.astype(F32)
    middle = rest.astype(BF16)
    return high, middle, (rest - middle.astype(F32)).astype(BF16)


def lane_cumsum(x):
    rows, width = x.shape
    ones = lax.broadcasted_iota(jnp.int32, (128, 128), 0) <= lax.broadcasted_iota(jnp.int32, (128, 128), 1)
    terms = jnp.concatenate(three_terms(x), axis=0)
    starts = range(0, width, 128)
    sums = mm(jnp.concatenate([terms[:, b : b + 128] for b in starts], axis=0), ones.astype(F32).astype(BF16))
    parts = []
    before = jnp.zeros((rows, 1), F32)
    for b in range(len(starts)):
        at = 3 * rows * b
        part = sums[at : at + rows] + sums[at + rows : at + 2 * rows] + sums[at + 2 * rows : at + 3 * rows]
        part = part + before
        before = part[:, 127:128]
        parts.append(part)
    return jnp.concatenate(parts, axis=1)


def first_kernel(
    n, ids_hbm, lens_hbm, adv_hbm, keys_hbm, values_hbm, pgates_hbm, gates_hbm, mask_hbm, q_hbm, c_hbm,
    *refs,
):
    msgs, (rows_ref, q, c) = refs[:n], refs[n : n + 3]
    keys, values, pgates, gates, mask, ids_ref, lens_ref, adv_ref, matrices, sems = refs[n + 3 :]
    pairs = [(pgates_hbm, pgates), (gates_hbm, gates), (lens_hbm, lens_ref), (adv_hbm, adv_ref), (mask_hbm, mask)]
    pairs += [(keys_hbm, keys), (values_hbm, values), (q_hbm, q), (c_hbm, c), (ids_hbm, ids_ref)]
    copies = [pltpu.make_async_copy(a, b, sems.at[i]) for i, (a, b) in enumerate(pairs)]
    for copy in copies:
        copy.start()
    count = gates.shape[0]
    slots = gates.shape[2]
    tokens = keys.shape[1]
    part = DH // n
    block = H * part
    targets = partners(n)

    def spread(at):
        for k in range(n):
            of = pl.ds(pl.multiple_of(targets[k] * part, part), part)
            msgs[k][at * part + (16 if at >= H else 0) : (at + 1) * part + (16 if at >= H else 0), :] = matrices[
                at, of, :
            ].astype(BF16)

    copies[0].wait()
    copies[1].wait()
    piece = jnp.concatenate([pgates[0], jnp.zeros((H, slots - tokens), F32)], axis=1)
    gate_rows = [gates[i] for i in range(count)] + [piece, jnp.zeros((16 - H * (count + 1), slots), F32)]
    cum = lane_cumsum(jnp.concatenate(gate_rows, axis=0))
    carried = jnp.exp(cum)
    place = lax.broadcasted_iota(jnp.int32, (1, slots), 1)
    for copy in copies[2:5]:
        copy.wait()
    rows = []
    factors = []
    for i in range(count):
        weight = adv_ref[i].astype(F32) / 1024.0
        opened = jnp.where(place < lens_ref[0, i], 1.0, 0.0)
        live = mask[i : i + 1, :].astype(F32) * opened * weight
        rows += [cum[H * i : H * i + H], carried[H * i : H * i + H] * opened, live, opened, jnp.zeros((2, slots), F32)]
        factors.append(carried[H * i : H * i + H] * live)
    piece = cum[H * count : H * count + H]
    total = piece[:, -1:]
    suffix = total - piece
    rows += [suffix, jnp.zeros((8 - H, slots), F32)]
    rows_ref[...] = jnp.concatenate(rows, axis=0)

    copies[5].wait()
    copies[6].wait()
    turned = keys[0].T
    later = jnp.exp(suffix[:, :tokens])
    for h in range(H):
        lanes = slice(h * DH, (h + 1) * DH)
        scaled = turned[lanes].astype(F32) * later[h : h + 1]
        high = scaled.astype(BF16)
        low = (scaled - high.astype(F32)).astype(BF16)
        both = mm(jnp.concatenate([high, low], axis=0), values[0, :, lanes])
        matrices[h] = both[:DH] + both[DH:]
        spread(h)
    copies[7].wait()
    copies[8].wait()
    for i in range(count):
        turned = q[i].T
        for h in range(H):
            lanes = slice(h * DH, (h + 1) * DH)
            scaled = (turned[lanes].astype(F32) * factors[i][h : h + 1]).astype(BF16)
            matrices[H * (1 + i) + h] = mm(scaled, c[i, :, lanes])
            spread(H * (1 + i) + h)
    copies[9].wait()
    notes = [jnp.broadcast_to(x[h : h + 1].astype(F32), (1, DH)) for x in three_terms(total) for h in range(H)]
    notes += [jnp.full((1, DH), ids_ref[i].astype(F32)) for i in range(count)]
    notes.append(jnp.zeros((16 - len(notes), DH), F32))
    notes = jnp.concatenate(notes, axis=0).astype(BF16)
    for k in range(n):
        msgs[k][block : block + 16, :] = notes


def noted_prompt(notes, i):
    return jnp.max(notes[3 * H + i : 3 * H + i + 1]).astype(jnp.int32)


def second_kernel(n, chips, cores, *refs):
    z_at = lax.axis_index("z")
    got, msgs, later_ref, sums = far_first(refs[:n]), refs[n + 1 : n + 1 + chips], refs[-2], refs[-1]
    part = DH // n
    block = H * part
    responses = (got[0].shape[0] - block - 16) // block
    place = partners(n)
    notes = [got[k][block : block + 16, :].astype(F32) for k in range(n)]
    logs = [x[0:H] + x[H : 2 * H] + x[2 * H : 3 * H] for x in notes]
    final = jnp.zeros((block, DH), F32)
    for k in range(n):
        later = jnp.zeros_like(logs[0])
        for other in range(n):
            if other != k:
                later = later + jnp.where(place[other] > place[k], logs[other], 0.0)
        if k == 0:
            later_ref[...] = jnp.concatenate([later, jnp.zeros((8 - H, DH), F32)], axis=0)
        decay = jnp.exp(later)
        decay = [jnp.broadcast_to(decay[h : h + 1], (part, DH)) for h in range(H)]
        final = final + jnp.concatenate(decay, axis=0) * got[k][0:block, :].astype(F32)
    sums[...] = jnp.zeros_like(sums)
    for k in range(n):
        for i in range(responses):
            at = block * (1 + i) + 16
            sums[noted_prompt(notes[k], i)] += got[k][at : at + block, :].astype(F32)
    final = final.astype(BF16)
    for k in range(chips):
        z = lax.rem(z_at + k, chips)
        msgs[k][0:block, :] = final
        for c in range(cores):
            msgs[k][(1 + c) * block : (2 + c) * block, :] = sums[z * cores + c].astype(BF16)


def swap_kernel(chips, *refs):
    got, sent_ref, kept_ref = refs[:chips], refs[chips + 1], refs[chips + 2]
    block = got[0].shape[0] // 3
    totals = []
    for c in range(2):
        total = got[0][(1 + c) * block : (2 + c) * block, :].astype(F32)
        for k in range(1, chips):
            total = total + got[k][(1 + c) * block : (2 + c) * block, :].astype(F32)
        totals.append(total)
    for k in range(chips):
        final = got[k][0:block, :]
        sent_ref[k * block : (k + 1) * block, :] = final
        kept_ref[k * block : (k + 1) * block, :] = final
    low = lax.axis_index("core") == 0
    sent_ref[chips * block :, :] = jnp.where(low, totals[1], totals[0]).astype(BF16)
    kept_ref[chips * block :, :] = jnp.where(low, totals[0], totals[1]).astype(BF16)


def third_kernel(n, chips, *refs):
    z_at, core = lax.axis_index("z"), lax.axis_index("core")
    noted, kept_ref, got_ref, msgs = far_first(refs[:n]), refs[n], refs[n + 1], refs[n + 3 :]
    block = H * DH // n
    responses = (noted[0].shape[0] - block - 16) // block
    total = kept_ref[chips * block :, :].astype(F32) + got_ref[chips * block :, :].astype(F32)
    total = total.astype(BF16)
    for k in range(n):
        notes = noted[k][block : block + 16, :].astype(F32)
        for i in range(responses):
            p = noted_prompt(notes, i)
            slot = lax.rem(z_at + chips - lax.div(p, 2), chips)
            at = pl.ds(pl.multiple_of(slot * block, block), block)
            same = lax.rem(p, 2) == core
            state = jnp.where(same, kept_ref[at, :].astype(F32), got_ref[at, :].astype(F32))
            msgs[k][i * block : (i + 1) * block, :] = state.astype(BF16)
        msgs[k][responses * block :, :] = total


def sweep_kernel(units, done, rows_ref, q_ref, k_ref, v_ref, c_ref, cols_ref, *refs):
    writes = len(done) > 0
    if writes:
        *refs, dk_hbm, dv_hbm, sems = refs
    out_ref, dq_ref, query_ref, grad_ref, dk_ref, dv_ref, token_ref = refs[-7:]
    fetches = []
    if cols_ref is None:
        cols_ref, k_vmem, v_vmem = refs[:3]
        sems = refs[-8]
        for r in range(k_ref.shape[0]):
            for a, b in ((k_ref, k_vmem), (v_ref, v_vmem)):
                fetches.append(pltpu.make_async_copy(a.at[r], b.at[r], sems.at[len(fetches)]))
                fetches[-1].start()
        cols_ref[...] = to_columns(rows_ref[...])
        k_ref, v_ref = k_vmem, v_vmem
        for fetch in fetches[:2]:
            fetch.wait()
    copies = []

    def send(r):
        for a, b in ((dk_ref, dk_hbm), (dv_ref, dv_hbm)):
            copies.append(pltpu.make_async_copy(a.at[r], b.at[r], sems.at[len(copies)]))
            copies[-1].start()

    for r in done:
        send(r)
    token_ref[...] = jnp.zeros_like(token_ref)
    quarter = HALF // 2
    causal = lax.broadcasted_iota(jnp.int32, (quarter, quarter), 0) >= lax.broadcasted_iota(
        jnp.int32, (quarter, quarter), 1
    )
    blank = jnp.zeros((quarter, quarter), BF16)
    blocks = q_ref.shape[1] // HALF

    def decayed(products, cum, row, diagonal):
        if not diagonal:
            decay = jnp.exp2(cum - row)
            return [(x * decay).astype(BF16) for x in products]
        first = jnp.exp2(jnp.where(causal, cum[:quarter] - row[:, :quarter], NEVER))
        left = jnp.exp2(cum[quarter:] - row[:, :quarter])
        right = jnp.exp2(jnp.where(causal, cum[quarter:] - row[:, quarter:], NEVER))
        results = []
        for x in products:
            upper = jnp.concatenate([(x[:quarter, :quarter] * first).astype(BF16), blank], axis=1)
            lower = [(x[quarter:, :quarter] * left).astype(BF16), (x[quarter:, quarter:] * right).astype(BF16)]
            results.append(jnp.concatenate([upper, jnp.concatenate(lower, axis=1)], axis=0))
        return results

    for r, h in units:
        lanes = slice(h * DH, (h + 1) * DH)
        cum = cols_ref[:, 8 * r + h : 8 * r + h + 1] * LOG2E
        row = rows_ref[8 * r + h : 8 * r + h + 1, :] * LOG2E
        live = cols_ref[:, 8 * r + 4 : 8 * r + 5]
        opened = cols_ref[:, 8 * r + 5 : 8 * r + 6]
        grad_all = (c_ref[r, :, lanes].astype(F32) * live).astype(BF16)
        carried = cols_ref[:, 8 * r + 2 + h : 8 * r + 3 + h]
        query_ref[r, :, lanes] = (q_ref[r, :, lanes].astype(F32) * carried).astype(BF16)
        grad_ref[r, :, lanes] = (grad_all.astype(F32) * carried).astype(BF16)
        query_turned = q_ref[r, :, lanes].T
        grad_turned = grad_all.T
        dk = [None] * blocks
        dv = [None] * blocks
        for t in range(blocks):
            at = slice(t * HALF, (t + 1) * HALF)
            query = q_ref[r, at, lanes]
            grad_out = grad_all[at]
            out = None
            dq = None
            for s in range(t + 1):
                of = slice(s * HALF, (s + 1) * HALF)
                key = k_ref[r, of, lanes]
                value = v_ref[r, of, lanes]
                mixing, scores = decayed(
                    [mm_nt(query, key), mm_nt(grad_out, value)], cum[at], row[:, of], s == t
                )
                o_new = mm(mixing, value)
                q_new = mm(scores, key)
                k_new = mm(query_turned[:, at], scores)
                v_new = mm(grad_turned[:, at], mixing)
                out = o_new if out is None else out + o_new
                dq = q_new if dq is None else dq + q_new
                dk[s] = k_new if dk[s] is None else dk[s] + k_new
                dv[s] = v_new if dv[s] is None else dv[s] + v_new
            out_ref[r, at, lanes] = out * opened[at]
            dq_ref[r, at, lanes] = dq
        for s in range(blocks):
            of = slice(s * HALF, (s + 1) * HALF)
            dk_ref[r, of, lanes] = dk[s].astype(BF16).T
            dv_ref[r, of, lanes] = dv[s].astype(BF16).T
        if writes and h == H - 1:
            send(r)
    for copy in copies + fetches[2:]:
        copy.wait()


def last_kernel(
    n, count, cols_ref, q_ref, grad_ref, po_ref, pdq_ref, keys_ref, values_ref, later_ref, *refs
):
    got, refs = refs[:n], refs[n + 1 :]
    out_hbm, dq_hbm, dk_hbm, dv_hbm, start, out_buf, dq_buf, dk_buf, dv_buf, sems = refs
    part = DH // n
    block = H * part
    place = partners(n)
    slots = q_ref.shape[1]
    tokens = keys_ref.shape[1]
    copies = []

    def send(a, b):
        copies.append(pltpu.make_async_copy(a, b, sems.at[len(copies)]))
        copies[-1].start()

    start[...] = jnp.zeros_like(start)
    for r in range(count + 1):
        for k in range(n):
            for h in range(H):
                of = pl.ds(pl.multiple_of(h * DH + place[k] * part, part), part)
                rows = got[k][r * block + h * part : r * block + (h + 1) * part, :]
                start[r, of, h * DH : (h + 1) * DH] = rows
    for r in range(count):
        for t in range(0, slots, HALF):
            at = slice(t, t + HALF)
            out_buf[r, at, :] = (po_ref[r, at, :] + mm(q_ref[r, at, :], start[r])).astype(BF16)
            dq_buf[r, at, :] = (pdq_ref[r, at, :] + mm_nt(grad_ref[r, at, :], start[r])).astype(BF16)
        send(out_buf.at[r], out_hbm.at[r])
        send(dq_buf.at[r], dq_hbm.at[r])
    factor = [
        jnp.exp(cols_ref[:tokens, 8 * count + h : 8 * count + h + 1] + later_ref[h : h + 1, 0:1]) for h in range(H)
    ]
    for buf, x in ((dk_buf, mm_nt(values_ref[0], start[count])), (dv_buf, mm(keys_ref[0], start[count]))):
        for h in range(H):
            lanes = slice(h * DH, (h + 1) * DH)
            buf[:, lanes] = (factor[h] * x[:, lanes]).astype(BF16)
    send(dk_buf, dk_hbm.at[0])
    send(dv_buf, dv_hbm.at[0])
    for copy in copies:
        copy.wait()


def exchange(xs, axis):
    n = lax.axis_size(axis)
    return [xs[0]] + [lax.ppermute(xs[k], axis, [(s, s ^ k) for s in range(n)]) for k in range(1, n)]


def exchange_ring(xs, axis):
    n = lax.axis_size(axis)
    return [xs[0]] + [lax.ppermute(xs[k], axis, [(s, (s + k) % n) for s in range(n)]) for k in range(1, n)]


def far_first(refs):
    return [refs[0], *refs[:0:-1]]


def partners(n):
    me = lax.axis_index("prompt")
    return [lax.bitwise_xor(me, k) for k in range(n)]


def shards(
    keys,
    values,
    prompt_gates,
    queries,
    resp_keys,
    resp_values,
    resp_gates,
    cotangent,
    group_ids,
    resp_lengths,
    loss_mask,
    advantages,
):
    n = lax.axis_size("prompt")
    chips = lax.axis_size("z")
    cores = lax.axis_size("core")
    responses, slots, width = queries.shape
    block = H * DH // n
    shape = jax.ShapeDtypeStruct

    outs = pl.pallas_call(
        lambda *refs: first_kernel(n, *refs),
        out_shape=[shape((block * (1 + responses) + 16, DH), BF16)] * n
        + [shape((8 * (responses + 1), slots), F32)]
        + [shape(queries.shape, BF16)] * 2,
        in_specs=[ANY] * 10,
        out_specs=[VMEM] * (n + 3),
        scratch_shapes=[
            pltpu.VMEM(keys.shape, BF16),
            pltpu.VMEM(values.shape, BF16),
            pltpu.VMEM(prompt_gates.shape, F32),
            pltpu.VMEM(resp_gates.shape, F32),
            pltpu.VMEM(loss_mask.shape, jnp.int32),
            pltpu.SMEM(group_ids.shape, jnp.int32),
            pltpu.SMEM(resp_lengths.shape, jnp.int32),
            pltpu.SMEM(advantages.shape, jnp.int32),
            pltpu.VMEM((H * (1 + responses), DH, DH), F32),
            pltpu.SemaphoreType.DMA((10,)),
        ],
        compiler_params=params(32),
        name="first",
    )(
        *[in_hbm(x) for x in (group_ids, resp_lengths, advantages, keys, values, prompt_gates, resp_gates)],
        *[in_hbm(x) for x in (loss_mask, queries, cotangent)],
    )
    msgs, (rows, queries, cotangent) = outs[:n], outs[n:]

    like = shape(queries.shape, F32)
    like_out = shape(queries.shape, BF16)

    held_shapes = [like, like] + [like_out] * 4 + [shape((8, 128), F32)]

    def first_sweep(units):
        outs = pl.pallas_call(
            lambda *refs: sweep_kernel(units, (), *refs[:5], None, *refs[5:8], refs[-1], *refs[8:-1]),
            out_shape=[shape((slots, 128), F32), like_out, like_out] + held_shapes,
            in_specs=[VMEM, VMEM, ANY, ANY, VMEM],
            out_specs=[VMEM] * 10,
            scratch_shapes=[pltpu.SemaphoreType.DMA((2 * responses,))],
            compiler_params=params(),
            name="sweep",
        )(rows, queries, in_hbm(resp_keys), in_hbm(resp_values), cotangent)
        return outs[0], outs[1], outs[2], outs[3:9], outs[9]

    def sweep(units, before, token, done=()):
        writes = len(done) > 0
        outs = pl.pallas_call(
            lambda *refs: sweep_kernel(units, done, *refs),
            out_shape=held_shapes + [like_out] * (2 * writes),
            in_specs=[VMEM] * 6 + [ANY] * 7,
            out_specs=[VMEM] * 7 + [ANY] * (2 * writes),
            scratch_shapes=[pltpu.SemaphoreType.DMA((2 * responses,))] * writes,
            input_output_aliases={7 + k: k for k in range(6)},
            compiler_params=params(),
            name="sweep",
        )(rows, queries, resp_keys, resp_values, cotangent, cols, token, *before)
        return (outs[:4] + outs[7:] if writes else outs[:6]), outs[6]

    units = [(r, h) for r in range(responses) for h in range(H)]
    got1 = far_first(exchange(msgs, "prompt"))
    cols, resp_keys, resp_values, held, token = first_sweep(units[:2])
    outs = pl.pallas_call(
        lambda *refs: second_kernel(n, chips, cores, *refs),
        out_shape=[shape(((1 + cores) * block, DH), BF16)] * chips + [shape((8, DH), F32)],
        in_specs=[VMEM] * n + [ANY],
        out_specs=[VMEM] * (chips + 1),
        scratch_shapes=[pltpu.VMEM((chips * cores, block, DH), F32)],
        compiler_params=params(),
        name="second",
    )(*got1, token)
    msgs, later = outs[:chips], outs[chips]
    got2 = exchange_ring(msgs, "z")
    held, token = sweep(units[2:5], held, later)
    sent, kept = pl.pallas_call(
        lambda *refs: swap_kernel(chips, *refs),
        out_shape=[shape(((chips + 1) * block, DH), BF16)] * 2,
        in_specs=[VMEM] * chips + [ANY],
        out_specs=[VMEM, VMEM],
        compiler_params=params(),
        name="swap",
    )(*got2, token)
    swapped = exchange([kept, sent], "core")[1]
    msgs = pl.pallas_call(
        lambda *refs: third_kernel(n, chips, *refs),
        out_shape=[shape(((responses + 1) * block, DH), BF16)] * n,
        in_specs=[VMEM] * (n + 2) + [ANY],
        out_specs=[VMEM] * n,
        compiler_params=params(),
        name="third",
    )(*got1, kept, swapped, token)
    got3 = exchange(msgs, "prompt")
    held, token = sweep(units[5:], held, msgs[0], range(responses - 2))
    partial_out, partial_dq, query, grad_out, resp_dk, resp_dv = held

    resp_out, resp_dq, prompt_dk, prompt_dv = pl.pallas_call(
        lambda *refs: last_kernel(n, responses, *refs),
        out_shape=[like_out] * 2 + [shape(keys.shape, BF16)] * 2,
        in_specs=[VMEM] * (8 + n) + [ANY],
        out_specs=[ANY] * 4,
        scratch_shapes=[
            pltpu.VMEM((responses + 1, width, width), BF16),
            pltpu.VMEM(queries.shape, BF16),
            pltpu.VMEM(queries.shape, BF16),
            pltpu.VMEM(keys.shape[1:], BF16),
            pltpu.VMEM(keys.shape[1:], BF16),
            pltpu.SemaphoreType.DMA((2 + 2 * responses,)),
        ],
        compiler_params=params(),
        name="last",
    )(cols, query, grad_out, partial_out, partial_dq, keys, values, later, *got3, token)
    return (resp_out, resp_dq, resp_dk, resp_dv, prompt_dk, prompt_dv)


def solution(mesh):
    n, count = mesh.shape["prompt"], mesh.shape["resp"]
    mesh = jax.sharding.Mesh(mesh.devices.reshape(n, count // 2, 2), ("prompt", "z", "core"))
    spread = P(("prompt", "z", "core"))
    three = P(("prompt", "z", "core"), None, None)
    two = P(("prompt", "z", "core"), None)
    prompt = P(("z", "core"), "prompt", None)
    return jax.shard_map(
        shards,
        mesh=mesh,
        in_specs=(
            prompt,
            prompt,
            P(("z", "core"), None, "prompt"),
            three,
            three,
            three,
            three,
            three,
            spread,
            two,
            two,
            spread,
        ),
        out_specs=(three, three, three, three, prompt, prompt),
        check_vma=False,
    )
```
